32 devices in a mesh: shard: 4 (over z), ctx: 4 (over y, x), tp: 2 (over core).
Axes of the slice: x: 2, y: 2, z: 4, core: 2. Of those that a mesh axis runs over, the one named last changes fastest.
Arguments:
- tokens: bfloat16 [8, 1024, 768], P('shard', 'ctx'), may hold values from -6 to 6
- lengths: int32 [8], P('shard'), may hold values from 256 to 1024, as said below
- norm1_gain: bfloat16 [768], P('shard'), may hold values from 0.5 to 1.5
- qkv_weight: bfloat16 [768, 3, 768], P('shard', None, 'tp'), may hold values from -0.21875 to 0.21875
- lr_weight: bfloat16 [768, 12], P('shard', 'tp'), may hold values from -0.4375 to 0.4375
- inner_w1: bfloat16 [12, 64, 256], P('tp', None, 'shard'), may hold values from -0.75 to 0.75
- inner_b1: bfloat16 [12, 256], P('tp', 'shard'), may hold values from -4 to 4
- inner_w2: bfloat16 [12, 64, 256], P('tp', None, 'shard'), may hold values from -0.375 to 0.375
- inner_b2: bfloat16 [12, 64], P('tp', 'shard'), may hold values from -4 to 4
- post_gain: bfloat16 [12, 64], P('tp', 'shard'), may hold values from 0.5 to 1.5
- post_bias: bfloat16 [12, 64], P('tp', 'shard'), may hold values from -4 to 4
- gate_weight: bfloat16 [768, 768], P('shard', 'tp'), may hold values from -0.21875 to 0.21875
- out_weight: bfloat16 [768, 768], P('tp', 'shard'), may hold values from -0.21875 to 0.21875
- norm2_gain: bfloat16 [768], P('shard'), may hold values from 0.5 to 1.5
- ffn_gate: bfloat16 [768, 2048], P('shard', 'tp'), may hold values from -0.21875 to 0.21875
- ffn_up: bfloat16 [768, 2048], P('shard', 'tp'), may hold values from -0.21875 to 0.21875
- ffn_down: bfloat16 [2048, 768], P('tp', 'shard'), may hold values from -0.125 to 0.125
- cotangent: bfloat16 [8, 1024, 768], P('shard', 'ctx'), may hold values from -6 to 6
Outputs:
- output: bfloat16 [8, 1024, 768], P('shard', 'ctx')
- input_grad: bfloat16 [8, 1024, 768], P('shard', 'ctx')
- grad_norm1_gain: float32 [768], P('shard')
- grad_qkv_weight: float32 [768, 3, 768], P('shard', None, 'tp')
- grad_lr_weight: float32 [768, 12], P('shard', 'tp')
- grad_inner_w1: float32 [12, 64, 256], P('tp', None, 'shard')
- grad_inner_b1: float32 [12, 256], P('tp', 'shard')
- grad_inner_w2: float32 [12, 64, 256], P('tp', None, 'shard')
- grad_inner_b2: float32 [12, 64], P('tp', 'shard')
- grad_post_gain: float32 [12, 64], P('tp', 'shard')
- grad_post_bias: float32 [12, 64], P('tp', 'shard')
- grad_gate_weight: float32 [768, 768], P('shard', 'tp')
- grad_out_weight: float32 [768, 768], P('tp', 'shard')
- grad_norm2_gain: float32 [768], P('shard')
- grad_ffn_gate: float32 [768, 2048], P('shard', 'tp')
- grad_ffn_up: float32 [768, 2048], P('shard', 'tp')
- grad_ffn_down: float32 [2048, 768], P('tp', 'shard')
The draws below stay inside these ranges and needn't reach their ends.
Inputs may be any that keep to these rules, and one draw needn't show every extreme that they name: Slot b holds lengths[b] valid positions at its start and padding after them; in every draw some slot is full.
All inputs are finite; a program needn't handle non-finite values.
Results may differ from the reference program's by a relative error of at most 0.0085.
Values may be sent and summed in bfloat16 or wider, within the bound.
No kernel may reach another device: no remote copies, remote signals or barrier semaphores. Data moves between devices by JAX's collectives and lax.ppermute only.
A program may use at most 192 MiB of HBM per device.

```python
import jax
import jax.numpy as jnp
from jax import lax

D = 768
HEADS = 12
HD = 64
INNER = 256
FF = 2048
MINI = 16
BATCH = 8
SEQ = 1024


def draw_lengths(key, part):
    chosen = jax.random.randint(jax.random.fold_in(key, 11), (BATCH,), SEQ // 4, SEQ + 1)
    full_slot = jax.random.randint(jax.random.fold_in(key, 12), (), 0, BATCH)
    return jnp.where(jnp.arange(BATCH) == full_slot, SEQ, chosen).astype(jnp.int32)


def block_scale(own_key, extent, pieces, smallest, high):
    def one(dim, shards_of):
        steps = jax.random.uniform(jax.random.fold_in(jax.random.fold_in(own_key, 6), dim), (shards_of,), jnp.float32, smallest / len(pieces), high / len(pieces))
        return jnp.repeat(jnp.exp(steps), extent[dim] // shards_of).reshape((-1,) + (1,) * (len(extent) - dim - 1))

    level = one(*pieces[0])
    for cut in pieces[1:]:
        level = level * one(*cut)
    return level


def gaussian(key, shape, deviation, bound, shards=(), held_as=jnp.bfloat16):
    values = jax.random.normal(key, shape, jnp.float32) * deviation
    if len(shards) > 0:
        values = block_scale(key, shape, shards, -0.22, 0.18) * values
    return jnp.clip(values, min=-bound, max=bound).astype(held_as)


def setup_inputs(seed: int = 0) -> dict:
    arg_keys = jax.random.split(jax.random.key(seed), 19)
    return {
        "tokens": gaussian(arg_keys[0], (BATCH, SEQ, D), 1.0, 6.0, ((0, 4), (1, 4))),
        "lengths": draw_lengths(jax.random.fold_in(arg_keys[18], 71), 0),
        "norm1_gain": jnp.clip(1.0 + 0.1 * jax.random.normal(arg_keys[2], (D,), jnp.float32), 0.5, 1.5).astype(jnp.bfloat16),
        "qkv_weight": gaussian(arg_keys[3], (D, 3, HEADS * HD), D ** -0.5, 0.21875, ((0, 4), (2, 2))),
        "lr_weight": gaussian(arg_keys[4], (D, HEADS), (D // 4) ** -0.5, 0.4375, ((0, 4), (1, 2))),
        "inner_w1": gaussian(arg_keys[5], (HEADS, HD, INNER), HD ** -0.5, 0.75, ((0, 2), (2, 4))),
        "inner_b1": gaussian(arg_keys[6], (HEADS, INNER), 0.3, 4.0, ((0, 2), (1, 4))),
        "inner_w2": gaussian(arg_keys[7], (HEADS, HD, INNER), INNER ** -0.5, 0.375, ((0, 2), (2, 4))),
        "inner_b2": gaussian(arg_keys[8], (HEADS, HD), 0.3, 4.0, ((0, 2), (1, 4))),
        "post_gain": jnp.clip(1.0 + 0.1 * jax.random.normal(arg_keys[9], (HEADS, HD), jnp.float32), 0.5, 1.5).astype(jnp.bfloat16),
        "post_bias": gaussian(arg_keys[10], (HEADS, HD), 0.3, 4.0, ((0, 2), (1, 4))),
        "gate_weight": gaussian(arg_keys[11], (D, HEADS * HD), D ** -0.5, 0.21875, ((0, 4), (1, 2))),
        "out_weight": gaussian(arg_keys[12], (HEADS * HD, D), (HEADS * HD) ** -0.5, 0.21875, ((0, 2), (1, 4))),
        "norm2_gain": jnp.clip(1.0 + 0.1 * jax.random.normal(arg_keys[13], (D,), jnp.float32), 0.5, 1.5).astype(jnp.bfloat16),
        "ffn_gate": gaussian(arg_keys[14], (D, FF), D ** -0.5, 0.21875, ((0, 4), (1, 2))),
        "ffn_up": gaussian(arg_keys[15], (D, FF), D ** -0.5, 0.21875, ((0, 4), (1, 2))),
        "ffn_down": gaussian(arg_keys[16], (FF, D), FF ** -0.5, 0.125, ((0, 2), (1, 4))),
        "cotangent": gaussian(arg_keys[17], (BATCH, SEQ, D), 1.0, 6.0, ((0, 4), (1, 4))),
    }


EPSILON = 1e-06
ETA_BASE = 0.5
HIGHEST = lax.Precision.HIGHEST

@jax.custom_vjp
def low(v):
    return lax.optimization_barrier(v.astype(jnp.bfloat16)).astype(jnp.float32)

@jax.custom_vjp
def low_back(v):
    return v

def low_keep(v):
    return (low(v), None)

def low_pass(kept, grad):
    return (grad,)

def back_keep(v):
    return (v, None)

def back_low(kept, grad):
    return (low(grad),)
low.defvjp(low_keep, low_pass)
low_back.defvjp(back_keep, back_low)

def gelu(value):
    return jax.nn.gelu(value, approximate=False)

def gelu_slope(value):
    return 0.5 * (1.0 + lax.erf(value * 0.7071067811865476)) + value * jnp.exp(-0.5 * value * value) * 0.3989422804014327

def contract(form, left, right):
    return jnp.einsum(form, left, right, precision=HIGHEST)

def inner_step(state, block):
    first, first_bias, second, second_bias = state
    queries, keys, values, rates = block
    width = queries.shape[-2]
    row_index = lax.broadcasted_iota(jnp.int32, (width, width), 0)
    col_index = lax.broadcasted_iota(jnp.int32, (width, width), 1)
    scale = jnp.where(col_index <= row_index, 1.0 / (row_index + 1).astype(jnp.float32), 0.0)
    mix_rate = scale * rates[..., None, :]
    key_pre = contract('...bi,...ij->...bj', keys, first) + first_bias[..., None, :]
    key_act = gelu(key_pre)
    key_out = contract('...bj,...oj->...bo', key_act, second) + second_bias[..., None, :]
    grad_two = key_out + keys - values
    grad_one = contract('...bo,...oj->...bj', grad_two, second) * gelu_slope(key_pre)
    mix_one = mix_rate * (contract('...ti,...si->...ts', queries, keys) + 1.0)
    query_pre = contract('...ti,...ij->...tj', queries, first) + first_bias[..., None, :] - contract('...ts,...sj->...tj', mix_one, grad_one)
    query_act = gelu(query_pre)
    mix_two = mix_rate * (contract('...tj,...sj->...ts', query_act, key_act) + 1.0)
    query_out = contract('...tj,...oj->...to', query_act, second) + second_bias[..., None, :] - contract('...ts,...so->...to', mix_two, grad_two)
    result = queries + query_out
    final_rate = rates[..., :, None] / width
    step_one = final_rate * grad_one
    step_two = final_rate * grad_two
    first = first - contract('...bi,...bj->...ij', keys, step_one)
    first_bias = first_bias - lax.optimization_barrier(jnp.sum(step_one, axis=-2))
    second = second - contract('...bo,...bj->...oj', step_two, key_act)
    second_bias = second_bias - lax.optimization_barrier(jnp.sum(step_two, axis=-2))
    return ((first, first_bias, second, second_bias), result)

def rms_norm(value, gain):
    return value * lax.rsqrt(lax.optimization_barrier(jnp.mean(value * value, axis=-1, keepdims=True)) + EPSILON) * gain

def head_norm(value, gain, bias):
    centered = value - lax.optimization_barrier(jnp.mean(value, axis=-1, keepdims=True))
    spread = lax.optimization_barrier(jnp.mean(centered * centered, axis=-1, keepdims=True))
    return centered * lax.rsqrt(spread + EPSILON) * gain + bias

def layer(inputs, live, params):
    gain_one, w_qkv, w_rate, init_first, init_first_bias, init_second, init_second_bias, norm_gain, norm_bias, w_gate, w_out, gain_two, w_ffn_gate, w_ffn_up, w_ffn_down = params
    count = inputs.shape[0]
    normed = low(rms_norm(inputs, gain_one))
    projected = low_back(jnp.einsum('gsd,dch->gsch', normed, w_qkv, precision=HIGHEST))
    projected = projected.reshape(count, SEQ, 3, HEADS, HD)
    rate_logit = low_back(jnp.einsum('gsd,dh->gsh', normed, w_rate, precision=HIGHEST))
    gate_pre = low_back(jnp.einsum('gsd,dh->gsh', normed, w_gate, precision=HIGHEST))
    eta = ETA_BASE / HD * jax.nn.sigmoid(rate_logit) * live[:, :, None]
    blocks_count = SEQ // MINI

    def to_blocks(value):
        return value.reshape(count, blocks_count, MINI, HEADS, HD).transpose(1, 0, 3, 2, 4)
    rate_blocks = eta.reshape(count, blocks_count, MINI, HEADS).transpose(1, 0, 3, 2)
    state = (jnp.broadcast_to(init_first, (count,) + init_first.shape), jnp.broadcast_to(init_first_bias, (count,) + init_first_bias.shape), jnp.broadcast_to(init_second, (count,) + init_second.shape), jnp.broadcast_to(init_second_bias, (count,) + init_second_bias.shape))
    _, results = lax.scan(jax.checkpoint(inner_step), state, (to_blocks(projected[:, :, 0]), to_blocks(projected[:, :, 1]), to_blocks(projected[:, :, 2]), rate_blocks))
    mixed = results.transpose(1, 0, 3, 2, 4).reshape(count, SEQ, HEADS, HD)
    normed_heads = head_norm(mixed, norm_gain, norm_bias).reshape(count, SEQ, HEADS * HD)
    post = low(gelu(gate_pre) * normed_heads)
    branch = low_back(jnp.einsum('gsh,hd->gsd', post, w_out, precision=HIGHEST))
    hidden = inputs + branch
    normed_two = low(rms_norm(hidden, gain_two))
    up_gate = low_back(jnp.einsum('gsd,df->gsf', normed_two, w_ffn_gate, precision=HIGHEST))
    up_lin = low_back(jnp.einsum('gsd,df->gsf', normed_two, w_ffn_up, precision=HIGHEST))
    act = low(jax.nn.silu(up_gate) * up_lin)
    feed = low_back(jnp.einsum('gsf,fd->gsd', act, w_ffn_down, precision=HIGHEST))
    return hidden + feed

def reference(tokens, lengths, norm1_gain, qkv_weight, lr_weight, inner_w1, inner_b1, inner_w2, inner_b2, post_gain, post_bias, gate_weight, out_weight, norm2_gain, ffn_gate, ffn_up, ffn_down, cotangent):
    params = tuple((p.astype(jnp.float32) for p in (norm1_gain, qkv_weight, lr_weight, inner_w1, inner_b1, inner_w2, inner_b2, post_gain, post_bias, gate_weight, out_weight, norm2_gain, ffn_gate, ffn_up, ffn_down)))
    slots = tokens.shape[0]
    group_size = 1
    for candidate in range(1, slots + 1):
        if slots % candidate == 0 and candidate * SEQ <= 4096:
            group_size = candidate
    groups = slots // group_size
    live_all = (lax.broadcasted_iota(jnp.int32, (slots, SEQ), 1) < lengths[:, None].astype(jnp.int32)).astype(jnp.float32)
    inputs = tokens.astype(jnp.float32).reshape(groups, group_size, SEQ, D)
    backs = (cotangent.astype(jnp.float32) * live_all[:, :, None]).reshape(groups, group_size, SEQ, D)
    lives = live_all.reshape(groups, group_size, SEQ)

    def one_group(totals, item):
        group_in, group_live, group_back = item
        result, pull = jax.vjp(lambda value, weights: layer(value, group_live, weights), group_in, params)
        grad_in, grad_params = pull(group_back)
        return (tuple((a + b for a, b in zip(totals, grad_params))), (result, grad_in))
    zeros = tuple((jnp.zeros_like(p) for p in params))
    totals, (results, grads_in) = lax.scan(one_group, zeros, (inputs, lives, backs))
    output = results.reshape(slots, SEQ, D).astype(jnp.bfloat16)
    input_grad = grads_in.reshape(slots, SEQ, D).astype(jnp.bfloat16)
    return (output, input_grad, totals[0], totals[1], totals[2], totals[3], totals[4], totals[5], totals[6], totals[7], totals[8], totals[9], totals[10], totals[11], totals[12], totals[13], totals[14])
```

```python
from functools import partial
import jax
import jax.numpy as jnp
from jax import lax
from jax.experimental import pallas as pl
from jax.experimental.pallas import tpu as pltpu
from jax.sharding import PartitionSpec as P

MINI = 16
EPSILON = 1e-06
ETA_BASE = 0.5
BF = jnp.bfloat16
F32 = jnp.float32


def mm(left, right):
    return lax.dot_general(left, right, (((1,), (0,)), ((), ())), preferred_element_type=F32)


def mm_nt(left, right):
    return lax.dot_general(left, right, (((1,), (1,)), ((), ())), preferred_element_type=F32)


def mm_tn(left, right):
    return lax.dot_general(left, right, (((0,), (0,)), ((), ())), preferred_element_type=F32)


def gelu_parts(value):
    cdf = 0.5 + 0.5 * lax.erf(value * 0.7071067811865476)
    pdf = jnp.exp(-0.5 * value * value) * 0.3989422804014327
    return cdf, pdf


def fwd_kernel(
    kq_ref, kmv_ref, qf_ref, aux_ref, w1i_ref, c1i_ref, w2i_ref, c2i_ref,
    mixed_ref, w1s_ref, w2s_ref, h_ref, r_ref, g1_ref, g2_ref, ga_ref, ug_ref, gp_ref,
    w1_ref, c1_ref, w2_ref, c2_ref, *, unroll,
):
    chains, group = kq_ref.shape[:2]

    @pl.when(pl.program_id(0) == 0)
    def _():
        w1_ref[...] = w1i_ref[...]
        c1_ref[...] = c1i_ref[...]
        w2_ref[...] = w2i_ref[...]
        c2_ref[...] = c2i_ref[...]

    every = range(chains)

    def step(j):
        kq = [kq_ref[i, j] for i in every]
        k = [kq[i][:MINI] for i in every]
        q = [kq[i][MINI:] for i in every]
        aux = [aux_ref[i, j] for i in every]
        mix = [aux[i][:, :MINI] for i in every]
        rate = [aux[i][:, MINI : MINI + 1] for i in every]
        kmv = [kmv_ref[i, j] for i in every]
        qf = [qf_ref[i, j] for i in every]
        w1 = [w1_ref[i] for i in every]
        w2 = [w2_ref[i] for i in every]
        c1 = [c1_ref[i] for i in every]
        c2 = [c2_ref[i] for i in every]
        w1b = [w1[i].astype(BF) for i in every]
        w2b = [w2[i].astype(BF) for i in every]
        both = [mm(kq[i], w1b[i]) + c1[i] for i in every]
        qk = [mm_nt(q[i], k[i]) for i in every]
        parts = [gelu_parts(both[i][:MINI]) for i in every]
        slope = [parts[i][0] + both[i][:MINI] * parts[i][1] for i in every]
        hb = [(both[i][:MINI] * parts[i][0]).astype(BF) for i in every]
        g2 = [mm_nt(hb[i], w2b[i]) + c2[i] + kmv[i] for i in every]
        g2b = [g2[i].astype(BF) for i in every]
        u = [mm(g2b[i], w2b[i]) for i in every]
        fg2 = [rate[i] * g2[i] for i in every]
        w2n = [w2[i] - mm_tn(fg2[i].astype(BF), hb[i]) for i in every]
        c2n = [c2[i] - jnp.sum(fg2[i], axis=0, keepdims=True) for i in every]
        g1 = [u[i] * slope[i] for i in every]
        fg1 = [rate[i] * g1[i] for i in every]
        w1n = [w1[i] - mm_tn(k[i], fg1[i].astype(BF)) for i in every]
        c1n = [c1[i] - jnp.sum(fg1[i], axis=0, keepdims=True) for i in every]
        g1b = [g1[i].astype(BF) for i in every]
        ug = [u[i] * (parts[i][1] * (2.0 - both[i][:MINI] * both[i][:MINI])) for i in every]
        s1 = [(mix[i] * (qk[i] + 1.0)).astype(BF) for i in every]
        pre = [both[i][MINI:] - mm(s1[i], g1b[i]) for i in every]
        parts_q = [gelu_parts(pre[i]) for i in every]
        gp = [parts_q[i][0] + pre[i] * parts_q[i][1] for i in every]
        rb = [(pre[i] * parts_q[i][0]).astype(BF) for i in every]
        s2 = [(mix[i] * (mm_nt(rb[i], hb[i]) + 1.0)).astype(BF) for i in every]
        mixed = [qf[i] + mm_nt(rb[i], w2b[i]) + c2[i] - mm(s2[i], g2b[i]) for i in every]
        for i in every:
            w1s_ref[i, j] = w1b[i]
            w2s_ref[i, j] = w2b[i]
            h_ref[i, j] = hb[i]
            r_ref[i, j] = rb[i]
            g1_ref[i, j] = g1b[i]
            g2_ref[i, j] = g2b[i]
            ga_ref[i, j] = slope[i]
            ug_ref[i, j] = ug[i]
            gp_ref[i, j] = gp[i]
            mixed_ref[i, j] = mixed[i]
            w1_ref[i] = w1n[i]
            w2_ref[i] = w2n[i]
            c1_ref[i] = c1n[i]
            c2_ref[i] = c2n[i]

    def body(turn, _):
        for within in range(unroll):
            step(turn * unroll + within)
        return 0

    lax.fori_loop(0, group // unroll, body, 0)


def bwd_kernel(
    d_ref, kq_ref, aux_ref, w1s_ref, w2s_ref, h_ref, r_ref, g1_ref, g2_ref, ga_ref, ug_ref, gp_ref,
    dq_ref, dk_ref, dv_ref, de_ref, dw1_ref, dc1_ref, dw2_ref, dc2_ref,
    *, unroll,
):
    chains, group = kq_ref.shape[:2]

    @pl.when(pl.program_id(0) == 0)
    def _():
        dw1_ref[...] = jnp.zeros_like(dw1_ref)
        dc1_ref[...] = jnp.zeros_like(dc1_ref)
        dw2_ref[...] = jnp.zeros_like(dw2_ref)
        dc2_ref[...] = jnp.zeros_like(dc2_ref)

    row = lax.broadcasted_iota(jnp.int32, (MINI, MINI), 0)
    col = lax.broadcasted_iota(jnp.int32, (MINI, MINI), 1)
    scale = jnp.where(col <= row, 1.0 / (row + 1).astype(F32), 0.0)
    eye = jnp.where(col == row, 1.0 / MINI, 0.0)

    every = range(chains)

    def step(j):
        def all_of(ref):
            return [ref[i, j] for i in every]

        d, kq, aux = all_of(d_ref), all_of(kq_ref), all_of(aux_ref)
        w1b, w2b, hb, rb, g1b, g2b = (
            all_of(ref) for ref in (w1s_ref, w2s_ref, h_ref, r_ref, g1_ref, g2_ref)
        )
        ga, ug, gp = all_of(ga_ref), all_of(ug_ref), all_of(gp_ref)
        dw1 = [dw1_ref[i] for i in every]
        dw2 = [dw2_ref[i] for i in every]
        dc1 = [dc1_ref[i] for i in every]
        dc2 = [dc2_ref[i] for i in every]
        k = [kq[i][:MINI] for i in every]
        q = [kq[i][MINI:] for i in every]
        mix = [aux[i][:, :MINI] for i in every]
        rate = [aux[i][:, MINI : MINI + 1] for i in every]
        g1 = [g1b[i].astype(F32) for i in every]
        g2 = [g2b[i].astype(F32) for i in every]
        dw1b = [dw1[i].astype(BF) for i in every]
        dw2b = [dw2[i].astype(BF) for i in every]
        t1 = [mm(k[i], dw1b[i]) + dc1[i] for i in every]
        t2 = [mm_nt(hb[i], dw2b[i]) + dc2[i] for i in every]
        db = [d[i].astype(BF) for i in every]
        ds2 = [-mm_nt(db[i], g2b[i]) for i in every]
        x2 = [mm_nt(rb[i], hb[i]) + 1.0 for i in every]
        x1 = [mm_nt(q[i], k[i]) + 1.0 for i in every]
        dx2 = [(ds2[i] * mix[i]).astype(BF) for i in every]
        dr = [mm(db[i], w2b[i]) + mm(dx2[i], hb[i]) for i in every]
        dp = [dr[i] * gp[i] for i in every]
        dpb = [dp[i].astype(BF) for i in every]
        dg1 = [-mm_tn((mix[i] * x1[i]).astype(BF), dpb[i]) - rate[i] * t1[i] for i in every]
        dub = [(dg1[i] * ga[i]).astype(BF) for i in every]
        dg2 = [
            mm_nt(dub[i], w2b[i]) - mm_tn((mix[i] * x2[i]).astype(BF), db[i]) - rate[i] * t2[i]
            for i in every
        ]
        dg2b = [dg2[i].astype(BF) for i in every]
        dh = [
            mm(dg2b[i], w2b[i]) + mm_tn(dx2[i], rb[i]) - mm((rate[i] * g2[i]).astype(BF), dw2b[i])
            for i in every
        ]
        da = [dg1[i] * ug[i] + dh[i] * ga[i] for i in every]
        dab = [da[i].astype(BF) for i in every]
        dw1n = [dw1[i] + mm_tn(kq[i], jnp.concatenate([dab[i], dpb[i]], axis=0)) for i in every]
        dc1n = [dc1[i] + jnp.sum(da[i] + dp[i], axis=0, keepdims=True) for i in every]
        dw2n = [
            dw2[i]
            + mm_tn(
                jnp.concatenate([db[i], dg2b[i], g2b[i]], axis=0),
                jnp.concatenate([rb[i], hb[i], dub[i]], axis=0),
            )
            for i in every
        ]
        dc2n = [dc2[i] + jnp.sum(d[i] + dg2[i], axis=0, keepdims=True) for i in every]
        ds1 = [-mm_nt(dpb[i], g1b[i]) for i in every]
        dx1 = [(ds1[i] * mix[i]).astype(BF) for i in every]
        dq = [d[i] + mm_nt(dpb[i], w1b[i]) + mm(dx1[i], k[i]) for i in every]
        dk = [
            dg2[i]
            - mm_nt((rate[i] * g1[i]).astype(BF), dw1b[i])
            + mm_tn(dx1[i], q[i])
            + mm_nt(dab[i], w1b[i])
            for i in every
        ]
        df = [
            -(
                jnp.sum(g1[i] * t1[i], axis=1, keepdims=True)
                + jnp.sum(g2[i] * t2[i], axis=1, keepdims=True)
            )
            for i in every
        ]
        de = [
            jnp.sum((ds2[i] * x2[i] + ds1[i] * x1[i]) * scale + eye * df[i], axis=0, keepdims=True)
            for i in every
        ]
        for i in every:
            dq_ref[i, j] = dq[i].astype(BF)
            dk_ref[i, j] = dk[i].astype(BF)
            dv_ref[i, j] = (-dg2[i]).astype(BF)
            de_ref[i, j] = de[i]
            dw1_ref[i] = dw1n[i]
            dc1_ref[i] = dc1n[i]
            dw2_ref[i] = dw2n[i]
            dc2_ref[i] = dc2n[i]

    def body(turn, _):
        for within in range(unroll):
            step(group - 1 - (turn * unroll + within))
        return 0

    lax.fori_loop(0, group // unroll, body, 0)


def run_fwd(kq, kmv, qf, aux, w1, c1, w2, c2, group=8, unroll=2):
    chains, count, _, hd = kq.shape
    inner = w1.shape[-1]
    steps = count // group

    def spec(rows, cols):
        return pl.BlockSpec((chains, group, rows, cols), lambda g: (0, g, 0, 0))

    def whole(rows, cols):
        return pl.BlockSpec((chains, rows, cols), lambda g: (0, 0, 0))

    def out(rows, cols, dtype):
        return jax.ShapeDtypeStruct((chains, count, rows, cols), dtype)

    return pl.pallas_call(
        partial(fwd_kernel, unroll=unroll),
        grid=(steps,),
        in_specs=[spec(2 * MINI, hd), spec(MINI, hd), spec(MINI, hd), spec(MINI, 128),
                  whole(hd, inner), whole(1, inner), whole(hd, inner), whole(1, hd)],
        out_specs=[spec(MINI, hd), spec(hd, inner), spec(hd, inner), spec(MINI, inner), spec(MINI, inner),
                   spec(MINI, inner), spec(MINI, hd), spec(MINI, inner), spec(MINI, inner), spec(MINI, inner)],
        out_shape=[out(MINI, hd, F32), out(hd, inner, BF), out(hd, inner, BF), out(MINI, inner, BF), out(MINI, inner, BF),
                   out(MINI, inner, BF), out(MINI, hd, BF), out(MINI, inner, F32), out(MINI, inner, F32), out(MINI, inner, F32)],
        scratch_shapes=[pltpu.VMEM((chains, hd, inner), F32), pltpu.VMEM((chains, 1, inner), F32),
                        pltpu.VMEM((chains, hd, inner), F32), pltpu.VMEM((chains, 1, hd), F32)],
        compiler_params=pltpu.CompilerParams(vmem_limit_bytes=48 << 20),
        cost_estimate=pl.CostEstimate(flops=60_000_000_000, bytes_accessed=40_000_000, transcendentals=0),
        name="chain_forward",
    )(kq, kmv, qf, aux, w1, c1, w2, c2)


def run_bwd(d, kq, aux, saved, group=8, unroll=2):
    chains, count, _, hd = kq.shape
    inner = saved[0].shape[-1]
    steps = count // group

    def spec(rows, cols):
        return pl.BlockSpec((chains, group, rows, cols), lambda g: (0, steps - 1 - g, 0, 0))

    def whole(rows, cols):
        return pl.BlockSpec((chains, rows, cols), lambda g: (0, 0, 0))

    def out(rows, cols, dtype):
        return jax.ShapeDtypeStruct((chains, count, rows, cols), dtype)

    def st(rows, cols):
        return jax.ShapeDtypeStruct((chains, rows, cols), F32)

    return pl.pallas_call(
        partial(bwd_kernel, unroll=unroll),
        grid=(steps,),
        in_specs=[spec(MINI, hd), spec(2 * MINI, hd), spec(MINI, 128), spec(hd, inner), spec(hd, inner),
                  spec(MINI, inner), spec(MINI, inner), spec(MINI, inner), spec(MINI, hd),
                  spec(MINI, inner), spec(MINI, inner), spec(MINI, inner)],
        out_specs=[spec(MINI, hd), spec(MINI, hd), spec(MINI, hd), spec(1, MINI),
                   whole(hd, inner), whole(1, inner), whole(hd, inner), whole(1, hd)],
        out_shape=[out(MINI, hd, BF), out(MINI, hd, BF), out(MINI, hd, BF), out(1, MINI, F32),
                   st(hd, inner), st(1, inner), st(hd, inner), st(1, hd)],
        compiler_params=pltpu.CompilerParams(vmem_limit_bytes=48 << 20),
        cost_estimate=pl.CostEstimate(flops=70_000_000_000, bytes_accessed=40_000_000, transcendentals=0),
        name="chain_backward",
    )(d, kq, aux, *saved)


def gelu(value):
    return jax.nn.gelu(value, approximate=False)


def gelu_slope(value):
    return (
        0.5 * (1.0 + lax.erf(value * 0.7071067811865476))
        + value * jnp.exp(-0.5 * value * value) * 0.3989422804014327
    )


def row_norm(value):
    return lax.rsqrt(jnp.mean(value * value, axis=-1, keepdims=True) + EPSILON)


def pieces_of(chains, depth, head_dim, inner_share, head_share):
    return (
        ("lr", (depth, chains)),
        ("w1", (chains, head_dim, inner_share)),
        ("w2", (chains, head_dim, inner_share)),
        ("b1", (chains, inner_share)),
        ("b2", (chains, head_share)),
        ("pg", (chains, head_share)),
        ("pb", (chains, head_share)),
        ("n1", (depth,)),
        ("n2", (depth,)),
    )


def size_of(shape):
    total = 1
    for extent in shape:
        total *= extent
    return total


def swap(value):
    return lax.ppermute(value, "tp", [(0, 1), (1, 0)])


def spread(value, axis):
    size = lax.axis_size(axis)
    me = lax.axis_index(axis)
    whole = lax.dynamic_update_index_in_dim(
        jnp.zeros((size,) + value.shape, value.dtype), value, me, 0
    )
    for bit in range(1, size):
        piece = lax.ppermute(value, axis, [(source, source ^ bit) for source in range(size)])
        whole = lax.dynamic_update_index_in_dim(whole, piece, me ^ bit, 0)
    return whole


def in_turn(first, second):
    return jnp.where(lax.axis_index("tp") == 0, jnp.stack([first, second]), jnp.stack([second, first]))


def on_device(
    tokens,
    lengths,
    norm1_gain,
    qkv_weight,
    lr_weight,
    inner_w1,
    inner_b1,
    inner_w2,
    inner_b2,
    post_gain,
    post_bias,
    gate_weight,
    out_weight,
    norm2_gain,
    ffn_gate,
    ffn_up,
    ffn_down,
    cotangent,
):
    micro, span, width = tokens.shape
    ring = lax.axis_size("ctx")
    shards = lax.axis_size("shard")
    pair = lax.axis_size("tp")
    place = lax.axis_index("ctx")
    core = lax.axis_index("tp")
    local_heads, head_dim, inner_share = inner_w1.shape
    head_share = inner_b2.shape[1]
    depth = norm1_gain.shape[0]
    inner = inner_share * shards
    total_heads = local_heads * pair
    chains = -(-total_heads // ring)
    span_all = ring * span
    count = span_all // MINI
    cols = chains * head_dim
    wide = 4 * cols

    row_tokens = lax.dynamic_index_in_dim(tokens, core, 0, keepdims=False)
    slot_tokens = spread(row_tokens, "ctx").reshape(span_all, width)

    first_head = jnp.minimum(place * chains, total_heads - chains)
    owner = first_head // local_heads
    local_first = first_head - owner * local_heads

    def of_heads(value, axis):
        return lax.dynamic_slice_in_dim(value, local_first, chains, axis)

    pieces = pieces_of(chains, depth, head_dim, inner_share, head_share)
    small_size = sum(size_of(shape) for _, shape in pieces)
    small_rows = -(-small_size // wide)
    small_rows = -(-(small_rows + depth) // 16) * 16 - depth
    half_rows = (small_rows + depth) // 2
    own = {
        "lr": of_heads(lr_weight, 1),
        "w1": of_heads(inner_w1, 0),
        "w2": of_heads(inner_w2, 0),
        "b1": of_heads(inner_b1, 0),
        "b2": of_heads(inner_b2, 0),
        "pg": of_heads(post_gain, 0),
        "pb": of_heads(post_bias, 0),
        "n1": norm1_gain,
        "n2": norm2_gain,
    }
    small = jnp.concatenate([own[name].reshape(-1) for name, _ in pieces])
    small = jnp.pad(small, (0, small_rows * wide - small_size)).reshape(small_rows, wide)
    qkv_heads = of_heads(qkv_weight.reshape(depth, 3, local_heads, head_dim), 2)
    gate_heads = of_heads(gate_weight.reshape(depth, local_heads, head_dim), 1)
    big = jnp.concatenate(
        [qkv_heads.reshape(depth, 3 * cols), gate_heads.reshape(depth, cols)], axis=1
    )
    packed = jnp.concatenate([big, small], axis=0)
    packed = jnp.where(core == owner, packed, swap(packed))
    packed = spread(lax.dynamic_slice_in_dim(packed, core * half_rows, half_rows, 0), "shard")
    packed = in_turn(packed, swap(packed))
    gathered = packed.transpose(1, 0, 2, 3).reshape(shards, depth + small_rows, wide)
    units = ffn_gate.shape[1]
    half_out = out_weight.shape[0]
    row_pack = jnp.concatenate([ffn_gate, ffn_up, ffn_down.T, out_weight.T], axis=1)
    part = depth // ring
    row_part = lax.dynamic_slice_in_dim(row_pack, place * part, part, 0)
    row_part, gathered = lax.optimization_barrier((row_part, gathered))
    row_part = spread(row_part, "shard")

    w_chain = gathered[:, :depth].reshape(width, wide)
    flat = gathered[:, depth:].reshape(shards, small_rows * wide)
    full = {}
    offset = 0
    for name, shape in pieces:
        full[name] = flat[:, offset : offset + size_of(shape)].reshape((shards,) + shape)
        offset += size_of(shape)
    w_rate = full["lr"].reshape(width, chains)
    gain_one = full["n1"].reshape(width).astype(F32)
    gain_two = full["n2"].reshape(width).astype(F32)

    def along(name):
        return jnp.moveaxis(full[name], 0, -2).reshape(full[name].shape[1:-1] + (-1,)).astype(F32)

    init_first, init_second = along("w1"), along("w2")
    init_first_bias, init_second_bias = along("b1"), along("b2")
    norm_gain, norm_bias = along("pg"), along("pb")

    slot_length = lax.dynamic_index_in_dim(lengths, core, 0, keepdims=False)
    live_all = (lax.iota(jnp.int32, span_all) < slot_length).astype(F32)
    slot_in = slot_tokens.astype(F32)
    unit_in = slot_in * row_norm(slot_in)
    normed_one = (unit_in * gain_one).astype(BF)
    projected = mm(normed_one, w_chain).reshape(span_all, 4, chains, head_dim).transpose(1, 2, 0, 3)
    queries, keys, values, gate_pre = (projected[i] for i in range(4))
    gate_rate = jax.nn.sigmoid(mm(normed_one, w_rate))
    eta = ETA_BASE / head_dim * gate_rate * live_all[:, None]
    eta_blocks = eta.T.reshape(chains, count, MINI)

    def blocks(value):
        return value.reshape(chains, count, MINI, value.shape[-1])

    row_index = lax.broadcasted_iota(jnp.int32, (MINI, MINI), 0)
    col_index = lax.broadcasted_iota(jnp.int32, (MINI, MINI), 1)
    scale = jnp.where(col_index <= row_index, 1.0 / (row_index + 1).astype(F32), 0.0)
    aux = jnp.concatenate(
        [
            scale * eta_blocks[:, :, None, :],
            eta_blocks[..., None] / MINI,
            jnp.zeros((chains, count, MINI, 128 - MINI - 1), F32),
        ],
        axis=-1,
    )
    kq = jnp.concatenate([blocks(keys), blocks(queries)], axis=2).astype(BF)
    kq, row_part = lax.optimization_barrier((kq, row_part))
    row_all = spread(row_part, "ctx")
    forward = run_fwd(
        kq,
        blocks(keys - values),
        blocks(queries),
        aux,
        init_first,
        init_first_bias[:, None],
        init_second,
        init_second_bias[:, None],
    )
    mixed, saved = forward[0].reshape(chains, span_all, head_dim), forward[1:]

    centered = mixed - jnp.mean(mixed, axis=-1, keepdims=True)
    scale_head = lax.rsqrt(jnp.mean(centered * centered, axis=-1, keepdims=True) + EPSILON)
    unit = centered * scale_head
    head_out = unit * norm_gain[:, None] + norm_bias[:, None]
    post_chain = (gelu(gate_pre) * head_out).astype(BF)

    def to_rows(value):
        return lax.all_to_all(value.reshape(ring, span, -1), "ctx", 0, 0)

    post = to_rows(post_chain.transpose(1, 0, 2).reshape(span_all, cols))
    post = post.transpose(1, 0, 2).reshape(span, ring * cols)[:, : total_heads * head_dim]

    w_own = row_all.transpose(1, 0, 2, 3).reshape(width, -1)
    w_other = swap(w_own)

    def split_up(value):
        return tuple(value[:, start : start + units] for start in range(0, 3 * units, units))

    halves = (split_up(w_own), split_up(w_other))
    w_out = jnp.concatenate(
        [
            jnp.where(core == 0, w_own[:, 3 * units :], w_other[:, 3 * units :]),
            jnp.where(core == 0, w_other[:, 3 * units :], w_own[:, 3 * units :]),
        ],
        axis=1,
    )
    row_in = row_tokens.astype(F32)
    hidden = row_in + mm_nt(post, w_out)
    scale_two = row_norm(hidden)
    normed_two = (hidden * scale_two * gain_two).astype(BF)
    position = place * span + lax.iota(jnp.int32, span)
    live = (position < slot_length).astype(F32)[:, None]
    cot = lax.dynamic_index_in_dim(cotangent, core, 0, keepdims=False)
    back = cot.astype(F32) * live
    back_low = back.astype(BF)
    feed = 0.0
    grad_two = 0.0
    sums = []
    for w_gate, w_up, w_down in halves:
        up_gate = mm(normed_two, w_gate)
        up_lin = mm(normed_two, w_up)
        gate = jax.nn.sigmoid(up_gate)
        act_low = (up_gate * gate * up_lin).astype(BF)
        feed = feed + mm_nt(act_low, w_down)
        grad_act = mm(back_low, w_down)
        grad_gate_low = (grad_act * up_lin * gate * (1.0 + up_gate * (1.0 - gate))).astype(BF)
        grad_lin_low = (grad_act * up_gate * gate).astype(BF)
        grad_two = grad_two + mm_nt(grad_gate_low, w_gate) + mm_nt(grad_lin_low, w_up)
        sums.append(
            [
                mm_tn(normed_two, grad_gate_low),
                mm_tn(normed_two, grad_lin_low),
                mm_tn(back_low, act_low),
            ]
        )
    output = (hidden + feed).astype(BF)
    lifted = grad_two * gain_two
    grad_hidden = (
        back
        + scale_two * lifted
        - hidden * scale_two**3 * jnp.mean(lifted * hidden, axis=-1, keepdims=True)
    )
    grad_gain_two = jnp.sum(grad_two * hidden * scale_two, axis=0)
    grad_hidden_low = grad_hidden.astype(BF)
    grad_post = mm(grad_hidden_low, w_out)

    grad_out = mm_tn(grad_hidden_low, post)
    grad_out_own = lax.dynamic_slice_in_dim(grad_out, core * half_out, half_out, 1)
    grad_out_other = lax.dynamic_slice_in_dim(grad_out, (1 - core) * half_out, half_out, 1)
    own_sum = jnp.concatenate(sums[0] + [grad_out_own], axis=1)
    other_sum = jnp.concatenate(sums[1] + [grad_out_other], axis=1).astype(BF)
    row_sum = (own_sum + swap(other_sum).astype(F32)).astype(BF)
    row_sum = lax.all_to_all(row_sum.reshape(shards * ring, part, -1), ("shard", "ctx"), 0, 0)

    grad_post = jnp.pad(grad_post.astype(BF), ((0, 0), (0, ring * cols - total_heads * head_dim)))
    grad_post = lax.all_to_all(grad_post.reshape(span, ring, cols).transpose(1, 0, 2), "ctx", 0, 0)
    grad_post = grad_post.reshape(span_all, chains, head_dim).transpose(1, 0, 2).astype(F32)
    grad_gate_pre = (grad_post * gelu_slope(gate_pre) * head_out).astype(BF)
    grad_head = grad_post * gelu(gate_pre)
    grad_norm_gain = jnp.sum(grad_head * unit, axis=1)
    grad_norm_bias = jnp.sum(grad_head, axis=1)
    lifted = grad_head * norm_gain[:, None]
    grad_mixed = scale_head * (
        lifted
        - jnp.mean(lifted, axis=-1, keepdims=True)
        - unit * jnp.mean(lifted * unit, axis=-1, keepdims=True)
    )
    grad_q, grad_k, grad_v, grad_eta, d_first, d_first_bias, d_second, d_second_bias = run_bwd(
        blocks(grad_mixed), kq, aux, saved
    )
    grad_eta = grad_eta.reshape(chains, span_all).T
    grad_rate = grad_eta * (ETA_BASE / head_dim) * gate_rate * (1.0 - gate_rate) * live_all[:, None]
    grad_rate_low = grad_rate.astype(BF)
    grad_all = jnp.stack(
        [value.reshape(chains, span_all, head_dim) for value in (grad_q, grad_k, grad_v, grad_gate_pre)]
    )
    grad_all = grad_all.transpose(2, 0, 1, 3).reshape(span_all, wide)
    back_part = mm_nt(grad_all, w_chain) + mm_nt(grad_rate_low, w_rate)
    grad_gain_one = jnp.sum(back_part * unit_in, axis=0)
    back_one = jnp.sum(to_rows(back_part.astype(BF)).astype(F32), axis=0)
    scale_one = row_norm(row_in)
    lifted = back_one * gain_one
    input_grad = (
        grad_hidden
        + scale_one * lifted
        - row_in * scale_one**3 * jnp.mean(lifted * row_in, axis=-1, keepdims=True)
    ).astype(BF)

    row_sum = spread(jnp.sum(row_sum.astype(F32), axis=0).astype(BF), "ctx")
    row_sum = row_sum.reshape(depth, -1).astype(F32)
    g_ffn_gate = row_sum[:, :units]
    g_ffn_up = row_sum[:, units : 2 * units]
    g_ffn_down = row_sum[:, 2 * units : 3 * units].T
    g_out = row_sum[:, 3 * units :].T

    grad_big = mm_tn(normed_one, grad_all)
    grad_lr = mm_tn(normed_one, grad_rate_low)

    def by_shard(value):
        split = value.reshape(value.shape[:-1] + (shards, -1))
        return jnp.moveaxis(split, -2, 0).reshape(shards, -1)

    flat = jnp.concatenate(
        [
            grad_lr.reshape(shards, -1),
            by_shard(d_first),
            by_shard(d_second),
            by_shard(d_first_bias),
            by_shard(d_second_bias),
            by_shard(grad_norm_gain),
            by_shard(grad_norm_bias),
            grad_gain_one.reshape(shards, -1),
            grad_gain_two.reshape(shards, -1),
        ],
        axis=1,
    )
    flat = jnp.pad(flat, ((0, 0), (0, small_rows * wide - small_size)))
    chain_sum = jnp.concatenate(
        [grad_big.reshape(shards, depth, wide), flat.reshape(shards, small_rows, wide)], axis=1
    ).astype(BF)
    kept_half = lax.dynamic_slice_in_dim(chain_sum, core * half_rows, half_rows, 1)
    sent_half = lax.dynamic_slice_in_dim(chain_sum, (1 - core) * half_rows, half_rows, 1)
    chain_sum = (kept_half.astype(F32) + swap(sent_half).astype(F32)).astype(BF)
    chain_sum = lax.all_to_all(chain_sum, "shard", 0, 0)
    chain_sum = spread(jnp.sum(chain_sum.astype(F32), axis=0).astype(BF), "ctx")
    chain_sum = in_turn(chain_sum, swap(chain_sum)).astype(F32)
    chain_sum = chain_sum.transpose(1, 0, 2, 3).reshape(ring, depth + small_rows, wide)
    places = local_heads // chains
    mine = lax.dynamic_slice_in_dim(chain_sum, core * places, places, 0)
    mine_big = mine[:, :depth].reshape(places, depth, 4, cols).transpose(1, 2, 0, 3)
    mine_big = mine_big.reshape(depth, 4, local_heads * head_dim)
    flat_all = chain_sum[:, depth:].reshape(ring, -1)
    flat_mine = mine[:, depth:].reshape(places, -1)
    parts = {}
    offset = 0
    for name, shape in pieces:
        source = flat_all if name in ("n1", "n2") else flat_mine
        parts[name] = source[:, offset : offset + size_of(shape)].reshape((source.shape[0],) + shape)
        offset += size_of(shape)

    def stacked(name):
        return parts[name].reshape((local_heads,) + parts[name].shape[2:])

    return (
        in_turn(output, swap(output)),
        in_turn(input_grad, swap(input_grad)),
        jnp.sum(parts["n1"], axis=0),
        mine_big[:, :3],
        parts["lr"].transpose(1, 0, 2).reshape(depth, local_heads),
        stacked("w1"),
        stacked("b1"),
        stacked("w2"),
        stacked("b2"),
        stacked("pg"),
        stacked("pb"),
        mine_big[:, 3],
        g_out,
        jnp.sum(parts["n2"], axis=0),
        g_ffn_gate,
        g_ffn_up,
        g_ffn_down,
    )


def solution(mesh):
    in_specs = (
        P("shard", "ctx", None),
        P("shard"),
        P("shard"),
        P("shard", None, "tp"),
        P("shard", "tp"),
        P("tp", None, "shard"),
        P("tp", "shard"),
        P("tp", None, "shard"),
        P("tp", "shard"),
        P("tp", "shard"),
        P("tp", "shard"),
        P("shard", "tp"),
        P("tp", "shard"),
        P("shard"),
        P("shard", "tp"),
        P("shard", "tp"),
        P("tp", "shard"),
        P("shard", "ctx", None),
    )
    out_specs = (
        P("shard", "ctx", None),
        P("shard", "ctx", None),
        P("shard"),
        P("shard", None, "tp"),
        P("shard", "tp"),
        P("tp", None, "shard"),
        P("tp", "shard"),
        P("tp", None, "shard"),
        P("tp", "shard"),
        P("tp", "shard"),
        P("tp", "shard"),
        P("shard", "tp"),
        P("tp", "shard"),
        P("shard"),
        P("shard", "tp"),
        P("shard", "tp"),
        P("tp", "shard"),
    )
    return jax.shard_map(
        on_device, mesh=mesh, in_specs=in_specs, out_specs=out_specs, check_vma=False
    )
```

```python
from functools import partial
import jax
import jax.numpy as jnp
from jax import lax
from jax.experimental import pallas as pl
from jax.experimental.pallas import tpu as pltpu
from jax.sharding import PartitionSpec as P

MINI = 16
EPSILON = 1e-06
ETA_BASE = 0.5
BF = jnp.bfloat16
F32 = jnp.float32


def mm(left, right):
    return lax.dot_general(left, right, (((1,), (0,)), ((), ())), preferred_element_type=F32)


def mm_nt(left, right):
    return lax.dot_general(left, right, (((1,), (1,)), ((), ())), preferred_element_type=F32)


def mm_tn(left, right):
    return lax.dot_general(left, right, (((0,), (0,)), ((), ())), preferred_element_type=F32)


def gelu_parts(value):
    cdf = 0.5 + 0.5 * lax.erf(value * 0.7071067811865476)
    pdf = jnp.exp(-0.5 * value * value) * 0.3989422804014327
    return cdf, pdf


def row_scale(value):
    return lax.rsqrt(jnp.mean(value * value, axis=-1, keepdims=True) + EPSILON)


def mini_scale():
    row = lax.broadcasted_iota(jnp.int32, (MINI, MINI), 0)
    col = lax.broadcasted_iota(jnp.int32, (MINI, MINI), 1)
    return row, col, jnp.where(col <= row, 1.0 / (row + 1).astype(F32), 0.0)


def fwd_kernel(
    length_ref, x_ref, gain_ref, wc_ref, lr_ref, lrt_ref, w1i_ref, c1i_ref, w2i_ref, c2i_ref, pg_ref, pb_ref,
    post_ref, kq_ref, mix_ref, rate_ref, fac_ref, gl_ref, gs_ref, unit_ref, hscale_ref,
    w1s_ref, w2s_ref, h_ref, r_ref, g1_ref, g2_ref, ga_ref, ug_ref, gp_ref,
    w1_ref, c1_ref, w2_ref, c2_ref, kmv_ref, qf_ref, s1_ref, mixed_ref, *, first, unroll,
):
    chains, group = kq_ref.shape[:2]
    rows = group * MINI
    head_dim = kq_ref.shape[-1]
    cols = chains * head_dim

    @pl.when(pl.program_id(0) == 0)
    def _():
        w1_ref[...] = w1i_ref[...]
        c1_ref[...] = c1i_ref[...]
        w2_ref[...] = w2i_ref[...]
        c2_ref[...] = c2i_ref[...]

    start = (first + pl.program_id(0)) * rows
    x = x_ref[...].astype(F32)
    normed = (x * row_scale(x) * gain_ref[...]).astype(BF)
    proj = mm(normed, wc_ref[...])
    length = length_ref[0]
    live_col = start + lax.broadcasted_iota(jnp.int32, (rows, 128), 0) < length
    live_row = start + lax.broadcasted_iota(jnp.int32, (lrt_ref.shape[0], rows), 1) < length
    eta_col = jnp.where(live_col, jax.nn.sigmoid(mm(normed, lr_ref[...])), 0.0) * (ETA_BASE / head_dim)
    rate = jax.nn.sigmoid(mm_nt(lrt_ref[...], normed))
    eta_row = jnp.where(live_row, rate, 0.0) * (ETA_BASE / head_dim)
    fac_ref[0] = eta_row * (1.0 - rate)
    scale = mini_scale()[2]
    for i in range(chains):
        at = i * head_dim
        q = proj[:, at : at + head_dim]
        k = proj[:, cols + at : cols + at + head_dim]
        v = proj[:, 2 * cols + at : 2 * cols + at + head_dim]
        kb, qb = k.astype(BF), q.astype(BF)
        kq_ref[i, :, :MINI] = kb.reshape(group, MINI, head_dim)
        kq_ref[i, :, MINI:] = qb.reshape(group, MINI, head_dim)
        kmv_ref[i] = (k - v).reshape(group, MINI, head_dim)
        qf_ref[i] = q.reshape(group, MINI, head_dim)
        rate_ref[i] = (eta_col[:, i : i + 1] * (1.0 / MINI)).reshape(group, MINI, 1)
        cross = mm_nt(qb, kb) + 1.0
        for j in range(group):
            piece = slice(j * MINI, j * MINI + MINI)
            mix = scale * eta_row[i : i + 1, piece]
            mix_ref[i, j] = mix
            s1_ref[i, j] = (mix * cross[piece, piece]).astype(BF)

    every = range(chains)

    def step(j):
        kq = [kq_ref[i, j] for i in every]
        k = [kq[i][:MINI] for i in every]
        mix = [mix_ref[i, j] for i in every]
        rate = [rate_ref[i, j] for i in every]
        s1 = [s1_ref[i, j] for i in every]
        kmv = [kmv_ref[i, j] for i in every]
        qf = [qf_ref[i, j] for i in every]
        w1 = [w1_ref[i] for i in every]
        w2 = [w2_ref[i] for i in every]
        c1 = [c1_ref[i] for i in every]
        c2 = [c2_ref[i] for i in every]
        w1b = [w1[i].astype(BF) for i in every]
        w2b = [w2[i].astype(BF) for i in every]
        both = [mm(kq[i], w1b[i]) + c1[i] for i in every]
        parts = [gelu_parts(both[i][:MINI]) for i in every]
        slope = [parts[i][0] + both[i][:MINI] * parts[i][1] for i in every]
        hb = [(both[i][:MINI] * parts[i][0]).astype(BF) for i in every]
        g2 = [mm_nt(hb[i], w2b[i]) + c2[i] + kmv[i] for i in every]
        g2b = [g2[i].astype(BF) for i in every]
        u = [mm(g2b[i], w2b[i]) for i in every]
        fg2 = [rate[i] * g2[i] for i in every]
        w2n = [w2[i] - mm_tn(fg2[i].astype(BF), hb[i]) for i in every]
        c2n = [c2[i] - jnp.sum(fg2[i], axis=0, keepdims=True) for i in every]
        g1 = [u[i] * slope[i] for i in every]
        fg1 = [rate[i] * g1[i] for i in every]
        w1n = [w1[i] - mm_tn(k[i], fg1[i].astype(BF)) for i in every]
        c1n = [c1[i] - jnp.sum(fg1[i], axis=0, keepdims=True) for i in every]
        g1b = [g1[i].astype(BF) for i in every]
        ug = [u[i] * (parts[i][1] * (2.0 - both[i][:MINI] * both[i][:MINI])) for i in every]
        pre = [both[i][MINI:] - mm(s1[i], g1b[i]) for i in every]
        parts_q = [gelu_parts(pre[i]) for i in every]
        gp = [parts_q[i][0] + pre[i] * parts_q[i][1] for i in every]
        rb = [(pre[i] * parts_q[i][0]).astype(BF) for i in every]
        s2 = [(mix[i] * (mm_nt(rb[i], hb[i]) + 1.0)).astype(BF) for i in every]
        mixed = [qf[i] + mm_nt(rb[i], w2b[i]) + c2[i] - mm(s2[i], g2b[i]) for i in every]
        for i in every:
            w1s_ref[i, j] = w1b[i]
            w2s_ref[i, j] = w2b[i]
            h_ref[i, j] = hb[i]
            r_ref[i, j] = rb[i]
            g1_ref[i, j] = g1b[i]
            g2_ref[i, j] = g2b[i]
            ga_ref[i, j] = slope[i]
            ug_ref[i, j] = ug[i]
            gp_ref[i, j] = gp[i]
            mixed_ref[i, j] = mixed[i]
            w1_ref[i] = w1n[i]
            w2_ref[i] = w2n[i]
            c1_ref[i] = c1n[i]
            c2_ref[i] = c2n[i]

    def body(turn, _):
        for within in range(unroll):
            step(turn * unroll + within)
        return 0

    lax.fori_loop(0, group // unroll, body, 0)

    for i in range(chains):
        at = i * head_dim
        gate = proj[:, 3 * cols + at : 3 * cols + at + head_dim]
        mixed = mixed_ref[i].reshape(rows, head_dim)
        centered = mixed - jnp.mean(mixed, axis=-1, keepdims=True)
        hscale = row_scale(centered)
        unit = centered * hscale
        out = unit * pg_ref[i] + pb_ref[i]
        cdf, pdf = gelu_parts(gate)
        post_ref[:, at : at + head_dim] = (gate * cdf * out).astype(BF)
        gl_ref[i] = gate * cdf
        gs_ref[i] = (cdf + gate * pdf) * out
        unit_ref[i] = unit
        hscale_ref[i] = hscale


def bwd_kernel(
    x_ref, gain_ref, wc_ref, lrt_ref, pg_ref, gpost_ref, w1i_ref, c1i_ref, w2i_ref, c2i_ref,
    kq_ref, mix_ref, rate_ref, fac_ref, gl_ref, gs_ref, unit_ref, hscale_ref,
    w1s_ref, w2s_ref, h_ref, r_ref, g1_ref, g2_ref, ga_ref, ug_ref, gp_ref,
    back_ref, gw_ref, glr_ref, gain_grad_ref, gpg_ref, gpb_ref, dw1_ref, dc1_ref, dw2_ref, dc2_ref,
    d_ref, dq_ref, dk_ref, dv_ref, de_ref, all_ref, *, unroll,
):
    chains, group = kq_ref.shape[:2]
    rows = group * MINI
    head_dim = kq_ref.shape[-1]
    cols = chains * head_dim

    @pl.when(pl.program_id(0) == 0)
    def _():
        dw1_ref[...] = w1i_ref[...]
        dc1_ref[...] = c1i_ref[...]
        dw2_ref[...] = w2i_ref[...]
        dc2_ref[...] = c2i_ref[...]
        gw_ref[...] = jnp.zeros_like(gw_ref)
        glr_ref[...] = jnp.zeros_like(glr_ref)
        gain_grad_ref[...] = jnp.zeros_like(gain_grad_ref)
        gpg_ref[...] = jnp.zeros_like(gpg_ref)
        gpb_ref[...] = jnp.zeros_like(gpb_ref)

    row, col, scale = mini_scale()
    eye = jnp.where(col == row, 1.0 / MINI, 0.0)
    gpost = gpost_ref[...].astype(F32)
    for i in range(chains):
        at = i * head_dim
        piece = gpost[:, at : at + head_dim]
        all_ref[:, 3 * cols + at : 3 * cols + at + head_dim] = (piece * gs_ref[i]).astype(BF)
        head = piece * gl_ref[i]
        unit = unit_ref[i]
        gpg_ref[i] += jnp.sum(head * unit, axis=0, keepdims=True)
        gpb_ref[i] += jnp.sum(head, axis=0, keepdims=True)
        lifted = head * pg_ref[i]
        grad = hscale_ref[i] * (
            lifted
            - jnp.mean(lifted, axis=-1, keepdims=True)
            - unit * jnp.mean(lifted * unit, axis=-1, keepdims=True)
        )
        d_ref[i] = grad.reshape(group, MINI, head_dim)

    every = range(chains)

    def step(j):
        def all_of(ref):
            return [ref[i, j] for i in every]

        d, kq = all_of(d_ref), all_of(kq_ref)
        w1b, w2b, hb, rb, g1b, g2b = (
            all_of(ref) for ref in (w1s_ref, w2s_ref, h_ref, r_ref, g1_ref, g2_ref)
        )
        ga, ug, gp = all_of(ga_ref), all_of(ug_ref), all_of(gp_ref)
        dw1 = [dw1_ref[i] for i in every]
        dw2 = [dw2_ref[i] for i in every]
        dc1 = [dc1_ref[i] for i in every]
        dc2 = [dc2_ref[i] for i in every]
        k = [kq[i][:MINI] for i in every]
        q = [kq[i][MINI:] for i in every]
        mix, rate = all_of(mix_ref), all_of(rate_ref)
        g1 = [g1b[i].astype(F32) for i in every]
        g2 = [g2b[i].astype(F32) for i in every]
        dw1b = [dw1[i].astype(BF) for i in every]
        dw2b = [dw2[i].astype(BF) for i in every]
        t1 = [mm(k[i], dw1b[i]) + dc1[i] for i in every]
        t2 = [mm_nt(hb[i], dw2b[i]) + dc2[i] for i in every]
        db = [d[i].astype(BF) for i in every]
        ds2 = [-mm_nt(db[i], g2b[i]) for i in every]
        x2 = [mm_nt(rb[i], hb[i]) + 1.0 for i in every]
        x1 = [mm_nt(q[i], k[i]) + 1.0 for i in every]
        dx2 = [(ds2[i] * mix[i]).astype(BF) for i in every]
        dr = [mm(db[i], w2b[i]) + mm(dx2[i], hb[i]) for i in every]
        dp = [dr[i] * gp[i] for i in every]
        dpb = [dp[i].astype(BF) for i in every]
        dg1 = [-mm_tn((mix[i] * x1[i]).astype(BF), dpb[i]) - rate[i] * t1[i] for i in every]
        dub = [(dg1[i] * ga[i]).astype(BF) for i in every]
        dg2 = [
            mm_nt(dub[i], w2b[i]) - mm_tn((mix[i] * x2[i]).astype(BF), db[i]) - rate[i] * t2[i]
            for i in every
        ]
        dg2b = [dg2[i].astype(BF) for i in every]
        dh = [
            mm(dg2b[i], w2b[i]) + mm_tn(dx2[i], rb[i]) - mm((rate[i] * g2[i]).astype(BF), dw2b[i])
            for i in every
        ]
        da = [dg1[i] * ug[i] + dh[i] * ga[i] for i in every]
        dab = [da[i].astype(BF) for i in every]
        dw1n = [dw1[i] + mm_tn(kq[i], jnp.concatenate([dab[i], dpb[i]], axis=0)) for i in every]
        dc1n = [dc1[i] + jnp.sum(da[i] + dp[i], axis=0, keepdims=True) for i in every]
        dw2n = [
            dw2[i]
            + mm_tn(
                jnp.concatenate([db[i], dg2b[i], g2b[i]], axis=0),
                jnp.concatenate([rb[i], hb[i], dub[i]], axis=0),
            )
            for i in every
        ]
        dc2n = [dc2[i] + jnp.sum(d[i] + dg2[i], axis=0, keepdims=True) for i in every]
        ds1 = [-mm_nt(dpb[i], g1b[i]) for i in every]
        dx1 = [(ds1[i] * mix[i]).astype(BF) for i in every]
        dq = [d[i] + mm_nt(dpb[i], w1b[i]) + mm(dx1[i], k[i]) for i in every]
        dk = [
            dg2[i]
            - mm_nt((rate[i] * g1[i]).astype(BF), dw1b[i])
            + mm_tn(dx1[i], q[i])
            + mm_nt(dab[i], w1b[i])
            for i in every
        ]
        df = [
            -(
                jnp.sum(g1[i] * t1[i], axis=1, keepdims=True)
                + jnp.sum(g2[i] * t2[i], axis=1, keepdims=True)
            )
            for i in every
        ]
        de = [
            jnp.sum((ds2[i] * x2[i] + ds1[i] * x1[i]) * scale + eye * df[i], axis=0, keepdims=True)
            for i in every
        ]
        for i in every:
            dq_ref[i, j] = dq[i].astype(BF)
            dk_ref[i, j] = dk[i].astype(BF)
            dv_ref[i, j] = (-dg2[i]).astype(BF)
            de_ref[i, j] = de[i]
            dw1_ref[i] = dw1n[i]
            dc1_ref[i] = dc1n[i]
            dw2_ref[i] = dw2n[i]
            dc2_ref[i] = dc2n[i]

    def body(turn, _):
        for within in range(unroll):
            step(group - 1 - (turn * unroll + within))
        return 0

    lax.fori_loop(0, group // unroll, body, 0)

    x = x_ref[...].astype(F32)
    unit_in = x * row_scale(x)
    normed = (unit_in * gain_ref[...]).astype(BF)
    lrt = lrt_ref[...]
    padded = lrt.shape[0]
    which = lax.broadcasted_iota(jnp.int32, (padded, rows), 0)
    rates = jnp.zeros((padded, rows), F32)
    for i in range(chains):
        at = i * head_dim
        all_ref[:, at : at + head_dim] = dq_ref[i].reshape(rows, head_dim)
        all_ref[:, cols + at : cols + at + head_dim] = dk_ref[i].reshape(rows, head_dim)
        all_ref[:, 2 * cols + at : 2 * cols + at + head_dim] = dv_ref[i].reshape(rows, head_dim)
        line = jnp.concatenate([de_ref[i, j] for j in range(group)], axis=1)
        rates = jnp.where(which == i, line, rates)
    rates = (rates * fac_ref[0]).astype(BF)
    grads = all_ref[...]
    back = mm_nt(grads, wc_ref[...]) + mm_tn(rates, lrt)
    gain_grad_ref[...] += jnp.sum(back * unit_in, axis=0, keepdims=True)
    back_ref[...] = back.astype(BF)
    gw_ref[...] += mm_tn(normed, grads)
    glr_ref[...] += mm(rates, normed)


GROUP = 8


def block_specs(chains, head_dim, inner, padded, place):
    rows = GROUP * MINI

    def mini(first, second):
        return pl.BlockSpec((chains, GROUP, first, second), lambda g: (0, place(g), 0, 0))

    def head(second):
        return pl.BlockSpec((chains, rows, second), lambda g: (0, place(g), 0))

    return [
        mini(2 * MINI, head_dim), mini(MINI, MINI), mini(MINI, 1),
        pl.BlockSpec((1, padded, rows), lambda g: (place(g), 0, 0)),
        head(head_dim), head(head_dim), head(head_dim), head(1),
        mini(head_dim, inner), mini(head_dim, inner), mini(MINI, inner), mini(MINI, inner),
        mini(MINI, inner), mini(MINI, head_dim), mini(MINI, inner), mini(MINI, inner), mini(MINI, inner),
    ]


def whole_spec(value):
    return pl.BlockSpec(value.shape, lambda g: (0,) * value.ndim)


def run_fwd(first, last, length, tokens, gain, wc, lr, lrt, pg, pb, state, unroll=2):
    width = tokens.shape[1]
    chains, head_dim, inner = state[0].shape
    rows = GROUP * MINI
    steps = last - first
    count = steps * GROUP
    padded = lrt.shape[0]

    def mini(first_size, second_size, dtype):
        return jax.ShapeDtypeStruct((chains, count, first_size, second_size), dtype)

    def head(second):
        return jax.ShapeDtypeStruct((chains, steps * rows, second), F32)

    row_spec = pl.BlockSpec((rows, width), lambda g: (first + g, 0))
    small = (gain, wc, lr, lrt, *state, pg, pb)
    return pl.pallas_call(
        partial(fwd_kernel, first=first, unroll=unroll),
        grid=(steps,),
        in_specs=[pl.BlockSpec(memory_space=pltpu.SMEM), row_spec] + [whole_spec(v) for v in small],
        out_specs=[pl.BlockSpec((rows, chains * head_dim), lambda g: (g, 0))]
        + block_specs(chains, head_dim, inner, padded, lambda g: g)
        + [whole_spec(v) for v in state],
        out_shape=[
            jax.ShapeDtypeStruct((steps * rows, chains * head_dim), BF),
            mini(2 * MINI, head_dim, BF), mini(MINI, MINI, F32), mini(MINI, 1, F32),
            jax.ShapeDtypeStruct((steps, padded, rows), F32),
            head(head_dim), head(head_dim), head(head_dim), head(1),
            mini(head_dim, inner, BF), mini(head_dim, inner, BF), mini(MINI, inner, BF), mini(MINI, inner, BF),
            mini(MINI, inner, BF), mini(MINI, head_dim, BF), mini(MINI, inner, F32), mini(MINI, inner, F32),
            mini(MINI, inner, F32),
        ]
        + [jax.ShapeDtypeStruct(v.shape, F32) for v in state],
        scratch_shapes=[
            pltpu.VMEM((chains, GROUP, MINI, head_dim), F32), pltpu.VMEM((chains, GROUP, MINI, head_dim), F32),
            pltpu.VMEM((chains, GROUP, MINI, MINI), BF), pltpu.VMEM((chains, GROUP, MINI, head_dim), F32),
        ],
        compiler_params=pltpu.CompilerParams(vmem_limit_bytes=50 << 20),
        cost_estimate=pl.CostEstimate(
            flops=9_000_000_000 * steps, bytes_accessed=5_000_000 * steps, transcendentals=0
        ),
        name="chain_forward",
    )(length, tokens, *small)


def run_bwd(first, last, tokens, gain, wc, lrt, pg, gpost, state, saved, unroll=2):
    width = tokens.shape[1]
    chains, head_dim, inner = state[0].shape
    rows = GROUP * MINI
    padded = lrt.shape[0]
    wide = wc.shape[1]
    steps = last - first

    def place(g):
        return steps - 1 - g

    def shape(*extent):
        return jax.ShapeDtypeStruct(extent, F32)

    small = (gain, wc, lrt, pg)
    outs = [
        shape(width, wide), shape(padded, width), shape(1, width), shape(chains, 1, head_dim), shape(chains, 1, head_dim),
        shape(chains, head_dim, inner), shape(chains, 1, inner), shape(chains, head_dim, inner), shape(chains, 1, head_dim),
    ]
    scratch = pltpu.VMEM((chains, GROUP, MINI, head_dim), BF)
    return pl.pallas_call(
        partial(bwd_kernel, unroll=unroll),
        grid=(steps,),
        in_specs=[pl.BlockSpec((rows, width), lambda g: (first + place(g), 0))]
        + [whole_spec(v) for v in small]
        + [pl.BlockSpec((rows, chains * head_dim), lambda g: (first + place(g), 0))]
        + [whole_spec(v) for v in state]
        + block_specs(chains, head_dim, inner, padded, place),
        out_specs=[pl.BlockSpec((rows, width), lambda g: (place(g), 0))] + [whole_spec(v) for v in outs],
        out_shape=[jax.ShapeDtypeStruct((steps * rows, width), BF)] + outs,
        scratch_shapes=[
            pltpu.VMEM((chains, GROUP, MINI, head_dim), F32), scratch, scratch, scratch,
            pltpu.VMEM((chains, GROUP, 1, MINI), F32), pltpu.VMEM((rows, wide), BF),
        ],
        compiler_params=pltpu.CompilerParams(vmem_limit_bytes=50 << 20),
        cost_estimate=pl.CostEstimate(
            flops=11_000_000_000 * steps, bytes_accessed=5_000_000 * steps, transcendentals=0
        ),
        name="chain_backward",
    )(tokens, *small, gpost, *state, *saved)


def row_norm(value):
    return lax.rsqrt(jnp.mean(value * value, axis=-1, keepdims=True) + EPSILON)


def pieces_of(chains, depth, head_dim, inner_share, head_share):
    return (
        ("lr", (depth, chains)),
        ("w1", (chains, head_dim, inner_share)),
        ("w2", (chains, head_dim, inner_share)),
        ("b1", (chains, inner_share)),
        ("b2", (chains, head_share)),
        ("pg", (chains, head_share)),
        ("pb", (chains, head_share)),
        ("n1", (depth,)),
        ("n2", (depth,)),
    )


def size_of(shape):
    total = 1
    for extent in shape:
        total *= extent
    return total


def swap(value):
    return lax.ppermute(value, "tp", [(0, 1), (1, 0)])


def place_kernel(spots_ref, *refs):
    *sources, target, sems = refs
    copies = [
        pltpu.make_async_copy(source, target.at[spots_ref[number]], sems.at[number])
        for number, source in enumerate(sources)
    ]
    for copy in copies:
        copy.start()
    for copy in copies:
        copy.wait()


def placed(pieces, spots):
    anywhere = pl.BlockSpec(memory_space=pl.ANY)
    return pl.pallas_call(
        place_kernel,
        in_specs=[pl.BlockSpec(memory_space=pltpu.SMEM)] + [anywhere] * len(pieces),
        out_specs=anywhere,
        out_shape=jax.ShapeDtypeStruct((len(pieces),) + pieces[0].shape, pieces[0].dtype),
        scratch_shapes=[pltpu.SemaphoreType.DMA((len(pieces),))],
        name="place_pieces",
    )(jnp.stack(spots).astype(jnp.int32), *pieces)


def exchanged(value, axis):
    size = lax.axis_size(axis)
    return [value] + [
        lax.ppermute(value, axis, [(source, source ^ bit) for source in range(size)])
        for bit in range(1, size)
    ]


def placed_along(pieces, axis):
    me = lax.axis_index(axis)
    return placed(pieces, [me ^ bit for bit in range(len(pieces))])


def spread(value, axis):
    return placed_along(exchanged(value, axis), axis)


def tied(*values):
    return lax.optimization_barrier(values)


def in_turn(first, second):
    return jnp.where(lax.axis_index("tp") == 0, jnp.stack([first, second]), jnp.stack([second, first]))


def on_device(
    tokens,
    lengths,
    norm1_gain,
    qkv_weight,
    lr_weight,
    inner_w1,
    inner_b1,
    inner_w2,
    inner_b2,
    post_gain,
    post_bias,
    gate_weight,
    out_weight,
    norm2_gain,
    ffn_gate,
    ffn_up,
    ffn_down,
    cotangent,
):
    micro, span, width = tokens.shape
    ring = lax.axis_size("ctx")
    shards = lax.axis_size("shard")
    pair = lax.axis_size("tp")
    place = lax.axis_index("ctx")
    core = lax.axis_index("tp")
    local_heads, head_dim, inner_share = inner_w1.shape
    head_share = inner_b2.shape[1]
    depth = norm1_gain.shape[0]
    inner = inner_share * shards
    total_heads = local_heads * pair
    chains = -(-total_heads // ring)
    span_all = ring * span
    count = span_all // MINI
    cols = chains * head_dim
    wide = 4 * cols

    row_tokens = lax.dynamic_index_in_dim(tokens, core, 0, keepdims=False)
    slot_tokens = spread(row_tokens, "ctx").reshape(span_all, width)

    first_head = jnp.minimum(place * chains, total_heads - chains)
    owner = first_head // local_heads
    local_first = first_head - owner * local_heads

    def of_heads(value, axis):
        return lax.dynamic_slice_in_dim(value, local_first, chains, axis)

    pieces = pieces_of(chains, depth, head_dim, inner_share, head_share)
    small_size = sum(size_of(shape) for _, shape in pieces)
    small_rows = -(-small_size // wide)
    small_rows = -(-(small_rows + depth) // 32) * 32 - depth
    half_rows = (small_rows + depth) // 2
    own = {
        "lr": of_heads(lr_weight, 1),
        "w1": of_heads(inner_w1, 0),
        "w2": of_heads(inner_w2, 0),
        "b1": of_heads(inner_b1, 0),
        "b2": of_heads(inner_b2, 0),
        "pg": of_heads(post_gain, 0),
        "pb": of_heads(post_bias, 0),
        "n1": norm1_gain,
        "n2": norm2_gain,
    }
    small = jnp.concatenate([own[name].reshape(-1) for name, _ in pieces])
    small = jnp.pad(small, (0, small_rows * wide - small_size)).reshape(small_rows, wide)
    qkv_heads = of_heads(qkv_weight.reshape(depth, 3, local_heads, head_dim), 2)
    gate_heads = of_heads(gate_weight.reshape(depth, local_heads, head_dim), 1)
    big = jnp.concatenate(
        [qkv_heads.reshape(depth, 3 * cols), gate_heads.reshape(depth, cols)], axis=1
    )
    packed = jnp.concatenate([big, small], axis=0)
    packed = jnp.where(core == owner, packed, swap(packed))
    packed = spread(lax.dynamic_slice_in_dim(packed, core * half_rows, half_rows, 0), "shard")
    packed = in_turn(packed, swap(packed))
    gathered = packed.transpose(1, 0, 2, 3).reshape(shards, depth + small_rows, wide)
    units = ffn_gate.shape[1]
    half_out = out_weight.shape[0]
    row_pack = jnp.concatenate([ffn_gate, ffn_up, ffn_down.T, out_weight.T], axis=1)
    part = depth // ring
    row_part = lax.dynamic_slice_in_dim(row_pack, place * part, part, 0)
    row_part, gathered = tied(row_part, gathered)
    row_parts = exchanged(row_part, "shard")

    w_chain = gathered[:, :depth].reshape(width, wide)
    flat = gathered[:, depth:].reshape(shards, small_rows * wide)
    full = {}
    offset = 0
    for name, shape in pieces:
        full[name] = flat[:, offset : offset + size_of(shape)].reshape((shards,) + shape)
        offset += size_of(shape)
    w_rate = full["lr"].reshape(width, chains)
    gain_one = full["n1"].reshape(width).astype(F32)
    gain_two = full["n2"].reshape(width).astype(F32)

    def along(name):
        return jnp.moveaxis(full[name], 0, -2).reshape(full[name].shape[1:-1] + (-1,)).astype(F32)

    init_first, init_second = along("w1"), along("w2")
    init_first_bias, init_second_bias = along("b1"), along("b2")
    norm_gain, norm_bias = along("pg"), along("pb")

    slot_length = lax.dynamic_index_in_dim(lengths, core, 0, keepdims=True)
    gain_row = gain_one[None]
    rate_cols = jnp.pad(w_rate, ((0, 0), (0, 128 - chains)))
    rate_rows = jnp.pad(w_rate.T, ((0, -chains % 16), (0, 0)))
    norm_gain, norm_bias = norm_gain[:, None], norm_bias[:, None]
    steps = span_all // (GROUP * MINI)
    middle = steps // 2
    state = (init_first, init_first_bias[:, None], init_second, init_second_bias[:, None])

    def forward(first, last, begin):
        done = run_fwd(
            first, last, slot_length, slot_tokens, gain_row, w_chain, rate_cols, rate_rows, norm_gain, norm_bias, begin
        )
        return done[0], done[1:-4], done[-4:]

    post_low, saved_low, state_low = forward(0, middle, state)
    state_low, row_parts = tied(state_low, row_parts)
    far = jnp.stack(row_parts[1:])
    state_low, far = tied(state_low, far)
    far_parts = exchanged(far, "ctx")
    post_high, saved_high, _ = forward(middle, steps, tuple(state_low))
    post_chain = jnp.concatenate([post_low, post_high])

    def to_rows(value):
        return lax.all_to_all(value.reshape(ring, span, -1), "ctx", 0, 0)

    post = to_rows(post_chain)
    post = post.transpose(1, 0, 2).reshape(span, ring * cols)[:, : total_heads * head_dim]

    far_parts, post = tied(far_parts, post)
    me = lax.axis_index("shard")
    blocks = [row_pack[start : start + part] for start in range(0, depth, part)]
    spots = [me * ring + number for number in range(ring)]
    for bit, group in enumerate(far_parts):
        for other in range(1, shards):
            blocks.append(group[other - 1])
            spots.append((me ^ other) * ring + (place ^ bit))
    w_own = placed(blocks, spots).reshape(width, -1)
    w_other = jnp.concatenate([swap(w_own[:, : 3 * units]), swap(w_own[:, 3 * units :])], axis=1)

    def split_up(value):
        return tuple(value[:, start : start + units] for start in range(0, 3 * units, units))

    halves = (split_up(w_own), split_up(w_other))
    w_out = jnp.concatenate(
        [
            jnp.where(core == 0, w_own[:, 3 * units :], w_other[:, 3 * units :]),
            jnp.where(core == 0, w_other[:, 3 * units :], w_own[:, 3 * units :]),
        ],
        axis=1,
    )
    row_in = row_tokens.astype(F32)
    hidden = row_in + mm_nt(post, w_out)
    scale_two = row_norm(hidden)
    normed_two = (hidden * scale_two * gain_two).astype(BF)
    position = place * span + lax.iota(jnp.int32, span)
    live = (position < slot_length[0]).astype(F32)[:, None]
    cot = lax.dynamic_index_in_dim(cotangent, core, 0, keepdims=False)
    back = cot.astype(F32) * live
    back_low = back.astype(BF)
    feed = 0.0
    grad_two = 0.0
    sums = []
    for w_gate, w_up, w_down in halves:
        up_gate = mm(normed_two, w_gate)
        up_lin = mm(normed_two, w_up)
        gate = jax.nn.sigmoid(up_gate)
        act_low = (up_gate * gate * up_lin).astype(BF)
        feed = feed + mm_nt(act_low, w_down)
        grad_act = mm(back_low, w_down)
        grad_gate_low = (grad_act * up_lin * gate * (1.0 + up_gate * (1.0 - gate))).astype(BF)
        grad_lin_low = (grad_act * up_gate * gate).astype(BF)
        grad_two = grad_two + mm_nt(grad_gate_low, w_gate) + mm_nt(grad_lin_low, w_up)
        sums.append(
            [
                mm_tn(normed_two, grad_gate_low),
                mm_tn(normed_two, grad_lin_low),
                mm_tn(back_low, act_low),
            ]
        )
    output = (hidden + feed).astype(BF)
    lifted = grad_two * gain_two
    grad_hidden = (
        back
        + scale_two * lifted
        - hidden * scale_two**3 * jnp.mean(lifted * hidden, axis=-1, keepdims=True)
    )
    grad_gain_two = jnp.sum(grad_two * hidden * scale_two, axis=0)
    grad_hidden_low = grad_hidden.astype(BF)
    grad_post = mm(grad_hidden_low, w_out)

    grad_out = mm_tn(grad_hidden_low, post)
    grad_out_own = lax.dynamic_slice_in_dim(grad_out, core * half_out, half_out, 1)
    grad_out_other = lax.dynamic_slice_in_dim(grad_out, (1 - core) * half_out, half_out, 1)
    own_sum = jnp.concatenate(sums[0] + [grad_out_own], axis=1)
    other_sum = jnp.concatenate(sums[1] + [grad_out_other], axis=1).astype(BF)
    row_sum = (own_sum + swap(other_sum).astype(F32)).astype(BF)
    row_sum = row_sum.reshape(shards, ring, part, -1).transpose(1, 0, 2, 3)
    cut = 2 * units
    sum_a = lax.all_to_all(row_sum[..., :cut], "ctx", 0, 0)
    sum_b = lax.all_to_all(row_sum[..., cut:], "ctx", 0, 0)

    def folded(value):
        return jnp.sum(value.astype(F32), axis=0).astype(BF)

    grad_post = jnp.pad(grad_post.astype(BF), ((0, 0), (0, ring * cols - total_heads * head_dim)))
    grad_post = lax.all_to_all(grad_post.reshape(span, ring, cols).transpose(1, 0, 2), "ctx", 0, 0)
    grad_post = grad_post.reshape(span_all, cols)

    def backward(first, last, begin, saved):
        done = run_bwd(
            first, last, slot_tokens, gain_row, w_chain, rate_rows, norm_gain, grad_post, begin, saved
        )
        return done[0], done[1:6], done[6:]

    begin = tuple(jnp.zeros_like(value) for value in state)
    grad_post, row_sum = tied(grad_post, row_sum)
    back_high, sums_high, ending = backward(middle, steps, begin, saved_high)
    ending, sum_a = tied(ending, sum_a)
    sum_a = folded(sum_a)
    ending, sum_a = tied(ending, sum_a)
    sum_a = lax.all_to_all(sum_a, "shard", 0, 0)
    back_low_half, sums_low, ending = backward(0, middle, tuple(ending), saved_low)
    ending, back_low_half, sum_a, sum_b = tied(ending, back_low_half, sum_a, sum_b)
    d_first, d_first_bias, d_second, d_second_bias = ending
    grad_big, grad_lr, grad_gain_one, grad_norm_gain, grad_norm_bias = (
        low + high for low, high in zip(sums_low, sums_high)
    )
    grad_lr = grad_lr[:chains].T
    back_part = jnp.concatenate([back_low_half, back_high])
    back_one = jnp.sum(to_rows(back_part).astype(F32), axis=0)
    scale_one = row_norm(row_in)
    lifted = back_one * gain_one
    input_grad = (
        grad_hidden
        + scale_one * lifted
        - row_in * scale_one**3 * jnp.mean(lifted * row_in, axis=-1, keepdims=True)
    ).astype(BF)

    sum_b = lax.all_to_all(folded(sum_b), "shard", 0, 0)
    row_sum = spread(jnp.concatenate([folded(sum_a), folded(sum_b)], axis=-1), "ctx")
    row_sum = row_sum.reshape(depth, -1).astype(F32)
    g_ffn_gate = row_sum[:, :units]
    g_ffn_up = row_sum[:, units : 2 * units]
    g_ffn_down = row_sum[:, 2 * units : 3 * units].T
    g_out = row_sum[:, 3 * units :].T


    def by_shard(value):
        split = value.reshape(value.shape[:-1] + (shards, -1))
        return jnp.moveaxis(split, -2, 0).reshape(shards, -1)

    flat = jnp.concatenate(
        [
            grad_lr.reshape(shards, -1),
            by_shard(d_first),
            by_shard(d_second),
            by_shard(d_first_bias[:, 0]),
            by_shard(d_second_bias[:, 0]),
            by_shard(grad_norm_gain[:, 0]),
            by_shard(grad_norm_bias[:, 0]),
            grad_gain_one.reshape(shards, -1),
            grad_gain_two.reshape(shards, -1),
        ],
        axis=1,
    )
    flat = jnp.pad(flat, ((0, 0), (0, small_rows * wide - small_size)))
    chain_sum = jnp.concatenate(
        [grad_big.reshape(shards, depth, wide), flat.reshape(shards, small_rows, wide)], axis=1
    ).astype(BF)
    kept_half = lax.dynamic_slice_in_dim(chain_sum, core * half_rows, half_rows, 1)
    sent_half = lax.dynamic_slice_in_dim(chain_sum, (1 - core) * half_rows, half_rows, 1)
    chain_sum = (kept_half.astype(F32) + swap(sent_half).astype(F32)).astype(BF)
    chain_sum = lax.all_to_all(chain_sum, "shard", 0, 0)
    chain_sum = spread(jnp.sum(chain_sum.astype(F32), axis=0).astype(BF), "ctx")
    chain_sum = in_turn(chain_sum, swap(chain_sum)).astype(F32)
    chain_sum = chain_sum.transpose(1, 0, 2, 3).reshape(ring, depth + small_rows, wide)
    places = local_heads // chains
    mine = lax.dynamic_slice_in_dim(chain_sum, core * places, places, 0)
    mine_big = mine[:, :depth].reshape(places, depth, 4, cols).transpose(1, 2, 0, 3)
    mine_big = mine_big.reshape(depth, 4, local_heads * head_dim)
    flat_all = chain_sum[:, depth:].reshape(ring, -1)
    flat_mine = mine[:, depth:].reshape(places, -1)
    parts = {}
    offset = 0
    for name, shape in pieces:
        source = flat_all if name in ("n1", "n2") else flat_mine
        parts[name] = source[:, offset : offset + size_of(shape)].reshape((source.shape[0],) + shape)
        offset += size_of(shape)

    def stacked(name):
        return parts[name].reshape((local_heads,) + parts[name].shape[2:])

    return (
        in_turn(output, swap(output)),
        in_turn(input_grad, swap(input_grad)),
        jnp.sum(parts["n1"], axis=0),
        mine_big[:, :3],
        parts["lr"].transpose(1, 0, 2).reshape(depth, local_heads),
        stacked("w1"),
        stacked("b1"),
        stacked("w2"),
        stacked("b2"),
        stacked("pg"),
        stacked("pb"),
        mine_big[:, 3],
        g_out,
        jnp.sum(parts["n2"], axis=0),
        g_ffn_gate,
        g_ffn_up,
        g_ffn_down,
    )


def solution(mesh):
    in_specs = (
        P("shard", "ctx", None),
        P("shard"),
        P("shard"),
        P("shard", None, "tp"),
        P("shard", "tp"),
        P("tp", None, "shard"),
        P("tp", "shard"),
        P("tp", None, "shard"),
        P("tp", "shard"),
        P("tp", "shard"),
        P("tp", "shard"),
        P("shard", "tp"),
        P("tp", "shard"),
        P("shard"),
        P("shard", "tp"),
        P("shard", "tp"),
        P("tp", "shard"),
        P("shard", "ctx", None),
    )
    out_specs = (
        P("shard", "ctx", None),
        P("shard", "ctx", None),
        P("shard"),
        P("shard", None, "tp"),
        P("shard", "tp"),
        P("tp", None, "shard"),
        P("tp", "shard"),
        P("tp", None, "shard"),
        P("tp", "shard"),
        P("tp", "shard"),
        P("tp", "shard"),
        P("shard", "tp"),
        P("tp", "shard"),
        P("shard"),
        P("shard", "tp"),
        P("shard", "tp"),
        P("tp", "shard"),
    )
    return jax.shard_map(
        on_device, mesh=mesh, in_specs=in_specs, out_specs=out_specs, check_vma=False
    )
```

```python
from functools import partial
import jax
import jax.numpy as jnp
from jax import lax
from jax.experimental import pallas as pl
from jax.experimental.pallas import tpu as pltpu
from jax.sharding import PartitionSpec as P

MINI = 16
EPSILON = 1e-06
ETA_BASE = 0.5
BF = jnp.bfloat16
F32 = jnp.float32


def mm(left, right):
    return lax.dot_general(left, right, (((1,), (0,)), ((), ())), preferred_element_type=F32)


def mm_nt(left, right):
    return lax.dot_general(left, right, (((1,), (1,)), ((), ())), preferred_element_type=F32)


def mm_tn(left, right):
    return lax.dot_general(left, right, (((0,), (0,)), ((), ())), preferred_element_type=F32)


def gelu_parts(value):
    cdf = 0.5 + 0.5 * lax.erf(value * 0.7071067811865476)
    pdf = jnp.exp(-0.5 * value * value) * 0.3989422804014327
    return cdf, pdf


def row_scale(value):
    return lax.rsqrt(jnp.mean(value * value, axis=-1, keepdims=True) + EPSILON)


def mini_scale():
    row = lax.broadcasted_iota(jnp.int32, (MINI, MINI), 0)
    col = lax.broadcasted_iota(jnp.int32, (MINI, MINI), 1)
    return row, col, jnp.where(col <= row, 1.0 / (row + 1).astype(F32), 0.0)


def fwd_kernel(
    length_ref, x_ref, gain_ref, wc_ref, lr_ref, lrt_ref, w1i_ref, c1i_ref, w2i_ref, c2i_ref, pg_ref, pb_ref,
    post_ref, kq_ref, mix_ref, rate_ref, fac_ref, gl_ref, gs_ref, unit_ref, hscale_ref,
    w1s_ref, w2s_ref, h_ref, r_ref, g1_ref, g2_ref, ga_ref, ug_ref, gp_ref,
    w1_ref, c1_ref, w2_ref, c2_ref, kmv_ref, qf_ref, s1_ref, mixed_ref, *, first, unroll,
):
    chains, group = kq_ref.shape[:2]
    rows = group * MINI
    head_dim = kq_ref.shape[-1]
    cols = chains * head_dim

    @pl.when(pl.program_id(0) == 0)
    def _():
        w1_ref[...] = w1i_ref[...]
        c1_ref[...] = c1i_ref[...]
        w2_ref[...] = w2i_ref[...]
        c2_ref[...] = c2i_ref[...]

    start = (first + pl.program_id(0)) * rows
    x = x_ref[...].astype(F32)
    normed = (x * row_scale(x) * gain_ref[...]).astype(BF)
    proj = mm(normed, wc_ref[...])
    length = length_ref[0]
    live_col = start + lax.broadcasted_iota(jnp.int32, (rows, 128), 0) < length
    live_row = start + lax.broadcasted_iota(jnp.int32, (lrt_ref.shape[0], rows), 1) < length
    eta_col = jnp.where(live_col, jax.nn.sigmoid(mm(normed, lr_ref[...])), 0.0) * (ETA_BASE / head_dim)
    rate = jax.nn.sigmoid(mm_nt(lrt_ref[...], normed))
    eta_row = jnp.where(live_row, rate, 0.0) * (ETA_BASE / head_dim)
    fac_ref[0] = eta_row * (1.0 - rate)
    scale = mini_scale()[2]
    for i in range(chains):
        at = i * head_dim
        q = proj[:, at : at + head_dim]
        k = proj[:, cols + at : cols + at + head_dim]
        v = proj[:, 2 * cols + at : 2 * cols + at + head_dim]
        kb, qb = k.astype(BF), q.astype(BF)
        kq_ref[i, :, :MINI] = kb.reshape(group, MINI, head_dim)
        kq_ref[i, :, MINI:] = qb.reshape(group, MINI, head_dim)
        kmv_ref[i] = (k - v).reshape(group, MINI, head_dim)
        qf_ref[i] = q.reshape(group, MINI, head_dim)
        rate_ref[i] = (eta_col[:, i : i + 1] * (1.0 / MINI)).reshape(group, MINI, 1)
        cross = mm_nt(qb, kb) + 1.0
        for j in range(group):
            piece = slice(j * MINI, j * MINI + MINI)
            mix = scale * eta_row[i : i + 1, piece]
            mix_ref[i, j] = mix
            s1_ref[i, j] = (mix * cross[piece, piece]).astype(BF)

    every = range(chains)

    def step(j):
        kq = [kq_ref[i, j] for i in every]
        k = [kq[i][:MINI] for i in every]
        mix = [mix_ref[i, j] for i in every]
        rate = [rate_ref[i, j] for i in every]
        s1 = [s1_ref[i, j] for i in every]
        kmv = [kmv_ref[i, j] for i in every]
        qf = [qf_ref[i, j] for i in every]
        w1 = [w1_ref[i] for i in every]
        w2 = [w2_ref[i] for i in every]
        c1 = [c1_ref[i] for i in every]
        c2 = [c2_ref[i] for i in every]
        w1b = [w1[i].astype(BF) for i in every]
        w2b = [w2[i].astype(BF) for i in every]
        both = [mm(kq[i], w1b[i]) + c1[i] for i in every]
        parts = [gelu_parts(both[i][:MINI]) for i in every]
        slope = [parts[i][0] + both[i][:MINI] * parts[i][1] for i in every]
        hb = [(both[i][:MINI] * parts[i][0]).astype(BF) for i in every]
        g2 = [mm_nt(hb[i], w2b[i]) + c2[i] + kmv[i] for i in every]
        g2b = [g2[i].astype(BF) for i in every]
        u = [mm(g2b[i], w2b[i]) for i in every]
        fg2 = [rate[i] * g2[i] for i in every]
        w2n = [w2[i] - mm_tn(fg2[i].astype(BF), hb[i]) for i in every]
        c2n = [c2[i] - jnp.sum(fg2[i], axis=0, keepdims=True) for i in every]
        g1 = [u[i] * slope[i] for i in every]
        fg1 = [rate[i] * g1[i] for i in every]
        w1n = [w1[i] - mm_tn(k[i], fg1[i].astype(BF)) for i in every]
        c1n = [c1[i] - jnp.sum(fg1[i], axis=0, keepdims=True) for i in every]
        g1b = [g1[i].astype(BF) for i in every]
        ug = [u[i] * (parts[i][1] * (2.0 - both[i][:MINI] * both[i][:MINI])) for i in every]
        pre = [both[i][MINI:] - mm(s1[i], g1b[i]) for i in every]
        parts_q = [gelu_parts(pre[i]) for i in every]
        gp = [parts_q[i][0] + pre[i] * parts_q[i][1] for i in every]
        rb = [(pre[i] * parts_q[i][0]).astype(BF) for i in every]
        s2 = [(mix[i] * (mm_nt(rb[i], hb[i]) + 1.0)).astype(BF) for i in every]
        mixed = [qf[i] + mm_nt(rb[i], w2b[i]) + c2[i] - mm(s2[i], g2b[i]) for i in every]
        for i in every:
            w1s_ref[i, j] = w1b[i]
            w2s_ref[i, j] = w2b[i]
            h_ref[i, j] = hb[i]
            r_ref[i, j] = rb[i]
            g1_ref[i, j] = g1b[i]
            g2_ref[i, j] = g2b[i]
            ga_ref[i, j] = slope[i]
            ug_ref[i, j] = ug[i]
            gp_ref[i, j] = gp[i]
            mixed_ref[i, j] = mixed[i]
            w1_ref[i] = w1n[i]
            w2_ref[i] = w2n[i]
            c1_ref[i] = c1n[i]
            c2_ref[i] = c2n[i]

    def body(turn, _):
        for within in range(unroll):
            step(turn * unroll + within)
        return 0

    lax.fori_loop(0, group // unroll, body, 0)

    for i in range(chains):
        at = i * head_dim
        gate = proj[:, 3 * cols + at : 3 * cols + at + head_dim]
        mixed = mixed_ref[i].reshape(rows, head_dim)
        centered = mixed - jnp.mean(mixed, axis=-1, keepdims=True)
        hscale = row_scale(centered)
        unit = centered * hscale
        out = unit * pg_ref[i] + pb_ref[i]
        cdf, pdf = gelu_parts(gate)
        post_ref[:, at : at + head_dim] = (gate * cdf * out).astype(BF)
        gl_ref[i] = gate * cdf
        gs_ref[i] = (cdf + gate * pdf) * out
        unit_ref[i] = unit
        hscale_ref[i] = hscale


def bwd_kernel(
    x_ref, gain_ref, wc_ref, lrt_ref, pg_ref, gpost_ref, w1i_ref, c1i_ref, w2i_ref, c2i_ref,
    kq_ref, mix_ref, rate_ref, fac_ref, gl_ref, gs_ref, unit_ref, hscale_ref,
    w1s_ref, w2s_ref, h_ref, r_ref, g1_ref, g2_ref, ga_ref, ug_ref, gp_ref,
    back_ref, gw_ref, glr_ref, gain_grad_ref, gpg_ref, gpb_ref, dw1_ref, dc1_ref, dw2_ref, dc2_ref,
    d_ref, dq_ref, dk_ref, dv_ref, de_ref, all_ref, *, unroll,
):
    chains, group = kq_ref.shape[:2]
    rows = group * MINI
    head_dim = kq_ref.shape[-1]
    cols = chains * head_dim

    @pl.when(pl.program_id(0) == 0)
    def _():
        dw1_ref[...] = w1i_ref[...]
        dc1_ref[...] = c1i_ref[...]
        dw2_ref[...] = w2i_ref[...]
        dc2_ref[...] = c2i_ref[...]
        gw_ref[...] = jnp.zeros_like(gw_ref)
        glr_ref[...] = jnp.zeros_like(glr_ref)
        gain_grad_ref[...] = jnp.zeros_like(gain_grad_ref)
        gpg_ref[...] = jnp.zeros_like(gpg_ref)
        gpb_ref[...] = jnp.zeros_like(gpb_ref)

    row, col, scale = mini_scale()
    eye = jnp.where(col == row, 1.0 / MINI, 0.0)
    gpost = gpost_ref[...].astype(F32)
    for i in range(chains):
        at = i * head_dim
        piece = gpost[:, at : at + head_dim]
        all_ref[:, 3 * cols + at : 3 * cols + at + head_dim] = (piece * gs_ref[i]).astype(BF)
        head = piece * gl_ref[i]
        unit = unit_ref[i]
        gpg_ref[i] += jnp.sum(head * unit, axis=0, keepdims=True)
        gpb_ref[i] += jnp.sum(head, axis=0, keepdims=True)
        lifted = head * pg_ref[i]
        grad = hscale_ref[i] * (
            lifted
            - jnp.mean(lifted, axis=-1, keepdims=True)
            - unit * jnp.mean(lifted * unit, axis=-1, keepdims=True)
        )
        d_ref[i] = grad.reshape(group, MINI, head_dim)

    every = range(chains)

    def step(j):
        def all_of(ref):
            return [ref[i, j] for i in every]

        d, kq = all_of(d_ref), all_of(kq_ref)
        w1b, w2b, hb, rb, g1b, g2b = (
            all_of(ref) for ref in (w1s_ref, w2s_ref, h_ref, r_ref, g1_ref, g2_ref)
        )
        ga, ug, gp = all_of(ga_ref), all_of(ug_ref), all_of(gp_ref)
        dw1 = [dw1_ref[i] for i in every]
        dw2 = [dw2_ref[i] for i in every]
        dc1 = [dc1_ref[i] for i in every]
        dc2 = [dc2_ref[i] for i in every]
        k = [kq[i][:MINI] for i in every]
        q = [kq[i][MINI:] for i in every]
        mix, rate = all_of(mix_ref), all_of(rate_ref)
        g1 = [g1b[i].astype(F32) for i in every]
        g2 = [g2b[i].astype(F32) for i in every]
        dw1b = [dw1[i].astype(BF) for i in every]
        dw2b = [dw2[i].astype(BF) for i in every]
        t1 = [mm(k[i], dw1b[i]) + dc1[i] for i in every]
        t2 = [mm_nt(hb[i], dw2b[i]) + dc2[i] for i in every]
        db = [d[i].astype(BF) for i in every]
        ds2 = [-mm_nt(db[i], g2b[i]) for i in every]
        x2 = [mm_nt(rb[i], hb[i]) + 1.0 for i in every]
        x1 = [mm_nt(q[i], k[i]) + 1.0 for i in every]
        dx2 = [(ds2[i] * mix[i]).astype(BF) for i in every]
        dr = [mm(db[i], w2b[i]) + mm(dx2[i], hb[i]) for i in every]
        dp = [dr[i] * gp[i] for i in every]
        dpb = [dp[i].astype(BF) for i in every]
        dg1 = [-mm_tn((mix[i] * x1[i]).astype(BF), dpb[i]) - rate[i] * t1[i] for i in every]
        dub = [(dg1[i] * ga[i]).astype(BF) for i in every]
        dg2 = [
            mm_nt(dub[i], w2b[i]) - mm_tn((mix[i] * x2[i]).astype(BF), db[i]) - rate[i] * t2[i]
            for i in every
        ]
        dg2b = [dg2[i].astype(BF) for i in every]
        dh = [
            mm(dg2b[i], w2b[i]) + mm_tn(dx2[i], rb[i]) - mm((rate[i] * g2[i]).astype(BF), dw2b[i])
            for i in every
        ]
        da = [dg1[i] * ug[i] + dh[i] * ga[i] for i in every]
        dab = [da[i].astype(BF) for i in every]
        dw1n = [dw1[i] + mm_tn(kq[i], jnp.concatenate([dab[i], dpb[i]], axis=0)) for i in every]
        dc1n = [dc1[i] + jnp.sum(da[i] + dp[i], axis=0, keepdims=True) for i in every]
        dw2n = [
            dw2[i]
            + mm_tn(
                jnp.concatenate([db[i], dg2b[i], g2b[i]], axis=0),
                jnp.concatenate([rb[i], hb[i], dub[i]], axis=0),
            )
            for i in every
        ]
        dc2n = [dc2[i] + jnp.sum(d[i] + dg2[i], axis=0, keepdims=True) for i in every]
        ds1 = [-mm_nt(dpb[i], g1b[i]) for i in every]
        dx1 = [(ds1[i] * mix[i]).astype(BF) for i in every]
        dq = [d[i] + mm_nt(dpb[i], w1b[i]) + mm(dx1[i], k[i]) for i in every]
        dk = [
            dg2[i]
            - mm_nt((rate[i] * g1[i]).astype(BF), dw1b[i])
            + mm_tn(dx1[i], q[i])
            + mm_nt(dab[i], w1b[i])
            for i in every
        ]
        df = [
            -(
                jnp.sum(g1[i] * t1[i], axis=1, keepdims=True)
                + jnp.sum(g2[i] * t2[i], axis=1, keepdims=True)
            )
            for i in every
        ]
        de = [
            jnp.sum((ds2[i] * x2[i] + ds1[i] * x1[i]) * scale + eye * df[i], axis=0, keepdims=True)
            for i in every
        ]
        for i in every:
            dq_ref[i, j] = dq[i].astype(BF)
            dk_ref[i, j] = dk[i].astype(BF)
            dv_ref[i, j] = (-dg2[i]).astype(BF)
            de_ref[i, j] = de[i]
            dw1_ref[i] = dw1n[i]
            dc1_ref[i] = dc1n[i]
            dw2_ref[i] = dw2n[i]
            dc2_ref[i] = dc2n[i]

    def body(turn, _):
        for within in range(unroll):
            step(group - 1 - (turn * unroll + within))
        return 0

    lax.fori_loop(0, group // unroll, body, 0)

    x = x_ref[...].astype(F32)
    unit_in = x * row_scale(x)
    normed = (unit_in * gain_ref[...]).astype(BF)
    lrt = lrt_ref[...]
    padded = lrt.shape[0]
    which = lax.broadcasted_iota(jnp.int32, (padded, rows), 0)
    rates = jnp.zeros((padded, rows), F32)
    for i in range(chains):
        at = i * head_dim
        all_ref[:, at : at + head_dim] = dq_ref[i].reshape(rows, head_dim)
        all_ref[:, cols + at : cols + at + head_dim] = dk_ref[i].reshape(rows, head_dim)
        all_ref[:, 2 * cols + at : 2 * cols + at + head_dim] = dv_ref[i].reshape(rows, head_dim)
        line = jnp.concatenate([de_ref[i, j] for j in range(group)], axis=1)
        rates = jnp.where(which == i, line, rates)
    rates = (rates * fac_ref[0]).astype(BF)
    grads = all_ref[...]
    back = mm_nt(grads, wc_ref[...]) + mm_tn(rates, lrt)
    gain_grad_ref[...] += jnp.sum(back * unit_in, axis=0, keepdims=True)
    back_ref[...] = back.astype(BF)
    gw_ref[...] += mm_tn(normed, grads)
    glr_ref[...] += mm(rates, normed)


GROUP = 8


def block_specs(chains, head_dim, inner, padded, place):
    rows = GROUP * MINI

    def mini(first, second):
        return pl.BlockSpec((chains, GROUP, first, second), lambda g: (0, place(g), 0, 0))

    def head(second):
        return pl.BlockSpec((chains, rows, second), lambda g: (0, place(g), 0))

    return [
        mini(2 * MINI, head_dim), mini(MINI, MINI), mini(MINI, 1),
        pl.BlockSpec((1, padded, rows), lambda g: (place(g), 0, 0)),
        head(head_dim), head(head_dim), head(head_dim), head(1),
        mini(head_dim, inner), mini(head_dim, inner), mini(MINI, inner), mini(MINI, inner),
        mini(MINI, inner), mini(MINI, head_dim), mini(MINI, inner), mini(MINI, inner), mini(MINI, inner),
    ]


def whole_spec(value):
    return pl.BlockSpec(value.shape, lambda g: (0,) * value.ndim)


def run_fwd(first, last, length, tokens, gain, wc, lr, lrt, pg, pb, state, unroll=2):
    width = tokens.shape[1]
    chains, head_dim, inner = state[0].shape
    rows = GROUP * MINI
    steps = last - first
    count = steps * GROUP
    padded = lrt.shape[0]

    def mini(first_size, second_size, dtype):
        return jax.ShapeDtypeStruct((chains, count, first_size, second_size), dtype)

    def head(second):
        return jax.ShapeDtypeStruct((chains, steps * rows, second), F32)

    row_spec = pl.BlockSpec((rows, width), lambda g: (first + g, 0))
    small = (gain, wc, lr, lrt, *state, pg, pb)
    return pl.pallas_call(
        partial(fwd_kernel, first=first, unroll=unroll),
        grid=(steps,),
        in_specs=[pl.BlockSpec(memory_space=pltpu.SMEM), row_spec] + [whole_spec(v) for v in small],
        out_specs=[pl.BlockSpec((rows, chains * head_dim), lambda g: (g, 0))]
        + block_specs(chains, head_dim, inner, padded, lambda g: g)
        + [whole_spec(v) for v in state],
        out_shape=[
            jax.ShapeDtypeStruct((steps * rows, chains * head_dim), BF),
            mini(2 * MINI, head_dim, BF), mini(MINI, MINI, F32), mini(MINI, 1, F32),
            jax.ShapeDtypeStruct((steps, padded, rows), F32),
            head(head_dim), head(head_dim), head(head_dim), head(1),
            mini(head_dim, inner, BF), mini(head_dim, inner, BF), mini(MINI, inner, BF), mini(MINI, inner, BF),
            mini(MINI, inner, BF), mini(MINI, head_dim, BF), mini(MINI, inner, F32), mini(MINI, inner, F32),
            mini(MINI, inner, F32),
        ]
        + [jax.ShapeDtypeStruct(v.shape, F32) for v in state],
        scratch_shapes=[
            pltpu.VMEM((chains, GROUP, MINI, head_dim), F32), pltpu.VMEM((chains, GROUP, MINI, head_dim), F32),
            pltpu.VMEM((chains, GROUP, MINI, MINI), BF), pltpu.VMEM((chains, GROUP, MINI, head_dim), F32),
        ],
        compiler_params=pltpu.CompilerParams(vmem_limit_bytes=50 << 20),
        cost_estimate=pl.CostEstimate(
            flops=9_000_000_000 * steps, bytes_accessed=5_000_000 * steps, transcendentals=0
        ),
        name="chain_forward",
    )(length, tokens, *small)


def run_bwd(first, last, tokens, gain, wc, lrt, pg, gpost, state, saved, unroll=2):
    width = tokens.shape[1]
    chains, head_dim, inner = state[0].shape
    rows = GROUP * MINI
    padded = lrt.shape[0]
    wide = wc.shape[1]
    steps = last - first

    def place(g):
        return steps - 1 - g

    def shape(*extent):
        return jax.ShapeDtypeStruct(extent, F32)

    small = (gain, wc, lrt, pg)
    outs = [
        shape(width, wide), shape(padded, width), shape(1, width), shape(chains, 1, head_dim), shape(chains, 1, head_dim),
        shape(chains, head_dim, inner), shape(chains, 1, inner), shape(chains, head_dim, inner), shape(chains, 1, head_dim),
    ]
    scratch = pltpu.VMEM((chains, GROUP, MINI, head_dim), BF)
    return pl.pallas_call(
        partial(bwd_kernel, unroll=unroll),
        grid=(steps,),
        in_specs=[pl.BlockSpec((rows, width), lambda g: (first + place(g), 0))]
        + [whole_spec(v) for v in small]
        + [pl.BlockSpec((rows, chains * head_dim), lambda g: (first + place(g), 0))]
        + [whole_spec(v) for v in state]
        + block_specs(chains, head_dim, inner, padded, place),
        out_specs=[pl.BlockSpec((rows, width), lambda g: (place(g), 0))] + [whole_spec(v) for v in outs],
        out_shape=[jax.ShapeDtypeStruct((steps * rows, width), BF)] + outs,
        scratch_shapes=[
            pltpu.VMEM((chains, GROUP, MINI, head_dim), F32), scratch, scratch, scratch,
            pltpu.VMEM((chains, GROUP, 1, MINI), F32), pltpu.VMEM((rows, wide), BF),
        ],
        compiler_params=pltpu.CompilerParams(vmem_limit_bytes=50 << 20),
        cost_estimate=pl.CostEstimate(
            flops=11_000_000_000 * steps, bytes_accessed=5_000_000 * steps, transcendentals=0
        ),
        name="chain_backward",
    )(tokens, *small, gpost, *state, *saved)


def row_norm(value):
    return lax.rsqrt(jnp.mean(value * value, axis=-1, keepdims=True) + EPSILON)


def pieces_of(chains, depth, head_dim, inner_share, head_share):
    return (
        ("lr", (depth, chains)),
        ("w1", (chains, head_dim, inner_share)),
        ("w2", (chains, head_dim, inner_share)),
        ("b1", (chains, inner_share)),
        ("b2", (chains, head_share)),
        ("pg", (chains, head_share)),
        ("pb", (chains, head_share)),
        ("n1", (depth,)),
        ("n2", (depth,)),
    )


def size_of(shape):
    total = 1
    for extent in shape:
        total *= extent
    return total


def swap(value):
    return lax.ppermute(value, "tp", [(0, 1), (1, 0)])


def place_kernel(spots_ref, *refs):
    *sources, target = refs
    for number, source in enumerate(sources):
        target[spots_ref[number]] = source[...]


def placed(pieces, spots):
    return pl.pallas_call(
        place_kernel,
        in_specs=[pl.BlockSpec(memory_space=pltpu.SMEM)]
        + [pl.BlockSpec(memory_space=pltpu.VMEM)] * len(pieces),
        out_specs=pl.BlockSpec(memory_space=pltpu.VMEM),
        out_shape=jax.ShapeDtypeStruct((len(pieces),) + pieces[0].shape, pieces[0].dtype),
        compiler_params=pltpu.CompilerParams(vmem_limit_bytes=40 << 20),
        name="place_pieces",
    )(jnp.stack(spots).astype(jnp.int32), *pieces)


def exchanged(value, axis):
    size = lax.axis_size(axis)
    return [value] + [
        lax.ppermute(value, axis, [(source, source ^ bit) for source in range(size)])
        for bit in range(1, size)
    ]


def scattered(value, axis):
    size = lax.axis_size(axis)
    me = lax.axis_index(axis)
    taken = [lax.dynamic_index_in_dim(value, me ^ bit, 0, keepdims=False) for bit in range(size)]
    return taken[:1] + [
        lax.ppermute(taken[bit], axis, [(source, source ^ bit) for source in range(size)])
        for bit in range(1, size)
    ]


def placed_along(pieces, axis):
    me = lax.axis_index(axis)
    return placed(pieces, [me ^ bit for bit in range(len(pieces))])


def spread(value, axis):
    return placed_along(exchanged(value, axis), axis)


def tied(*values):
    return lax.optimization_barrier(values)


def in_turn(first, second):
    return jnp.where(lax.axis_index("tp") == 0, jnp.stack([first, second]), jnp.stack([second, first]))


def on_device(
    tokens,
    lengths,
    norm1_gain,
    qkv_weight,
    lr_weight,
    inner_w1,
    inner_b1,
    inner_w2,
    inner_b2,
    post_gain,
    post_bias,
    gate_weight,
    out_weight,
    norm2_gain,
    ffn_gate,
    ffn_up,
    ffn_down,
    cotangent,
):
    micro, span, width = tokens.shape
    ring = lax.axis_size("ctx")
    shards = lax.axis_size("shard")
    pair = lax.axis_size("tp")
    place = lax.axis_index("ctx")
    core = lax.axis_index("tp")
    local_heads, head_dim, inner_share = inner_w1.shape
    head_share = inner_b2.shape[1]
    depth = norm1_gain.shape[0]
    inner = inner_share * shards
    total_heads = local_heads * pair
    chains = -(-total_heads // ring)
    span_all = ring * span
    count = span_all // MINI
    cols = chains * head_dim
    wide = 4 * cols

    row_tokens = lax.dynamic_index_in_dim(tokens, core, 0, keepdims=False)
    slot_tokens = spread(row_tokens, "ctx").reshape(span_all, width)

    first_head = jnp.minimum(place * chains, total_heads - chains)
    owner = first_head // local_heads
    local_first = first_head - owner * local_heads

    def of_heads(value, axis):
        return lax.dynamic_slice_in_dim(value, local_first, chains, axis)

    pieces = pieces_of(chains, depth, head_dim, inner_share, head_share)
    small_size = sum(size_of(shape) for _, shape in pieces)
    small_rows = -(-small_size // wide)
    small_rows = -(-(small_rows + depth) // 32) * 32 - depth
    half_rows = (small_rows + depth) // 2
    own = {
        "lr": of_heads(lr_weight, 1),
        "w1": of_heads(inner_w1, 0),
        "w2": of_heads(inner_w2, 0),
        "b1": of_heads(inner_b1, 0),
        "b2": of_heads(inner_b2, 0),
        "pg": of_heads(post_gain, 0),
        "pb": of_heads(post_bias, 0),
        "n1": norm1_gain,
        "n2": norm2_gain,
    }
    small = jnp.concatenate([own[name].reshape(-1) for name, _ in pieces])
    small = jnp.pad(small, (0, small_rows * wide - small_size)).reshape(small_rows, wide)
    qkv_heads = of_heads(qkv_weight.reshape(depth, 3, local_heads, head_dim), 2)
    gate_heads = of_heads(gate_weight.reshape(depth, local_heads, head_dim), 1)
    big = jnp.concatenate(
        [qkv_heads.reshape(depth, 3 * cols), gate_heads.reshape(depth, cols)], axis=1
    )
    packed = jnp.concatenate([big, small], axis=0)
    packed = jnp.where(core == owner, packed, swap(packed))
    packed = spread(lax.dynamic_slice_in_dim(packed, core * half_rows, half_rows, 0), "shard")
    packed = in_turn(packed, swap(packed))
    gathered = packed.transpose(1, 0, 2, 3).reshape(shards, depth + small_rows, wide)
    units = ffn_gate.shape[1]
    half_out = out_weight.shape[0]
    row_pack = jnp.concatenate([ffn_gate, ffn_up, ffn_down.T, out_weight.T], axis=1)
    part = depth // ring
    row_part = lax.dynamic_slice_in_dim(row_pack, place * part, part, 0)
    row_part, gathered = tied(row_part, gathered)
    row_parts = exchanged(row_part, "shard")

    w_chain = gathered[:, :depth].reshape(width, wide)
    flat = gathered[:, depth:].reshape(shards, small_rows * wide)
    full = {}
    offset = 0
    for name, shape in pieces:
        full[name] = flat[:, offset : offset + size_of(shape)].reshape((shards,) + shape)
        offset += size_of(shape)
    w_rate = full["lr"].reshape(width, chains)
    gain_one = full["n1"].reshape(width).astype(F32)
    gain_two = full["n2"].reshape(width).astype(F32)

    def along(name):
        return jnp.moveaxis(full[name], 0, -2).reshape(full[name].shape[1:-1] + (-1,)).astype(F32)

    init_first, init_second = along("w1"), along("w2")
    init_first_bias, init_second_bias = along("b1"), along("b2")
    norm_gain, norm_bias = along("pg"), along("pb")

    slot_length = lax.dynamic_index_in_dim(lengths, core, 0, keepdims=True)
    gain_row = gain_one[None]
    rate_cols = jnp.pad(w_rate, ((0, 0), (0, 128 - chains)))
    rate_rows = jnp.pad(w_rate.T, ((0, -chains % 16), (0, 0)))
    norm_gain, norm_bias = norm_gain[:, None], norm_bias[:, None]
    steps = span_all // (GROUP * MINI)
    middle = steps // 2
    state = (init_first, init_first_bias[:, None], init_second, init_second_bias[:, None])

    def forward(first, last, begin):
        done = run_fwd(
            first, last, slot_length, slot_tokens, gain_row, w_chain, rate_cols, rate_rows, norm_gain, norm_bias, begin
        )
        return done[0], done[1:-4], done[-4:]

    post_low, saved_low, state_low = forward(0, middle, state)
    state_low, row_parts = tied(state_low, row_parts)
    far = jnp.stack(row_parts[1:])
    state_low, far = tied(state_low, far)
    far_parts = exchanged(far, "ctx")
    post_high, saved_high, _ = forward(middle, steps, tuple(state_low))
    post_chain = jnp.concatenate([post_low, post_high])

    def to_rows(value):
        return lax.all_to_all(value.reshape(ring, span, -1), "ctx", 0, 0)

    post = to_rows(post_chain)
    post = post.transpose(1, 0, 2).reshape(span, ring * cols)[:, : total_heads * head_dim]

    far_parts, post = tied(far_parts, post)
    me = lax.axis_index("shard")
    blocks = [row_pack[start : start + part] for start in range(0, depth, part)]
    spots = [me * ring + number for number in range(ring)]
    for bit, group in enumerate(far_parts):
        for other in range(1, shards):
            blocks.append(group[other - 1])
            spots.append((me ^ other) * ring + (place ^ bit))
    w_own = placed(blocks, spots).reshape(width, -1)
    w_other = jnp.concatenate([swap(w_own[:, : 3 * units]), swap(w_own[:, 3 * units :])], axis=1)

    def split_up(value):
        return tuple(value[:, start : start + units] for start in range(0, 3 * units, units))

    halves = (split_up(w_own), split_up(w_other))
    w_out = jnp.concatenate(
        [
            jnp.where(core == 0, w_own[:, 3 * units :], w_other[:, 3 * units :]),
            jnp.where(core == 0, w_other[:, 3 * units :], w_own[:, 3 * units :]),
        ],
        axis=1,
    )
    row_in = row_tokens.astype(F32)
    hidden = row_in + mm_nt(post, w_out)
    scale_two = row_norm(hidden)
    normed_two = (hidden * scale_two * gain_two).astype(BF)
    position = place * span + lax.iota(jnp.int32, span)
    live = (position < slot_length[0]).astype(F32)[:, None]
    cot = lax.dynamic_index_in_dim(cotangent, core, 0, keepdims=False)
    back = cot.astype(F32) * live
    back_low = back.astype(BF)
    feed = 0.0
    grad_two = 0.0
    sums = []
    for w_gate, w_up, w_down in halves:
        up_gate = mm(normed_two, w_gate)
        up_lin = mm(normed_two, w_up)
        gate = jax.nn.sigmoid(up_gate)
        act_low = (up_gate * gate * up_lin).astype(BF)
        feed = feed + mm_nt(act_low, w_down)
        grad_act = mm(back_low, w_down)
        grad_gate_low = (grad_act * up_lin * gate * (1.0 + up_gate * (1.0 - gate))).astype(BF)
        grad_lin_low = (grad_act * up_gate * gate).astype(BF)
        grad_two = grad_two + mm_nt(grad_gate_low, w_gate) + mm_nt(grad_lin_low, w_up)
        sums.append(
            [
                mm_tn(normed_two, grad_gate_low),
                mm_tn(normed_two, grad_lin_low),
                mm_tn(back_low, act_low),
            ]
        )
    output = (hidden + feed).astype(BF)
    lifted = grad_two * gain_two
    grad_hidden = (
        back
        + scale_two * lifted
        - hidden * scale_two**3 * jnp.mean(lifted * hidden, axis=-1, keepdims=True)
    )
    grad_gain_two = jnp.sum(grad_two * hidden * scale_two, axis=0)
    grad_hidden_low = grad_hidden.astype(BF)
    grad_post = mm(grad_hidden_low, w_out)

    grad_out = mm_tn(grad_hidden_low, post)
    grad_out_own = lax.dynamic_slice_in_dim(grad_out, core * half_out, half_out, 1)
    grad_out_other = lax.dynamic_slice_in_dim(grad_out, (1 - core) * half_out, half_out, 1)
    own_sum = jnp.concatenate(sums[0] + [grad_out_own], axis=1)
    other_sum = jnp.concatenate(sums[1] + [grad_out_other], axis=1).astype(BF)
    row_sum = (own_sum + swap(other_sum).astype(F32)).astype(BF)
    row_sum = row_sum.reshape(shards, ring, part, -1).transpose(1, 0, 2, 3)
    cut = 2 * units
    sum_a = scattered(row_sum[..., :cut], "ctx")
    sum_b = scattered(row_sum[..., cut:], "ctx")

    def folded(values):
        return sum(value.astype(F32) for value in values).astype(BF)

    grad_post = jnp.pad(grad_post.astype(BF), ((0, 0), (0, ring * cols - total_heads * head_dim)))
    grad_post = lax.all_to_all(grad_post.reshape(span, ring, cols).transpose(1, 0, 2), "ctx", 0, 0)
    grad_post = grad_post.reshape(span_all, cols)

    def backward(first, last, begin, saved):
        done = run_bwd(
            first, last, slot_tokens, gain_row, w_chain, rate_rows, norm_gain, grad_post, begin, saved
        )
        return done[0], done[1:6], done[6:]

    begin = tuple(jnp.zeros_like(value) for value in state)
    grad_post, row_sum = tied(grad_post, row_sum)
    back_high, sums_high, ending = backward(middle, steps, begin, saved_high)
    ending, sum_a = tied(ending, sum_a)
    sum_a = folded(sum_a)
    ending, sum_a = tied(ending, sum_a)
    sum_a = scattered(sum_a, "shard")
    back_low_half, sums_low, ending = backward(0, middle, tuple(ending), saved_low)
    ending, back_low_half, sum_a, sum_b = tied(ending, back_low_half, sum_a, sum_b)
    d_first, d_first_bias, d_second, d_second_bias = ending
    grad_big, grad_lr, grad_gain_one, grad_norm_gain, grad_norm_bias = (
        low + high for low, high in zip(sums_low, sums_high)
    )
    grad_lr = grad_lr[:chains].T
    back_part = jnp.concatenate([back_low_half, back_high])
    back_one = jnp.sum(to_rows(back_part).astype(F32), axis=0)
    scale_one = row_norm(row_in)
    lifted = back_one * gain_one
    input_grad = (
        grad_hidden
        + scale_one * lifted
        - row_in * scale_one**3 * jnp.mean(lifted * row_in, axis=-1, keepdims=True)
    ).astype(BF)

    sum_b = scattered(folded(sum_b), "shard")
    row_sum = spread(jnp.concatenate([folded(sum_a), folded(sum_b)], axis=-1), "ctx")
    row_sum = row_sum.reshape(depth, -1).astype(F32)
    g_ffn_gate = row_sum[:, :units]
    g_ffn_up = row_sum[:, units : 2 * units]
    g_ffn_down = row_sum[:, 2 * units : 3 * units].T
    g_out = row_sum[:, 3 * units :].T


    def by_shard(value):
        split = value.reshape(value.shape[:-1] + (shards, -1))
        return jnp.moveaxis(split, -2, 0).reshape(shards, -1)

    flat = jnp.concatenate(
        [
            grad_lr.reshape(shards, -1),
            by_shard(d_first),
            by_shard(d_second),
            by_shard(d_first_bias[:, 0]),
            by_shard(d_second_bias[:, 0]),
            by_shard(grad_norm_gain[:, 0]),
            by_shard(grad_norm_bias[:, 0]),
            grad_gain_one.reshape(shards, -1),
            grad_gain_two.reshape(shards, -1),
        ],
        axis=1,
    )
    flat = jnp.pad(flat, ((0, 0), (0, small_rows * wide - small_size)))
    chain_sum = jnp.concatenate(
        [grad_big.reshape(shards, depth, wide), flat.reshape(shards, small_rows, wide)], axis=1
    ).astype(BF)
    kept_half = lax.dynamic_slice_in_dim(chain_sum, core * half_rows, half_rows, 1)
    sent_half = lax.dynamic_slice_in_dim(chain_sum, (1 - core) * half_rows, half_rows, 1)
    chain_sum = (kept_half.astype(F32) + swap(sent_half).astype(F32)).astype(BF)
    chain_sum = spread(folded(scattered(chain_sum, "shard")), "ctx")
    chain_sum = in_turn(chain_sum, swap(chain_sum)).astype(F32)
    chain_sum = chain_sum.transpose(1, 0, 2, 3).reshape(ring, depth + small_rows, wide)
    places = local_heads // chains
    mine = lax.dynamic_slice_in_dim(chain_sum, core * places, places, 0)
    mine_big = mine[:, :depth].reshape(places, depth, 4, cols).transpose(1, 2, 0, 3)
    mine_big = mine_big.reshape(depth, 4, local_heads * head_dim)
    flat_all = chain_sum[:, depth:].reshape(ring, -1)
    flat_mine = mine[:, depth:].reshape(places, -1)
    parts = {}
    offset = 0
    for name, shape in pieces:
        source = flat_all if name in ("n1", "n2") else flat_mine
        parts[name] = source[:, offset : offset + size_of(shape)].reshape((source.shape[0],) + shape)
        offset += size_of(shape)

    def stacked(name):
        return parts[name].reshape((local_heads,) + parts[name].shape[2:])

    return (
        in_turn(output, swap(output)),
        in_turn(input_grad, swap(input_grad)),
        jnp.sum(parts["n1"], axis=0),
        mine_big[:, :3],
        parts["lr"].transpose(1, 0, 2).reshape(depth, local_heads),
        stacked("w1"),
        stacked("b1"),
        stacked("w2"),
        stacked("b2"),
        stacked("pg"),
        stacked("pb"),
        mine_big[:, 3],
        g_out,
        jnp.sum(parts["n2"], axis=0),
        g_ffn_gate,
        g_ffn_up,
        g_ffn_down,
    )


def solution(mesh):
    in_specs = (
        P("shard", "ctx", None),
        P("shard"),
        P("shard"),
        P("shard", None, "tp"),
        P("shard", "tp"),
        P("tp", None, "shard"),
        P("tp", "shard"),
        P("tp", None, "shard"),
        P("tp", "shard"),
        P("tp", "shard"),
        P("tp", "shard"),
        P("shard", "tp"),
        P("tp", "shard"),
        P("shard"),
        P("shard", "tp"),
        P("shard", "tp"),
        P("tp", "shard"),
        P("shard", "ctx", None),
    )
    out_specs = (
        P("shard", "ctx", None),
        P("shard", "ctx", None),
        P("shard"),
        P("shard", None, "tp"),
        P("shard", "tp"),
        P("tp", None, "shard"),
        P("tp", "shard"),
        P("tp", None, "shard"),
        P("tp", "shard"),
        P("tp", "shard"),
        P("tp", "shard"),
        P("shard", "tp"),
        P("tp", "shard"),
        P("shard"),
        P("shard", "tp"),
        P("shard", "tp"),
        P("tp", "shard"),
    )
    return jax.shard_map(
        on_device, mesh=mesh, in_specs=in_specs, out_specs=out_specs, check_vma=False
    )
```

```python
from functools import partial
import jax
import jax.numpy as jnp
from jax import lax
from jax.experimental import pallas as pl
from jax.experimental.pallas import tpu as pltpu
from jax.sharding import PartitionSpec as P

MINI = 16
EPSILON = 1e-06
ETA_BASE = 0.5
BF = jnp.bfloat16
F32 = jnp.float32


def mm(left, right):
    return lax.dot_general(left, right, (((1,), (0,)), ((), ())), preferred_element_type=F32)


def mm_nt(left, right):
    return lax.dot_general(left, right, (((1,), (1,)), ((), ())), preferred_element_type=F32)


def mm_tn(left, right):
    return lax.dot_general(left, right, (((0,), (0,)), ((), ())), preferred_element_type=F32)


def gelu_parts(value):
    cdf = 0.5 + 0.5 * lax.erf(value * 0.7071067811865476)
    pdf = jnp.exp(-0.5 * value * value) * 0.3989422804014327
    return cdf, pdf


def row_scale(value):
    return lax.rsqrt(jnp.mean(value * value, axis=-1, keepdims=True) + EPSILON)


def mini_masks(rows):
    row = lax.broadcasted_iota(jnp.int32, (rows, rows), 0)
    col = lax.broadcasted_iota(jnp.int32, (rows, rows), 1)
    within = (lax.div(row, MINI) == lax.div(col, MINI)) & (col <= row)
    scale = jnp.where(within, 1.0 / (lax.rem(row, MINI) + 1).astype(F32), 0.0)
    return scale, jnp.where(row == col, 1.0 / MINI, 0.0)


def minis(value):
    return [value[at : at + MINI] for at in range(0, value.shape[0], MINI)]


def flat_rows(value):
    return value.reshape(value.shape[0] * value.shape[1], value.shape[2])


def fwd_kernel(
    length_ref, x_ref, gain_ref, wc_ref, lr_ref, lrt_ref, w1i_ref, c1i_ref, w2i_ref, c2i_ref, pg_ref, pb_ref,
    post_ref, kq_ref, rate_ref, fac_ref, gl_ref, gs_ref, unit_ref, hscale_ref,
    w1s_ref, w2s_ref, h_ref, r_ref, g1_ref, g2_ref, ga_ref, ug_ref, gp_ref,
    w1_ref, c1_ref, w2_ref, c2_ref, kmv_ref, next_ref, kk_ref, pq_ref, c2s_ref, *, first,
):
    chains, group = kq_ref.shape[:2]
    rows = group * MINI
    head_dim = kq_ref.shape[-1]
    cols = chains * head_dim
    every = range(chains)

    @pl.when(pl.program_id(0) == 0)
    def _():
        w1_ref[...] = w1i_ref[...]
        c1_ref[...] = c1i_ref[...]
        w2_ref[...] = w2i_ref[...]
        c2_ref[...] = c2i_ref[...]

    start = (first + pl.program_id(0)) * rows
    padded = lrt_ref.shape[0]
    x = x_ref[...].astype(F32)
    normed = (x * row_scale(x) * gain_ref[...]).astype(BF)
    proj = mm(normed, wc_ref[...])
    length = length_ref[0]
    live_col = start + lax.broadcasted_iota(jnp.int32, (rows, 128), 0) < length
    live_row = start + lax.broadcasted_iota(jnp.int32, (padded, rows), 1) < length
    eta_col = jnp.where(live_col, jax.nn.sigmoid(mm(normed, lr_ref[...])), 0.0) * (ETA_BASE / head_dim)
    rate = jax.nn.sigmoid(mm_nt(lrt_ref[...], normed))
    eta_row = jnp.where(live_row, rate, 0.0) * (ETA_BASE / head_dim)
    fac_ref[0, :padded] = eta_row * (1.0 - rate)
    fac_ref[0, padded:] = eta_row
    for i in every:
        at = i * head_dim
        k = proj[:, cols + at : cols + at + head_dim]
        v = proj[:, 2 * cols + at : 2 * cols + at + head_dim]
        kb, qb = k.astype(BF), proj[:, at : at + head_dim].astype(BF)
        k_minis = kb.reshape(group, MINI, head_dim)
        q_minis = qb.reshape(group, MINI, head_dim)
        kq_ref[i, :, :MINI] = k_minis
        kq_ref[i, :, MINI:] = q_minis
        next_ref[i, : group - 1, :MINI] = k_minis[1:]
        next_ref[i, group - 1 :, :MINI] = k_minis[:1]
        next_ref[i, :, MINI:] = q_minis
        kmv_ref[i] = (k - v).reshape(group, MINI, head_dim)
        rate_ref[i] = (eta_col[:, i : i + 1] * (1.0 / MINI)).reshape(group, MINI, 1)
        cross = (mm_nt(kb, kb) + 1.0) * (eta_row[i : i + 1] * (1.0 / MINI))
        for j in range(group - 1):
            at = j * MINI
            kk_ref[i, j] = cross[at + MINI : at + 2 * MINI, at : at + MINI].astype(BF)

    key_pre = [mm(kq_ref[i, 0, :MINI], w1_ref[i].astype(BF)) + c1_ref[i] for i in every]
    for j in range(group):
        rate = [rate_ref[i, j] for i in every]
        kmv = [kmv_ref[i, j] for i in every]
        stacked = [next_ref[i, j] for i in every]
        k = [kq_ref[i, j, :MINI] for i in every]
        kk = [kk_ref[i, j] for i in every] if j < group - 1 else None
        w1 = [w1_ref[i] for i in every]
        w2 = [w2_ref[i] for i in every]
        c1 = [c1_ref[i] for i in every]
        c2 = [c2_ref[i] for i in every]
        w1b = [w1[i].astype(BF) for i in every]
        w2b = [w2[i].astype(BF) for i in every]
        parts = [gelu_parts(key_pre[i]) for i in every]
        hb = [(key_pre[i] * parts[i][0]).astype(BF) for i in every]
        g2 = [mm_nt(hb[i], w2b[i]) + c2[i] + kmv[i] for i in every]
        slope = [parts[i][0] + key_pre[i] * parts[i][1] for i in every]
        curve = [parts[i][1] * (2.0 - key_pre[i] * key_pre[i]) for i in every]
        both = [mm(stacked[i], w1b[i]) + c1[i] for i in every]
        g2b = [g2[i].astype(BF) for i in every]
        u = [mm(g2b[i], w2b[i]) for i in every]
        fg2 = [rate[i] * g2[i] for i in every]
        w2n = [w2[i] - mm_tn(fg2[i].astype(BF), hb[i]) for i in every]
        c2n = [c2[i] - jnp.sum(fg2[i], axis=0, keepdims=True) for i in every]
        g1 = [u[i] * slope[i] for i in every]
        g1b = [g1[i].astype(BF) for i in every]
        if j < group - 1:
            key_pre = [both[i][:MINI] - mm(kk[i], g1b[i]) for i in every]
        fg1 = [rate[i] * g1[i] for i in every]
        w1n = [w1[i] - mm_tn(k[i], fg1[i].astype(BF)) for i in every]
        c1n = [c1[i] - jnp.sum(fg1[i], axis=0, keepdims=True) for i in every]
        for i in every:
            w1s_ref[i, j] = w1b[i]
            w2s_ref[i, j] = w2b[i]
            c2s_ref[i, j] = c2[i]
            h_ref[i, j] = hb[i]
            g1_ref[i, j] = g1b[i]
            g2_ref[i, j] = g2b[i]
            ga_ref[i, j] = slope[i]
            ug_ref[i, j] = u[i] * curve[i]
            pq_ref[i, j] = both[i][MINI:]
            w1_ref[i] = w1n[i]
            w2_ref[i] = w2n[i]
            c1_ref[i] = c1n[i]
            c2_ref[i] = c2n[i]

    scale = mini_masks(rows)[0]
    for i in every:
        at = i * head_dim
        q = proj[:, at : at + head_dim]
        gate = proj[:, 3 * cols + at : 3 * cols + at + head_dim]
        kb, qb = flat_rows(kq_ref[i, :, :MINI]), flat_rows(kq_ref[i, :, MINI:])
        hb, g1b, g2b = flat_rows(h_ref[i]), flat_rows(g1_ref[i]), flat_rows(g2_ref[i])
        mix = scale * eta_row[i : i + 1]
        query_pre = flat_rows(pq_ref[i]) - mm((mix * (mm_nt(qb, kb) + 1.0)).astype(BF), g1b)
        cdf, pdf = gelu_parts(query_pre)
        gp_ref[i] = (cdf + query_pre * pdf).reshape(group, MINI, -1)
        rb = (query_pre * cdf).astype(BF)
        r_ref[i] = rb.reshape(group, MINI, -1)
        s2 = (mix * (mm_nt(rb, hb) + 1.0)).astype(BF)
        through = [mm_nt(piece, w2s_ref[i, j]) + c2s_ref[i, j] for j, piece in enumerate(minis(rb))]
        mixed = q + jnp.concatenate(through, axis=0) - mm(s2, g2b)
        centered = mixed - jnp.mean(mixed, axis=-1, keepdims=True)
        hscale = row_scale(centered)
        unit = centered * hscale
        out = unit * pg_ref[i] + pb_ref[i]
        cdf, pdf = gelu_parts(gate)
        post_ref[:, at : at + head_dim] = (gate * cdf * out).astype(BF)
        gl_ref[i] = gate * cdf
        gs_ref[i] = (cdf + gate * pdf) * out
        unit_ref[i] = unit
        hscale_ref[i] = hscale


def bwd_kernel(
    x_ref, gain_ref, wc_ref, lrt_ref, pg_ref, gpost_ref, w1i_ref, c1i_ref, w2i_ref, c2i_ref,
    kq_ref, rate_ref, fac_ref, gl_ref, gs_ref, unit_ref, hscale_ref,
    w1s_ref, w2s_ref, h_ref, r_ref, g1_ref, g2_ref, ga_ref, ug_ref, gp_ref,
    back_ref, gw_ref, glr_ref, gain_grad_ref, gpg_ref, gpb_ref, dw1_ref, dc1_ref, dw2_ref, dc2_ref,
    d_ref, g1a_ref, g2a_ref, ha_ref, ka_ref, dp_ref, kc_ref, dk_ref, da_ref, df_ref, de_ref, all_ref,
):
    chains, group = kq_ref.shape[:2]
    rows = group * MINI
    head_dim = kq_ref.shape[-1]
    cols = chains * head_dim
    every = range(chains)

    @pl.when(pl.program_id(0) == 0)
    def _():
        dw1_ref[...] = w1i_ref[...]
        dc1_ref[...] = c1i_ref[...]
        dw2_ref[...] = w2i_ref[...]
        dc2_ref[...] = c2i_ref[...]
        gw_ref[...] = jnp.zeros_like(gw_ref)
        glr_ref[...] = jnp.zeros_like(glr_ref)
        gain_grad_ref[...] = jnp.zeros_like(gain_grad_ref)
        gpg_ref[...] = jnp.zeros_like(gpg_ref)
        gpb_ref[...] = jnp.zeros_like(gpb_ref)

    scale, eye = mini_masks(rows)
    padded = lrt_ref.shape[0]
    gpost = gpost_ref[...].astype(F32)
    for i in every:
        at = i * head_dim
        piece = gpost[:, at : at + head_dim]
        all_ref[:, 3 * cols + at : 3 * cols + at + head_dim] = (piece * gs_ref[i]).astype(BF)
        head = piece * gl_ref[i]
        unit = unit_ref[i]
        gpg_ref[i] += jnp.sum(head * unit, axis=0, keepdims=True)
        gpb_ref[i] += jnp.sum(head, axis=0, keepdims=True)
        lifted = head * pg_ref[i]
        d = hscale_ref[i] * (
            lifted
            - jnp.mean(lifted, axis=-1, keepdims=True)
            - unit * jnp.mean(lifted * unit, axis=-1, keepdims=True)
        )
        d_ref[i] = d.reshape(group, MINI, head_dim)
        db = d.astype(BF)
        kb, qb = flat_rows(kq_ref[i, :, :MINI]), flat_rows(kq_ref[i, :, MINI:])
        hb, rb, g1b, g2b = (flat_rows(ref[i]) for ref in (h_ref, r_ref, g1_ref, g2_ref))
        mix = scale * fac_ref[0, padded + i : padded + i + 1]
        ds2 = -mm_nt(db, g2b)
        x2 = mm_nt(rb, hb) + 1.0
        x1 = mm_nt(qb, kb) + 1.0
        dx2 = (ds2 * mix).astype(BF)
        dr = jnp.concatenate([mm(part, w2s_ref[i, j]) for j, part in enumerate(minis(db))], axis=0)
        dp = (dr + mm(dx2, hb)) * flat_rows(gp_ref[i])
        dpb = dp.astype(BF)
        ds1 = -mm_nt(dpb, g1b)
        dx1 = (ds1 * mix).astype(BF)
        dq = jnp.concatenate([mm_nt(part, w1s_ref[i, j]) for j, part in enumerate(minis(dpb))], axis=0)
        all_ref[:, at : at + head_dim] = (d + dq + mm(dx1, kb)).astype(BF)
        g1a_ref[i] = -mm_tn((mix * x1).astype(BF), dpb).reshape(group, MINI, -1)
        g2a_ref[i] = -mm_tn((mix * x2).astype(BF), db).reshape(group, MINI, -1)
        ha_ref[i] = mm_tn(dx2, rb).reshape(group, MINI, -1)
        ka_ref[i] = mm_tn(dx1, qb).reshape(group, MINI, -1)
        dp_ref[i] = dpb.reshape(group, MINI, -1)
        de_ref[i] = jnp.sum((ds2 * x2 + ds1 * x1) * scale, axis=0, keepdims=True)
        kk = mm_nt(kb, kb) + 1.0
        kx = mm_nt(kb, qb) + 1.0
        for j in range(group - 1):
            own, after = slice(j * MINI, (j + 1) * MINI), slice((j + 1) * MINI, (j + 2) * MINI)
            kc_ref[i, j] = jnp.concatenate([kk[own, after], kx[own, after]], axis=1).astype(BF)

    t1 = [mm(kq_ref[i, group - 1, :MINI], dw1_ref[i].astype(BF)) + dc1_ref[i] for i in every]
    for j in reversed(range(group)):

        def all_of(ref):
            return [ref[i, j] for i in every]

        d, kq, rate, w2b, hb, rb, g1b, g2b = (
            all_of(ref) for ref in (d_ref, kq_ref, rate_ref, w2s_ref, h_ref, r_ref, g1_ref, g2_ref)
        )
        ga, ug, dpb, g1a, g2a, ha = (
            all_of(ref) for ref in (ga_ref, ug_ref, dp_ref, g1a_ref, g2a_ref, ha_ref)
        )
        dw1 = [dw1_ref[i] for i in every]
        dw2 = [dw2_ref[i] for i in every]
        dc1 = [dc1_ref[i] for i in every]
        dc2 = [dc2_ref[i] for i in every]
        g1 = [g1b[i].astype(F32) for i in every]
        g2 = [g2b[i].astype(F32) for i in every]
        dw1b = [dw1[i].astype(BF) for i in every]
        dw2b = [dw2[i].astype(BF) for i in every]
        dg1 = [g1a[i] - rate[i] * t1[i] for i in every]
        dub = [(dg1[i] * ga[i]).astype(BF) for i in every]
        through = [mm_nt(dub[i], w2b[i]) for i in every]
        t2 = [mm_nt(hb[i], dw2b[i]) + dc2[i] for i in every]
        dha = [ha[i] - mm((rate[i] * g2[i]).astype(BF), dw2b[i]) for i in every]
        dg2 = [through[i] + (g2a[i] - rate[i] * t2[i]) for i in every]
        dg2b = [dg2[i].astype(BF) for i in every]
        dh = [mm(dg2b[i], w2b[i]) + dha[i] for i in every]
        if j > 0:
            base = [mm(kq_ref[i, j - 1, :MINI], dw1b[i]) + dc1[i] for i in every]
        dk = [dg2[i] - mm_nt((rate[i] * g1[i]).astype(BF), dw1b[i]) for i in every]
        df = [
            -(
                jnp.sum(g1[i] * t1[i], axis=1, keepdims=True)
                + jnp.sum(g2[i] * t2[i], axis=1, keepdims=True)
            )
            for i in every
        ]
        da = [dg1[i] * ug[i] + dh[i] * ga[i] for i in every]
        dab = [da[i].astype(BF) for i in every]
        both = [jnp.concatenate([dab[i], dpb[i]], axis=0) for i in every]
        if j > 0:
            t1 = [base[i] + mm(kc_ref[i, j - 1], both[i]) for i in every]
        dw1n = [dw1[i] + mm_tn(kq[i], both[i]) for i in every]
        dc1n = [dc1[i] + jnp.sum(da[i] + dpb[i].astype(F32), axis=0, keepdims=True) for i in every]
        dw2n = [
            dw2[i]
            + mm_tn(
                jnp.concatenate([d[i].astype(BF), dg2b[i], g2b[i]], axis=0),
                jnp.concatenate([rb[i], hb[i], dub[i]], axis=0),
            )
            for i in every
        ]
        dc2n = [dc2[i] + jnp.sum(d[i] + dg2[i], axis=0, keepdims=True) for i in every]
        for i in every:
            piece, at = slice(j * MINI, (j + 1) * MINI), 2 * cols + i * head_dim
            all_ref[piece, at : at + head_dim] = (-dg2[i]).astype(BF)
            dk_ref[i, j] = dk[i]
            da_ref[i, j] = dab[i]
            df_ref[i, j] = df[i]
            dw1_ref[i] = dw1n[i]
            dc1_ref[i] = dc1n[i]
            dw2_ref[i] = dw2n[i]
            dc2_ref[i] = dc2n[i]

    x = x_ref[...].astype(F32)
    unit_in = x * row_scale(x)
    normed = (unit_in * gain_ref[...]).astype(BF)
    lrt = lrt_ref[...]
    which = lax.broadcasted_iota(jnp.int32, (padded, rows), 0)
    rates = jnp.zeros((padded, rows), F32)
    for i in every:
        at = cols + i * head_dim
        dk = jnp.concatenate([mm_nt(da_ref[i, j], w1s_ref[i, j]) for j in range(group)], axis=0)
        all_ref[:, at : at + head_dim] = (flat_rows(dk_ref[i]) + flat_rows(ka_ref[i]) + dk).astype(BF)
        line = de_ref[i] + jnp.sum(eye * flat_rows(df_ref[i]), axis=0, keepdims=True)
        rates = jnp.where(which == i, line, rates)
    rates = (rates * fac_ref[0, :padded]).astype(BF)
    grads = all_ref[...]
    back = mm_nt(grads, wc_ref[...]) + mm_tn(rates, lrt)
    gain_grad_ref[...] += jnp.sum(back * unit_in, axis=0, keepdims=True)
    back_ref[...] = back.astype(BF)
    gw_ref[...] += mm_tn(normed, grads)
    glr_ref[...] += mm(rates, normed)


GROUP = 8


def block_specs(chains, head_dim, inner, padded, place):
    rows = GROUP * MINI

    def mini(first, second):
        return pl.BlockSpec((chains, GROUP, first, second), lambda g: (0, place(g), 0, 0))

    def head(second):
        return pl.BlockSpec((chains, rows, second), lambda g: (0, place(g), 0))

    return [
        mini(2 * MINI, head_dim), mini(MINI, 1),
        pl.BlockSpec((1, 2 * padded, rows), lambda g: (place(g), 0, 0)),
        head(head_dim), head(head_dim), head(head_dim), head(1),
        mini(head_dim, inner), mini(head_dim, inner), mini(MINI, inner), mini(MINI, inner),
        mini(MINI, inner), mini(MINI, head_dim), mini(MINI, inner), mini(MINI, inner), mini(MINI, inner),
    ]


def whole_spec(value):
    return pl.BlockSpec(value.shape, lambda g: (0,) * value.ndim)


def run_fwd(first, last, length, tokens, gain, wc, lr, lrt, pg, pb, state):
    width = tokens.shape[1]
    chains, head_dim, inner = state[0].shape
    rows = GROUP * MINI
    steps = last - first
    count = steps * GROUP
    padded = lrt.shape[0]

    def mini(first_size, second_size, dtype):
        return jax.ShapeDtypeStruct((chains, count, first_size, second_size), dtype)

    def head(second):
        return jax.ShapeDtypeStruct((chains, steps * rows, second), F32)

    row_spec = pl.BlockSpec((rows, width), lambda g: (first + g, 0))
    small = (gain, wc, lr, lrt, *state, pg, pb)
    return pl.pallas_call(
        partial(fwd_kernel, first=first),
        grid=(steps,),
        in_specs=[pl.BlockSpec(memory_space=pltpu.SMEM), row_spec] + [whole_spec(v) for v in small],
        out_specs=[pl.BlockSpec((rows, chains * head_dim), lambda g: (g, 0))]
        + block_specs(chains, head_dim, inner, padded, lambda g: g)
        + [whole_spec(v) for v in state],
        out_shape=[
            jax.ShapeDtypeStruct((steps * rows, chains * head_dim), BF),
            mini(2 * MINI, head_dim, BF), mini(MINI, 1, F32),
            jax.ShapeDtypeStruct((steps, 2 * padded, rows), F32),
            head(head_dim), head(head_dim), head(head_dim), head(1),
            mini(head_dim, inner, BF), mini(head_dim, inner, BF), mini(MINI, inner, BF), mini(MINI, inner, BF),
            mini(MINI, inner, BF), mini(MINI, head_dim, BF), mini(MINI, inner, F32), mini(MINI, inner, F32),
            mini(MINI, inner, F32),
        ]
        + [jax.ShapeDtypeStruct(v.shape, F32) for v in state],
        scratch_shapes=[
            pltpu.VMEM((chains, GROUP, MINI, head_dim), F32),
            pltpu.VMEM((chains, GROUP, 2 * MINI, head_dim), BF),
            pltpu.VMEM((chains, GROUP, MINI, MINI), BF),
            pltpu.VMEM((chains, GROUP, MINI, inner), F32),
            pltpu.VMEM((chains, GROUP, 1, head_dim), F32),
        ],
        compiler_params=pltpu.CompilerParams(vmem_limit_bytes=50 << 20),
        cost_estimate=pl.CostEstimate(
            flops=9_000_000_000 * steps, bytes_accessed=5_000_000 * steps, transcendentals=0
        ),
        name="chain_forward",
    )(length, tokens, *small)


def run_bwd(first, last, tokens, gain, wc, lrt, pg, gpost, state, saved):
    width = tokens.shape[1]
    chains, head_dim, inner = state[0].shape
    rows = GROUP * MINI
    padded = lrt.shape[0]
    wide = wc.shape[1]
    steps = last - first

    def place(g):
        return steps - 1 - g

    def shape(*extent):
        return jax.ShapeDtypeStruct(extent, F32)

    small = (gain, wc, lrt, pg)
    outs = [
        shape(width, wide), shape(padded, width), shape(1, width), shape(chains, 1, head_dim), shape(chains, 1, head_dim),
        shape(chains, head_dim, inner), shape(chains, 1, inner), shape(chains, head_dim, inner), shape(chains, 1, head_dim),
    ]

    def scratch(first_size, second_size, dtype):
        return pltpu.VMEM((chains, GROUP, first_size, second_size), dtype)

    return pl.pallas_call(
        bwd_kernel,
        grid=(steps,),
        in_specs=[pl.BlockSpec((rows, width), lambda g: (first + place(g), 0))]
        + [whole_spec(v) for v in small]
        + [pl.BlockSpec((rows, chains * head_dim), lambda g: (first + place(g), 0))]
        + [whole_spec(v) for v in state]
        + block_specs(chains, head_dim, inner, padded, place),
        out_specs=[pl.BlockSpec((rows, width), lambda g: (place(g), 0))] + [whole_spec(v) for v in outs],
        out_shape=[jax.ShapeDtypeStruct((steps * rows, width), BF)] + outs,
        scratch_shapes=[
            scratch(MINI, head_dim, F32), scratch(MINI, inner, F32), scratch(MINI, head_dim, F32),
            scratch(MINI, inner, F32), scratch(MINI, head_dim, F32), scratch(MINI, inner, BF),
            scratch(MINI, 2 * MINI, BF), scratch(MINI, head_dim, F32), scratch(MINI, inner, BF),
            scratch(MINI, 1, F32), pltpu.VMEM((chains, 1, rows), F32), pltpu.VMEM((rows, wide), BF),
        ],
        compiler_params=pltpu.CompilerParams(vmem_limit_bytes=50 << 20),
        cost_estimate=pl.CostEstimate(
            flops=11_000_000_000 * steps, bytes_accessed=5_000_000 * steps, transcendentals=0
        ),
        name="chain_backward",
    )(tokens, *small, gpost, *state, *saved)


def row_norm(value):
    return lax.rsqrt(jnp.mean(value * value, axis=-1, keepdims=True) + EPSILON)


def pieces_of(chains, depth, head_dim, inner_share, head_share):
    return (
        ("lr", (depth, chains)),
        ("w1", (chains, head_dim, inner_share)),
        ("w2", (chains, head_dim, inner_share)),
        ("b1", (chains, inner_share)),
        ("b2", (chains, head_share)),
        ("pg", (chains, head_share)),
        ("pb", (chains, head_share)),
        ("n1", (depth,)),
        ("n2", (depth,)),
    )


def size_of(shape):
    total = 1
    for extent in shape:
        total *= extent
    return total


def swap(value):
    return lax.ppermute(value, "tp", [(0, 1), (1, 0)])


def place_kernel(spots_ref, *refs):
    *sources, target = refs
    for number, source in enumerate(sources):
        target[spots_ref[number]] = source[...]


def placed(pieces, spots):
    return pl.pallas_call(
        place_kernel,
        in_specs=[pl.BlockSpec(memory_space=pltpu.SMEM)]
        + [pl.BlockSpec(memory_space=pltpu.VMEM)] * len(pieces),
        out_specs=pl.BlockSpec(memory_space=pltpu.VMEM),
        out_shape=jax.ShapeDtypeStruct((len(pieces),) + pieces[0].shape, pieces[0].dtype),
        compiler_params=pltpu.CompilerParams(vmem_limit_bytes=40 << 20),
        name="place_pieces",
    )(jnp.stack(spots).astype(jnp.int32), *pieces)


def exchanged(value, axis):
    size = lax.axis_size(axis)
    return [value] + [
        lax.ppermute(value, axis, [(source, source ^ bit) for source in range(size)])
        for bit in range(1, size)
    ]


def scattered(value, axis):
    size = lax.axis_size(axis)
    me = lax.axis_index(axis)
    taken = [lax.dynamic_index_in_dim(value, me ^ bit, 0, keepdims=False) for bit in range(size)]
    return taken[:1] + [
        lax.ppermute(taken[bit], axis, [(source, source ^ bit) for source in range(size)])
        for bit in range(1, size)
    ]


def placed_along(pieces, axis):
    me = lax.axis_index(axis)
    return placed(pieces, [me ^ bit for bit in range(len(pieces))])


def spread(value, axis):
    return placed_along(exchanged(value, axis), axis)


def tied(*values):
    return lax.optimization_barrier(values)


def in_turn(first, second):
    return jnp.where(lax.axis_index("tp") == 0, jnp.stack([first, second]), jnp.stack([second, first]))


def on_device(
    tokens,
    lengths,
    norm1_gain,
    qkv_weight,
    lr_weight,
    inner_w1,
    inner_b1,
    inner_w2,
    inner_b2,
    post_gain,
    post_bias,
    gate_weight,
    out_weight,
    norm2_gain,
    ffn_gate,
    ffn_up,
    ffn_down,
    cotangent,
):
    micro, span, width = tokens.shape
    ring = lax.axis_size("ctx")
    shards = lax.axis_size("shard")
    pair = lax.axis_size("tp")
    place = lax.axis_index("ctx")
    core = lax.axis_index("tp")
    local_heads, head_dim, inner_share = inner_w1.shape
    head_share = inner_b2.shape[1]
    depth = norm1_gain.shape[0]
    inner = inner_share * shards
    total_heads = local_heads * pair
    chains = -(-total_heads // ring)
    span_all = ring * span
    count = span_all // MINI
    cols = chains * head_dim
    wide = 4 * cols

    row_tokens = lax.dynamic_index_in_dim(tokens, core, 0, keepdims=False)
    slot_tokens = spread(row_tokens, "ctx").reshape(span_all, width)

    first_head = jnp.minimum(place * chains, total_heads - chains)
    owner = first_head // local_heads
    local_first = first_head - owner * local_heads

    def of_heads(value, axis):
        return lax.dynamic_slice_in_dim(value, local_first, chains, axis)

    pieces = pieces_of(chains, depth, head_dim, inner_share, head_share)
    small_size = sum(size_of(shape) for _, shape in pieces)
    small_rows = -(-small_size // wide)
    small_rows = -(-(small_rows + depth) // 32) * 32 - depth
    half_rows = (small_rows + depth) // 2
    own = {
        "lr": of_heads(lr_weight, 1),
        "w1": of_heads(inner_w1, 0),
        "w2": of_heads(inner_w2, 0),
        "b1": of_heads(inner_b1, 0),
        "b2": of_heads(inner_b2, 0),
        "pg": of_heads(post_gain, 0),
        "pb": of_heads(post_bias, 0),
        "n1": norm1_gain,
        "n2": norm2_gain,
    }
    small = jnp.concatenate([own[name].reshape(-1) for name, _ in pieces])
    small = jnp.pad(small, (0, small_rows * wide - small_size)).reshape(small_rows, wide)
    qkv_heads = of_heads(qkv_weight.reshape(depth, 3, local_heads, head_dim), 2)
    gate_heads = of_heads(gate_weight.reshape(depth, local_heads, head_dim), 1)
    big = jnp.concatenate(
        [qkv_heads.reshape(depth, 3 * cols), gate_heads.reshape(depth, cols)], axis=1
    )
    packed = jnp.concatenate([big, small], axis=0)
    packed = jnp.where(core == owner, packed, swap(packed))
    packed = spread(lax.dynamic_slice_in_dim(packed, core * half_rows, half_rows, 0), "shard")
    packed = in_turn(packed, swap(packed))
    gathered = packed.transpose(1, 0, 2, 3).reshape(shards, depth + small_rows, wide)
    units = ffn_gate.shape[1]
    half_out = out_weight.shape[0]
    row_pack = jnp.concatenate([ffn_gate, ffn_up, ffn_down.T, out_weight.T], axis=1)
    part = depth // ring
    row_part = lax.dynamic_slice_in_dim(row_pack, place * part, part, 0)
    row_part, gathered = tied(row_part, gathered)
    row_parts = exchanged(row_part, "shard")

    w_chain = gathered[:, :depth].reshape(width, wide)
    flat = gathered[:, depth:].reshape(shards, small_rows * wide)
    full = {}
    offset = 0
    for name, shape in pieces:
        full[name] = flat[:, offset : offset + size_of(shape)].reshape((shards,) + shape)
        offset += size_of(shape)
    w_rate = full["lr"].reshape(width, chains)
    gain_one = full["n1"].reshape(width).astype(F32)
    gain_two = full["n2"].reshape(width).astype(F32)

    def along(name):
        return jnp.moveaxis(full[name], 0, -2).reshape(full[name].shape[1:-1] + (-1,)).astype(F32)

    init_first, init_second = along("w1"), along("w2")
    init_first_bias, init_second_bias = along("b1"), along("b2")
    norm_gain, norm_bias = along("pg"), along("pb")

    slot_length = lax.dynamic_index_in_dim(lengths, core, 0, keepdims=True)
    gain_row = gain_one[None]
    rate_cols = jnp.pad(w_rate, ((0, 0), (0, 128 - chains)))
    rate_rows = jnp.pad(w_rate.T, ((0, -chains % 16), (0, 0)))
    norm_gain, norm_bias = norm_gain[:, None], norm_bias[:, None]
    steps = span_all // (GROUP * MINI)
    middle = steps // 2
    state = (init_first, init_first_bias[:, None], init_second, init_second_bias[:, None])

    def forward(first, last, begin):
        done = run_fwd(
            first, last, slot_length, slot_tokens, gain_row, w_chain, rate_cols, rate_rows, norm_gain, norm_bias, begin
        )
        return done[0], done[1:-4], done[-4:]

    post_low, saved_low, state_low = forward(0, middle, state)
    state_low, row_parts = tied(state_low, row_parts)
    far = jnp.stack(row_parts[1:])
    state_low, far = tied(state_low, far)
    far_parts = exchanged(far, "ctx")
    post_high, saved_high, _ = forward(middle, steps, tuple(state_low))
    post_chain = jnp.concatenate([post_low, post_high])

    def to_rows(value):
        return lax.all_to_all(value.reshape(ring, span, -1), "ctx", 0, 0)

    post = to_rows(post_chain)
    post = post.transpose(1, 0, 2).reshape(span, ring * cols)[:, : total_heads * head_dim]

    far_parts, post = tied(far_parts, post)
    me = lax.axis_index("shard")
    blocks = [row_pack[start : start + part] for start in range(0, depth, part)]
    spots = [me * ring + number for number in range(ring)]
    for bit, group in enumerate(far_parts):
        for other in range(1, shards):
            blocks.append(group[other - 1])
            spots.append((me ^ other) * ring + (place ^ bit))
    w_own = placed(blocks, spots).reshape(width, -1)
    w_other = jnp.concatenate([swap(w_own[:, : 3 * units]), swap(w_own[:, 3 * units :])], axis=1)

    def split_up(value):
        return tuple(value[:, start : start + units] for start in range(0, 3 * units, units))

    halves = (split_up(w_own), split_up(w_other))
    w_out = jnp.concatenate(
        [
            jnp.where(core == 0, w_own[:, 3 * units :], w_other[:, 3 * units :]),
            jnp.where(core == 0, w_other[:, 3 * units :], w_own[:, 3 * units :]),
        ],
        axis=1,
    )
    row_in = row_tokens.astype(F32)
    hidden = row_in + mm_nt(post, w_out)
    scale_two = row_norm(hidden)
    normed_two = (hidden * scale_two * gain_two).astype(BF)
    position = place * span + lax.iota(jnp.int32, span)
    live = (position < slot_length[0]).astype(F32)[:, None]
    cot = lax.dynamic_index_in_dim(cotangent, core, 0, keepdims=False)
    back = cot.astype(F32) * live
    back_low = back.astype(BF)
    feed = 0.0
    grad_two = 0.0
    sums = []
    for w_gate, w_up, w_down in halves:
        up_gate = mm(normed_two, w_gate)
        up_lin = mm(normed_two, w_up)
        gate = jax.nn.sigmoid(up_gate)
        act_low = (up_gate * gate * up_lin).astype(BF)
        feed = feed + mm_nt(act_low, w_down)
        grad_act = mm(back_low, w_down)
        grad_gate_low = (grad_act * up_lin * gate * (1.0 + up_gate * (1.0 - gate))).astype(BF)
        grad_lin_low = (grad_act * up_gate * gate).astype(BF)
        grad_two = grad_two + mm_nt(grad_gate_low, w_gate) + mm_nt(grad_lin_low, w_up)
        sums.append(
            [
                mm_tn(normed_two, grad_gate_low),
                mm_tn(normed_two, grad_lin_low),
                mm_tn(back_low, act_low),
            ]
        )
    output = (hidden + feed).astype(BF)
    lifted = grad_two * gain_two
    grad_hidden = (
        back
        + scale_two * lifted
        - hidden * scale_two**3 * jnp.mean(lifted * hidden, axis=-1, keepdims=True)
    )
    grad_gain_two = jnp.sum(grad_two * hidden * scale_two, axis=0)
    grad_hidden_low = grad_hidden.astype(BF)
    grad_post = mm(grad_hidden_low, w_out)

    grad_out = mm_tn(grad_hidden_low, post)
    grad_out_own = lax.dynamic_slice_in_dim(grad_out, core * half_out, half_out, 1)
    grad_out_other = lax.dynamic_slice_in_dim(grad_out, (1 - core) * half_out, half_out, 1)
    own_sum = jnp.concatenate(sums[0] + [grad_out_own], axis=1)
    other_sum = jnp.concatenate(sums[1] + [grad_out_other], axis=1).astype(BF)
    row_sum = (own_sum + swap(other_sum).astype(F32)).astype(BF)
    row_sum = row_sum.reshape(shards, ring, part, -1).transpose(1, 0, 2, 3)
    cut = 2 * units
    sum_a = scattered(row_sum[..., :cut], "ctx")
    sum_b = scattered(row_sum[..., cut:], "ctx")

    def folded(values):
        return sum(value.astype(F32) for value in values).astype(BF)

    grad_post = jnp.pad(grad_post.astype(BF), ((0, 0), (0, ring * cols - total_heads * head_dim)))
    grad_post = lax.all_to_all(grad_post.reshape(span, ring, cols).transpose(1, 0, 2), "ctx", 0, 0)
    grad_post = grad_post.reshape(span_all, cols)

    def backward(first, last, begin, saved):
        done = run_bwd(
            first, last, slot_tokens, gain_row, w_chain, rate_rows, norm_gain, grad_post, begin, saved
        )
        return done[0], done[1:6], done[6:]

    begin = tuple(jnp.zeros_like(value) for value in state)
    grad_post, row_sum = tied(grad_post, row_sum)
    back_high, sums_high, ending = backward(middle, steps, begin, saved_high)
    ending, sum_a = tied(ending, sum_a)
    sum_a = folded(sum_a)
    ending, sum_a = tied(ending, sum_a)
    sum_a = scattered(sum_a, "shard")
    back_low_half, sums_low, ending = backward(0, middle, tuple(ending), saved_low)
    ending, back_low_half, sum_a, sum_b = tied(ending, back_low_half, sum_a, sum_b)
    d_first, d_first_bias, d_second, d_second_bias = ending
    grad_big, grad_lr, grad_gain_one, grad_norm_gain, grad_norm_bias = (
        low + high for low, high in zip(sums_low, sums_high)
    )
    grad_lr = grad_lr[:chains].T
    back_part = jnp.concatenate([back_low_half, back_high])
    back_one = jnp.sum(to_rows(back_part).astype(F32), axis=0)
    scale_one = row_norm(row_in)
    lifted = back_one * gain_one
    input_grad = (
        grad_hidden
        + scale_one * lifted
        - row_in * scale_one**3 * jnp.mean(lifted * row_in, axis=-1, keepdims=True)
    ).astype(BF)

    sum_b = scattered(folded(sum_b), "shard")
    row_sum = spread(jnp.concatenate([folded(sum_a), folded(sum_b)], axis=-1), "ctx")
    row_sum = row_sum.reshape(depth, -1).astype(F32)
    g_ffn_gate = row_sum[:, :units]
    g_ffn_up = row_sum[:, units : 2 * units]
    g_ffn_down = row_sum[:, 2 * units : 3 * units].T
    g_out = row_sum[:, 3 * units :].T


    def by_shard(value):
        split = value.reshape(value.shape[:-1] + (shards, -1))
        return jnp.moveaxis(split, -2, 0).reshape(shards, -1)

    flat = jnp.concatenate(
        [
            grad_lr.reshape(shards, -1),
            by_shard(d_first),
            by_shard(d_second),
            by_shard(d_first_bias[:, 0]),
            by_shard(d_second_bias[:, 0]),
            by_shard(grad_norm_gain[:, 0]),
            by_shard(grad_norm_bias[:, 0]),
            grad_gain_one.reshape(shards, -1),
            grad_gain_two.reshape(shards, -1),
        ],
        axis=1,
    )
    flat = jnp.pad(flat, ((0, 0), (0, small_rows * wide - small_size)))
    chain_sum = jnp.concatenate(
        [grad_big.reshape(shards, depth, wide), flat.reshape(shards, small_rows, wide)], axis=1
    ).astype(BF)
    kept_half = lax.dynamic_slice_in_dim(chain_sum, core * half_rows, half_rows, 1)
    sent_half = lax.dynamic_slice_in_dim(chain_sum, (1 - core) * half_rows, half_rows, 1)
    chain_sum = (kept_half.astype(F32) + swap(sent_half).astype(F32)).astype(BF)
    chain_sum = spread(folded(scattered(chain_sum, "shard")), "ctx")
    chain_sum = in_turn(chain_sum, swap(chain_sum)).astype(F32)
    chain_sum = chain_sum.transpose(1, 0, 2, 3).reshape(ring, depth + small_rows, wide)
    places = local_heads // chains
    mine = lax.dynamic_slice_in_dim(chain_sum, core * places, places, 0)
    mine_big = mine[:, :depth].reshape(places, depth, 4, cols).transpose(1, 2, 0, 3)
    mine_big = mine_big.reshape(depth, 4, local_heads * head_dim)
    flat_all = chain_sum[:, depth:].reshape(ring, -1)
    flat_mine = mine[:, depth:].reshape(places, -1)
    parts = {}
    offset = 0
    for name, shape in pieces:
        source = flat_all if name in ("n1", "n2") else flat_mine
        parts[name] = source[:, offset : offset + size_of(shape)].reshape((source.shape[0],) + shape)
        offset += size_of(shape)

    def stacked(name):
        return parts[name].reshape((local_heads,) + parts[name].shape[2:])

    return (
        in_turn(output, swap(output)),
        in_turn(input_grad, swap(input_grad)),
        jnp.sum(parts["n1"], axis=0),
        mine_big[:, :3],
        parts["lr"].transpose(1, 0, 2).reshape(depth, local_heads),
        stacked("w1"),
        stacked("b1"),
        stacked("w2"),
        stacked("b2"),
        stacked("pg"),
        stacked("pb"),
        mine_big[:, 3],
        g_out,
        jnp.sum(parts["n2"], axis=0),
        g_ffn_gate,
        g_ffn_up,
        g_ffn_down,
    )


def solution(mesh):
    in_specs = (
        P("shard", "ctx", None),
        P("shard"),
        P("shard"),
        P("shard", None, "tp"),
        P("shard", "tp"),
        P("tp", None, "shard"),
        P("tp", "shard"),
        P("tp", None, "shard"),
        P("tp", "shard"),
        P("tp", "shard"),
        P("tp", "shard"),
        P("shard", "tp"),
        P("tp", "shard"),
        P("shard"),
        P("shard", "tp"),
        P("shard", "tp"),
        P("tp", "shard"),
        P("shard", "ctx", None),
    )
    out_specs = (
        P("shard", "ctx", None),
        P("shard", "ctx", None),
        P("shard"),
        P("shard", None, "tp"),
        P("shard", "tp"),
        P("tp", None, "shard"),
        P("tp", "shard"),
        P("tp", None, "shard"),
        P("tp", "shard"),
        P("tp", "shard"),
        P("tp", "shard"),
        P("shard", "tp"),
        P("tp", "shard"),
        P("shard"),
        P("shard", "tp"),
        P("shard", "tp"),
        P("tp", "shard"),
    )
    return jax.shard_map(
        on_device, mesh=mesh, in_specs=in_specs, out_specs=out_specs, check_vma=False
    )
```

```python
from functools import partial
import jax
import jax.numpy as jnp
from jax import lax
from jax.experimental import pallas as pl
from jax.experimental.pallas import tpu as pltpu
from jax.sharding import PartitionSpec as P

MINI = 16
EPSILON = 1e-06
ETA_BASE = 0.5
BF = jnp.bfloat16
F32 = jnp.float32


def mm(left, right):
    return lax.dot_general(left, right, (((1,), (0,)), ((), ())), preferred_element_type=F32)


def mm_nt(left, right):
    return lax.dot_general(left, right, (((1,), (1,)), ((), ())), preferred_element_type=F32)


def mm_tn(left, right):
    return lax.dot_general(left, right, (((0,), (0,)), ((), ())), preferred_element_type=F32)


def gelu_parts(value):
    cdf = 0.5 + 0.5 * lax.erf(value * 0.7071067811865476)
    pdf = jnp.exp(-0.5 * value * value) * 0.3989422804014327
    return cdf, pdf


def row_scale(value):
    return lax.rsqrt(jnp.mean(value * value, axis=-1, keepdims=True) + EPSILON)


def mini_masks(rows):
    row = lax.broadcasted_iota(jnp.int32, (rows, rows), 0)
    col = lax.broadcasted_iota(jnp.int32, (rows, rows), 1)
    within = (lax.div(row, MINI) == lax.div(col, MINI)) & (col <= row)
    scale = jnp.where(within, 1.0 / (lax.rem(row, MINI) + 1).astype(F32), 0.0)
    return scale, jnp.where(row == col, 1.0 / MINI, 0.0)


def minis(value):
    return [value[at : at + MINI] for at in range(0, value.shape[0], MINI)]


def flat_rows(value):
    return value.reshape(value.shape[0] * value.shape[1], value.shape[2])


def fwd_kernel(
    length_ref, x_ref, gain_ref, wc_ref, lr_ref, lrt_ref, w1i_ref, c1i_ref, w2i_ref, c2i_ref, pg_ref, pb_ref,
    post_ref, kq_ref, rate_ref, fac_ref, gl_ref, gs_ref, unit_ref, hscale_ref,
    w1s_ref, w2s_ref, h_ref, r_ref, g1_ref, g2_ref, ga_ref, ug_ref, gp_ref,
    w1_ref, c1_ref, w2_ref, c2_ref, kmv_ref, next_ref, kk_ref, pq_ref, c2s_ref, *, first,
):
    chains, group = kq_ref.shape[:2]
    rows = group * MINI
    head_dim = kq_ref.shape[-1]
    cols = chains * head_dim
    every = range(chains)

    @pl.when(pl.program_id(0) == 0)
    def _():
        w1_ref[...] = w1i_ref[...]
        c1_ref[...] = c1i_ref[...]
        w2_ref[...] = w2i_ref[...]
        c2_ref[...] = c2i_ref[...]

    start = (first + pl.program_id(0)) * rows
    padded = lrt_ref.shape[0]
    x = x_ref[...].astype(F32)
    normed = (x * row_scale(x) * gain_ref[...]).astype(BF)
    proj = mm(normed, wc_ref[...])
    length = length_ref[0]
    live_col = start + lax.broadcasted_iota(jnp.int32, (rows, 128), 0) < length
    live_row = start + lax.broadcasted_iota(jnp.int32, (padded, rows), 1) < length
    eta_col = jnp.where(live_col, jax.nn.sigmoid(mm(normed, lr_ref[...])), 0.0) * (ETA_BASE / head_dim)
    rate = jax.nn.sigmoid(mm_nt(lrt_ref[...], normed))
    eta_row = jnp.where(live_row, rate, 0.0) * (ETA_BASE / head_dim)
    fac_ref[0, :padded] = eta_row * (1.0 - rate)
    fac_ref[0, padded:] = eta_row
    for i in every:
        at = i * head_dim
        k = proj[:, cols + at : cols + at + head_dim]
        v = proj[:, 2 * cols + at : 2 * cols + at + head_dim]
        kb, qb = k.astype(BF), proj[:, at : at + head_dim].astype(BF)
        k_minis = kb.reshape(group, MINI, head_dim)
        q_minis = qb.reshape(group, MINI, head_dim)
        kq_ref[i, :, :MINI] = k_minis
        kq_ref[i, :, MINI:] = q_minis
        next_ref[i, : group - 1, :MINI] = k_minis[1:]
        next_ref[i, group - 1 :, :MINI] = k_minis[:1]
        next_ref[i, :, MINI:] = q_minis
        kmv_ref[i] = (k - v).reshape(group, MINI, head_dim)
        rate_ref[i] = (eta_col[:, i : i + 1] * (1.0 / MINI)).reshape(group, MINI, 1)
        cross = (mm_nt(kb, kb) + 1.0) * (eta_row[i : i + 1] * (1.0 / MINI))
        for j in range(group - 1):
            at = j * MINI
            kk_ref[i, j] = cross[at + MINI : at + 2 * MINI, at : at + MINI].astype(BF)

    key_pre = [mm(kq_ref[i, 0, :MINI], w1_ref[i].astype(BF)) + c1_ref[i] for i in every]
    for j in range(group):
        rate = [rate_ref[i, j] for i in every]
        kmv = [kmv_ref[i, j] for i in every]
        stacked = [next_ref[i, j] for i in every]
        k = [kq_ref[i, j, :MINI] for i in every]
        kk = [kk_ref[i, j] for i in every] if j < group - 1 else None
        w1 = [w1_ref[i] for i in every]
        w2 = [w2_ref[i] for i in every]
        c1 = [c1_ref[i] for i in every]
        c2 = [c2_ref[i] for i in every]
        w1b = [w1[i].astype(BF) for i in every]
        w2b = [w2[i].astype(BF) for i in every]
        parts = [gelu_parts(key_pre[i]) for i in every]
        hb = [(key_pre[i] * parts[i][0]).astype(BF) for i in every]
        g2 = [mm_nt(hb[i], w2b[i]) + c2[i] + kmv[i] for i in every]
        slope = [parts[i][0] + key_pre[i] * parts[i][1] for i in every]
        curve = [parts[i][1] * (2.0 - key_pre[i] * key_pre[i]) for i in every]
        both = [mm(stacked[i], w1b[i]) + c1[i] for i in every]
        g2b = [g2[i].astype(BF) for i in every]
        u = [mm(g2b[i], w2b[i]) for i in every]
        fg2 = [rate[i] * g2[i] for i in every]
        w2n = [w2[i] - mm_tn(fg2[i].astype(BF), hb[i]) for i in every]
        c2n = [c2[i] - jnp.sum(fg2[i], axis=0, keepdims=True) for i in every]
        g1 = [u[i] * slope[i] for i in every]
        g1b = [g1[i].astype(BF) for i in every]
        if j < group - 1:
            key_pre = [both[i][:MINI] - mm(kk[i], g1b[i]) for i in every]
        fg1 = [rate[i] * g1[i] for i in every]
        w1n = [w1[i] - mm_tn(k[i], fg1[i].astype(BF)) for i in every]
        c1n = [c1[i] - jnp.sum(fg1[i], axis=0, keepdims=True) for i in every]
        for i in every:
            w1s_ref[i, j] = w1b[i]
            w2s_ref[i, j] = w2b[i]
            c2s_ref[i, j] = c2[i]
            h_ref[i, j] = hb[i]
            g1_ref[i, j] = g1b[i]
            g2_ref[i, j] = g2b[i]
            ga_ref[i, j] = slope[i]
            ug_ref[i, j] = u[i] * curve[i]
            pq_ref[i, j] = both[i][MINI:]
            w1_ref[i] = w1n[i]
            w2_ref[i] = w2n[i]
            c1_ref[i] = c1n[i]
            c2_ref[i] = c2n[i]

    scale = mini_masks(rows)[0]
    for i in every:
        at = i * head_dim
        q = proj[:, at : at + head_dim]
        gate = proj[:, 3 * cols + at : 3 * cols + at + head_dim]
        kb, qb = flat_rows(kq_ref[i, :, :MINI]), flat_rows(kq_ref[i, :, MINI:])
        hb, g1b, g2b = flat_rows(h_ref[i]), flat_rows(g1_ref[i]), flat_rows(g2_ref[i])
        mix = scale * eta_row[i : i + 1]
        query_pre = flat_rows(pq_ref[i]) - mm((mix * (mm_nt(qb, kb) + 1.0)).astype(BF), g1b)
        cdf, pdf = gelu_parts(query_pre)
        gp_ref[i] = (cdf + query_pre * pdf).reshape(group, MINI, -1)
        rb = (query_pre * cdf).astype(BF)
        r_ref[i] = rb.reshape(group, MINI, -1)
        s2 = (mix * (mm_nt(rb, hb) + 1.0)).astype(BF)
        through = [mm_nt(piece, w2s_ref[i, j]) + c2s_ref[i, j] for j, piece in enumerate(minis(rb))]
        mixed = q + jnp.concatenate(through, axis=0) - mm(s2, g2b)
        centered = mixed - jnp.mean(mixed, axis=-1, keepdims=True)
        hscale = row_scale(centered)
        unit = centered * hscale
        out = unit * pg_ref[i] + pb_ref[i]
        cdf, pdf = gelu_parts(gate)
        post_ref[:, at : at + head_dim] = (gate * cdf * out).astype(BF)
        gl_ref[i] = gate * cdf
        gs_ref[i] = (cdf + gate * pdf) * out
        unit_ref[i] = unit
        hscale_ref[i] = hscale


def bwd_kernel(
    x_ref, gain_ref, wc_ref, lrt_ref, pg_ref, gpost_ref, w1i_ref, c1i_ref, w2i_ref, c2i_ref,
    kq_ref, rate_ref, fac_ref, gl_ref, gs_ref, unit_ref, hscale_ref,
    w1s_ref, w2s_ref, h_ref, r_ref, g1_ref, g2_ref, ga_ref, ug_ref, gp_ref,
    back_ref, gw_ref, glr_ref, gain_grad_ref, gpg_ref, gpb_ref, dw1_ref, dc1_ref, dw2_ref, dc2_ref,
    d_ref, g1a_ref, g2a_ref, ha_ref, ka_ref, dp_ref, kc_ref, dk_ref, da_ref, df_ref, de_ref, all_ref,
):
    chains, group = kq_ref.shape[:2]
    rows = group * MINI
    head_dim = kq_ref.shape[-1]
    cols = chains * head_dim
    every = range(chains)

    @pl.when(pl.program_id(0) == 0)
    def _():
        dw1_ref[...] = w1i_ref[...]
        dc1_ref[...] = c1i_ref[...]
        dw2_ref[...] = w2i_ref[...]
        dc2_ref[...] = c2i_ref[...]
        gw_ref[...] = jnp.zeros_like(gw_ref)
        glr_ref[...] = jnp.zeros_like(glr_ref)
        gain_grad_ref[...] = jnp.zeros_like(gain_grad_ref)
        gpg_ref[...] = jnp.zeros_like(gpg_ref)
        gpb_ref[...] = jnp.zeros_like(gpb_ref)

    scale, eye = mini_masks(rows)
    padded = lrt_ref.shape[0]
    gpost = gpost_ref[...].astype(F32)
    for i in every:
        at = i * head_dim
        piece = gpost[:, at : at + head_dim]
        all_ref[:, 3 * cols + at : 3 * cols + at + head_dim] = (piece * gs_ref[i]).astype(BF)
        head = piece * gl_ref[i]
        unit = unit_ref[i]
        gpg_ref[i] += jnp.sum(head * unit, axis=0, keepdims=True)
        gpb_ref[i] += jnp.sum(head, axis=0, keepdims=True)
        lifted = head * pg_ref[i]
        d = hscale_ref[i] * (
            lifted
            - jnp.mean(lifted, axis=-1, keepdims=True)
            - unit * jnp.mean(lifted * unit, axis=-1, keepdims=True)
        )
        d_ref[i] = d.reshape(group, MINI, head_dim)
        db = d.astype(BF)
        kb, qb = flat_rows(kq_ref[i, :, :MINI]), flat_rows(kq_ref[i, :, MINI:])
        hb, rb, g1b, g2b = (flat_rows(ref[i]) for ref in (h_ref, r_ref, g1_ref, g2_ref))
        mix = scale * fac_ref[0, padded + i : padded + i + 1]
        ds2 = -mm_nt(db, g2b)
        x2 = mm_nt(rb, hb) + 1.0
        x1 = mm_nt(qb, kb) + 1.0
        dx2 = (ds2 * mix).astype(BF)
        dr = jnp.concatenate([mm(part, w2s_ref[i, j]) for j, part in enumerate(minis(db))], axis=0)
        dp = (dr + mm(dx2, hb)) * flat_rows(gp_ref[i])
        dpb = dp.astype(BF)
        ds1 = -mm_nt(dpb, g1b)
        dx1 = (ds1 * mix).astype(BF)
        dq = jnp.concatenate([mm_nt(part, w1s_ref[i, j]) for j, part in enumerate(minis(dpb))], axis=0)
        all_ref[:, at : at + head_dim] = (d + dq + mm(dx1, kb)).astype(BF)
        g1a_ref[i] = -mm_tn((mix * x1).astype(BF), dpb).reshape(group, MINI, -1)
        g2a_ref[i] = -mm_tn((mix * x2).astype(BF), db).reshape(group, MINI, -1)
        ha_ref[i] = mm_tn(dx2, rb).reshape(group, MINI, -1)
        ka_ref[i] = mm_tn(dx1, qb).reshape(group, MINI, -1)
        dp_ref[i] = dpb.reshape(group, MINI, -1)
        de_ref[i] = jnp.sum((ds2 * x2 + ds1 * x1) * scale, axis=0, keepdims=True)
        kk = mm_nt(kb, kb) + 1.0
        kx = mm_nt(kb, qb) + 1.0
        for j in range(group - 1):
            own, after = slice(j * MINI, (j + 1) * MINI), slice((j + 1) * MINI, (j + 2) * MINI)
            kc_ref[i, j] = jnp.concatenate([kk[own, after], kx[own, after]], axis=1).astype(BF)

    t1 = [mm(kq_ref[i, group - 1, :MINI], dw1_ref[i].astype(BF)) + dc1_ref[i] for i in every]
    for j in reversed(range(group)):

        def all_of(ref):
            return [ref[i, j] for i in every]

        d, kq, rate, w2b, hb, rb, g1b, g2b = (
            all_of(ref) for ref in (d_ref, kq_ref, rate_ref, w2s_ref, h_ref, r_ref, g1_ref, g2_ref)
        )
        ga, ug, dpb, g1a, g2a, ha = (
            all_of(ref) for ref in (ga_ref, ug_ref, dp_ref, g1a_ref, g2a_ref, ha_ref)
        )
        dw1 = [dw1_ref[i] for i in every]
        dw2 = [dw2_ref[i] for i in every]
        dc1 = [dc1_ref[i] for i in every]
        dc2 = [dc2_ref[i] for i in every]
        g1 = [g1b[i].astype(F32) for i in every]
        g2 = [g2b[i].astype(F32) for i in every]
        dw1b = [dw1[i].astype(BF) for i in every]
        dw2b = [dw2[i].astype(BF) for i in every]
        dg1 = [g1a[i] - rate[i] * t1[i] for i in every]
        dub = [(dg1[i] * ga[i]).astype(BF) for i in every]
        through = [mm_nt(dub[i], w2b[i]) for i in every]
        t2 = [mm_nt(hb[i], dw2b[i]) + dc2[i] for i in every]
        dha = [ha[i] - mm((rate[i] * g2[i]).astype(BF), dw2b[i]) for i in every]
        dg2 = [through[i] + (g2a[i] - rate[i] * t2[i]) for i in every]
        dg2b = [dg2[i].astype(BF) for i in every]
        dh = [mm(dg2b[i], w2b[i]) + dha[i] for i in every]
        if j > 0:
            base = [mm(kq_ref[i, j - 1, :MINI], dw1b[i]) + dc1[i] for i in every]
        dk = [dg2[i] - mm_nt((rate[i] * g1[i]).astype(BF), dw1b[i]) for i in every]
        df = [
            -(
                jnp.sum(g1[i] * t1[i], axis=1, keepdims=True)
                + jnp.sum(g2[i] * t2[i], axis=1, keepdims=True)
            )
            for i in every
        ]
        da = [dg1[i] * ug[i] + dh[i] * ga[i] for i in every]
        dab = [da[i].astype(BF) for i in every]
        both = [jnp.concatenate([dab[i], dpb[i]], axis=0) for i in every]
        if j > 0:
            t1 = [base[i] + mm(kc_ref[i, j - 1], both[i]) for i in every]
        dw1n = [dw1[i] + mm_tn(kq[i], both[i]) for i in every]
        dc1n = [dc1[i] + jnp.sum(da[i] + dpb[i].astype(F32), axis=0, keepdims=True) for i in every]
        dw2n = [
            dw2[i]
            + mm_tn(
                jnp.concatenate([d[i].astype(BF), dg2b[i], g2b[i]], axis=0),
                jnp.concatenate([rb[i], hb[i], dub[i]], axis=0),
            )
            for i in every
        ]
        dc2n = [dc2[i] + jnp.sum(d[i] + dg2[i], axis=0, keepdims=True) for i in every]
        for i in every:
            piece, at = slice(j * MINI, (j + 1) * MINI), 2 * cols + i * head_dim
            all_ref[piece, at : at + head_dim] = (-dg2[i]).astype(BF)
            dk_ref[i, j] = dk[i]
            da_ref[i, j] = dab[i]
            df_ref[i, j] = df[i]
            dw1_ref[i] = dw1n[i]
            dc1_ref[i] = dc1n[i]
            dw2_ref[i] = dw2n[i]
            dc2_ref[i] = dc2n[i]

    x = x_ref[...].astype(F32)
    unit_in = x * row_scale(x)
    normed = (unit_in * gain_ref[...]).astype(BF)
    lrt = lrt_ref[...]
    which = lax.broadcasted_iota(jnp.int32, (padded, rows), 0)
    rates = jnp.zeros((padded, rows), F32)
    for i in every:
        at = cols + i * head_dim
        dk = jnp.concatenate([mm_nt(da_ref[i, j], w1s_ref[i, j]) for j in range(group)], axis=0)
        all_ref[:, at : at + head_dim] = (flat_rows(dk_ref[i]) + flat_rows(ka_ref[i]) + dk).astype(BF)
        line = de_ref[i] + jnp.sum(eye * flat_rows(df_ref[i]), axis=0, keepdims=True)
        rates = jnp.where(which == i, line, rates)
    rates = (rates * fac_ref[0, :padded]).astype(BF)
    grads = all_ref[...]
    back = mm_nt(grads, wc_ref[...]) + mm_tn(rates, lrt)
    gain_grad_ref[...] += jnp.sum(back * unit_in, axis=0, keepdims=True)
    back_ref[...] = back.astype(BF)
    gw_ref[...] += mm_tn(normed, grads)
    glr_ref[...] += mm(rates, normed)


GROUP = 8


def block_specs(chains, head_dim, inner, padded, place):
    rows = GROUP * MINI

    def mini(first, second):
        return pl.BlockSpec((chains, GROUP, first, second), lambda g: (0, place(g), 0, 0))

    def head(second):
        return pl.BlockSpec((chains, rows, second), lambda g: (0, place(g), 0))

    return [
        mini(2 * MINI, head_dim), mini(MINI, 1),
        pl.BlockSpec((1, 2 * padded, rows), lambda g: (place(g), 0, 0)),
        head(head_dim), head(head_dim), head(head_dim), head(1),
        mini(head_dim, inner), mini(head_dim, inner), mini(MINI, inner), mini(MINI, inner),
        mini(MINI, inner), mini(MINI, head_dim), mini(MINI, inner), mini(MINI, inner), mini(MINI, inner),
    ]


def whole_spec(value):
    return pl.BlockSpec(value.shape, lambda g: (0,) * value.ndim)


def run_fwd(first, last, length, tokens, gain, wc, lr, lrt, pg, pb, state):
    width = tokens.shape[1]
    chains, head_dim, inner = state[0].shape
    rows = GROUP * MINI
    steps = last - first
    count = steps * GROUP
    padded = lrt.shape[0]

    def mini(first_size, second_size, dtype):
        return jax.ShapeDtypeStruct((chains, count, first_size, second_size), dtype)

    def head(second):
        return jax.ShapeDtypeStruct((chains, steps * rows, second), F32)

    row_spec = pl.BlockSpec((rows, width), lambda g: (first + g, 0))
    small = (gain, wc, lr, lrt, *state, pg, pb)
    return pl.pallas_call(
        partial(fwd_kernel, first=first),
        grid=(steps,),
        in_specs=[pl.BlockSpec(memory_space=pltpu.SMEM), row_spec] + [whole_spec(v) for v in small],
        out_specs=[pl.BlockSpec((rows, chains * head_dim), lambda g: (g, 0))]
        + block_specs(chains, head_dim, inner, padded, lambda g: g)
        + [whole_spec(v) for v in state],
        out_shape=[
            jax.ShapeDtypeStruct((steps * rows, chains * head_dim), BF),
            mini(2 * MINI, head_dim, BF), mini(MINI, 1, F32),
            jax.ShapeDtypeStruct((steps, 2 * padded, rows), F32),
            head(head_dim), head(head_dim), head(head_dim), head(1),
            mini(head_dim, inner, BF), mini(head_dim, inner, BF), mini(MINI, inner, BF), mini(MINI, inner, BF),
            mini(MINI, inner, BF), mini(MINI, head_dim, BF), mini(MINI, inner, F32), mini(MINI, inner, F32),
            mini(MINI, inner, F32),
        ]
        + [jax.ShapeDtypeStruct(v.shape, F32) for v in state],
        scratch_shapes=[
            pltpu.VMEM((chains, GROUP, MINI, head_dim), F32),
            pltpu.VMEM((chains, GROUP, 2 * MINI, head_dim), BF),
            pltpu.VMEM((chains, GROUP, MINI, MINI), BF),
            pltpu.VMEM((chains, GROUP, MINI, inner), F32),
            pltpu.VMEM((chains, GROUP, 1, head_dim), F32),
        ],
        compiler_params=pltpu.CompilerParams(vmem_limit_bytes=50 << 20),
        cost_estimate=pl.CostEstimate(
            flops=9_000_000_000 * steps, bytes_accessed=5_000_000 * steps, transcendentals=0
        ),
        name="chain_forward",
    )(length, tokens, *small)


def run_bwd(first, last, tokens, gain, wc, lrt, pg, gpost, state, saved):
    width = tokens.shape[1]
    chains, head_dim, inner = state[0].shape
    rows = GROUP * MINI
    padded = lrt.shape[0]
    wide = wc.shape[1]
    steps = last - first

    def place(g):
        return steps - 1 - g

    def shape(*extent):
        return jax.ShapeDtypeStruct(extent, F32)

    small = (gain, wc, lrt, pg)
    outs = [
        shape(width, wide), shape(padded, width), shape(1, width), shape(chains, 1, head_dim), shape(chains, 1, head_dim),
        shape(chains, head_dim, inner), shape(chains, 1, inner), shape(chains, head_dim, inner), shape(chains, 1, head_dim),
    ]

    def scratch(first_size, second_size, dtype):
        return pltpu.VMEM((chains, GROUP, first_size, second_size), dtype)

    return pl.pallas_call(
        bwd_kernel,
        grid=(steps,),
        in_specs=[pl.BlockSpec((rows, width), lambda g: (first + place(g), 0))]
        + [whole_spec(v) for v in small]
        + [pl.BlockSpec((rows, chains * head_dim), lambda g: (first + place(g), 0))]
        + [whole_spec(v) for v in state]
        + block_specs(chains, head_dim, inner, padded, place),
        out_specs=[pl.BlockSpec((rows, width), lambda g: (place(g), 0))] + [whole_spec(v) for v in outs],
        out_shape=[jax.ShapeDtypeStruct((steps * rows, width), BF)] + outs,
        scratch_shapes=[
            scratch(MINI, head_dim, F32), scratch(MINI, inner, F32), scratch(MINI, head_dim, F32),
            scratch(MINI, inner, F32), scratch(MINI, head_dim, F32), scratch(MINI, inner, BF),
            scratch(MINI, 2 * MINI, BF), scratch(MINI, head_dim, F32), scratch(MINI, inner, BF),
            scratch(MINI, 1, F32), pltpu.VMEM((chains, 1, rows), F32), pltpu.VMEM((rows, wide), BF),
        ],
        compiler_params=pltpu.CompilerParams(vmem_limit_bytes=50 << 20),
        cost_estimate=pl.CostEstimate(
            flops=11_000_000_000 * steps, bytes_accessed=5_000_000 * steps, transcendentals=0
        ),
        name="chain_backward",
    )(tokens, *small, gpost, *state, *saved)


def row_norm(value):
    return lax.rsqrt(jnp.mean(value * value, axis=-1, keepdims=True) + EPSILON)


def pieces_of(chains, depth, head_dim, inner_share, head_share):
    return (
        ("lr", (depth, chains)),
        ("w1", (chains, head_dim, inner_share)),
        ("w2", (chains, head_dim, inner_share)),
        ("b1", (chains, inner_share)),
        ("b2", (chains, head_share)),
        ("pg", (chains, head_share)),
        ("pb", (chains, head_share)),
        ("n1", (depth,)),
        ("n2", (depth,)),
    )


def size_of(shape):
    total = 1
    for extent in shape:
        total *= extent
    return total


def swap(value):
    return lax.ppermute(value, "tp", [(0, 1), (1, 0)])


def rows_kernel(
    spot_ref, post_ref, own_ref, other_ref, x_ref, cot_ref, gain_ref,
    out_ref, grad_ref, gpost_ref, acts_ref, normed_ref, low_ref, cat_ref, back_ref, gain_grad_ref,
):
    core, start, length = spot_ref[0], spot_ref[1], spot_ref[2]
    span, width = x_ref.shape
    cols = post_ref.shape[2]
    units = acts_ref.shape[3]
    places = cat_ref.shape[2] // cols
    x = x_ref[...].astype(F32)
    live = start + lax.broadcasted_iota(jnp.int32, (span, width), 0) < length
    back = jnp.where(live, cot_ref[...].astype(F32), 0.0)
    back_low = back.astype(BF)
    back_ref[...] = back_low
    halves = ((own_ref, core), (other_ref, 1 - core))
    hidden = x
    for half, (w_ref, side) in enumerate(halves):
        joined = jnp.concatenate([post_ref[side * places + p] for p in range(places)], axis=1)
        cat_ref[half] = joined
        hidden = hidden + mm_nt(joined, w_ref[:, 3 * units :])
    scale = row_scale(hidden)
    gain = gain_ref[...]
    normed = (hidden * scale * gain).astype(BF)
    normed_ref[...] = normed
    feed = jnp.zeros((span, width), F32)
    grad = jnp.zeros((span, width), F32)
    step = min(units, 512)
    for half, (w_ref, _) in enumerate(halves):
        for at in range(0, units, step):
            w_gate = w_ref[:, at : at + step]
            w_up = w_ref[:, units + at : units + at + step]
            w_down = w_ref[:, 2 * units + at : 2 * units + at + step]
            up_gate = mm(normed, w_gate)
            up_lin = mm(normed, w_up)
            grad_act = mm(back_low, w_down)
            gate = jax.nn.sigmoid(up_gate)
            silu = up_gate * gate
            act = (silu * up_lin).astype(BF)
            grad_gate = (grad_act * up_lin * (gate * (1.0 + up_gate * (1.0 - gate)))).astype(BF)
            grad_lin = (grad_act * silu).astype(BF)
            acts_ref[half, 0, :, at : at + step] = grad_gate
            acts_ref[half, 1, :, at : at + step] = grad_lin
            acts_ref[half, 2, :, at : at + step] = act
            feed += mm_nt(act, w_down)
            grad += mm_nt(grad_gate, w_gate) + mm_nt(grad_lin, w_up)
    out_ref[...] = (hidden + feed).astype(BF)
    lifted = grad * gain
    hat = hidden * scale
    gain_grad_ref[...] = jnp.sum(grad * hat, axis=0, keepdims=True)
    total = back + scale * (lifted - hat * jnp.mean(lifted * hat, axis=-1, keepdims=True))
    grad_ref[...] = total
    low = total.astype(BF)
    low_ref[...] = low
    for p in range(2 * places, gpost_ref.shape[0]):
        gpost_ref[p] = jnp.zeros(gpost_ref.shape[1:], BF)
    for w_ref, side in halves:
        gpost = mm(low, w_ref[:, 3 * units :]).astype(BF)
        for p in range(places):
            gpost_ref[side * places + p] = gpost[:, p * cols : (p + 1) * cols]


def run_rows(spots, post, own, other, x, cot, gain, half_out):
    ring, span, cols = post.shape
    width = x.shape[1]
    units = (own.shape[1] - half_out) // 3
    vmem = pl.BlockSpec(memory_space=pltpu.VMEM)

    def shape(extent, dtype):
        return jax.ShapeDtypeStruct(extent, dtype)

    return pl.pallas_call(
        rows_kernel,
        in_specs=[pl.BlockSpec(memory_space=pltpu.SMEM)] + [vmem] * 6,
        out_specs=[vmem] * 9,
        out_shape=[
            shape((span, width), BF), shape((span, width), F32), shape((ring, span, cols), BF),
            shape((2, 3, span, units), BF), shape((span, width), BF), shape((span, width), BF),
            shape((2, span, half_out), BF), shape((span, width), BF), shape((1, width), F32),
        ],
        compiler_params=pltpu.CompilerParams(vmem_limit_bytes=52 << 20),
        cost_estimate=pl.CostEstimate(flops=20_000_000_000, bytes_accessed=20_000_000, transcendentals=0),
        name="rows_main",
    )(spots, post, own, other, x, cot, gain)


def products(pairs, parts, store):
    start = 0
    for left, right in zip(pairs, parts):
        size = right.shape[-1]
        step = 512 if size % 512 == 0 else size
        for at in range(0, size, step):
            store(start + at, mm_tn(left[...], right[:, at : at + step]))
        start += size


def sums_other_kernel(*refs):
    *sources, out_ref = refs
    count = len(sources) // 2

    def store(at, value):
        out_ref[:, at : at + value.shape[1]] = value.astype(BF)

    products(sources[:count], sources[count:], store)


def sums_own_kernel(place_ref, other_ref, *refs, count, outs):
    sources, out_refs, held_ref = refs[: 2 * count], refs[2 * count : 2 * count + outs], refs[-1]

    def store(at, value):
        piece = slice(at, at + value.shape[1])
        held_ref[:, piece] = (value + other_ref[:, piece].astype(F32)).astype(BF)

    products(sources[:count], sources[count:], store)
    shards, part = out_refs[0].shape[:2]
    for bit, out_ref in enumerate(out_refs):
        for z in range(shards):
            at = pl.multiple_of((z * outs + (place_ref[0] ^ bit)) * part, part)
            out_ref[z] = held_ref[pl.ds(at, part), :]


def run_sums(lefts, rights, other=None, place=None, shards=1, ring=1):
    width = lefts[0].shape[1]
    total = sum(right.shape[1] for right in rights)
    vmem = pl.BlockSpec(memory_space=pltpu.VMEM)
    count = len(lefts)
    params = pltpu.CompilerParams(vmem_limit_bytes=40 << 20)
    cost = pl.CostEstimate(flops=5_000_000_000, bytes_accessed=6_000_000, transcendentals=0)
    if other is None:
        return pl.pallas_call(
            sums_other_kernel,
            in_specs=[vmem] * (2 * count),
            out_specs=vmem,
            out_shape=jax.ShapeDtypeStruct((width, total), BF),
            compiler_params=params,
            cost_estimate=cost,
            name="sums_other",
        )(*lefts, *rights)
    part = width // (shards * ring)
    return pl.pallas_call(
        partial(sums_own_kernel, count=count, outs=ring),
        in_specs=[pl.BlockSpec(memory_space=pltpu.SMEM)] + [vmem] * (2 * count + 1),
        out_specs=[vmem] * ring,
        out_shape=[jax.ShapeDtypeStruct((shards, part, total), BF)] * ring,
        scratch_shapes=[pltpu.VMEM((width, total), BF)],
        compiler_params=params,
        cost_estimate=cost,
        name="sums_own",
    )(place, other, *lefts, *rights)


def assemble_kernel(spots_ref, pack_ref, *refs):
    *far_refs, out_ref = refs
    me, place = spots_ref[0], spots_ref[1]
    ring = len(far_refs)
    part = out_ref.shape[1]
    for number in range(ring):
        out_ref[me * ring + number] = pack_ref[number * part : (number + 1) * part]
    for bit, far_ref in enumerate(far_refs):
        for other in range(far_ref.shape[0]):
            out_ref[(me ^ (other + 1)) * ring + (place ^ bit)] = far_ref[other]


def run_assemble(spots, pack, far_parts, shards):
    vmem = pl.BlockSpec(memory_space=pltpu.VMEM)
    ring = len(far_parts)
    part = pack.shape[0] // ring
    return pl.pallas_call(
        assemble_kernel,
        in_specs=[pl.BlockSpec(memory_space=pltpu.SMEM)] + [vmem] * (1 + ring),
        out_specs=vmem,
        out_shape=jax.ShapeDtypeStruct((shards * ring, part, pack.shape[1]), BF),
        compiler_params=pltpu.CompilerParams(vmem_limit_bytes=40 << 20),
        name="assemble_rows",
    )(spots, pack, *far_parts)


def place_kernel(spots_ref, *refs):
    *sources, target = refs
    for number, source in enumerate(sources):
        target[spots_ref[number]] = source[...]


def placed(pieces, spots):
    return pl.pallas_call(
        place_kernel,
        in_specs=[pl.BlockSpec(memory_space=pltpu.SMEM)]
        + [pl.BlockSpec(memory_space=pltpu.VMEM)] * len(pieces),
        out_specs=pl.BlockSpec(memory_space=pltpu.VMEM),
        out_shape=jax.ShapeDtypeStruct((len(pieces),) + pieces[0].shape, pieces[0].dtype),
        compiler_params=pltpu.CompilerParams(vmem_limit_bytes=40 << 20),
        name="place_pieces",
    )(jnp.stack(spots).astype(jnp.int32), *pieces)


def exchanged(value, axis):
    size = lax.axis_size(axis)
    return [value] + [
        lax.ppermute(value, axis, [(source, source ^ bit) for source in range(size)])
        for bit in range(1, size)
    ]


def sent(taken, axis):
    return taken[:1] + [
        lax.ppermute(taken[bit], axis, [(source, source ^ bit) for source in range(len(taken))])
        for bit in range(1, len(taken))
    ]


def scattered(value, axis):
    size = lax.axis_size(axis)
    me = lax.axis_index(axis)
    return sent([lax.dynamic_index_in_dim(value, me ^ bit, 0, keepdims=False) for bit in range(size)], axis)


def placed_along(pieces, axis):
    me = lax.axis_index(axis)
    return placed(pieces, [me ^ bit for bit in range(len(pieces))])


def spread(value, axis):
    return placed_along(exchanged(value, axis), axis)


def tied(*values):
    return lax.optimization_barrier(values)


def in_turn(first, second):
    return jnp.where(lax.axis_index("tp") == 0, jnp.stack([first, second]), jnp.stack([second, first]))


def on_device(
    tokens,
    lengths,
    norm1_gain,
    qkv_weight,
    lr_weight,
    inner_w1,
    inner_b1,
    inner_w2,
    inner_b2,
    post_gain,
    post_bias,
    gate_weight,
    out_weight,
    norm2_gain,
    ffn_gate,
    ffn_up,
    ffn_down,
    cotangent,
):
    micro, span, width = tokens.shape
    ring = lax.axis_size("ctx")
    shards = lax.axis_size("shard")
    pair = lax.axis_size("tp")
    place = lax.axis_index("ctx")
    core = lax.axis_index("tp")
    local_heads, head_dim, inner_share = inner_w1.shape
    head_share = inner_b2.shape[1]
    depth = norm1_gain.shape[0]
    inner = inner_share * shards
    total_heads = local_heads * pair
    chains = -(-total_heads // ring)
    span_all = ring * span
    count = span_all // MINI
    cols = chains * head_dim
    wide = 4 * cols

    row_tokens = lax.dynamic_index_in_dim(tokens, core, 0, keepdims=False)
    slot_tokens = spread(row_tokens, "ctx").reshape(span_all, width)

    first_head = jnp.minimum(place * chains, total_heads - chains)
    owner = first_head // local_heads
    local_first = first_head - owner * local_heads

    def of_heads(value, axis):
        return lax.dynamic_slice_in_dim(value, local_first, chains, axis)

    pieces = pieces_of(chains, depth, head_dim, inner_share, head_share)
    small_size = sum(size_of(shape) for _, shape in pieces)
    small_rows = -(-small_size // wide)
    small_rows = -(-(small_rows + depth) // 32) * 32 - depth
    half_rows = (small_rows + depth) // 2
    own = {
        "lr": of_heads(lr_weight, 1),
        "w1": of_heads(inner_w1, 0),
        "w2": of_heads(inner_w2, 0),
        "b1": of_heads(inner_b1, 0),
        "b2": of_heads(inner_b2, 0),
        "pg": of_heads(post_gain, 0),
        "pb": of_heads(post_bias, 0),
        "n1": norm1_gain,
        "n2": norm2_gain,
    }
    small = jnp.concatenate([own[name].reshape(-1) for name, _ in pieces])
    small = jnp.pad(small, (0, small_rows * wide - small_size)).reshape(small_rows, wide)
    qkv_heads = of_heads(qkv_weight.reshape(depth, 3, local_heads, head_dim), 2)
    gate_heads = of_heads(gate_weight.reshape(depth, local_heads, head_dim), 1)
    big = jnp.concatenate(
        [qkv_heads.reshape(depth, 3 * cols), gate_heads.reshape(depth, cols)], axis=1
    )
    packed = jnp.concatenate([big, small], axis=0)
    packed = jnp.where(core == owner, packed, swap(packed))
    packed = spread(lax.dynamic_slice_in_dim(packed, core * half_rows, half_rows, 0), "shard")
    packed = in_turn(packed, swap(packed))
    gathered = packed.transpose(1, 0, 2, 3).reshape(shards, depth + small_rows, wide)
    units = ffn_gate.shape[1]
    half_out = out_weight.shape[0]
    row_pack = jnp.concatenate([ffn_gate, ffn_up, ffn_down.T, out_weight.T], axis=1)
    part = depth // ring
    row_part = lax.dynamic_slice_in_dim(row_pack, place * part, part, 0)
    row_part, gathered = tied(row_part, gathered)
    row_parts = exchanged(row_part, "shard")

    w_chain = gathered[:, :depth].reshape(width, wide)
    flat = gathered[:, depth:].reshape(shards, small_rows * wide)
    full = {}
    offset = 0
    for name, shape in pieces:
        full[name] = flat[:, offset : offset + size_of(shape)].reshape((shards,) + shape)
        offset += size_of(shape)
    w_rate = full["lr"].reshape(width, chains)
    gain_one = full["n1"].reshape(width).astype(F32)
    gain_two = full["n2"].reshape(width).astype(F32)

    def along(name):
        return jnp.moveaxis(full[name], 0, -2).reshape(full[name].shape[1:-1] + (-1,)).astype(F32)

    init_first, init_second = along("w1"), along("w2")
    init_first_bias, init_second_bias = along("b1"), along("b2")
    norm_gain, norm_bias = along("pg"), along("pb")

    slot_length = lax.dynamic_index_in_dim(lengths, core, 0, keepdims=True)
    gain_row = gain_one[None]
    rate_cols = jnp.pad(w_rate, ((0, 0), (0, 128 - chains)))
    rate_rows = jnp.pad(w_rate.T, ((0, -chains % 16), (0, 0)))
    norm_gain, norm_bias = norm_gain[:, None], norm_bias[:, None]
    steps = span_all // (GROUP * MINI)
    middle = steps // 2
    state = (init_first, init_first_bias[:, None], init_second, init_second_bias[:, None])

    def forward(first, last, begin):
        done = run_fwd(
            first, last, slot_length, slot_tokens, gain_row, w_chain, rate_cols, rate_rows, norm_gain, norm_bias, begin
        )
        return done[0], done[1:-4], done[-4:]

    post_low, saved_low, state_low = forward(0, middle, state)
    state_low, row_parts = tied(state_low, row_parts)
    far = jnp.stack(row_parts[1:])
    state_low, far = tied(state_low, far)
    far_parts = exchanged(far, "ctx")
    post_high, saved_high, _ = forward(middle, steps, tuple(state_low))
    post_high, far_parts = tied(post_high, far_parts)
    post_chain = jnp.concatenate([post_low, post_high])

    def to_rows(value):
        return lax.all_to_all(value.reshape(ring, span, -1), "ctx", 0, 0)

    post = to_rows(post_chain)

    number = jnp.stack([lax.axis_index("shard"), place]).astype(jnp.int32)
    w_own = run_assemble(number, row_pack, far_parts, shards).reshape(width, -1)
    w_other = swap(w_own)
    spots = jnp.stack([core, place * span, slot_length[0]]).astype(jnp.int32)
    cot = lax.dynamic_index_in_dim(cotangent, core, 0, keepdims=False)
    output, grad_hidden, grad_post, acts, normed_two, grad_hidden_low, joined, back_low, grad_gain_two = run_rows(
        spots, post, w_own, w_other, row_tokens, cot, gain_two[None], half_out
    )
    row_in = row_tokens.astype(F32)
    grad_gain_two = grad_gain_two[0]

    def folded(values):
        return sum(value.astype(F32) for value in values).astype(BF)

    own_place = jnp.stack([place]).astype(jnp.int32)

    def operands(half, second):
        if second:
            return (back_low, grad_hidden_low), (acts[half, 2], joined[half])
        return (normed_two, normed_two), (acts[half, 0], acts[half, 1])

    def taken(second):
        other = swap(run_sums(*operands(1, second)))
        if part % 16 == 0:
            return list(run_sums(*operands(0, second), other, own_place, shards, ring))
        own = run_sums(*operands(0, second)).astype(F32)
        both = (own + other.astype(F32)).astype(BF).reshape(shards, ring, part, -1)
        return [lax.dynamic_index_in_dim(both, place ^ bit, 1, keepdims=False) for bit in range(ring)]

    grad_post = lax.all_to_all(grad_post, "ctx", 0, 0)
    grad_post = grad_post.reshape(span_all, cols)

    def backward(first, last, begin, saved):
        done = run_bwd(
            first, last, slot_tokens, gain_row, w_chain, rate_rows, norm_gain, grad_post, begin, saved
        )
        return done[0], done[1:6], done[6:]

    begin = tuple(jnp.zeros_like(value) for value in state)
    taken_a, taken_b = taken(False), taken(True)
    grad_post, taken_a, taken_b = tied(grad_post, taken_a, taken_b)
    sum_a, sum_b = sent(taken_a, "ctx"), sent(taken_b, "ctx")
    back_high, sums_high, ending = backward(middle, steps, begin, saved_high)
    ending, sum_a = tied(ending, sum_a)
    sum_a = folded(sum_a)
    ending, sum_a = tied(ending, sum_a)
    sum_a = scattered(sum_a, "shard")
    back_low_half, sums_low, ending = backward(0, middle, tuple(ending), saved_low)
    ending, back_low_half, sum_a, sum_b = tied(ending, back_low_half, sum_a, sum_b)
    d_first, d_first_bias, d_second, d_second_bias = ending
    grad_big, grad_lr, grad_gain_one, grad_norm_gain, grad_norm_bias = (
        low + high for low, high in zip(sums_low, sums_high)
    )
    grad_lr = grad_lr[:chains].T
    back_part = jnp.concatenate([back_low_half, back_high])
    back_one = jnp.sum(to_rows(back_part).astype(F32), axis=0)
    scale_one = row_norm(row_in)
    lifted = back_one * gain_one
    input_grad = (
        grad_hidden
        + scale_one * lifted
        - row_in * scale_one**3 * jnp.mean(lifted * row_in, axis=-1, keepdims=True)
    ).astype(BF)

    sum_b = scattered(folded(sum_b), "shard")
    row_sum = spread(jnp.concatenate([folded(sum_a), folded(sum_b)], axis=-1), "ctx")
    row_sum = row_sum.reshape(depth, -1).astype(F32)
    g_ffn_gate = row_sum[:, :units]
    g_ffn_up = row_sum[:, units : 2 * units]
    g_ffn_down = row_sum[:, 2 * units : 3 * units].T
    g_out = row_sum[:, 3 * units :].T


    def by_shard(value):
        split = value.reshape(value.shape[:-1] + (shards, -1))
        return jnp.moveaxis(split, -2, 0).reshape(shards, -1)

    flat = jnp.concatenate(
        [
            grad_lr.reshape(shards, -1),
            by_shard(d_first),
            by_shard(d_second),
            by_shard(d_first_bias[:, 0]),
            by_shard(d_second_bias[:, 0]),
            by_shard(grad_norm_gain[:, 0]),
            by_shard(grad_norm_bias[:, 0]),
            grad_gain_one.reshape(shards, -1),
            grad_gain_two.reshape(shards, -1),
        ],
        axis=1,
    )
    flat = jnp.pad(flat, ((0, 0), (0, small_rows * wide - small_size)))
    chain_sum = jnp.concatenate(
        [grad_big.reshape(shards, depth, wide), flat.reshape(shards, small_rows, wide)], axis=1
    ).astype(BF)
    kept_half = lax.dynamic_slice_in_dim(chain_sum, core * half_rows, half_rows, 1)
    sent_half = lax.dynamic_slice_in_dim(chain_sum, (1 - core) * half_rows, half_rows, 1)
    chain_sum = (kept_half.astype(F32) + swap(sent_half).astype(F32)).astype(BF)
    chain_sum = spread(folded(scattered(chain_sum, "shard")), "ctx")
    chain_sum = in_turn(chain_sum, swap(chain_sum)).astype(F32)
    chain_sum = chain_sum.transpose(1, 0, 2, 3).reshape(ring, depth + small_rows, wide)
    places = local_heads // chains
    mine = lax.dynamic_slice_in_dim(chain_sum, core * places, places, 0)
    mine_big = mine[:, :depth].reshape(places, depth, 4, cols).transpose(1, 2, 0, 3)
    mine_big = mine_big.reshape(depth, 4, local_heads * head_dim)
    flat_all = chain_sum[:, depth:].reshape(ring, -1)
    flat_mine = mine[:, depth:].reshape(places, -1)
    parts = {}
    offset = 0
    for name, shape in pieces:
        source = flat_all if name in ("n1", "n2") else flat_mine
        parts[name] = source[:, offset : offset + size_of(shape)].reshape((source.shape[0],) + shape)
        offset += size_of(shape)

    def stacked(name):
        return parts[name].reshape((local_heads,) + parts[name].shape[2:])

    return (
        in_turn(output, swap(output)),
        in_turn(input_grad, swap(input_grad)),
        jnp.sum(parts["n1"], axis=0),
        mine_big[:, :3],
        parts["lr"].transpose(1, 0, 2).reshape(depth, local_heads),
        stacked("w1"),
        stacked("b1"),
        stacked("w2"),
        stacked("b2"),
        stacked("pg"),
        stacked("pb"),
        mine_big[:, 3],
        g_out,
        jnp.sum(parts["n2"], axis=0),
        g_ffn_gate,
        g_ffn_up,
        g_ffn_down,
    )


def solution(mesh):
    in_specs = (
        P("shard", "ctx", None),
        P("shard"),
        P("shard"),
        P("shard", None, "tp"),
        P("shard", "tp"),
        P("tp", None, "shard"),
        P("tp", "shard"),
        P("tp", None, "shard"),
        P("tp", "shard"),
        P("tp", "shard"),
        P("tp", "shard"),
        P("shard", "tp"),
        P("tp", "shard"),
        P("shard"),
        P("shard", "tp"),
        P("shard", "tp"),
        P("tp", "shard"),
        P("shard", "ctx", None),
    )
    out_specs = (
        P("shard", "ctx", None),
        P("shard", "ctx", None),
        P("shard"),
        P("shard", None, "tp"),
        P("shard", "tp"),
        P("tp", None, "shard"),
        P("tp", "shard"),
        P("tp", None, "shard"),
        P("tp", "shard"),
        P("tp", "shard"),
        P("tp", "shard"),
        P("shard", "tp"),
        P("tp", "shard"),
        P("shard"),
        P("shard", "tp"),
        P("shard", "tp"),
        P("tp", "shard"),
    )
    return jax.shard_map(
        on_device, mesh=mesh, in_specs=in_specs, out_specs=out_specs, check_vma=False
    )
```

```python
from functools import partial
import jax
import jax.numpy as jnp
from jax import lax
from jax.experimental import pallas as pl
from jax.experimental.pallas import tpu as pltpu
from jax.sharding import PartitionSpec as P

MINI = 16
EPSILON = 1e-06
ETA_BASE = 0.5
BF = jnp.bfloat16
F32 = jnp.float32


def mm(left, right):
    return lax.dot_general(left, right, (((1,), (0,)), ((), ())), preferred_element_type=F32)


def mm_nt(left, right):
    return lax.dot_general(left, right, (((1,), (1,)), ((), ())), preferred_element_type=F32)


def mm_tn(left, right):
    return lax.dot_general(left, right, (((0,), (0,)), ((), ())), preferred_element_type=F32)


def gelu_parts(value):
    cdf = 0.5 + 0.5 * lax.erf(value * 0.7071067811865476)
    pdf = jnp.exp(-0.5 * value * value) * 0.3989422804014327
    return cdf, pdf


def row_scale(value):
    return lax.rsqrt(jnp.mean(value * value, axis=-1, keepdims=True) + EPSILON)


def mini_masks(rows):
    row = lax.broadcasted_iota(jnp.int32, (rows, rows), 0)
    col = lax.broadcasted_iota(jnp.int32, (rows, rows), 1)
    within = (lax.div(row, MINI) == lax.div(col, MINI)) & (col <= row)
    scale = jnp.where(within, 1.0 / (lax.rem(row, MINI) + 1).astype(F32), 0.0)
    return scale, jnp.where(row == col, 1.0 / MINI, 0.0)


def minis(value):
    return [value[at : at + MINI] for at in range(0, value.shape[0], MINI)]


def flat_rows(value):
    return value.reshape(value.shape[0] * value.shape[1], value.shape[2])


def fwd_kernel(
    length_ref, x_ref, gain_ref, wc_ref, lrt_ref, w1i_ref, c1i_ref, w2i_ref, c2i_ref, pg_ref, pb_ref,
    post_ref, kq_ref, rate_ref, fac_ref, gl_ref, gs_ref, unit_ref, hscale_ref,
    w1s_ref, w2s_ref, h_ref, r_ref, g1_ref, g2_ref, ga_ref, ug_ref, gp_ref,
    w1_ref, c1_ref, w2_ref, c2_ref, kmv_ref, next_ref, kk_ref, pq_ref, c2s_ref, *, first,
):
    chains, group = kq_ref.shape[:2]
    rows = group * MINI
    head_dim = kq_ref.shape[-1]
    cols = chains * head_dim
    every = range(chains)

    @pl.when(pl.program_id(0) == 0)
    def _():
        w1_ref[...] = w1i_ref[...]
        c1_ref[...] = c1i_ref[...]
        w2_ref[...] = w2i_ref[...]
        c2_ref[...] = c2i_ref[...]

    start = (first + pl.program_id(0)) * rows
    padded = lrt_ref.shape[0]
    x = x_ref[...].astype(F32)
    normed = (x * row_scale(x) * gain_ref[...]).astype(BF)
    proj = mm(normed, wc_ref[...])
    length = length_ref[0]
    live_col = start + lax.broadcasted_iota(jnp.int32, (rows, padded), 0) < length
    live_row = start + lax.broadcasted_iota(jnp.int32, (padded, rows), 1) < length
    eta_col = jnp.where(live_col, jax.nn.sigmoid(mm_nt(normed, lrt_ref[...])), 0.0) * (ETA_BASE / head_dim)
    rate = jax.nn.sigmoid(mm_nt(lrt_ref[...], normed))
    eta_row = jnp.where(live_row, rate, 0.0) * (ETA_BASE / head_dim)
    fac_ref[0, :padded] = eta_row * (1.0 - rate)
    fac_ref[0, padded:] = eta_row
    for i in every:
        at = i * head_dim
        k = proj[:, cols + at : cols + at + head_dim]
        v = proj[:, 2 * cols + at : 2 * cols + at + head_dim]
        kb, qb = k.astype(BF), proj[:, at : at + head_dim].astype(BF)
        k_minis = kb.reshape(group, MINI, head_dim)
        q_minis = qb.reshape(group, MINI, head_dim)
        kq_ref[i, :, :MINI] = k_minis
        kq_ref[i, :, MINI:] = q_minis
        next_ref[i, : group - 1, :MINI] = k_minis[1:]
        next_ref[i, group - 1 :, :MINI] = k_minis[:1]
        next_ref[i, :, MINI:] = q_minis
        kmv_ref[i] = (k - v).reshape(group, MINI, head_dim)
        rate_ref[i] = (eta_col[:, i : i + 1] * (1.0 / MINI)).reshape(group, MINI, 1)
        cross = (mm_nt(kb, kb) + 1.0) * (eta_row[i : i + 1] * (1.0 / MINI))
        for j in range(group - 1):
            at = j * MINI
            kk_ref[i, j] = cross[at + MINI : at + 2 * MINI, at : at + MINI].astype(BF)

    key_pre = [mm(kq_ref[i, 0, :MINI], w1_ref[i].astype(BF)) + c1_ref[i] for i in every]
    for j in range(group):
        rate = [rate_ref[i, j] for i in every]
        kmv = [kmv_ref[i, j] for i in every]
        stacked = [next_ref[i, j] for i in every]
        k = [kq_ref[i, j, :MINI] for i in every]
        kk = [kk_ref[i, j] for i in every] if j < group - 1 else None
        w1 = [w1_ref[i] for i in every]
        w2 = [w2_ref[i] for i in every]
        c1 = [c1_ref[i] for i in every]
        c2 = [c2_ref[i] for i in every]
        w1b = [w1[i].astype(BF) for i in every]
        w2b = [w2[i].astype(BF) for i in every]
        parts = [gelu_parts(key_pre[i]) for i in every]
        hb = [(key_pre[i] * parts[i][0]).astype(BF) for i in every]
        g2 = [mm_nt(hb[i], w2b[i]) + c2[i] + kmv[i] for i in every]
        slope = [parts[i][0] + key_pre[i] * parts[i][1] for i in every]
        curve = [parts[i][1] * (2.0 - key_pre[i] * key_pre[i]) for i in every]
        both = [mm(stacked[i], w1b[i]) + c1[i] for i in every]
        g2b = [g2[i].astype(BF) for i in every]
        u = [mm(g2b[i], w2b[i]) for i in every]
        fg2 = [rate[i] * g2[i] for i in every]
        w2n = [w2[i] - mm_tn(fg2[i].astype(BF), hb[i]) for i in every]
        c2n = [c2[i] - jnp.sum(fg2[i], axis=0, keepdims=True) for i in every]
        g1 = [u[i] * slope[i] for i in every]
        g1b = [g1[i].astype(BF) for i in every]
        if j < group - 1:
            key_pre = [both[i][:MINI] - mm(kk[i], g1b[i]) for i in every]
        fg1 = [rate[i] * g1[i] for i in every]
        w1n = [w1[i] - mm_tn(k[i], fg1[i].astype(BF)) for i in every]
        c1n = [c1[i] - jnp.sum(fg1[i], axis=0, keepdims=True) for i in every]
        for i in every:
            w1s_ref[i, j] = w1b[i]
            w2s_ref[i, j] = w2b[i]
            c2s_ref[i, j] = c2[i]
            h_ref[i, j] = hb[i]
            g1_ref[i, j] = g1b[i]
            g2_ref[i, j] = g2b[i]
            ga_ref[i, j] = slope[i]
            ug_ref[i, j] = u[i] * curve[i]
            pq_ref[i, j] = both[i][MINI:]
            w1_ref[i] = w1n[i]
            w2_ref[i] = w2n[i]
            c1_ref[i] = c1n[i]
            c2_ref[i] = c2n[i]

    scale = mini_masks(rows)[0]
    for i in every:
        at = i * head_dim
        q = proj[:, at : at + head_dim]
        gate = proj[:, 3 * cols + at : 3 * cols + at + head_dim]
        kb, qb = flat_rows(kq_ref[i, :, :MINI]), flat_rows(kq_ref[i, :, MINI:])
        hb, g1b, g2b = flat_rows(h_ref[i]), flat_rows(g1_ref[i]), flat_rows(g2_ref[i])
        mix = scale * eta_row[i : i + 1]
        query_pre = flat_rows(pq_ref[i]) - mm((mix * (mm_nt(qb, kb) + 1.0)).astype(BF), g1b)
        cdf, pdf = gelu_parts(query_pre)
        gp_ref[i] = (cdf + query_pre * pdf).reshape(group, MINI, -1)
        rb = (query_pre * cdf).astype(BF)
        r_ref[i] = rb.reshape(group, MINI, -1)
        s2 = (mix * (mm_nt(rb, hb) + 1.0)).astype(BF)
        through = [mm_nt(piece, w2s_ref[i, j]) + c2s_ref[i, j] for j, piece in enumerate(minis(rb))]
        mixed = q + jnp.concatenate(through, axis=0) - mm(s2, g2b)
        centered = mixed - jnp.mean(mixed, axis=-1, keepdims=True)
        hscale = row_scale(centered)
        unit = centered * hscale
        out = unit * pg_ref[i] + pb_ref[i]
        cdf, pdf = gelu_parts(gate)
        post_ref[:, at : at + head_dim] = (gate * cdf * out).astype(BF)
        gl_ref[i] = gate * cdf
        gs_ref[i] = (cdf + gate * pdf) * out
        unit_ref[i] = unit
        hscale_ref[i] = hscale


def bwd_kernel(
    x_ref, gain_ref, wc_ref, lrt_ref, pg_ref, gpost_ref,
    gwi_ref, glri_ref, gaini_ref, gpgi_ref, gpbi_ref, w1i_ref, c1i_ref, w2i_ref, c2i_ref,
    kq_ref, rate_ref, fac_ref, gl_ref, gs_ref, unit_ref, hscale_ref,
    w1s_ref, w2s_ref, h_ref, r_ref, g1_ref, g2_ref, ga_ref, ug_ref, gp_ref,
    back_ref, gw_ref, glr_ref, gain_grad_ref, gpg_ref, gpb_ref, dw1_ref, dc1_ref, dw2_ref, dc2_ref,
    d_ref, g1a_ref, g2a_ref, ha_ref, ka_ref, dp_ref, kc_ref, dk_ref, da_ref, df_ref, de_ref, all_ref,
):
    chains, group = kq_ref.shape[:2]
    rows = group * MINI
    head_dim = kq_ref.shape[-1]
    cols = chains * head_dim
    every = range(chains)

    @pl.when(pl.program_id(0) == 0)
    def _():
        dw1_ref[...] = w1i_ref[...]
        dc1_ref[...] = c1i_ref[...]
        dw2_ref[...] = w2i_ref[...]
        dc2_ref[...] = c2i_ref[...]
        gw_ref[...] = gwi_ref[...]
        glr_ref[...] = glri_ref[...]
        gain_grad_ref[...] = gaini_ref[...]
        gpg_ref[...] = gpgi_ref[...]
        gpb_ref[...] = gpbi_ref[...]

    scale, eye = mini_masks(rows)
    padded = lrt_ref.shape[0]
    gpost = gpost_ref[...].astype(F32)
    for i in every:
        at = i * head_dim
        piece = gpost[:, at : at + head_dim]
        all_ref[:, 3 * cols + at : 3 * cols + at + head_dim] = (piece * gs_ref[i]).astype(BF)
        head = piece * gl_ref[i]
        unit = unit_ref[i]
        gpg_ref[i] += jnp.sum(head * unit, axis=0, keepdims=True)
        gpb_ref[i] += jnp.sum(head, axis=0, keepdims=True)
        lifted = head * pg_ref[i]
        d = hscale_ref[i] * (
            lifted
            - jnp.mean(lifted, axis=-1, keepdims=True)
            - unit * jnp.mean(lifted * unit, axis=-1, keepdims=True)
        )
        d_ref[i] = d.reshape(group, MINI, head_dim)
        db = d.astype(BF)
        kb, qb = flat_rows(kq_ref[i, :, :MINI]), flat_rows(kq_ref[i, :, MINI:])
        hb, rb, g1b, g2b = (flat_rows(ref[i]) for ref in (h_ref, r_ref, g1_ref, g2_ref))
        mix = scale * fac_ref[0, padded + i : padded + i + 1]
        ds2 = -mm_nt(db, g2b)
        x2 = mm_nt(rb, hb) + 1.0
        x1 = mm_nt(qb, kb) + 1.0
        dx2 = (ds2 * mix).astype(BF)
        dr = jnp.concatenate([mm(part, w2s_ref[i, j]) for j, part in enumerate(minis(db))], axis=0)
        dp = (dr + mm(dx2, hb)) * flat_rows(gp_ref[i])
        dpb = dp.astype(BF)
        ds1 = -mm_nt(dpb, g1b)
        dx1 = (ds1 * mix).astype(BF)
        dq = jnp.concatenate([mm_nt(part, w1s_ref[i, j]) for j, part in enumerate(minis(dpb))], axis=0)
        all_ref[:, at : at + head_dim] = (d + dq + mm(dx1, kb)).astype(BF)
        g1a_ref[i] = -mm_tn((mix * x1).astype(BF), dpb).reshape(group, MINI, -1)
        g2a_ref[i] = -mm_tn((mix * x2).astype(BF), db).reshape(group, MINI, -1)
        ha_ref[i] = mm_tn(dx2, rb).reshape(group, MINI, -1)
        ka_ref[i] = mm_tn(dx1, qb).reshape(group, MINI, -1)
        dp_ref[i] = dpb.reshape(group, MINI, -1)
        de_ref[i] = jnp.sum((ds2 * x2 + ds1 * x1) * scale, axis=0, keepdims=True)
        kk = mm_nt(kb, kb) + 1.0
        kx = mm_nt(kb, qb) + 1.0
        for j in range(group - 1):
            own, after = slice(j * MINI, (j + 1) * MINI), slice((j + 1) * MINI, (j + 2) * MINI)
            kc_ref[i, j] = jnp.concatenate([kk[own, after], kx[own, after]], axis=1).astype(BF)

    t1 = [mm(kq_ref[i, group - 1, :MINI], dw1_ref[i].astype(BF)) + dc1_ref[i] for i in every]
    for j in reversed(range(group)):

        def all_of(ref):
            return [ref[i, j] for i in every]

        d, kq, rate, w2b, hb, rb, g1b, g2b = (
            all_of(ref) for ref in (d_ref, kq_ref, rate_ref, w2s_ref, h_ref, r_ref, g1_ref, g2_ref)
        )
        ga, ug, dpb, g1a, g2a, ha = (
            all_of(ref) for ref in (ga_ref, ug_ref, dp_ref, g1a_ref, g2a_ref, ha_ref)
        )
        dw1 = [dw1_ref[i] for i in every]
        dw2 = [dw2_ref[i] for i in every]
        dc1 = [dc1_ref[i] for i in every]
        dc2 = [dc2_ref[i] for i in every]
        g1 = [g1b[i].astype(F32) for i in every]
        g2 = [g2b[i].astype(F32) for i in every]
        dw1b = [dw1[i].astype(BF) for i in every]
        dw2b = [dw2[i].astype(BF) for i in every]
        dg1 = [g1a[i] - rate[i] * t1[i] for i in every]
        dub = [(dg1[i] * ga[i]).astype(BF) for i in every]
        through = [mm_nt(dub[i], w2b[i]) for i in every]
        t2 = [mm_nt(hb[i], dw2b[i]) + dc2[i] for i in every]
        dha = [ha[i] - mm((rate[i] * g2[i]).astype(BF), dw2b[i]) for i in every]
        dg2 = [through[i] + (g2a[i] - rate[i] * t2[i]) for i in every]
        dg2b = [dg2[i].astype(BF) for i in every]
        dh = [mm(dg2b[i], w2b[i]) + dha[i] for i in every]
        if j > 0:
            base = [mm(kq_ref[i, j - 1, :MINI], dw1b[i]) + dc1[i] for i in every]
        dk = [dg2[i] - mm_nt((rate[i] * g1[i]).astype(BF), dw1b[i]) for i in every]
        df = [
            -(
                jnp.sum(g1[i] * t1[i], axis=1, keepdims=True)
                + jnp.sum(g2[i] * t2[i], axis=1, keepdims=True)
            )
            for i in every
        ]
        da = [dg1[i] * ug[i] + dh[i] * ga[i] for i in every]
        dab = [da[i].astype(BF) for i in every]
        both = [jnp.concatenate([dab[i], dpb[i]], axis=0) for i in every]
        if j > 0:
            t1 = [base[i] + mm(kc_ref[i, j - 1], both[i]) for i in every]
        dw1n = [dw1[i] + mm_tn(kq[i], both[i]) for i in every]
        dc1n = [dc1[i] + jnp.sum(da[i] + dpb[i].astype(F32), axis=0, keepdims=True) for i in every]
        dw2n = [
            dw2[i]
            + mm_tn(
                jnp.concatenate([d[i].astype(BF), dg2b[i], g2b[i]], axis=0),
                jnp.concatenate([rb[i], hb[i], dub[i]], axis=0),
            )
            for i in every
        ]
        dc2n = [dc2[i] + jnp.sum(d[i] + dg2[i], axis=0, keepdims=True) for i in every]
        for i in every:
            piece, at = slice(j * MINI, (j + 1) * MINI), 2 * cols + i * head_dim
            all_ref[piece, at : at + head_dim] = (-dg2[i]).astype(BF)
            dk_ref[i, j] = dk[i]
            da_ref[i, j] = dab[i]
            df_ref[i, j] = df[i]
            dw1_ref[i] = dw1n[i]
            dc1_ref[i] = dc1n[i]
            dw2_ref[i] = dw2n[i]
            dc2_ref[i] = dc2n[i]

    x = x_ref[...].astype(F32)
    unit_in = x * row_scale(x)
    normed = (unit_in * gain_ref[...]).astype(BF)
    lrt = lrt_ref[...]
    which = lax.broadcasted_iota(jnp.int32, (padded, rows), 0)
    rates = jnp.zeros((padded, rows), F32)
    for i in every:
        at = cols + i * head_dim
        dk = jnp.concatenate([mm_nt(da_ref[i, j], w1s_ref[i, j]) for j in range(group)], axis=0)
        all_ref[:, at : at + head_dim] = (flat_rows(dk_ref[i]) + flat_rows(ka_ref[i]) + dk).astype(BF)
        line = de_ref[i] + jnp.sum(eye * flat_rows(df_ref[i]), axis=0, keepdims=True)
        rates = jnp.where(which == i, line, rates)
    rates = (rates * fac_ref[0, :padded]).astype(BF)
    grads = all_ref[...]
    back = mm_nt(grads, wc_ref[...]) + mm_tn(rates, lrt)
    gain_grad_ref[...] += jnp.sum(back * unit_in, axis=0, keepdims=True)
    back_ref[...] = back.astype(BF)
    gw_ref[...] += mm_tn(normed, grads)
    glr_ref[...] += mm(rates, normed)


GROUP = 8


def block_specs(chains, head_dim, inner, padded, place):
    rows = GROUP * MINI

    def mini(first, second):
        return pl.BlockSpec((chains, GROUP, first, second), lambda g: (0, place(g), 0, 0))

    def head(second):
        return pl.BlockSpec((chains, rows, second), lambda g: (0, place(g), 0))

    return [
        mini(2 * MINI, head_dim), mini(MINI, 1),
        pl.BlockSpec((1, 2 * padded, rows), lambda g: (place(g), 0, 0)),
        head(head_dim), head(head_dim), head(head_dim), head(1),
        mini(head_dim, inner), mini(head_dim, inner), mini(MINI, inner), mini(MINI, inner),
        mini(MINI, inner), mini(MINI, head_dim), mini(MINI, inner), mini(MINI, inner), mini(MINI, inner),
    ]


def whole_spec(value):
    return pl.BlockSpec(value.shape, lambda g: (0,) * value.ndim)


def run_fwd(first, last, length, tokens, gain, wc, lrt, pg, pb, state):
    width = tokens.shape[1]
    chains, head_dim, inner = state[0].shape
    rows = GROUP * MINI
    steps = last - first
    count = steps * GROUP
    padded = lrt.shape[0]

    def mini(first_size, second_size, dtype):
        return jax.ShapeDtypeStruct((chains, count, first_size, second_size), dtype)

    def head(second):
        return jax.ShapeDtypeStruct((chains, steps * rows, second), F32)

    row_spec = pl.BlockSpec((rows, width), lambda g: (first + g, 0))
    small = (gain, wc, lrt, *state, pg, pb)
    return pl.pallas_call(
        partial(fwd_kernel, first=first),
        grid=(steps,),
        in_specs=[pl.BlockSpec(memory_space=pltpu.SMEM), row_spec] + [whole_spec(v) for v in small],
        out_specs=[pl.BlockSpec((rows, chains * head_dim), lambda g: (g, 0))]
        + block_specs(chains, head_dim, inner, padded, lambda g: g)
        + [whole_spec(v) for v in state],
        out_shape=[
            jax.ShapeDtypeStruct((steps * rows, chains * head_dim), BF),
            mini(2 * MINI, head_dim, BF), mini(MINI, 1, F32),
            jax.ShapeDtypeStruct((steps, 2 * padded, rows), F32),
            head(head_dim), head(head_dim), head(head_dim), head(1),
            mini(head_dim, inner, BF), mini(head_dim, inner, BF), mini(MINI, inner, BF), mini(MINI, inner, BF),
            mini(MINI, inner, BF), mini(MINI, head_dim, BF), mini(MINI, inner, F32), mini(MINI, inner, F32),
            mini(MINI, inner, F32),
        ]
        + [jax.ShapeDtypeStruct(v.shape, F32) for v in state],
        scratch_shapes=[
            pltpu.VMEM((chains, GROUP, MINI, head_dim), F32),
            pltpu.VMEM((chains, GROUP, 2 * MINI, head_dim), BF),
            pltpu.VMEM((chains, GROUP, MINI, MINI), BF),
            pltpu.VMEM((chains, GROUP, MINI, inner), F32),
            pltpu.VMEM((chains, GROUP, 1, head_dim), F32),
        ],
        compiler_params=pltpu.CompilerParams(vmem_limit_bytes=50 << 20),
        cost_estimate=pl.CostEstimate(
            flops=9_000_000_000 * steps, bytes_accessed=5_000_000 * steps, transcendentals=0
        ),
        name="chain_forward",
    )(length, tokens, *small)


def run_bwd(first, last, base, tokens, gain, wc, lrt, pg, gpost, state, saved):
    width = tokens.shape[1]
    chains, head_dim, inner = state[5].shape
    rows = GROUP * MINI
    padded = lrt.shape[0]
    wide = wc.shape[1]
    steps = last - first

    def place(g):
        return steps - 1 - g

    def shape(*extent):
        return jax.ShapeDtypeStruct(extent, F32)

    small = (gain, wc, lrt, pg)
    outs = [shape(*value.shape) for value in state]

    def scratch(first_size, second_size, dtype):
        return pltpu.VMEM((chains, GROUP, first_size, second_size), dtype)

    return pl.pallas_call(
        bwd_kernel,
        grid=(steps,),
        in_specs=[pl.BlockSpec((rows, width), lambda g: (first + place(g), 0))]
        + [whole_spec(v) for v in small]
        + [pl.BlockSpec((rows, chains * head_dim), lambda g: (first + place(g), 0))]
        + [whole_spec(v) for v in state]
        + block_specs(chains, head_dim, inner, padded, lambda g: first - base + place(g)),
        out_specs=[pl.BlockSpec((rows, width), lambda g: (place(g), 0))] + [whole_spec(v) for v in outs],
        out_shape=[jax.ShapeDtypeStruct((steps * rows, width), BF)] + outs,
        scratch_shapes=[
            scratch(MINI, head_dim, F32), scratch(MINI, inner, F32), scratch(MINI, head_dim, F32),
            scratch(MINI, inner, F32), scratch(MINI, head_dim, F32), scratch(MINI, inner, BF),
            scratch(MINI, 2 * MINI, BF), scratch(MINI, head_dim, F32), scratch(MINI, inner, BF),
            scratch(MINI, 1, F32), pltpu.VMEM((chains, 1, rows), F32), pltpu.VMEM((rows, wide), BF),
        ],
        compiler_params=pltpu.CompilerParams(vmem_limit_bytes=50 << 20),
        cost_estimate=pl.CostEstimate(
            flops=11_000_000_000 * steps, bytes_accessed=5_000_000 * steps, transcendentals=0
        ),
        name="chain_backward",
    )(tokens, *small, gpost, *state, *saved)


def swap(value):
    return lax.ppermute(value, "tp", [(0, 1), (1, 0)])


def rows_kernel(
    spot_ref, post_ref, own_ref, other_ref, x_ref, cot_ref, gain_ref,
    out_ref, grad_ref, gpost_ref, normed_ref, low_ref, back_ref, gain_grad_ref, cat0_ref, cat1_ref, *act_refs,
):
    core, start, length = spot_ref[0], spot_ref[1], spot_ref[2]
    span, width = x_ref.shape
    cols = post_ref.shape[2]
    units = act_refs[0].shape[1]
    places = cat0_ref.shape[1] // cols
    x = x_ref[...].astype(F32)
    live = start + lax.broadcasted_iota(jnp.int32, (span, width), 0) < length
    back = jnp.where(live, cot_ref[...].astype(F32), 0.0)
    back_low = back.astype(BF)
    back_ref[...] = back_low
    halves = ((own_ref, core), (other_ref, 1 - core))
    hidden = x
    for half, (w_ref, side) in enumerate(halves):
        joined = jnp.concatenate([post_ref[side * places + p] for p in range(places)], axis=1)
        (cat0_ref, cat1_ref)[half][...] = joined
        hidden = hidden + mm_nt(joined, w_ref[:, 3 * units :])
    scale = row_scale(hidden)
    gain = gain_ref[...]
    normed = (hidden * scale * gain).astype(BF)
    normed_ref[...] = normed
    feed = jnp.zeros((span, width), F32)
    grad = jnp.zeros((span, width), F32)
    step = min(units, 512)
    for half, (w_ref, _) in enumerate(halves):
        for at in range(0, units, step):
            w_gate = w_ref[:, at : at + step]
            w_up = w_ref[:, units + at : units + at + step]
            w_down = w_ref[:, 2 * units + at : 2 * units + at + step]
            up_gate = mm(normed, w_gate)
            up_lin = mm(normed, w_up)
            grad_act = mm(back_low, w_down)
            gate = jax.nn.sigmoid(up_gate)
            silu = up_gate * gate
            act = (silu * up_lin).astype(BF)
            grad_gate = (grad_act * up_lin * (gate * (1.0 + up_gate * (1.0 - gate)))).astype(BF)
            grad_lin = (grad_act * silu).astype(BF)
            act_refs[3 * half + 0][:, at : at + step] = grad_gate
            act_refs[3 * half + 1][:, at : at + step] = grad_lin
            act_refs[3 * half + 2][:, at : at + step] = act
            feed += mm_nt(act, w_down)
            grad += mm_nt(grad_gate, w_gate) + mm_nt(grad_lin, w_up)
    out_ref[...] = (hidden + feed).astype(BF)
    lifted = grad * gain
    hat = hidden * scale
    gain_grad_ref[...] = jnp.sum(grad * hat, axis=0, keepdims=True)
    total = back + scale * (lifted - hat * jnp.mean(lifted * hat, axis=-1, keepdims=True))
    grad_ref[...] = total
    low = total.astype(BF)
    low_ref[...] = low
    for p in range(2 * places, gpost_ref.shape[0]):
        gpost_ref[p] = jnp.zeros(gpost_ref.shape[1:], BF)
    for w_ref, side in halves:
        gpost = mm(low, w_ref[:, 3 * units :]).astype(BF)
        for p in range(places):
            gpost_ref[side * places + p] = gpost[:, p * cols : (p + 1) * cols]


def run_rows(spots, post, own, other, x, cot, gain, half_out):
    ring, span, cols = post.shape
    width = x.shape[1]
    units = (own.shape[1] - half_out) // 3
    vmem = pl.BlockSpec(memory_space=pltpu.VMEM)

    def shape(extent, dtype):
        return jax.ShapeDtypeStruct(extent, dtype)

    return pl.pallas_call(
        rows_kernel,
        in_specs=[pl.BlockSpec(memory_space=pltpu.SMEM)] + [vmem] * 6,
        out_specs=[vmem] * 15,
        out_shape=[
            shape((span, width), BF), shape((span, width), F32), shape((ring, span, cols), BF),
            shape((span, width), BF), shape((span, width), BF), shape((span, width), BF), shape((1, width), F32),
        ]
        + [shape((span, half_out), BF)] * 2
        + [shape((span, units), BF)] * 6,
        compiler_params=pltpu.CompilerParams(vmem_limit_bytes=52 << 20),
        cost_estimate=pl.CostEstimate(flops=20_000_000_000, bytes_accessed=20_000_000, transcendentals=0),
        name="rows_main",
    )(spots, post, own, other, x, cot, gain)


def products(pairs, parts, store):
    start = 0
    for left, right in zip(pairs, parts):
        size = right.shape[-1]
        step = 512 if size % 512 == 0 else size
        for at in range(0, size, step):
            store(start + at, mm_tn(left[...], right[:, at : at + step]))
        start += size


def sums_other_kernel(*refs):
    *sources, out_ref = refs
    count = len(sources) // 2

    def store(at, value):
        out_ref[:, at : at + value.shape[1]] = value.astype(BF)

    products(sources[:count], sources[count:], store)


def sums_own_kernel(place_ref, other_ref, *refs, count, outs):
    sources, out_refs, held_ref = refs[: 2 * count], refs[2 * count : 2 * count + outs], refs[-1]

    def store(at, value):
        piece = slice(at, at + value.shape[1])
        held_ref[:, piece] = (value + other_ref[:, piece].astype(F32)).astype(BF)

    products(sources[:count], sources[count:], store)
    shards, part = out_refs[0].shape[:2]
    for bit, out_ref in enumerate(out_refs):
        for z in range(shards):
            at = pl.multiple_of((z * outs + (place_ref[0] ^ bit)) * part, part)
            out_ref[z] = held_ref[pl.ds(at, part), :]


def run_sums(lefts, rights, other=None, place=None, shards=1, ring=1):
    width = lefts[0].shape[1]
    total = sum(right.shape[1] for right in rights)
    vmem = pl.BlockSpec(memory_space=pltpu.VMEM)
    count = len(lefts)
    params = pltpu.CompilerParams(vmem_limit_bytes=40 << 20)
    cost = pl.CostEstimate(flops=5_000_000_000, bytes_accessed=6_000_000, transcendentals=0)
    if other is None:
        return pl.pallas_call(
            sums_other_kernel,
            in_specs=[vmem] * (2 * count),
            out_specs=vmem,
            out_shape=jax.ShapeDtypeStruct((width, total), BF),
            compiler_params=params,
            cost_estimate=cost,
            name="sums_other",
        )(*lefts, *rights)
    part = width // (shards * ring)
    return pl.pallas_call(
        partial(sums_own_kernel, count=count, outs=ring),
        in_specs=[pl.BlockSpec(memory_space=pltpu.SMEM)] + [vmem] * (2 * count + 1),
        out_specs=[vmem] * ring,
        out_shape=[jax.ShapeDtypeStruct((shards, part, total), BF)] * ring,
        scratch_shapes=[pltpu.VMEM((width, total), BF)],
        compiler_params=params,
        cost_estimate=cost,
        name="sums_own",
    )(place, other, *lefts, *rights)


def assemble_kernel(spots_ref, pack_ref, *refs):
    *far_refs, out_ref = refs
    me, place = spots_ref[0], spots_ref[1]
    ring = len(far_refs)
    part = out_ref.shape[1]
    for number in range(ring):
        out_ref[me * ring + number] = pack_ref[number * part : (number + 1) * part]
    for bit, far_ref in enumerate(far_refs):
        for other in range(far_ref.shape[0]):
            out_ref[(me ^ (other + 1)) * ring + (place ^ bit)] = far_ref[other]


def run_assemble(spots, pack, far_parts, shards):
    vmem = pl.BlockSpec(memory_space=pltpu.VMEM)
    ring = len(far_parts)
    part = pack.shape[0] // ring
    return pl.pallas_call(
        assemble_kernel,
        in_specs=[pl.BlockSpec(memory_space=pltpu.SMEM)] + [vmem] * (1 + ring),
        out_specs=vmem,
        out_shape=jax.ShapeDtypeStruct((shards * ring, part, pack.shape[1]), BF),
        compiler_params=pltpu.CompilerParams(vmem_limit_bytes=40 << 20),
        name="assemble_rows",
    )(spots, pack, *far_parts)


SMALL = 64


def small_spots(chains, depth, inner_share):
    side = 2 * chains * inner_share
    return side, {
        "lr": 0, "n1": chains, "n2": chains + 1, "b1": chains + 2,
        "b2": 2 * chains + 2, "pg": 3 * chains + 2, "pb": 4 * chains + 2,
    }


def pack_weights_kernel(
    pick_ref, qkv_ref, gate_ref, lr_ref, n1_ref, n2_ref, w1_ref, b1_ref, w2_ref, b2_ref, pg_ref, pb_ref,
    out_ref, small_ref, *, chains,
):
    depth = gate_ref.shape[0]
    heads, head_dim, inner_share = w1_ref.shape
    cols = chains * head_dim
    all_cols = heads * head_dim
    side, spots = small_spots(chains, depth, inner_share)
    small_ref[...] = jnp.zeros_like(small_ref)

    def put(name, i, value):
        row = spots[name] + i
        small_ref[row : row + 1, side : side + value.shape[1]] = value.astype(F32)

    for option in range(heads // chains):

        @pl.when(pick_ref[0] == option)
        def _():
            at = option * cols
            for which in range(3):
                start = which * all_cols + at
                out_ref[:depth, which * cols : (which + 1) * cols] = qkv_ref[:, start : start + cols]
            out_ref[:depth, 3 * cols :] = gate_ref[:, at : at + cols]
            for i in range(chains):
                head = option * chains + i
                lanes = slice(i * inner_share, (i + 1) * inner_share)
                small_ref[:, lanes] = w1_ref[head].astype(F32)
                lanes = slice((chains + i) * inner_share, (chains + i + 1) * inner_share)
                small_ref[:, lanes] = w2_ref[head].astype(F32)
                for name, ref in (("lr", lr_ref), ("b1", b1_ref), ("b2", b2_ref), ("pg", pg_ref), ("pb", pb_ref)):
                    put(name, i, ref[head : head + 1, :])

    put("n1", 0, n1_ref[...])
    put("n2", 0, n2_ref[...])
    out_ref[depth:, :] = small_ref[...].astype(BF)


def halves_by_core(core, mine_ref, other_ref, work):
    @pl.when(core == 0)
    def _():
        work(mine_ref, other_ref)

    @pl.when(core != 0)
    def _():
        work(other_ref, mine_ref)


def unpack_weights_kernel(
    core_ref, mine_ref, other_ref,
    wc_ref, lrt_ref, n1_ref, n2_ref, w1_ref, b1_ref, w2_ref, b2_ref, pg_ref, pb_ref, lines_ref,
):
    shards, half, _ = mine_ref.shape
    chains, _, inner = w1_ref.shape
    inner_share = inner // shards
    depth = 2 * half - SMALL
    head_share = b2_ref.shape[2] // shards
    side, spots = small_spots(chains, depth, inner_share)
    lines_ref[...] = jnp.zeros_like(lines_ref)

    def work(low_ref, high_ref):
        for z in range(shards):
            wc_ref[z * depth : z * depth + half] = low_ref[z]
            wc_ref[z * depth + half : (z + 1) * depth] = high_ref[z, : depth - half]
            small = high_ref[z, depth - half :].astype(F32)

            def get(name, i, size):
                row = spots[name] + i
                return small[row : row + 1, side : side + size]

            here = slice(z * depth, (z + 1) * depth)
            n1_ref[:, here] = get("n1", 0, depth)
            n2_ref[:, here] = get("n2", 0, depth)
            for i in range(chains):
                lines_ref[i : i + 1, here] = get("lr", i, depth)
                lanes = slice(z * inner_share, (z + 1) * inner_share)
                w1_ref[i, :, lanes] = small[:, i * inner_share : (i + 1) * inner_share]
                w2_ref[i, :, lanes] = small[:, (chains + i) * inner_share : (chains + i + 1) * inner_share]
                b1_ref[i, :, lanes] = get("b1", i, inner_share)
                lanes = slice(z * head_share, (z + 1) * head_share)
                for name, ref in (("b2", b2_ref), ("pg", pg_ref), ("pb", pb_ref)):
                    ref[i, :, lanes] = get(name, i, head_share)

    halves_by_core(core_ref[0], mine_ref, other_ref, work)
    lrt_ref[...] = lines_ref[...].astype(BF)


def pack_grads_kernel(
    core_ref, gw_ref, glr_ref, n1_ref, n2_ref, w1_ref, b1_ref, w2_ref, b2_ref, pg_ref, pb_ref,
    keep_ref, send_ref, small_ref,
):
    shards, half, _ = keep_ref.shape
    chains, _, inner = w1_ref.shape
    inner_share = inner // shards
    depth = 2 * half - SMALL
    head_share = b2_ref.shape[2] // shards
    side, spots = small_spots(chains, depth, inner_share)

    def work(low_ref, high_ref):
        for z in range(shards):
            small_ref[...] = jnp.zeros_like(small_ref)

            def put(name, i, value):
                row = spots[name] + i
                small_ref[row : row + 1, side : side + value.shape[1]] = value

            here = slice(z * depth, (z + 1) * depth)
            low_ref[z] = gw_ref[z * depth : z * depth + half].astype(BF)
            high_ref[z, : depth - half] = gw_ref[z * depth + half : (z + 1) * depth].astype(BF)
            put("n1", 0, n1_ref[:, here])
            put("n2", 0, n2_ref[:, here])
            for i in range(chains):
                put("lr", i, glr_ref[i : i + 1, here])
                lanes = slice(z * inner_share, (z + 1) * inner_share)
                small_ref[:, i * inner_share : (i + 1) * inner_share] = w1_ref[i, :, lanes]
                small_ref[:, (chains + i) * inner_share : (chains + i + 1) * inner_share] = w2_ref[i, :, lanes]
                put("b1", i, b1_ref[i, :, lanes])
                lanes = slice(z * head_share, (z + 1) * head_share)
                for name, ref in (("b2", b2_ref), ("pg", pg_ref), ("pb", pb_ref)):
                    put(name, i, ref[i, :, lanes])
            high_ref[z, depth - half :] = small_ref[...].astype(BF)

    halves_by_core(core_ref[0], keep_ref, send_ref, work)


def unpack_grads_kernel(
    core_ref, mine_ref, other_ref,
    qkv_ref, gate_ref, lrt_ref, n1_ref, n2_ref, w1_ref, b1_ref, w2_ref, b2_ref, pg_ref, pb_ref, *, chains,
):
    ring, half, wide = mine_ref.shape
    cols = wide // 4
    heads, _, inner_share = w1_ref.shape
    depth = gate_ref.shape[0]
    head_share = b2_ref.shape[1]
    places = heads // chains
    side, spots = small_spots(chains, depth, inner_share)
    core = core_ref[0]

    def work(low_ref, high_ref):
        for p in range(places):
            place = core * places + p
            big = jnp.concatenate([low_ref[place], high_ref[place, : depth - half]], axis=0).astype(F32)
            small = high_ref[place, depth - half :].astype(F32)
            at = p * cols
            for which in range(3):
                qkv_ref[:, which, at : at + cols] = big[:, which * cols : (which + 1) * cols]
            gate_ref[:, at : at + cols] = big[:, 3 * cols :]
            for i in range(chains):
                head = p * chains + i
                w1_ref[head] = small[:, i * inner_share : (i + 1) * inner_share]
                w2_ref[head] = small[:, (chains + i) * inner_share : (chains + i + 1) * inner_share]
                for name, ref, size in (
                    ("lr", lrt_ref, depth), ("b1", b1_ref, inner_share), ("b2", b2_ref, head_share),
                    ("pg", pg_ref, head_share), ("pb", pb_ref, head_share),
                ):
                    row = spots[name] + i
                    ref[head : head + 1, :] = small[row : row + 1, side : side + size]
        for name, ref in (("n1", n1_ref), ("n2", n2_ref)):
            row = spots[name]
            total = jnp.zeros((1, depth), F32)
            for place in range(ring):
                lines = high_ref[place, depth - half :].astype(F32)
                total = total + lines[row : row + 1, side : side + depth]
            ref[...] = total

    halves_by_core(core, mine_ref, other_ref, work)


def add_and_deal_kernel(place_ref, keep_ref, other_ref, *out_refs):
    for bit, out_ref in enumerate(out_refs):
        which = place_ref[0] ^ bit
        out_ref[...] = (keep_ref[which].astype(F32) + other_ref[which].astype(F32)).astype(BF)


def in_vmem(kernel, name, shapes, scratch, scalars, *operands):
    vmem = pl.BlockSpec(memory_space=pltpu.VMEM)
    return pl.pallas_call(
        kernel,
        in_specs=[pl.BlockSpec(memory_space=pltpu.SMEM)] + [vmem] * len(operands),
        out_specs=[vmem] * len(shapes),
        out_shape=[jax.ShapeDtypeStruct(extent, dtype) for extent, dtype in shapes],
        scratch_shapes=[pltpu.VMEM(extent, F32) for extent in scratch],
        compiler_params=pltpu.CompilerParams(vmem_limit_bytes=40 << 20),
        name=name,
    )(jnp.stack(scalars).astype(jnp.int32), *operands)


def place_kernel(spots_ref, *refs):
    *sources, target = refs
    for number, source in enumerate(sources):
        target[spots_ref[number]] = source[...]


def placed(pieces, spots):
    return pl.pallas_call(
        place_kernel,
        in_specs=[pl.BlockSpec(memory_space=pltpu.SMEM)]
        + [pl.BlockSpec(memory_space=pltpu.VMEM)] * len(pieces),
        out_specs=pl.BlockSpec(memory_space=pltpu.VMEM),
        out_shape=jax.ShapeDtypeStruct((len(pieces),) + pieces[0].shape, pieces[0].dtype),
        compiler_params=pltpu.CompilerParams(vmem_limit_bytes=40 << 20),
        name="place_pieces",
    )(jnp.stack(spots).astype(jnp.int32), *pieces)


def exchanged(value, axis):
    size = lax.axis_size(axis)
    return [value] + [
        lax.ppermute(value, axis, [(source, source ^ bit) for source in range(size)])
        for bit in range(1, size)
    ]


def sent(taken, axis):
    return taken[:1] + [
        lax.ppermute(taken[bit], axis, [(source, source ^ bit) for source in range(len(taken))])
        for bit in range(1, len(taken))
    ]


def scattered(value, axis):
    size = lax.axis_size(axis)
    me = lax.axis_index(axis)
    return sent([lax.dynamic_index_in_dim(value, me ^ bit, 0, keepdims=False) for bit in range(size)], axis)


def placed_along(pieces, axis):
    me = lax.axis_index(axis)
    return placed(pieces, [me ^ bit for bit in range(len(pieces))])


def spread(value, axis):
    return placed_along(exchanged(value, axis), axis)


def tied(*values):
    return lax.optimization_barrier(values)


def in_turn(first, second):
    return jnp.where(lax.axis_index("tp") == 0, jnp.stack([first, second]), jnp.stack([second, first]))


def on_device(
    tokens,
    lengths,
    norm1_gain,
    qkv_weight,
    lr_weight,
    inner_w1,
    inner_b1,
    inner_w2,
    inner_b2,
    post_gain,
    post_bias,
    gate_weight,
    out_weight,
    norm2_gain,
    ffn_gate,
    ffn_up,
    ffn_down,
    cotangent,
):
    micro, span, width = tokens.shape
    ring = lax.axis_size("ctx")
    shards = lax.axis_size("shard")
    pair = lax.axis_size("tp")
    place = lax.axis_index("ctx")
    core = lax.axis_index("tp")
    local_heads, head_dim, inner_share = inner_w1.shape
    head_share = inner_b2.shape[1]
    depth = norm1_gain.shape[0]
    inner = inner_share * shards
    total_heads = local_heads * pair
    chains = -(-total_heads // ring)
    span_all = ring * span
    count = span_all // MINI
    cols = chains * head_dim
    wide = 4 * cols

    row_tokens = lax.dynamic_index_in_dim(tokens, core, 0, keepdims=False)
    slot_tokens = spread(row_tokens, "ctx").reshape(span_all, width)

    first_head = jnp.minimum(place * chains, total_heads - chains)
    owner = first_head // local_heads
    local_first = first_head - owner * local_heads

    packed = in_vmem(
        partial(pack_weights_kernel, chains=chains), "pack_weights",
        [((depth + SMALL, wide), BF)], [(SMALL, wide)], [local_first // chains],
        qkv_weight.reshape(depth, -1), gate_weight, lr_weight.T, norm1_gain[None], norm2_gain[None],
        inner_w1, inner_b1, inner_w2, inner_b2, post_gain, post_bias,
    )[0]
    half_rows = (depth + SMALL) // 2
    packed = jnp.where(core == owner, packed, swap(packed))
    gathered = spread(lax.dynamic_slice_in_dim(packed, core * half_rows, half_rows, 0), "shard")

    units = ffn_gate.shape[1]
    half_out = out_weight.shape[0]
    row_pack = jnp.concatenate([ffn_gate, ffn_up, ffn_down.T, out_weight.T], axis=1)
    part = depth // ring
    row_part = lax.dynamic_slice_in_dim(row_pack, place * part, part, 0)
    row_part, gathered = tied(row_part, gathered)
    row_parts = exchanged(row_part, "shard")

    padded = -(-chains // 16) * 16
    w_chain, rate_rows, gain_row, gain_two, *rest = in_vmem(
        unpack_weights_kernel, "unpack_weights",
        [
            ((width, wide), BF), ((padded, width), BF), ((1, width), F32), ((1, width), F32),
            ((chains, head_dim, inner), F32), ((chains, 1, inner), F32),
            ((chains, head_dim, inner), F32), ((chains, 1, head_dim), F32),
            ((chains, 1, head_dim), F32), ((chains, 1, head_dim), F32),
        ],
        [(padded, width)], [core], gathered, swap(gathered),
    )
    state, (norm_gain, norm_bias) = tuple(rest[:4]), rest[4:]

    slot_length = lax.dynamic_index_in_dim(lengths, core, 0, keepdims=True)
    steps = span_all // (GROUP * MINI)
    middle = steps // 2

    def forward(first, last, begin):
        done = run_fwd(
            first, last, slot_length, slot_tokens, gain_row, w_chain, rate_rows, norm_gain, norm_bias, begin
        )
        return done[0], done[1:-4], done[-4:]

    post_low, saved_low, state_low = forward(0, middle, state)
    state_low, row_parts = tied(state_low, row_parts)
    far = jnp.stack(row_parts[1:])
    state_low, far = tied(state_low, far)
    far_parts = exchanged(far, "ctx")
    post_high, saved_high, _ = forward(middle, steps, tuple(state_low))
    post_high, far_parts = tied(post_high, far_parts)
    post_chain = jnp.concatenate([post_low, post_high])

    def to_rows(value):
        return lax.all_to_all(value.reshape(ring, span, -1), "ctx", 0, 0)

    post = to_rows(post_chain)

    number = jnp.stack([lax.axis_index("shard"), place]).astype(jnp.int32)
    w_own = run_assemble(number, row_pack, far_parts, shards).reshape(width, -1)
    w_other = swap(w_own)
    spots = jnp.stack([core, place * span, slot_length[0]]).astype(jnp.int32)
    cot = lax.dynamic_index_in_dim(cotangent, core, 0, keepdims=False)
    output, grad_hidden, grad_post, normed_two, grad_hidden_low, back_low, grad_gain_two, *kept = run_rows(
        spots, post, w_own, w_other, row_tokens, cot, gain_two, half_out
    )
    row_in = row_tokens.astype(F32)
    joined, acts = kept[:2], (kept[2:5], kept[5:])

    def folded(values):
        return sum(value.astype(F32) for value in values).astype(BF)

    own_place = jnp.stack([place]).astype(jnp.int32)

    def operands(half, second):
        if second:
            return (back_low, grad_hidden_low), (acts[half][2], joined[half])
        return (normed_two, normed_two), (acts[half][0], acts[half][1])

    def other_sums(second):
        return swap(run_sums(*operands(1, second)))

    def taken(second, other):
        if part % 16 == 0:
            return list(run_sums(*operands(0, second), other, own_place, shards, ring))
        own = run_sums(*operands(0, second)).astype(F32)
        both = (own + other.astype(F32)).astype(BF).reshape(shards, ring, part, -1)
        return [lax.dynamic_index_in_dim(both, place ^ bit, 1, keepdims=False) for bit in range(ring)]

    grad_post = lax.all_to_all(grad_post, "ctx", 0, 0)
    grad_post = grad_post.reshape(span_all, cols)

    def backward(first, last, base, begin, saved):
        done = run_bwd(
            first, last, base, slot_tokens, gain_row, w_chain, rate_rows, norm_gain, grad_post, begin, saved
        )
        return done[0], tuple(done[1:])

    sums = ((width, wide), (padded, width), (1, width), (chains, 1, head_dim), (chains, 1, head_dim))
    begin = tuple(jnp.zeros(extent, F32) for extent in sums + tuple(value.shape for value in state))
    other_a, other_b = other_sums(False), other_sums(True)
    (grad_post, sum_rights) = tied(grad_post, (other_a, other_b))
    taken_a, taken_b = taken(False, sum_rights[0]), taken(True, sum_rights[1])
    grad_post, taken_a, taken_b = tied(grad_post, taken_a, taken_b)
    sum_a, sum_b = sent(taken_a, "ctx"), sent(taken_b, "ctx")
    back_high, ending = backward(middle, steps, middle, begin, saved_high)
    ending, sum_a = tied(ending, sum_a)
    sum_a = folded(sum_a)
    ending, sum_a = tied(ending, sum_a)
    sum_a = scattered(sum_a, "shard")
    back_low_half, ending = backward(0, middle, 0, ending, saved_low)
    ending, back_low_half, sum_a, sum_b = tied(ending, back_low_half, sum_a, sum_b)
    back_part = jnp.concatenate([back_low_half, back_high])
    back_one = jnp.sum(to_rows(back_part).astype(F32), axis=0)
    scale_one = row_scale(row_in)
    lifted = back_one * gain_row
    input_grad = (
        grad_hidden
        + scale_one * lifted
        - row_in * scale_one**3 * jnp.mean(lifted * row_in, axis=-1, keepdims=True)
    ).astype(BF)

    sum_b = scattered(folded(sum_b), "shard")
    row_sum = spread(jnp.concatenate([folded(sum_a), folded(sum_b)], axis=-1), "ctx")
    row_sum = row_sum.reshape(depth, -1).astype(F32)
    g_ffn_gate = row_sum[:, :units]
    g_ffn_up = row_sum[:, units : 2 * units]
    g_ffn_down = row_sum[:, 2 * units : 3 * units].T
    g_out = row_sum[:, 3 * units :].T

    grad_big, grad_lr, grad_gain_one, grad_norm_gain, grad_norm_bias, *grad_state = ending
    block = ((shards, half_rows, wide), BF)
    keep, send = in_vmem(
        pack_grads_kernel, "pack_grads", [block, block], [(SMALL, wide)], [core],
        grad_big, grad_lr, grad_gain_one, grad_gain_two, *grad_state, grad_norm_gain, grad_norm_bias,
    )
    dealt = in_vmem(
        add_and_deal_kernel, "add_and_deal", [((half_rows, wide), BF)] * shards, [],
        [lax.axis_index("shard")], keep, swap(send),
    )
    chain_sum = spread(folded(sent(list(dealt), "shard")), "ctx")
    g_qkv, g_gate, g_lr, g_n1, g_n2, *g_rest = in_vmem(
        partial(unpack_grads_kernel, chains=chains), "unpack_grads",
        [
            ((depth, 3, local_heads * head_dim), F32), ((depth, local_heads * head_dim), F32),
            ((local_heads, depth), F32), ((1, depth), F32), ((1, depth), F32),
            (inner_w1.shape, F32), (inner_b1.shape, F32), (inner_w2.shape, F32), (inner_b2.shape, F32),
            (post_gain.shape, F32), (post_bias.shape, F32),
        ],
        [], [core], chain_sum, swap(chain_sum),
    )

    return (
        in_turn(output, swap(output)),
        in_turn(input_grad, swap(input_grad)),
        g_n1[0],
        g_qkv,
        g_lr.T,
        *g_rest,
        g_gate,
        g_out,
        g_n2[0],
        g_ffn_gate,
        g_ffn_up,
        g_ffn_down,
    )


def solution(mesh):
    in_specs = (
        P("shard", "ctx", None),
        P("shard"),
        P("shard"),
        P("shard", None, "tp"),
        P("shard", "tp"),
        P("tp", None, "shard"),
        P("tp", "shard"),
        P("tp", None, "shard"),
        P("tp", "shard"),
        P("tp", "shard"),
        P("tp", "shard"),
        P("shard", "tp"),
        P("tp", "shard"),
        P("shard"),
        P("shard", "tp"),
        P("shard", "tp"),
        P("tp", "shard"),
        P("shard", "ctx", None),
    )
    out_specs = (
        P("shard", "ctx", None),
        P("shard", "ctx", None),
        P("shard"),
        P("shard", None, "tp"),
        P("shard", "tp"),
        P("tp", None, "shard"),
        P("tp", "shard"),
        P("tp", None, "shard"),
        P("tp", "shard"),
        P("tp", "shard"),
        P("tp", "shard"),
        P("shard", "tp"),
        P("tp", "shard"),
        P("shard"),
        P("shard", "tp"),
        P("shard", "tp"),
        P("tp", "shard"),
    )
    return jax.shard_map(
        on_device, mesh=mesh, in_specs=in_specs, out_specs=out_specs, check_vma=False
    )
```

```python
from functools import partial
import jax
import jax.numpy as jnp
from jax import lax
from jax.experimental import pallas as pl
from jax.experimental.pallas import tpu as pltpu
from jax.sharding import PartitionSpec as P

MINI = 16
EPSILON = 1e-06
ETA_BASE = 0.5
BF = jnp.bfloat16
F32 = jnp.float32


def mm(left, right):
    return lax.dot_general(left, right, (((1,), (0,)), ((), ())), preferred_element_type=F32)


def mm_nt(left, right):
    return lax.dot_general(left, right, (((1,), (1,)), ((), ())), preferred_element_type=F32)


def mm_tn(left, right):
    return lax.dot_general(left, right, (((0,), (0,)), ((), ())), preferred_element_type=F32)


def gelu_parts(value):
    cdf = 0.5 + 0.5 * lax.erf(value * 0.7071067811865476)
    pdf = jnp.exp(-0.5 * value * value) * 0.3989422804014327
    return cdf, pdf


def row_scale(value):
    return lax.rsqrt(jnp.mean(value * value, axis=-1, keepdims=True) + EPSILON)


def mini_masks(rows):
    row = lax.broadcasted_iota(jnp.int32, (rows, rows), 0)
    col = lax.broadcasted_iota(jnp.int32, (rows, rows), 1)
    within = (lax.div(row, MINI) == lax.div(col, MINI)) & (col <= row)
    scale = jnp.where(within, 1.0 / (lax.rem(row, MINI) + 1).astype(F32), 0.0)
    return scale, jnp.where(row == col, 1.0 / MINI, 0.0)


def minis(value):
    return [value[at : at + MINI] for at in range(0, value.shape[0], MINI)]


def flat_rows(value):
    return value.reshape(value.shape[0] * value.shape[1], value.shape[2])


def fwd_kernel(
    length_ref, x_ref, gain_ref, wc_ref, lrt_ref, w1i_ref, c1i_ref, w2i_ref, c2i_ref, pg_ref, pb_ref,
    post_ref, kq_ref, rate_ref, fac_ref, gl_ref, gs_ref, unit_ref, hscale_ref,
    w1s_ref, w2s_ref, h_ref, r_ref, g1_ref, g2_ref, ga_ref, ug_ref, gp_ref,
    w1_ref, c1_ref, w2_ref, c2_ref, kmv_ref, next_ref, kk_ref, pq_ref, c2s_ref, *, first,
):
    chains, group = kq_ref.shape[:2]
    rows = group * MINI
    head_dim = kq_ref.shape[-1]
    cols = chains * head_dim
    every = range(chains)

    @pl.when(pl.program_id(0) == 0)
    def _():
        w1_ref[...] = w1i_ref[...]
        c1_ref[...] = c1i_ref[...]
        w2_ref[...] = w2i_ref[...]
        c2_ref[...] = c2i_ref[...]

    start = (first + pl.program_id(0)) * rows
    padded = lrt_ref.shape[0]
    x = x_ref[...].astype(F32)
    normed = (x * row_scale(x) * gain_ref[...]).astype(BF)
    proj = mm(normed, wc_ref[...])
    length = length_ref[0]
    live_col = start + lax.broadcasted_iota(jnp.int32, (rows, padded), 0) < length
    live_row = start + lax.broadcasted_iota(jnp.int32, (padded, rows), 1) < length
    eta_col = jnp.where(live_col, jax.nn.sigmoid(mm_nt(normed, lrt_ref[...])), 0.0) * (ETA_BASE / head_dim)
    rate = jax.nn.sigmoid(mm_nt(lrt_ref[...], normed))
    eta_row = jnp.where(live_row, rate, 0.0) * (ETA_BASE / head_dim)
    fac_ref[0, :padded] = eta_row * (1.0 - rate)
    fac_ref[0, padded:] = eta_row
    for i in every:
        at = i * head_dim
        k = proj[:, cols + at : cols + at + head_dim]
        v = proj[:, 2 * cols + at : 2 * cols + at + head_dim]
        kb, qb = k.astype(BF), proj[:, at : at + head_dim].astype(BF)
        k_minis = kb.reshape(group, MINI, head_dim)
        q_minis = qb.reshape(group, MINI, head_dim)
        kq_ref[i, :, :MINI] = k_minis
        kq_ref[i, :, MINI:] = q_minis
        next_ref[i, : group - 1, :MINI] = k_minis[1:]
        next_ref[i, group - 1 :, :MINI] = k_minis[:1]
        next_ref[i, :, MINI:] = q_minis
        kmv_ref[i] = (k - v).reshape(group, MINI, head_dim)
        rate_ref[i] = (eta_col[:, i : i + 1] * (1.0 / MINI)).reshape(group, MINI, 1)
        cross = (mm_nt(kb, kb) + 1.0) * (eta_row[i : i + 1] * (1.0 / MINI))
        for j in range(group - 1):
            at = j * MINI
            kk_ref[i, j] = cross[at + MINI : at + 2 * MINI, at : at + MINI].astype(BF)

    key_pre = [mm(kq_ref[i, 0, :MINI], w1_ref[i].astype(BF)) + c1_ref[i] for i in every]
    for j in range(group):
        rate = [rate_ref[i, j] for i in every]
        kmv = [kmv_ref[i, j] for i in every]
        stacked = [next_ref[i, j] for i in every]
        k = [kq_ref[i, j, :MINI] for i in every]
        kk = [kk_ref[i, j] for i in every] if j < group - 1 else None
        w1 = [w1_ref[i] for i in every]
        w2 = [w2_ref[i] for i in every]
        c1 = [c1_ref[i] for i in every]
        c2 = [c2_ref[i] for i in every]
        w1b = [w1[i].astype(BF) for i in every]
        w2b = [w2[i].astype(BF) for i in every]
        parts = [gelu_parts(key_pre[i]) for i in every]
        hb = [(key_pre[i] * parts[i][0]).astype(BF) for i in every]
        g2 = [mm_nt(hb[i], w2b[i]) + c2[i] + kmv[i] for i in every]
        slope = [parts[i][0] + key_pre[i] * parts[i][1] for i in every]
        curve = [parts[i][1] * (2.0 - key_pre[i] * key_pre[i]) for i in every]
        both = [mm(stacked[i], w1b[i]) + c1[i] for i in every]
        g2b = [g2[i].astype(BF) for i in every]
        u = [mm(g2b[i], w2b[i]) for i in every]
        fg2 = [rate[i] * g2[i] for i in every]
        w2n = [w2[i] - mm_tn(fg2[i].astype(BF), hb[i]) for i in every]
        c2n = [c2[i] - jnp.sum(fg2[i], axis=0, keepdims=True) for i in every]
        g1 = [u[i] * slope[i] for i in every]
        g1b = [g1[i].astype(BF) for i in every]
        if j < group - 1:
            key_pre = [both[i][:MINI] - mm(kk[i], g1b[i]) for i in every]
        fg1 = [rate[i] * g1[i] for i in every]
        w1n = [w1[i] - mm_tn(k[i], fg1[i].astype(BF)) for i in every]
        c1n = [c1[i] - jnp.sum(fg1[i], axis=0, keepdims=True) for i in every]
        for i in every:
            w1s_ref[i, j] = w1b[i]
            w2s_ref[i, j] = w2b[i]
            c2s_ref[i, j] = c2[i]
            h_ref[i, j] = hb[i]
            g1_ref[i, j] = g1b[i]
            g2_ref[i, j] = g2b[i]
            ga_ref[i, j] = slope[i]
            ug_ref[i, j] = u[i] * curve[i]
            pq_ref[i, j] = both[i][MINI:]
            w1_ref[i] = w1n[i]
            w2_ref[i] = w2n[i]
            c1_ref[i] = c1n[i]
            c2_ref[i] = c2n[i]

    scale = mini_masks(rows)[0]
    for i in every:
        at = i * head_dim
        q = proj[:, at : at + head_dim]
        gate = proj[:, 3 * cols + at : 3 * cols + at + head_dim]
        kb, qb = flat_rows(kq_ref[i, :, :MINI]), flat_rows(kq_ref[i, :, MINI:])
        hb, g1b, g2b = flat_rows(h_ref[i]), flat_rows(g1_ref[i]), flat_rows(g2_ref[i])
        mix = scale * eta_row[i : i + 1]
        query_pre = flat_rows(pq_ref[i]) - mm((mix * (mm_nt(qb, kb) + 1.0)).astype(BF), g1b)
        cdf, pdf = gelu_parts(query_pre)
        gp_ref[i] = (cdf + query_pre * pdf).reshape(group, MINI, -1)
        rb = (query_pre * cdf).astype(BF)
        r_ref[i] = rb.reshape(group, MINI, -1)
        s2 = (mix * (mm_nt(rb, hb) + 1.0)).astype(BF)
        through = [mm_nt(piece, w2s_ref[i, j]) + c2s_ref[i, j] for j, piece in enumerate(minis(rb))]
        mixed = q + jnp.concatenate(through, axis=0) - mm(s2, g2b)
        centered = mixed - jnp.mean(mixed, axis=-1, keepdims=True)
        hscale = row_scale(centered)
        unit = centered * hscale
        out = unit * pg_ref[i] + pb_ref[i]
        cdf, pdf = gelu_parts(gate)
        post_ref[:, at : at + head_dim] = (gate * cdf * out).astype(BF)
        gl_ref[i] = gate * cdf
        gs_ref[i] = (cdf + gate * pdf) * out
        unit_ref[i] = unit
        hscale_ref[i] = hscale


def bwd_kernel(
    x_ref, gain_ref, wc_ref, lrt_ref, pg_ref, gpost_ref,
    gwi_ref, glri_ref, gaini_ref, gpgi_ref, gpbi_ref, w1i_ref, c1i_ref, w2i_ref, c2i_ref,
    kq_ref, rate_ref, fac_ref, gl_ref, gs_ref, unit_ref, hscale_ref,
    w1s_ref, w2s_ref, h_ref, r_ref, g1_ref, g2_ref, ga_ref, ug_ref, gp_ref,
    back_ref, gw_ref, glr_ref, gain_grad_ref, gpg_ref, gpb_ref, dw1_ref, dc1_ref, dw2_ref, dc2_ref,
    d_ref, g1a_ref, g2a_ref, ha_ref, ka_ref, dp_ref, kc_ref, dk_ref, da_ref, df_ref, de_ref, all_ref,
):
    chains, group = kq_ref.shape[:2]
    rows = group * MINI
    head_dim = kq_ref.shape[-1]
    cols = chains * head_dim
    every = range(chains)

    @pl.when(pl.program_id(0) == 0)
    def _():
        dw1_ref[...] = w1i_ref[...]
        dc1_ref[...] = c1i_ref[...]
        dw2_ref[...] = w2i_ref[...]
        dc2_ref[...] = c2i_ref[...]
        gw_ref[...] = gwi_ref[...]
        glr_ref[...] = glri_ref[...]
        gain_grad_ref[...] = gaini_ref[...]
        gpg_ref[...] = gpgi_ref[...]
        gpb_ref[...] = gpbi_ref[...]

    scale, eye = mini_masks(rows)
    padded = lrt_ref.shape[0]
    gpost = gpost_ref[...].astype(F32)
    for i in every:
        at = i * head_dim
        piece = gpost[:, at : at + head_dim]
        all_ref[:, 3 * cols + at : 3 * cols + at + head_dim] = (piece * gs_ref[i]).astype(BF)
        head = piece * gl_ref[i]
        unit = unit_ref[i]
        gpg_ref[i] += jnp.sum(head * unit, axis=0, keepdims=True)
        gpb_ref[i] += jnp.sum(head, axis=0, keepdims=True)
        lifted = head * pg_ref[i]
        d = hscale_ref[i] * (
            lifted
            - jnp.mean(lifted, axis=-1, keepdims=True)
            - unit * jnp.mean(lifted * unit, axis=-1, keepdims=True)
        )
        d_ref[i] = d.reshape(group, MINI, head_dim)
        db = d.astype(BF)
        kb, qb = flat_rows(kq_ref[i, :, :MINI]), flat_rows(kq_ref[i, :, MINI:])
        hb, rb, g1b, g2b = (flat_rows(ref[i]) for ref in (h_ref, r_ref, g1_ref, g2_ref))
        mix = scale * fac_ref[0, padded + i : padded + i + 1]
        ds2 = -mm_nt(db, g2b)
        x2 = mm_nt(rb, hb) + 1.0
        x1 = mm_nt(qb, kb) + 1.0
        dx2 = (ds2 * mix).astype(BF)
        dr = jnp.concatenate([mm(part, w2s_ref[i, j]) for j, part in enumerate(minis(db))], axis=0)
        dp = (dr + mm(dx2, hb)) * flat_rows(gp_ref[i])
        dpb = dp.astype(BF)
        ds1 = -mm_nt(dpb, g1b)
        dx1 = (ds1 * mix).astype(BF)
        dq = jnp.concatenate([mm_nt(part, w1s_ref[i, j]) for j, part in enumerate(minis(dpb))], axis=0)
        all_ref[:, at : at + head_dim] = (d + dq + mm(dx1, kb)).astype(BF)
        g1a_ref[i] = -mm_tn((mix * x1).astype(BF), dpb).reshape(group, MINI, -1)
        g2a_ref[i] = -mm_tn((mix * x2).astype(BF), db).reshape(group, MINI, -1)
        ha_ref[i] = mm_tn(dx2, rb).reshape(group, MINI, -1)
        ka_ref[i] = mm_tn(dx1, qb).reshape(group, MINI, -1)
        dp_ref[i] = dpb.reshape(group, MINI, -1)
        de_ref[i] = jnp.sum((ds2 * x2 + ds1 * x1) * scale, axis=0, keepdims=True)
        kk = mm_nt(kb, kb) + 1.0
        kx = mm_nt(kb, qb) + 1.0
        for j in range(group - 1):
            own, after = slice(j * MINI, (j + 1) * MINI), slice((j + 1) * MINI, (j + 2) * MINI)
            kc_ref[i, j] = jnp.concatenate([kk[own, after], kx[own, after]], axis=1).astype(BF)

    t1 = [mm(kq_ref[i, group - 1, :MINI], dw1_ref[i].astype(BF)) + dc1_ref[i] for i in every]
    for j in reversed(range(group)):

        def all_of(ref):
            return [ref[i, j] for i in every]

        d, kq, rate, w2b, hb, rb, g1b, g2b = (
            all_of(ref) for ref in (d_ref, kq_ref, rate_ref, w2s_ref, h_ref, r_ref, g1_ref, g2_ref)
        )
        ga, ug, dpb, g1a, g2a, ha = (
            all_of(ref) for ref in (ga_ref, ug_ref, dp_ref, g1a_ref, g2a_ref, ha_ref)
        )
        dw1 = [dw1_ref[i] for i in every]
        dw2 = [dw2_ref[i] for i in every]
        dc1 = [dc1_ref[i] for i in every]
        dc2 = [dc2_ref[i] for i in every]
        g1 = [g1b[i].astype(F32) for i in every]
        g2 = [g2b[i].astype(F32) for i in every]
        dw1b = [dw1[i].astype(BF) for i in every]
        dw2b = [dw2[i].astype(BF) for i in every]
        dg1 = [g1a[i] - rate[i] * t1[i] for i in every]
        dub = [(dg1[i] * ga[i]).astype(BF) for i in every]
        through = [mm_nt(dub[i], w2b[i]) for i in every]
        t2 = [mm_nt(hb[i], dw2b[i]) + dc2[i] for i in every]
        dha = [ha[i] - mm((rate[i] * g2[i]).astype(BF), dw2b[i]) for i in every]
        dg2 = [through[i] + (g2a[i] - rate[i] * t2[i]) for i in every]
        dg2b = [dg2[i].astype(BF) for i in every]
        dh = [mm(dg2b[i], w2b[i]) + dha[i] for i in every]
        if j > 0:
            base = [mm(kq_ref[i, j - 1, :MINI], dw1b[i]) + dc1[i] for i in every]
        dk = [dg2[i] - mm_nt((rate[i] * g1[i]).astype(BF), dw1b[i]) for i in every]
        df = [
            -(
                jnp.sum(g1[i] * t1[i], axis=1, keepdims=True)
                + jnp.sum(g2[i] * t2[i], axis=1, keepdims=True)
            )
            for i in every
        ]
        da = [dg1[i] * ug[i] + dh[i] * ga[i] for i in every]
        dab = [da[i].astype(BF) for i in every]
        both = [jnp.concatenate([dab[i], dpb[i]], axis=0) for i in every]
        if j > 0:
            t1 = [base[i] + mm(kc_ref[i, j - 1], both[i]) for i in every]
        dw1n = [dw1[i] + mm_tn(kq[i], both[i]) for i in every]
        dc1n = [dc1[i] + jnp.sum(da[i] + dpb[i].astype(F32), axis=0, keepdims=True) for i in every]
        dw2n = [
            dw2[i]
            + mm_tn(
                jnp.concatenate([d[i].astype(BF), dg2b[i], g2b[i]], axis=0),
                jnp.concatenate([rb[i], hb[i], dub[i]], axis=0),
            )
            for i in every
        ]
        dc2n = [dc2[i] + jnp.sum(d[i] + dg2[i], axis=0, keepdims=True) for i in every]
        for i in every:
            piece, at = slice(j * MINI, (j + 1) * MINI), 2 * cols + i * head_dim
            all_ref[piece, at : at + head_dim] = (-dg2[i]).astype(BF)
            dk_ref[i, j] = dk[i]
            da_ref[i, j] = dab[i]
            df_ref[i, j] = df[i]
            dw1_ref[i] = dw1n[i]
            dc1_ref[i] = dc1n[i]
            dw2_ref[i] = dw2n[i]
            dc2_ref[i] = dc2n[i]

    x = x_ref[...].astype(F32)
    unit_in = x * row_scale(x)
    normed = (unit_in * gain_ref[...]).astype(BF)
    lrt = lrt_ref[...]
    which = lax.broadcasted_iota(jnp.int32, (padded, rows), 0)
    rates = jnp.zeros((padded, rows), F32)
    for i in every:
        at = cols + i * head_dim
        dk = jnp.concatenate([mm_nt(da_ref[i, j], w1s_ref[i, j]) for j in range(group)], axis=0)
        all_ref[:, at : at + head_dim] = (flat_rows(dk_ref[i]) + flat_rows(ka_ref[i]) + dk).astype(BF)
        line = de_ref[i] + jnp.sum(eye * flat_rows(df_ref[i]), axis=0, keepdims=True)
        rates = jnp.where(which == i, line, rates)
    rates = (rates * fac_ref[0, :padded]).astype(BF)
    grads = all_ref[...]
    back = mm_nt(grads, wc_ref[...]) + mm_tn(rates, lrt)
    gain_grad_ref[...] += jnp.sum(back * unit_in, axis=0, keepdims=True)
    back_ref[...] = back.astype(BF)
    gw_ref[...] += mm_tn(normed, grads)
    glr_ref[...] += mm(rates, normed)


GROUP = 8


def block_specs(chains, head_dim, inner, padded, place):
    rows = GROUP * MINI

    def mini(first, second):
        return pl.BlockSpec((chains, GROUP, first, second), lambda g: (0, place(g), 0, 0))

    def head(second):
        return pl.BlockSpec((chains, rows, second), lambda g: (0, place(g), 0))

    return [
        mini(2 * MINI, head_dim), mini(MINI, 1),
        pl.BlockSpec((1, 2 * padded, rows), lambda g: (place(g), 0, 0)),
        head(head_dim), head(head_dim), head(head_dim), head(1),
        mini(head_dim, inner), mini(head_dim, inner), mini(MINI, inner), mini(MINI, inner),
        mini(MINI, inner), mini(MINI, head_dim), mini(MINI, inner), mini(MINI, inner), mini(MINI, inner),
    ]


def whole_spec(value):
    return pl.BlockSpec(value.shape, lambda g: (0,) * value.ndim)


def run_fwd(first, last, length, tokens, gain, wc, lrt, pg, pb, state):
    width = tokens.shape[1]
    chains, head_dim, inner = state[0].shape
    rows = GROUP * MINI
    steps = last - first
    count = steps * GROUP
    padded = lrt.shape[0]

    def mini(first_size, second_size, dtype):
        return jax.ShapeDtypeStruct((chains, count, first_size, second_size), dtype)

    def head(second):
        return jax.ShapeDtypeStruct((chains, steps * rows, second), F32)

    row_spec = pl.BlockSpec((rows, width), lambda g: (first + g, 0))
    small = (gain, wc, lrt, *state, pg, pb)
    return pl.pallas_call(
        partial(fwd_kernel, first=first),
        grid=(steps,),
        in_specs=[pl.BlockSpec(memory_space=pltpu.SMEM), row_spec] + [whole_spec(v) for v in small],
        out_specs=[pl.BlockSpec((rows, chains * head_dim), lambda g: (g, 0))]
        + block_specs(chains, head_dim, inner, padded, lambda g: g)
        + [whole_spec(v) for v in state],
        out_shape=[
            jax.ShapeDtypeStruct((steps * rows, chains * head_dim), BF),
            mini(2 * MINI, head_dim, BF), mini(MINI, 1, F32),
            jax.ShapeDtypeStruct((steps, 2 * padded, rows), F32),
            head(head_dim), head(head_dim), head(head_dim), head(1),
            mini(head_dim, inner, BF), mini(head_dim, inner, BF), mini(MINI, inner, BF), mini(MINI, inner, BF),
            mini(MINI, inner, BF), mini(MINI, head_dim, BF), mini(MINI, inner, F32), mini(MINI, inner, F32),
            mini(MINI, inner, F32),
        ]
        + [jax.ShapeDtypeStruct(v.shape, F32) for v in state],
        scratch_shapes=[
            pltpu.VMEM((chains, GROUP, MINI, head_dim), F32),
            pltpu.VMEM((chains, GROUP, 2 * MINI, head_dim), BF),
            pltpu.VMEM((chains, GROUP, MINI, MINI), BF),
            pltpu.VMEM((chains, GROUP, MINI, inner), F32),
            pltpu.VMEM((chains, GROUP, 1, head_dim), F32),
        ],
        compiler_params=pltpu.CompilerParams(vmem_limit_bytes=50 << 20),
        cost_estimate=pl.CostEstimate(
            flops=9_000_000_000 * steps, bytes_accessed=5_000_000 * steps, transcendentals=0
        ),
        name="chain_forward",
    )(length, tokens, *small)


def run_bwd(first, last, base, tokens, gain, wc, lrt, pg, gpost, state, saved):
    width = tokens.shape[1]
    chains, head_dim, inner = state[5].shape
    rows = GROUP * MINI
    padded = lrt.shape[0]
    wide = wc.shape[1]
    steps = last - first

    def place(g):
        return steps - 1 - g

    def shape(*extent):
        return jax.ShapeDtypeStruct(extent, F32)

    small = (gain, wc, lrt, pg)
    outs = [shape(*value.shape) for value in state]

    def scratch(first_size, second_size, dtype):
        return pltpu.VMEM((chains, GROUP, first_size, second_size), dtype)

    return pl.pallas_call(
        bwd_kernel,
        grid=(steps,),
        in_specs=[pl.BlockSpec((rows, width), lambda g: (first + place(g), 0))]
        + [whole_spec(v) for v in small]
        + [pl.BlockSpec((rows, chains * head_dim), lambda g: (first + place(g), 0))]
        + [whole_spec(v) for v in state]
        + block_specs(chains, head_dim, inner, padded, lambda g: first - base + place(g)),
        out_specs=[pl.BlockSpec((rows, width), lambda g: (place(g), 0))] + [whole_spec(v) for v in outs],
        out_shape=[jax.ShapeDtypeStruct((steps * rows, width), BF)] + outs,
        scratch_shapes=[
            scratch(MINI, head_dim, F32), scratch(MINI, inner, F32), scratch(MINI, head_dim, F32),
            scratch(MINI, inner, F32), scratch(MINI, head_dim, F32), scratch(MINI, inner, BF),
            scratch(MINI, 2 * MINI, BF), scratch(MINI, head_dim, F32), scratch(MINI, inner, BF),
            scratch(MINI, 1, F32), pltpu.VMEM((chains, 1, rows), F32), pltpu.VMEM((rows, wide), BF),
        ],
        compiler_params=pltpu.CompilerParams(vmem_limit_bytes=50 << 20),
        cost_estimate=pl.CostEstimate(
            flops=11_000_000_000 * steps, bytes_accessed=5_000_000 * steps, transcendentals=0
        ),
        name="chain_backward",
    )(tokens, *small, gpost, *state, *saved)


def swap(value):
    return lax.ppermute(value, "tp", [(0, 1), (1, 0)])


def rows_kernel(
    spot_ref, post_ref, own_ref, other_ref, x_ref, cot_ref, gain_ref,
    out_ref, grad_ref, gpost_ref, normed_ref, low_ref, back_ref, gain_grad_ref, cat0_ref, cat1_ref, *act_refs,
):
    core, start, length = spot_ref[0], spot_ref[1], spot_ref[2]
    span, width = x_ref.shape
    cols = post_ref.shape[2]
    units = act_refs[0].shape[1]
    places = cat0_ref.shape[1] // cols
    x = x_ref[...].astype(F32)
    live = start + lax.broadcasted_iota(jnp.int32, (span, width), 0) < length
    back = jnp.where(live, cot_ref[...].astype(F32), 0.0)
    back_low = back.astype(BF)
    back_ref[...] = back_low
    halves = ((own_ref, core), (other_ref, 1 - core))
    hidden = x
    for half, (w_ref, side) in enumerate(halves):
        joined = jnp.concatenate([post_ref[side * places + p] for p in range(places)], axis=1)
        (cat0_ref, cat1_ref)[half][...] = joined
        hidden = hidden + mm_nt(joined, w_ref[:, 3 * units :])
    scale = row_scale(hidden)
    gain = gain_ref[...]
    normed = (hidden * scale * gain).astype(BF)
    normed_ref[...] = normed
    feed = jnp.zeros((span, width), F32)
    grad = jnp.zeros((span, width), F32)
    step = min(units, 512)
    for half, (w_ref, _) in enumerate(halves):
        for at in range(0, units, step):
            w_gate = w_ref[:, at : at + step]
            w_up = w_ref[:, units + at : units + at + step]
            w_down = w_ref[:, 2 * units + at : 2 * units + at + step]
            up_gate = mm(normed, w_gate)
            up_lin = mm(normed, w_up)
            grad_act = mm(back_low, w_down)
            gate = jax.nn.sigmoid(up_gate)
            silu = up_gate * gate
            act = (silu * up_lin).astype(BF)
            grad_gate = (grad_act * up_lin * (gate * (1.0 + up_gate * (1.0 - gate)))).astype(BF)
            grad_lin = (grad_act * silu).astype(BF)
            act_refs[3 * half + 0][:, at : at + step] = grad_gate
            act_refs[3 * half + 1][:, at : at + step] = grad_lin
            act_refs[3 * half + 2][:, at : at + step] = act
            feed += mm_nt(act, w_down)
            grad += mm_nt(grad_gate, w_gate) + mm_nt(grad_lin, w_up)
    out_ref[...] = (hidden + feed).astype(BF)
    lifted = grad * gain
    hat = hidden * scale
    gain_grad_ref[...] = jnp.sum(grad * hat, axis=0, keepdims=True)
    total = back + scale * (lifted - hat * jnp.mean(lifted * hat, axis=-1, keepdims=True))
    grad_ref[...] = total
    low = total.astype(BF)
    low_ref[...] = low
    for p in range(2 * places, gpost_ref.shape[0]):
        gpost_ref[p] = jnp.zeros(gpost_ref.shape[1:], BF)
    for w_ref, side in halves:
        gpost = mm(low, w_ref[:, 3 * units :]).astype(BF)
        for p in range(places):
            gpost_ref[side * places + p] = gpost[:, p * cols : (p + 1) * cols]


def run_rows(spots, post, own, other, x, cot, gain, half_out):
    ring, span, cols = post.shape
    width = x.shape[1]
    units = (own.shape[1] - half_out) // 3
    vmem = pl.BlockSpec(memory_space=pltpu.VMEM)

    def shape(extent, dtype):
        return jax.ShapeDtypeStruct(extent, dtype)

    return pl.pallas_call(
        rows_kernel,
        in_specs=[pl.BlockSpec(memory_space=pltpu.SMEM)] + [vmem] * 6,
        out_specs=[vmem] * 15,
        out_shape=[
            shape((span, width), BF), shape((span, width), F32), shape((ring, span, cols), BF),
            shape((span, width), BF), shape((span, width), BF), shape((span, width), BF), shape((1, width), F32),
        ]
        + [shape((span, half_out), BF)] * 2
        + [shape((span, units), BF)] * 6,
        compiler_params=pltpu.CompilerParams(vmem_limit_bytes=52 << 20),
        cost_estimate=pl.CostEstimate(flops=20_000_000_000, bytes_accessed=20_000_000, transcendentals=0),
        name="rows_main",
    )(spots, post, own, other, x, cot, gain)


def products(pairs, parts, store):
    start = 0
    for left, right in zip(pairs, parts):
        size = right.shape[-1]
        step = 512 if size % 512 == 0 else size
        for at in range(0, size, step):
            store(start + at, mm_tn(left[...], right[:, at : at + step]))
        start += size


def sums_other_kernel(*refs):
    *sources, out_ref = refs
    count = len(sources) // 2

    def store(at, value):
        out_ref[:, at : at + value.shape[1]] = value.astype(BF)

    products(sources[:count], sources[count:], store)


def sums_own_kernel(place_ref, other_ref, *refs, count, outs):
    sources, out_refs, held_ref = refs[: 2 * count], refs[2 * count : 2 * count + outs], refs[-1]

    def store(at, value):
        piece = slice(at, at + value.shape[1])
        held_ref[:, piece] = (value + other_ref[:, piece].astype(F32)).astype(BF)

    products(sources[:count], sources[count:], store)
    for bit, out_ref in enumerate(out_refs):
        blocks, part = out_ref.shape[:2]
        for number in range(blocks):
            at = pl.multiple_of((number * outs + (place_ref[0] ^ bit)) * part, part)
            out_ref[number] = held_ref[pl.ds(at, part), :]


def run_sums(lefts, rights, other=None, place=None, blocks=1, outs=1):
    width = lefts[0].shape[1]
    total = sum(right.shape[1] for right in rights)
    vmem = pl.BlockSpec(memory_space=pltpu.VMEM)
    count = len(lefts)
    params = pltpu.CompilerParams(vmem_limit_bytes=40 << 20)
    cost = pl.CostEstimate(flops=5_000_000_000, bytes_accessed=6_000_000, transcendentals=0)
    if other is None:
        return pl.pallas_call(
            sums_other_kernel,
            in_specs=[vmem] * (2 * count),
            out_specs=vmem,
            out_shape=jax.ShapeDtypeStruct((width, total), BF),
            compiler_params=params,
            cost_estimate=cost,
            name="sums_other",
        )(*lefts, *rights)
    part = width // (blocks * outs)
    return pl.pallas_call(
        partial(sums_own_kernel, count=count, outs=outs),
        in_specs=[pl.BlockSpec(memory_space=pltpu.SMEM)] + [vmem] * (2 * count + 1),
        out_specs=[vmem] * outs,
        out_shape=[jax.ShapeDtypeStruct((blocks, part, total), BF)] * outs,
        scratch_shapes=[pltpu.VMEM((width, total), BF)],
        compiler_params=params,
        cost_estimate=cost,
        name="sums_own",
    )(place, other, *lefts, *rights)


def assemble_kernel(spots_ref, pack_ref, *refs, ring):
    far_refs, near_ref, out_ref = refs[:ring], refs[ring], refs[-1]
    me, place = spots_ref[0], spots_ref[1]
    part = out_ref.shape[1]
    cut = far_refs[0].shape[2]
    for number in range(ring):
        piece = slice(number * part, (number + 1) * part)
        out_ref[me * ring + number, :, :cut] = pack_ref[piece, :cut]
        for z in range(near_ref.shape[0]):
            out_ref[z * ring + number, :, cut:] = near_ref[z, piece]
    for bit, far_ref in enumerate(far_refs):
        for other in range(far_ref.shape[0]):
            out_ref[(me ^ (other + 1)) * ring + (place ^ bit), :, :cut] = far_ref[other]


def run_assemble(spots, pack, far_parts, near_parts):
    vmem = pl.BlockSpec(memory_space=pltpu.VMEM)
    ring = len(far_parts)
    part = pack.shape[0] // ring
    return pl.pallas_call(
        partial(assemble_kernel, ring=ring),
        in_specs=[pl.BlockSpec(memory_space=pltpu.SMEM)] + [vmem] * (2 + ring),
        out_specs=vmem,
        out_shape=jax.ShapeDtypeStruct((near_parts.shape[0] * ring, part, pack.shape[1]), BF),
        compiler_params=pltpu.CompilerParams(vmem_limit_bytes=40 << 20),
        name="assemble_rows",
    )(spots, pack, *far_parts, near_parts)


SMALL = 64


def small_spots(chains, depth, inner_share):
    side = 2 * chains * inner_share
    return side, {
        "lr": 0, "n1": chains, "n2": chains + 1, "b1": chains + 2,
        "b2": 2 * chains + 2, "pg": 3 * chains + 2, "pb": 4 * chains + 2,
    }


def pack_weights_kernel(
    pick_ref, qkv_ref, gate_ref, lr_ref, n1_ref, n2_ref, w1_ref, b1_ref, w2_ref, b2_ref, pg_ref, pb_ref,
    out_ref, small_ref, *, chains,
):
    depth = gate_ref.shape[0]
    heads, head_dim, inner_share = w1_ref.shape
    cols = chains * head_dim
    all_cols = heads * head_dim
    side, spots = small_spots(chains, depth, inner_share)
    small_ref[...] = jnp.zeros_like(small_ref)

    def put(name, i, value):
        row = spots[name] + i
        small_ref[row : row + 1, side : side + value.shape[1]] = value.astype(F32)

    for option in range(heads // chains):

        @pl.when(pick_ref[0] == option)
        def _():
            at = option * cols
            for which in range(3):
                start = which * all_cols + at
                out_ref[:depth, which * cols : (which + 1) * cols] = qkv_ref[:, start : start + cols]
            out_ref[:depth, 3 * cols :] = gate_ref[:, at : at + cols]
            for i in range(chains):
                head = option * chains + i
                lanes = slice(i * inner_share, (i + 1) * inner_share)
                small_ref[:, lanes] = w1_ref[head].astype(F32)
                lanes = slice((chains + i) * inner_share, (chains + i + 1) * inner_share)
                small_ref[:, lanes] = w2_ref[head].astype(F32)
                for name, ref in (("lr", lr_ref), ("b1", b1_ref), ("b2", b2_ref), ("pg", pg_ref), ("pb", pb_ref)):
                    put(name, i, ref[head : head + 1, :])

    put("n1", 0, n1_ref[...])
    put("n2", 0, n2_ref[...])
    out_ref[depth:, :] = small_ref[...].astype(BF)


def halves_by_core(core, mine_ref, other_ref, work):
    @pl.when(core == 0)
    def _():
        work(mine_ref, other_ref)

    @pl.when(core != 0)
    def _():
        work(other_ref, mine_ref)


def unpack_weights_kernel(
    core_ref, mine_ref, other_ref,
    wc_ref, lrt_ref, n1_ref, n2_ref, w1_ref, b1_ref, w2_ref, b2_ref, pg_ref, pb_ref, lines_ref,
):
    shards, half, _ = mine_ref.shape
    chains, _, inner = w1_ref.shape
    inner_share = inner // shards
    depth = 2 * half - SMALL
    head_share = b2_ref.shape[2] // shards
    side, spots = small_spots(chains, depth, inner_share)
    lines_ref[...] = jnp.zeros_like(lines_ref)

    def work(low_ref, high_ref):
        for z in range(shards):
            wc_ref[z * depth : z * depth + half] = low_ref[z]
            wc_ref[z * depth + half : (z + 1) * depth] = high_ref[z, : depth - half]
            small = high_ref[z, depth - half :].astype(F32)

            def get(name, i, size):
                row = spots[name] + i
                return small[row : row + 1, side : side + size]

            here = slice(z * depth, (z + 1) * depth)
            n1_ref[:, here] = get("n1", 0, depth)
            n2_ref[:, here] = get("n2", 0, depth)
            for i in range(chains):
                lines_ref[i : i + 1, here] = get("lr", i, depth)
                lanes = slice(z * inner_share, (z + 1) * inner_share)
                w1_ref[i, :, lanes] = small[:, i * inner_share : (i + 1) * inner_share]
                w2_ref[i, :, lanes] = small[:, (chains + i) * inner_share : (chains + i + 1) * inner_share]
                b1_ref[i, :, lanes] = get("b1", i, inner_share)
                lanes = slice(z * head_share, (z + 1) * head_share)
                for name, ref in (("b2", b2_ref), ("pg", pg_ref), ("pb", pb_ref)):
                    ref[i, :, lanes] = get(name, i, head_share)

    halves_by_core(core_ref[0], mine_ref, other_ref, work)
    lrt_ref[...] = lines_ref[...].astype(BF)


def pack_grads_kernel(
    core_ref, gw_ref, glr_ref, n1_ref, n2_ref, w1_ref, b1_ref, w2_ref, b2_ref, pg_ref, pb_ref,
    keep_ref, send_ref, small_ref,
):
    shards, half, _ = keep_ref.shape
    chains, _, inner = w1_ref.shape
    inner_share = inner // shards
    depth = 2 * half - SMALL
    head_share = b2_ref.shape[2] // shards
    side, spots = small_spots(chains, depth, inner_share)

    def work(low_ref, high_ref):
        for z in range(shards):
            small_ref[...] = jnp.zeros_like(small_ref)

            def put(name, i, value):
                row = spots[name] + i
                small_ref[row : row + 1, side : side + value.shape[1]] = value

            here = slice(z * depth, (z + 1) * depth)
            low_ref[z] = gw_ref[z * depth : z * depth + half].astype(BF)
            high_ref[z, : depth - half] = gw_ref[z * depth + half : (z + 1) * depth].astype(BF)
            put("n1", 0, n1_ref[:, here])
            put("n2", 0, n2_ref[:, here])
            for i in range(chains):
                put("lr", i, glr_ref[i : i + 1, here])
                lanes = slice(z * inner_share, (z + 1) * inner_share)
                small_ref[:, i * inner_share : (i + 1) * inner_share] = w1_ref[i, :, lanes]
                small_ref[:, (chains + i) * inner_share : (chains + i + 1) * inner_share] = w2_ref[i, :, lanes]
                put("b1", i, b1_ref[i, :, lanes])
                lanes = slice(z * head_share, (z + 1) * head_share)
                for name, ref in (("b2", b2_ref), ("pg", pg_ref), ("pb", pb_ref)):
                    put(name, i, ref[i, :, lanes])
            high_ref[z, depth - half :] = small_ref[...].astype(BF)

    halves_by_core(core_ref[0], keep_ref, send_ref, work)


def unpack_grads_kernel(
    core_ref, mine_ref, other_ref,
    qkv_ref, gate_ref, lrt_ref, n1_ref, n2_ref, w1_ref, b1_ref, w2_ref, b2_ref, pg_ref, pb_ref, *, chains,
):
    ring, half, wide = mine_ref.shape
    cols = wide // 4
    heads, _, inner_share = w1_ref.shape
    depth = gate_ref.shape[0]
    head_share = b2_ref.shape[1]
    places = heads // chains
    side, spots = small_spots(chains, depth, inner_share)
    core = core_ref[0]

    def work(low_ref, high_ref):
        for p in range(places):
            place = core * places + p
            big = jnp.concatenate([low_ref[place], high_ref[place, : depth - half]], axis=0).astype(F32)
            small = high_ref[place, depth - half :].astype(F32)
            at = p * cols
            for which in range(3):
                qkv_ref[:, which, at : at + cols] = big[:, which * cols : (which + 1) * cols]
            gate_ref[:, at : at + cols] = big[:, 3 * cols :]
            for i in range(chains):
                head = p * chains + i
                w1_ref[head] = small[:, i * inner_share : (i + 1) * inner_share]
                w2_ref[head] = small[:, (chains + i) * inner_share : (chains + i + 1) * inner_share]
                for name, ref, size in (
                    ("lr", lrt_ref, depth), ("b1", b1_ref, inner_share), ("b2", b2_ref, head_share),
                    ("pg", pg_ref, head_share), ("pb", pb_ref, head_share),
                ):
                    row = spots[name] + i
                    ref[head : head + 1, :] = small[row : row + 1, side : side + size]
        for name, ref in (("n1", n1_ref), ("n2", n2_ref)):
            row = spots[name]
            total = jnp.zeros((1, depth), F32)
            for place in range(ring):
                lines = high_ref[place, depth - half :].astype(F32)
                total = total + lines[row : row + 1, side : side + depth]
            ref[...] = total

    halves_by_core(core, mine_ref, other_ref, work)


def add_and_deal_kernel(place_ref, keep_ref, other_ref, *out_refs):
    for bit, out_ref in enumerate(out_refs):
        which = place_ref[0] ^ bit
        out_ref[...] = (keep_ref[which].astype(F32) + other_ref[which].astype(F32)).astype(BF)


def in_vmem(kernel, name, shapes, scratch, scalars, *operands):
    vmem = pl.BlockSpec(memory_space=pltpu.VMEM)
    return pl.pallas_call(
        kernel,
        in_specs=[pl.BlockSpec(memory_space=pltpu.SMEM)] + [vmem] * len(operands),
        out_specs=[vmem] * len(shapes),
        out_shape=[jax.ShapeDtypeStruct(extent, dtype) for extent, dtype in shapes],
        scratch_shapes=[pltpu.VMEM(extent, F32) for extent in scratch],
        compiler_params=pltpu.CompilerParams(vmem_limit_bytes=40 << 20),
        name=name,
    )(jnp.stack(scalars).astype(jnp.int32), *operands)


def place_kernel(spots_ref, *refs):
    *sources, target = refs
    for number, source in enumerate(sources):
        target[spots_ref[number]] = source[...]


def placed(pieces, spots):
    return pl.pallas_call(
        place_kernel,
        in_specs=[pl.BlockSpec(memory_space=pltpu.SMEM)]
        + [pl.BlockSpec(memory_space=pltpu.VMEM)] * len(pieces),
        out_specs=pl.BlockSpec(memory_space=pltpu.VMEM),
        out_shape=jax.ShapeDtypeStruct((len(pieces),) + pieces[0].shape, pieces[0].dtype),
        compiler_params=pltpu.CompilerParams(vmem_limit_bytes=40 << 20),
        name="place_pieces",
    )(jnp.stack(spots).astype(jnp.int32), *pieces)


def exchanged(value, axis):
    size = lax.axis_size(axis)
    return [value] + [
        lax.ppermute(value, axis, [(source, source ^ bit) for source in range(size)])
        for bit in range(1, size)
    ]


def sent(taken, axis):
    return taken[:1] + [
        lax.ppermute(taken[bit], axis, [(source, source ^ bit) for source in range(len(taken))])
        for bit in range(1, len(taken))
    ]


def scattered(value, axis):
    size = lax.axis_size(axis)
    me = lax.axis_index(axis)
    return sent([lax.dynamic_index_in_dim(value, me ^ bit, 0, keepdims=False) for bit in range(size)], axis)


def placed_along(pieces, axis):
    me = lax.axis_index(axis)
    return placed(pieces, [me ^ bit for bit in range(len(pieces))])


def spread(value, axis):
    return placed_along(exchanged(value, axis), axis)


def tied(*values):
    return lax.optimization_barrier(values)


def in_turn(first, second):
    return jnp.where(lax.axis_index("tp") == 0, jnp.stack([first, second]), jnp.stack([second, first]))


def on_device(
    tokens,
    lengths,
    norm1_gain,
    qkv_weight,
    lr_weight,
    inner_w1,
    inner_b1,
    inner_w2,
    inner_b2,
    post_gain,
    post_bias,
    gate_weight,
    out_weight,
    norm2_gain,
    ffn_gate,
    ffn_up,
    ffn_down,
    cotangent,
):
    micro, span, width = tokens.shape
    ring = lax.axis_size("ctx")
    shards = lax.axis_size("shard")
    pair = lax.axis_size("tp")
    place = lax.axis_index("ctx")
    core = lax.axis_index("tp")
    local_heads, head_dim, inner_share = inner_w1.shape
    head_share = inner_b2.shape[1]
    depth = norm1_gain.shape[0]
    inner = inner_share * shards
    total_heads = local_heads * pair
    chains = -(-total_heads // ring)
    span_all = ring * span
    count = span_all // MINI
    cols = chains * head_dim
    wide = 4 * cols

    row_tokens = lax.dynamic_index_in_dim(tokens, core, 0, keepdims=False)
    token_parts = exchanged(row_tokens, "ctx")

    first_head = jnp.minimum(place * chains, total_heads - chains)
    owner = first_head // local_heads
    local_first = first_head - owner * local_heads

    packed = in_vmem(
        partial(pack_weights_kernel, chains=chains), "pack_weights",
        [((depth + SMALL, wide), BF)], [(SMALL, wide)], [local_first // chains],
        qkv_weight.reshape(depth, -1), gate_weight, lr_weight.T, norm1_gain[None], norm2_gain[None],
        inner_w1, inner_b1, inner_w2, inner_b2, post_gain, post_bias,
    )[0]
    half_rows = (depth + SMALL) // 2
    packed = jnp.where(core == owner, packed, swap(packed))
    gathered = exchanged(lax.dynamic_slice_in_dim(packed, core * half_rows, half_rows, 0), "shard")
    gathered, token_parts = tied(gathered, token_parts)

    units = ffn_gate.shape[1]
    half_out = out_weight.shape[0]
    row_pack = jnp.concatenate([ffn_gate, ffn_up, ffn_down.T, out_weight.T], axis=1)
    part = depth // ring
    cut = 3 * row_pack.shape[1] // 4 // 128 * 128
    row_near = row_pack[:, cut:]
    row_part = lax.dynamic_slice(row_pack, (place * part, 0), (part, cut))
    row_part, row_near, gathered = tied(row_part, row_near, gathered)
    row_parts = exchanged(row_part, "shard")
    slot_tokens = placed_along(token_parts, "ctx").reshape(span_all, width)
    gathered = placed_along(gathered, "shard")

    padded = -(-chains // 16) * 16
    w_chain, rate_rows, gain_row, gain_two, *rest = in_vmem(
        unpack_weights_kernel, "unpack_weights",
        [
            ((width, wide), BF), ((padded, width), BF), ((1, width), F32), ((1, width), F32),
            ((chains, head_dim, inner), F32), ((chains, 1, inner), F32),
            ((chains, head_dim, inner), F32), ((chains, 1, head_dim), F32),
            ((chains, 1, head_dim), F32), ((chains, 1, head_dim), F32),
        ],
        [(padded, width)], [core], gathered, swap(gathered),
    )
    state, (norm_gain, norm_bias) = tuple(rest[:4]), rest[4:]

    slot_length = lax.dynamic_index_in_dim(lengths, core, 0, keepdims=True)
    steps = span_all // (GROUP * MINI)
    middle = 3 * steps // 8

    def forward(first, last, begin):
        done = run_fwd(
            first, last, slot_length, slot_tokens, gain_row, w_chain, rate_rows, norm_gain, norm_bias, begin
        )
        return done[0], done[1:-4], done[-4:]

    post_low, saved_low, state_low = forward(0, middle, state)
    state_low, row_parts = tied(state_low, row_parts)
    far = jnp.stack(row_parts[1:])
    state_low, far = tied(state_low, far)
    row_near, far = tied(row_near, far)
    far_parts, near_parts = exchanged(far, "ctx"), lax.all_gather(row_near, "shard", axis=0)
    post_high, saved_high, _ = forward(middle, steps, tuple(state_low))
    post_high, far_parts, near_parts = tied(post_high, far_parts, near_parts)
    post_chain = jnp.concatenate([post_low, post_high])

    def to_rows(value):
        return lax.all_to_all(value.reshape(ring, span, -1), "ctx", 0, 0)

    post = to_rows(post_chain)

    number = jnp.stack([lax.axis_index("shard"), place]).astype(jnp.int32)
    w_own = run_assemble(number, row_pack, far_parts, near_parts).reshape(width, -1)
    w_other = swap(w_own)
    spots = jnp.stack([core, place * span, slot_length[0]]).astype(jnp.int32)
    cot = lax.dynamic_index_in_dim(cotangent, core, 0, keepdims=False)
    output, grad_hidden, grad_post, normed_two, grad_hidden_low, back_low, grad_gain_two, *kept = run_rows(
        spots, post, w_own, w_other, row_tokens, cot, gain_two, half_out
    )
    row_in = row_tokens.astype(F32)
    joined, acts = kept[:2], (kept[2:5], kept[5:])

    def folded(values):
        return sum(value.astype(F32) for value in values).astype(BF)

    me = lax.axis_index("shard")

    def operands(half, second):
        if second:
            return (back_low, grad_hidden_low), (acts[half][2], joined[half])
        return (normed_two, normed_two), (acts[half][0], acts[half][1])

    def other_sums(second):
        return swap(run_sums(*operands(1, second)))

    def taken(second, other):
        if part % 16 == 0:
            if second:
                here = jnp.zeros((1,), jnp.int32)
                return run_sums(*operands(0, second), other, here, shards * ring)[0]
            here = jnp.stack([place]).astype(jnp.int32)
            return list(run_sums(*operands(0, second), other, here, shards, ring))
        own = run_sums(*operands(0, second)).astype(F32)
        both = (own + other.astype(F32)).astype(BF).reshape(shards, ring, part, -1)
        if second:
            return both
        return [lax.dynamic_index_in_dim(both, place ^ bit, 1, keepdims=False) for bit in range(ring)]

    grad_post = lax.all_to_all(grad_post, "ctx", 0, 0)
    grad_post = grad_post.reshape(span_all, cols)

    def backward(first, last, base, begin, saved):
        done = run_bwd(
            first, last, base, slot_tokens, gain_row, w_chain, rate_rows, norm_gain, grad_post, begin, saved
        )
        return done[0], tuple(done[1:])

    sums = ((width, wide), (padded, width), (1, width), (chains, 1, head_dim), (chains, 1, head_dim))
    begin = tuple(jnp.zeros(extent, F32) for extent in sums + tuple(value.shape for value in state))
    other_a, other_b = other_sums(False), other_sums(True)
    (grad_post, sum_rights) = tied(grad_post, (other_a, other_b))
    taken_a, taken_b = taken(False, sum_rights[0]), taken(True, sum_rights[1])
    grad_post, taken_a, taken_b = tied(grad_post, taken_a, taken_b)
    taken_b = taken_b.reshape(shards, ring, part, -1)
    sum_a, sum_b = sent(taken_a, "ctx"), lax.all_to_all(taken_b, "shard", 0, 0)
    back_high, ending = backward(middle, steps, middle, begin, saved_high)
    ending, sum_a, sum_b = tied(ending, sum_a, sum_b)
    sum_a, sum_b = folded(sum_a), folded(sum_b)
    ending, sum_a, sum_b = tied(ending, sum_a, sum_b)
    sum_a, sum_b = scattered(sum_a, "shard"), scattered(sum_b, "ctx")
    back_low_half, ending = backward(0, middle, 0, ending, saved_low)
    ending, back_low_half, sum_a, sum_b = tied(ending, back_low_half, sum_a, sum_b)
    back_part = jnp.concatenate([back_low_half, back_high])
    grad_big, grad_lr, grad_gain_one, grad_norm_gain, grad_norm_bias, *grad_state = ending
    block = ((shards, half_rows, wide), BF)
    keep, send = in_vmem(
        pack_grads_kernel, "pack_grads", [block, block], [(SMALL, wide)], [core],
        grad_big, grad_lr, grad_gain_one, grad_gain_two, *grad_state, grad_norm_gain, grad_norm_bias,
    )
    dealt = in_vmem(
        add_and_deal_kernel, "add_and_deal", [((half_rows, wide), BF)] * shards, [],
        [lax.axis_index("shard")], keep, swap(send),
    )
    back_rows = to_rows(back_part)
    chain_sum = sent(list(dealt), "shard")
    chain_sum, back_rows, sum_a, sum_b = tied(chain_sum, back_rows, sum_a, sum_b)
    chain_sum = spread(folded(chain_sum), "ctx")
    g_qkv, g_gate, g_lr, g_n1, g_n2, *g_rest = in_vmem(
        partial(unpack_grads_kernel, chains=chains), "unpack_grads",
        [
            ((depth, 3, local_heads * head_dim), F32), ((depth, local_heads * head_dim), F32),
            ((local_heads, depth), F32), ((1, depth), F32), ((1, depth), F32),
            (inner_w1.shape, F32), (inner_b1.shape, F32), (inner_w2.shape, F32), (inner_b2.shape, F32),
            (post_gain.shape, F32), (post_bias.shape, F32),
        ],
        [], [core], chain_sum, swap(chain_sum),
    )

    row_sum = spread(jnp.concatenate([folded(sum_a), folded(sum_b)], axis=-1), "ctx")
    row_sum = row_sum.reshape(depth, -1).astype(F32)
    g_ffn_gate = row_sum[:, :units]
    g_ffn_up = row_sum[:, units : 2 * units]
    g_ffn_down = row_sum[:, 2 * units : 3 * units].T
    g_out = row_sum[:, 3 * units :].T

    back_one = jnp.sum(back_rows.astype(F32), axis=0)
    scale_one = row_scale(row_in)
    lifted = back_one * gain_row
    input_grad = (
        grad_hidden
        + scale_one * lifted
        - row_in * scale_one**3 * jnp.mean(lifted * row_in, axis=-1, keepdims=True)
    ).astype(BF)


    return (
        in_turn(output, swap(output)),
        in_turn(input_grad, swap(input_grad)),
        g_n1[0],
        g_qkv,
        g_lr.T,
        *g_rest,
        g_gate,
        g_out,
        g_n2[0],
        g_ffn_gate,
        g_ffn_up,
        g_ffn_down,
    )


def solution(mesh):
    in_specs = (
        P("shard", "ctx", None),
        P("shard"),
        P("shard"),
        P("shard", None, "tp"),
        P("shard", "tp"),
        P("tp", None, "shard"),
        P("tp", "shard"),
        P("tp", None, "shard"),
        P("tp", "shard"),
        P("tp", "shard"),
        P("tp", "shard"),
        P("shard", "tp"),
        P("tp", "shard"),
        P("shard"),
        P("shard", "tp"),
        P("shard", "tp"),
        P("tp", "shard"),
        P("shard", "ctx", None),
    )
    out_specs = (
        P("shard", "ctx", None),
        P("shard", "ctx", None),
        P("shard"),
        P("shard", None, "tp"),
        P("shard", "tp"),
        P("tp", None, "shard"),
        P("tp", "shard"),
        P("tp", None, "shard"),
        P("tp", "shard"),
        P("tp", "shard"),
        P("tp", "shard"),
        P("shard", "tp"),
        P("tp", "shard"),
        P("shard"),
        P("shard", "tp"),
        P("shard", "tp"),
        P("tp", "shard"),
    )
    return jax.shard_map(
        on_device, mesh=mesh, in_specs=in_specs, out_specs=out_specs, check_vma=False
    )
```

```python
from functools import partial
import jax
import jax.numpy as jnp
from jax import lax
from jax.experimental import pallas as pl
from jax.experimental.pallas import tpu as pltpu
from jax.sharding import PartitionSpec as P

MINI = 16
EPSILON = 1e-06
ETA_BASE = 0.5
BF = jnp.bfloat16
F32 = jnp.float32


def mm(left, right):
    return lax.dot_general(left, right, (((1,), (0,)), ((), ())), preferred_element_type=F32)


def mm_nt(left, right):
    return lax.dot_general(left, right, (((1,), (1,)), ((), ())), preferred_element_type=F32)


def mm_tn(left, right):
    return lax.dot_general(left, right, (((0,), (0,)), ((), ())), preferred_element_type=F32)


def gelu_parts(value):
    cdf = 0.5 + 0.5 * lax.erf(value * 0.7071067811865476)
    pdf = jnp.exp(-0.5 * value * value) * 0.3989422804014327
    return cdf, pdf


def row_scale(value):
    return lax.rsqrt(jnp.mean(value * value, axis=-1, keepdims=True) + EPSILON)


def mini_masks(rows):
    row = lax.broadcasted_iota(jnp.int32, (rows, rows), 0)
    col = lax.broadcasted_iota(jnp.int32, (rows, rows), 1)
    within = (lax.div(row, MINI) == lax.div(col, MINI)) & (col <= row)
    scale = jnp.where(within, 1.0 / (lax.rem(row, MINI) + 1).astype(F32), 0.0)
    return scale, jnp.where(row == col, 1.0 / MINI, 0.0)


def minis(value):
    return [value[at : at + MINI] for at in range(0, value.shape[0], MINI)]


def flat_rows(value):
    return value.reshape(value.shape[0] * value.shape[1], value.shape[2])


class Rows:
    def __init__(self, ref, start, size):
        self.ref, self.start, self.size = ref, start, size

    def spot(self, key):
        key = key if isinstance(key, tuple) else (key, slice(None))
        first, last = 0, self.size
        if len(key) == 3:
            first, last, _ = key[2].indices(self.size)
        return key[0], key[1], slice(self.start + first, self.start + last)

    def __getitem__(self, key):
        return self.ref[self.spot(key)]

    def __setitem__(self, key, value):
        self.ref[self.spot(key)] = value


class Plane:
    def __init__(self, ref, number, lane=None):
        self.ref, self.number = ref, number
        self.lanes = slice(None) if lane is None else slice(lane, lane + 1)

    def __getitem__(self, key):
        if isinstance(key, tuple):
            return self.ref[key[0], self.number, key[1] * MINI : (key[1] + 1) * MINI, self.lanes]
        return self.ref[key, self.number, :, self.lanes]

    def __setitem__(self, key, value):
        self.ref[key, self.number, :, self.lanes] = value


def named_parts(narrow_ref, plane_ref, state_ref, low_ref, high_ref):
    head_dim = narrow_ref.shape[3]
    return (
        Rows(narrow_ref, 0, 2 * MINI), Rows(narrow_ref, 2 * MINI, MINI),
        *(Plane(plane_ref, number) for number in range(3)), Plane(plane_ref, 3, 0), Plane(plane_ref, 3, 1),
        Rows(state_ref, 0, head_dim), Rows(state_ref, head_dim, head_dim),
        *(Rows(low_ref, at, MINI) for at in (0, MINI, 2 * MINI)),
        *(Rows(high_ref, at, MINI) for at in (0, MINI, 2 * MINI)),
    )


def fwd_kernel(
    length_ref, x_ref, gain_ref, wc_ref, lrt_ref, w1i_ref, c1i_ref, w2i_ref, c2i_ref, pg_ref, pb_ref,
    post_ref, fac_ref, narrow_ref, plane_ref, state_ref, low_ref, high_ref,
    w1_ref, c1_ref, w2_ref, c2_ref, kmv_ref, next_ref, kk_ref, pq_ref, c2s_ref, *, first,
):
    kq_ref, g2_ref, gl_ref, gs_ref, unit_ref, rate_ref, hscale_ref, w1s_ref, w2s_ref, h_ref, r_ref, g1_ref, *rest = (
        named_parts(narrow_ref, plane_ref, state_ref, low_ref, high_ref)
    )
    ga_ref, ug_ref, gp_ref = rest
    chains, group, _, head_dim = narrow_ref.shape
    rows = group * MINI
    cols = chains * head_dim
    every = range(chains)

    @pl.when(pl.program_id(0) == 0)
    def _():
        w1_ref[...] = w1i_ref[...]
        c1_ref[...] = c1i_ref[...]
        w2_ref[...] = w2i_ref[...]
        c2_ref[...] = c2i_ref[...]

    start = (first + pl.program_id(0)) * rows
    padded = lrt_ref.shape[0]
    x = x_ref[...].astype(F32)
    normed = (x * row_scale(x) * gain_ref[...]).astype(BF)
    proj = mm(normed, wc_ref[...])
    length = length_ref[0]
    live_col = start + lax.broadcasted_iota(jnp.int32, (rows, padded), 0) < length
    live_row = start + lax.broadcasted_iota(jnp.int32, (padded, rows), 1) < length
    eta_col = jnp.where(live_col, jax.nn.sigmoid(mm_nt(normed, lrt_ref[...])), 0.0) * (ETA_BASE / head_dim)
    rate = jax.nn.sigmoid(mm_nt(lrt_ref[...], normed))
    eta_row = jnp.where(live_row, rate, 0.0) * (ETA_BASE / head_dim)
    fac_ref[0, :padded] = eta_row * (1.0 - rate)
    fac_ref[0, padded:] = eta_row
    for i in every:
        at = i * head_dim
        k = proj[:, cols + at : cols + at + head_dim]
        v = proj[:, 2 * cols + at : 2 * cols + at + head_dim]
        kb, qb = k.astype(BF), proj[:, at : at + head_dim].astype(BF)
        k_minis = kb.reshape(group, MINI, head_dim)
        q_minis = qb.reshape(group, MINI, head_dim)
        kq_ref[i, :, :MINI] = k_minis
        kq_ref[i, :, MINI:] = q_minis
        next_ref[i, : group - 1, :MINI] = k_minis[1:]
        next_ref[i, group - 1 :, :MINI] = k_minis[:1]
        next_ref[i, :, MINI:] = q_minis
        kmv_ref[i] = (k - v).reshape(group, MINI, head_dim)
        rate_ref[i] = eta_col[:, i : i + 1] * (1.0 / MINI)
        cross = (mm_nt(kb, kb) + 1.0) * (eta_row[i : i + 1] * (1.0 / MINI))
        for j in range(group - 1):
            at = j * MINI
            kk_ref[i, j] = cross[at + MINI : at + 2 * MINI, at : at + MINI].astype(BF)

    key_pre = [mm(kq_ref[i, 0, :MINI], w1_ref[i].astype(BF)) + c1_ref[i] for i in every]
    for j in range(group):
        rate = [rate_ref[i, j] for i in every]
        kmv = [kmv_ref[i, j] for i in every]
        stacked = [next_ref[i, j] for i in every]
        k = [kq_ref[i, j, :MINI] for i in every]
        kk = [kk_ref[i, j] for i in every] if j < group - 1 else None
        w1 = [w1_ref[i] for i in every]
        w2 = [w2_ref[i] for i in every]
        c1 = [c1_ref[i] for i in every]
        c2 = [c2_ref[i] for i in every]
        w1b = [w1[i].astype(BF) for i in every]
        w2b = [w2[i].astype(BF) for i in every]
        parts = [gelu_parts(key_pre[i]) for i in every]
        hb = [(key_pre[i] * parts[i][0]).astype(BF) for i in every]
        g2 = [mm_nt(hb[i], w2b[i]) + c2[i] + kmv[i] for i in every]
        slope = [parts[i][0] + key_pre[i] * parts[i][1] for i in every]
        curve = [parts[i][1] * (2.0 - key_pre[i] * key_pre[i]) for i in every]
        both = [mm(stacked[i], w1b[i]) + c1[i] for i in every]
        g2b = [g2[i].astype(BF) for i in every]
        u = [mm(g2b[i], w2b[i]) for i in every]
        fg2 = [rate[i] * g2[i] for i in every]
        w2n = [w2[i] - mm_tn(fg2[i].astype(BF), hb[i]) for i in every]
        c2n = [c2[i] - jnp.sum(fg2[i], axis=0, keepdims=True) for i in every]
        g1 = [u[i] * slope[i] for i in every]
        g1b = [g1[i].astype(BF) for i in every]
        if j < group - 1:
            key_pre = [both[i][:MINI] - mm(kk[i], g1b[i]) for i in every]
        fg1 = [rate[i] * g1[i] for i in every]
        w1n = [w1[i] - mm_tn(k[i], fg1[i].astype(BF)) for i in every]
        c1n = [c1[i] - jnp.sum(fg1[i], axis=0, keepdims=True) for i in every]
        for i in every:
            w1s_ref[i, j] = w1b[i]
            w2s_ref[i, j] = w2b[i]
            c2s_ref[i, j] = c2[i]
            h_ref[i, j] = hb[i]
            g1_ref[i, j] = g1b[i]
            g2_ref[i, j] = g2b[i]
            ga_ref[i, j] = slope[i]
            ug_ref[i, j] = u[i] * curve[i]
            pq_ref[i, j] = both[i][MINI:]
            w1_ref[i] = w1n[i]
            w2_ref[i] = w2n[i]
            c1_ref[i] = c1n[i]
            c2_ref[i] = c2n[i]

    scale = mini_masks(rows)[0]
    for i in every:
        at = i * head_dim
        q = proj[:, at : at + head_dim]
        gate = proj[:, 3 * cols + at : 3 * cols + at + head_dim]
        kb, qb = flat_rows(kq_ref[i, :, :MINI]), flat_rows(kq_ref[i, :, MINI:])
        hb, g1b, g2b = flat_rows(h_ref[i]), flat_rows(g1_ref[i]), flat_rows(g2_ref[i])
        mix = scale * eta_row[i : i + 1]
        query_pre = flat_rows(pq_ref[i]) - mm((mix * (mm_nt(qb, kb) + 1.0)).astype(BF), g1b)
        cdf, pdf = gelu_parts(query_pre)
        gp_ref[i] = (cdf + query_pre * pdf).reshape(group, MINI, -1)
        rb = (query_pre * cdf).astype(BF)
        r_ref[i] = rb.reshape(group, MINI, -1)
        s2 = (mix * (mm_nt(rb, hb) + 1.0)).astype(BF)
        through = [mm_nt(piece, w2s_ref[i, j]) + c2s_ref[i, j] for j, piece in enumerate(minis(rb))]
        mixed = q + jnp.concatenate(through, axis=0) - mm(s2, g2b)
        centered = mixed - jnp.mean(mixed, axis=-1, keepdims=True)
        hscale = row_scale(centered)
        unit = centered * hscale
        out = unit * pg_ref[i] + pb_ref[i]
        cdf, pdf = gelu_parts(gate)
        post_ref[:, at : at + head_dim] = (gate * cdf * out).astype(BF)
        gl_ref[i] = gate * cdf
        gs_ref[i] = (cdf + gate * pdf) * out
        unit_ref[i] = unit
        hscale_ref[i] = hscale


def bwd_kernel(
    x_ref, gain_ref, wc_ref, lrt_ref, pg_ref, gpost_ref,
    fac_ref, narrow_ref, plane_ref, state_ref, low_ref, high_ref, *refs, begun,
):
    before, refs = (refs[:9], refs[9:]) if begun else ((), refs)
    (back_ref, gw_ref, glr_ref, gain_grad_ref, gpg_ref, gpb_ref, dw1_ref, dc1_ref, dw2_ref, dc2_ref, d_ref, g1a_ref, g2a_ref, ha_ref, ka_ref, dp_ref, kc_ref, dk_ref, da_ref, df_ref, de_ref, all_ref) = refs
    kq_ref, g2_ref, gl_ref, gs_ref, unit_ref, rate_ref, hscale_ref, w1s_ref, w2s_ref, h_ref, r_ref, g1_ref, *rest = (
        named_parts(narrow_ref, plane_ref, state_ref, low_ref, high_ref)
    )
    ga_ref, ug_ref, gp_ref = rest
    chains, group, _, head_dim = narrow_ref.shape
    rows = group * MINI
    cols = chains * head_dim
    every = range(chains)

    @pl.when(pl.program_id(0) == 0)
    def _():
        totals = (gw_ref, glr_ref, gain_grad_ref, gpg_ref, gpb_ref, dw1_ref, dc1_ref, dw2_ref, dc2_ref)
        for number, total in enumerate(totals):
            total[...] = before[number][...] if begun else jnp.zeros_like(total)

    scale, eye = mini_masks(rows)
    padded = lrt_ref.shape[0]
    gpost = gpost_ref[...].astype(F32)
    for i in every:
        at = i * head_dim
        piece = gpost[:, at : at + head_dim]
        all_ref[:, 3 * cols + at : 3 * cols + at + head_dim] = (piece * gs_ref[i]).astype(BF)
        head = piece * gl_ref[i]
        unit = unit_ref[i]
        gpg_ref[i] += jnp.sum(head * unit, axis=0, keepdims=True)
        gpb_ref[i] += jnp.sum(head, axis=0, keepdims=True)
        lifted = head * pg_ref[i]
        d = hscale_ref[i] * (
            lifted
            - jnp.mean(lifted, axis=-1, keepdims=True)
            - unit * jnp.mean(lifted * unit, axis=-1, keepdims=True)
        )
        d_ref[i] = d.reshape(group, MINI, head_dim)
        db = d.astype(BF)
        kb, qb = flat_rows(kq_ref[i, :, :MINI]), flat_rows(kq_ref[i, :, MINI:])
        hb, rb, g1b, g2b = (flat_rows(ref[i]) for ref in (h_ref, r_ref, g1_ref, g2_ref))
        mix = scale * fac_ref[0, padded + i : padded + i + 1]
        ds2 = -mm_nt(db, g2b)
        x2 = mm_nt(rb, hb) + 1.0
        x1 = mm_nt(qb, kb) + 1.0
        dx2 = (ds2 * mix).astype(BF)
        dr = jnp.concatenate([mm(part, w2s_ref[i, j]) for j, part in enumerate(minis(db))], axis=0)
        dp = (dr + mm(dx2, hb)) * flat_rows(gp_ref[i])
        dpb = dp.astype(BF)
        ds1 = -mm_nt(dpb, g1b)
        dx1 = (ds1 * mix).astype(BF)
        dq = jnp.concatenate([mm_nt(part, w1s_ref[i, j]) for j, part in enumerate(minis(dpb))], axis=0)
        all_ref[:, at : at + head_dim] = (d + dq + mm(dx1, kb)).astype(BF)
        g1a_ref[i] = -mm_tn((mix * x1).astype(BF), dpb).reshape(group, MINI, -1)
        g2a_ref[i] = -mm_tn((mix * x2).astype(BF), db).reshape(group, MINI, -1)
        ha_ref[i] = mm_tn(dx2, rb).reshape(group, MINI, -1)
        ka_ref[i] = mm_tn(dx1, qb).reshape(group, MINI, -1)
        dp_ref[i] = dpb.reshape(group, MINI, -1)
        de_ref[i] = jnp.sum((ds2 * x2 + ds1 * x1) * scale, axis=0, keepdims=True)
        kk = mm_nt(kb, kb) + 1.0
        kx = mm_nt(kb, qb) + 1.0
        for j in range(group - 1):
            own, after = slice(j * MINI, (j + 1) * MINI), slice((j + 1) * MINI, (j + 2) * MINI)
            kc_ref[i, j] = jnp.concatenate([kk[own, after], kx[own, after]], axis=1).astype(BF)

    t1 = [mm(kq_ref[i, group - 1, :MINI], dw1_ref[i].astype(BF)) + dc1_ref[i] for i in every]
    for j in reversed(range(group)):

        def all_of(ref):
            return [ref[i, j] for i in every]

        d, kq, rate, w2b, hb, rb, g1b, g2b = (
            all_of(ref) for ref in (d_ref, kq_ref, rate_ref, w2s_ref, h_ref, r_ref, g1_ref, g2_ref)
        )
        ga, ug, dpb, g1a, g2a, ha = (
            all_of(ref) for ref in (ga_ref, ug_ref, dp_ref, g1a_ref, g2a_ref, ha_ref)
        )
        dw1 = [dw1_ref[i] for i in every]
        dw2 = [dw2_ref[i] for i in every]
        dc1 = [dc1_ref[i] for i in every]
        dc2 = [dc2_ref[i] for i in every]
        g1 = [g1b[i].astype(F32) for i in every]
        g2 = [g2b[i].astype(F32) for i in every]
        dw1b = [dw1[i].astype(BF) for i in every]
        dw2b = [dw2[i].astype(BF) for i in every]
        dg1 = [g1a[i] - rate[i] * t1[i] for i in every]
        dub = [(dg1[i] * ga[i]).astype(BF) for i in every]
        through = [mm_nt(dub[i], w2b[i]) for i in every]
        t2 = [mm_nt(hb[i], dw2b[i]) + dc2[i] for i in every]
        dha = [ha[i] - mm((rate[i] * g2[i]).astype(BF), dw2b[i]) for i in every]
        dg2 = [through[i] + (g2a[i] - rate[i] * t2[i]) for i in every]
        dg2b = [dg2[i].astype(BF) for i in every]
        dh = [mm(dg2b[i], w2b[i]) + dha[i] for i in every]
        if j > 0:
            base = [mm(kq_ref[i, j - 1, :MINI], dw1b[i]) + dc1[i] for i in every]
        dk = [dg2[i] - mm_nt((rate[i] * g1[i]).astype(BF), dw1b[i]) for i in every]
        df = [
            -(
                jnp.sum(g1[i] * t1[i], axis=1, keepdims=True)
                + jnp.sum(g2[i] * t2[i], axis=1, keepdims=True)
            )
            for i in every
        ]
        da = [dg1[i] * ug[i] + dh[i] * ga[i] for i in every]
        dab = [da[i].astype(BF) for i in every]
        both = [jnp.concatenate([dab[i], dpb[i]], axis=0) for i in every]
        if j > 0:
            t1 = [base[i] + mm(kc_ref[i, j - 1], both[i]) for i in every]
        dw1n = [dw1[i] + mm_tn(kq[i], both[i]) for i in every]
        dc1n = [dc1[i] + jnp.sum(da[i] + dpb[i].astype(F32), axis=0, keepdims=True) for i in every]
        dw2n = [
            dw2[i]
            + mm_tn(
                jnp.concatenate([d[i].astype(BF), dg2b[i], g2b[i]], axis=0),
                jnp.concatenate([rb[i], hb[i], dub[i]], axis=0),
            )
            for i in every
        ]
        dc2n = [dc2[i] + jnp.sum(d[i] + dg2[i], axis=0, keepdims=True) for i in every]
        for i in every:
            piece, at = slice(j * MINI, (j + 1) * MINI), 2 * cols + i * head_dim
            all_ref[piece, at : at + head_dim] = (-dg2[i]).astype(BF)
            dk_ref[i, j] = dk[i]
            da_ref[i, j] = dab[i]
            df_ref[i, j] = df[i]
            dw1_ref[i] = dw1n[i]
            dc1_ref[i] = dc1n[i]
            dw2_ref[i] = dw2n[i]
            dc2_ref[i] = dc2n[i]

    x = x_ref[...].astype(F32)
    unit_in = x * row_scale(x)
    normed = (unit_in * gain_ref[...]).astype(BF)
    lrt = lrt_ref[...]
    which = lax.broadcasted_iota(jnp.int32, (padded, rows), 0)
    rates = jnp.zeros((padded, rows), F32)
    for i in every:
        at = cols + i * head_dim
        dk = jnp.concatenate([mm_nt(da_ref[i, j], w1s_ref[i, j]) for j in range(group)], axis=0)
        all_ref[:, at : at + head_dim] = (flat_rows(dk_ref[i]) + flat_rows(ka_ref[i]) + dk).astype(BF)
        line = de_ref[i] + jnp.sum(eye * flat_rows(df_ref[i]), axis=0, keepdims=True)
        rates = jnp.where(which == i, line, rates)
    rates = (rates * fac_ref[0, :padded]).astype(BF)
    grads = all_ref[...]
    back = mm_nt(grads, wc_ref[...]) + mm_tn(rates, lrt)
    gain_grad_ref[...] += jnp.sum(back * unit_in, axis=0, keepdims=True)
    back_ref[...] = back.astype(BF)
    gw_ref[...] += mm_tn(normed, grads)
    glr_ref[...] += mm(rates, normed)


GROUP = 8


def block_specs(chains, head_dim, inner, padded, place):
    rows = GROUP * MINI

    def mini(first, second):
        return pl.BlockSpec((chains, GROUP, first, second), lambda g: (0, place(g), 0, 0))

    return [
        pl.BlockSpec((1, 2 * padded, rows), lambda g: (place(g), 0, 0)),
        mini(3 * MINI, head_dim),
        pl.BlockSpec((chains, 4, rows, head_dim), lambda g: (0, 0, place(g), 0)),
        mini(2 * head_dim, inner), mini(3 * MINI, inner), mini(3 * MINI, inner),
    ]


def whole_spec(value):
    return pl.BlockSpec(value.shape, lambda g: (0,) * value.ndim)


def run_fwd(first, last, length, tokens, gain, wc, lrt, pg, pb, state):
    width = tokens.shape[1]
    chains, head_dim, inner = state[0].shape
    rows = GROUP * MINI
    steps = last - first
    count = steps * GROUP
    padded = lrt.shape[0]

    def mini(first_size, second_size, dtype):
        return jax.ShapeDtypeStruct((chains, count, first_size, second_size), dtype)

    row_spec = pl.BlockSpec((rows, width), lambda g: (first + g, 0))
    small = (gain, wc, lrt, *state, pg, pb)
    return pl.pallas_call(
        partial(fwd_kernel, first=first),
        grid=(steps,),
        in_specs=[pl.BlockSpec(memory_space=pltpu.SMEM), row_spec] + [whole_spec(v) for v in small],
        out_specs=[pl.BlockSpec((rows, chains * head_dim), lambda g: (g, 0))]
        + block_specs(chains, head_dim, inner, padded, lambda g: g)
        + [whole_spec(v) for v in state],
        out_shape=[
            jax.ShapeDtypeStruct((steps * rows, chains * head_dim), BF),
            jax.ShapeDtypeStruct((steps, 2 * padded, rows), F32),
            mini(3 * MINI, head_dim, BF),
            jax.ShapeDtypeStruct((chains, 4, steps * rows, head_dim), F32),
            mini(2 * head_dim, inner, BF), mini(3 * MINI, inner, BF), mini(3 * MINI, inner, F32),
        ]
        + [jax.ShapeDtypeStruct(v.shape, F32) for v in state],
        scratch_shapes=[
            pltpu.VMEM((chains, GROUP, MINI, head_dim), F32),
            pltpu.VMEM((chains, GROUP, 2 * MINI, head_dim), BF),
            pltpu.VMEM((chains, GROUP, MINI, MINI), BF),
            pltpu.VMEM((chains, GROUP, MINI, inner), F32),
            pltpu.VMEM((chains, GROUP, 1, head_dim), F32),
        ],
        compiler_params=pltpu.CompilerParams(vmem_limit_bytes=50 << 20),
        cost_estimate=pl.CostEstimate(
            flops=9_000_000_000 * steps, bytes_accessed=5_000_000 * steps, transcendentals=0
        ),
        name="chain_forward",
    )(length, tokens, *small)


def run_bwd(first, last, base, tokens, gain, wc, lrt, pg, gpost, shapes, state, saved):
    width = tokens.shape[1]
    chains, head_dim, inner = shapes[5]
    rows = GROUP * MINI
    padded = lrt.shape[0]
    wide = wc.shape[1]
    steps = last - first

    def place(g):
        return steps - 1 - g

    def shape(*extent):
        return jax.ShapeDtypeStruct(extent, F32)

    small = (gain, wc, lrt, pg)
    outs = [shape(*extent) for extent in shapes]

    def scratch(first_size, second_size, dtype):
        return pltpu.VMEM((chains, GROUP, first_size, second_size), dtype)

    return pl.pallas_call(
        partial(bwd_kernel, begun=len(state) > 0),
        grid=(steps,),
        in_specs=[pl.BlockSpec((rows, width), lambda g: (first + place(g), 0))]
        + [whole_spec(v) for v in small]
        + [pl.BlockSpec((rows, chains * head_dim), lambda g: (first + place(g), 0))]
        + block_specs(chains, head_dim, inner, padded, lambda g: first - base + place(g))
        + [whole_spec(v) for v in state],
        out_specs=[pl.BlockSpec((rows, width), lambda g: (place(g), 0))] + [whole_spec(v) for v in outs],
        out_shape=[jax.ShapeDtypeStruct((steps * rows, width), BF)] + outs,
        scratch_shapes=[
            scratch(MINI, head_dim, F32), scratch(MINI, inner, F32), scratch(MINI, head_dim, F32),
            scratch(MINI, inner, F32), scratch(MINI, head_dim, F32), scratch(MINI, inner, BF),
            scratch(MINI, 2 * MINI, BF), scratch(MINI, head_dim, F32), scratch(MINI, inner, BF),
            scratch(MINI, 1, F32), pltpu.VMEM((chains, 1, rows), F32), pltpu.VMEM((rows, wide), BF),
        ],
        compiler_params=pltpu.CompilerParams(vmem_limit_bytes=50 << 20),
        cost_estimate=pl.CostEstimate(
            flops=11_000_000_000 * steps, bytes_accessed=5_000_000 * steps, transcendentals=0
        ),
        name="chain_backward",
    )(tokens, *small, gpost, *saved, *state)


def swap(value):
    return lax.ppermute(value, "tp", [(0, 1), (1, 0)])


def rows_kernel(
    spot_ref, post_ref, own_ref, other_ref, x_ref, cot_ref, gain_ref,
    out_ref, grad_ref, normed_ref, low_ref, back_ref, gain_grad_ref, cat0_ref, cat1_ref, *act_refs,
):
    *act_refs, gpost_ref = act_refs
    core, start, length = spot_ref[0], spot_ref[1], spot_ref[2]
    span, width = x_ref.shape
    cols = post_ref.shape[2]
    units = act_refs[0].shape[1]
    places = cat0_ref.shape[1] // cols
    x = x_ref[...].astype(F32)
    live = start + lax.broadcasted_iota(jnp.int32, (span, width), 0) < length
    back = jnp.where(live, cot_ref[...].astype(F32), 0.0)
    back_low = back.astype(BF)
    back_ref[...] = back_low
    halves = ((own_ref, core), (other_ref, 1 - core))
    hidden = x
    for half, (w_ref, side) in enumerate(halves):
        joined = jnp.concatenate([post_ref[side * places + p] for p in range(places)], axis=1)
        (cat0_ref, cat1_ref)[half][...] = joined
        hidden = hidden + mm_nt(joined, w_ref[:, 3 * units :])
    scale = row_scale(hidden)
    gain = gain_ref[...]
    normed = (hidden * scale * gain).astype(BF)
    normed_ref[...] = normed
    feed = jnp.zeros((span, width), F32)
    grad = jnp.zeros((span, width), F32)
    step = min(units, 512)
    for half, (w_ref, _) in enumerate(halves):
        for at in range(0, units, step):
            w_gate = w_ref[:, at : at + step]
            w_up = w_ref[:, units + at : units + at + step]
            w_down = w_ref[:, 2 * units + at : 2 * units + at + step]
            up_gate = mm(normed, w_gate)
            up_lin = mm(normed, w_up)
            grad_act = mm(back_low, w_down)
            gate = jax.nn.sigmoid(up_gate)
            silu = up_gate * gate
            act = (silu * up_lin).astype(BF)
            grad_gate = (grad_act * up_lin * (gate * (1.0 + up_gate * (1.0 - gate)))).astype(BF)
            grad_lin = (grad_act * silu).astype(BF)
            act_refs[3 * half + 0][:, at : at + step] = grad_gate
            act_refs[3 * half + 1][:, at : at + step] = grad_lin
            act_refs[3 * half + 2][:, at : at + step] = act
            feed += mm_nt(act, w_down)
            grad += mm_nt(grad_gate, w_gate) + mm_nt(grad_lin, w_up)
    out_ref[...] = (hidden + feed).astype(BF)
    lifted = grad * gain
    hat = hidden * scale
    gain_grad_ref[...] = jnp.sum(grad * hat, axis=0, keepdims=True)
    total = back + scale * (lifted - hat * jnp.mean(lifted * hat, axis=-1, keepdims=True))
    grad_ref[...] = total
    low = total.astype(BF)
    low_ref[...] = low
    for p in range(2 * places, gpost_ref.shape[0]):
        gpost_ref[p] = jnp.zeros(gpost_ref.shape[1:], BF)
    deal_refs = act_refs[6:]
    for w_ref, side in halves:
        gpost = mm(low, w_ref[:, 3 * units :]).astype(BF)
        for p in range(places):
            gpost_ref[side * places + p] = gpost[:, p * cols : (p + 1) * cols]
    for bit, deal_ref in enumerate(deal_refs):
        deal_ref[...] = gpost_ref[spot_ref[3] ^ bit]


def run_rows(spots, post, own, other, x, cot, gain, half_out):
    ring, span, cols = post.shape
    width = x.shape[1]
    units = (own.shape[1] - half_out) // 3
    vmem = pl.BlockSpec(memory_space=pltpu.VMEM)

    def shape(extent, dtype):
        return jax.ShapeDtypeStruct(extent, dtype)

    return pl.pallas_call(
        rows_kernel,
        in_specs=[pl.BlockSpec(memory_space=pltpu.SMEM)] + [vmem] * 6,
        out_specs=[vmem] * (14 + ring),
        out_shape=[
            shape((span, width), BF), shape((span, width), F32),
            shape((span, width), BF), shape((span, width), BF), shape((span, width), BF), shape((1, width), F32),
        ]
        + [shape((span, half_out), BF)] * 2
        + [shape((span, units), BF)] * 6
        + [shape((span, cols), BF)] * ring,
        scratch_shapes=[pltpu.VMEM((ring, span, cols), BF)],
        compiler_params=pltpu.CompilerParams(vmem_limit_bytes=52 << 20),
        cost_estimate=pl.CostEstimate(flops=20_000_000_000, bytes_accessed=20_000_000, transcendentals=0),
        name="rows_main",
    )(spots, post, own, other, x, cot, gain)


def products(pairs, parts, store):
    start = 0
    for left, right in zip(pairs, parts):
        size = right.shape[-1]
        step = 512 if size % 512 == 0 else size
        for at in range(0, size, step):
            store(start + at, mm_tn(left[...], right[:, at : at + step]))
        start += size


def sums_other_kernel(*refs):
    *sources, out_ref = refs
    count = len(sources) // 2

    def store(at, value):
        out_ref[:, at : at + value.shape[1]] = value.astype(BF)

    products(sources[:count], sources[count:], store)


def sums_own_kernel(place_ref, other_ref, *refs, count, outs):
    sources, out_refs, held_ref = refs[: 2 * count], refs[2 * count : 2 * count + outs], refs[-1]

    def store(at, value):
        piece = slice(at, at + value.shape[1])
        held_ref[:, piece] = (value + other_ref[:, piece].astype(F32)).astype(BF)

    products(sources[:count], sources[count:], store)
    for bit, out_ref in enumerate(out_refs):
        blocks, part = out_ref.shape[:2]
        for number in range(blocks):
            at = pl.multiple_of((number * outs + (place_ref[0] ^ bit)) * part, part)
            out_ref[number] = held_ref[pl.ds(at, part), :]


def run_sums(lefts, rights, other=None, place=None, blocks=1, outs=1):
    width = lefts[0].shape[1]
    total = sum(right.shape[1] for right in rights)
    vmem = pl.BlockSpec(memory_space=pltpu.VMEM)
    count = len(lefts)
    params = pltpu.CompilerParams(vmem_limit_bytes=40 << 20)
    cost = pl.CostEstimate(flops=5_000_000_000, bytes_accessed=6_000_000, transcendentals=0)
    if other is None:
        return pl.pallas_call(
            sums_other_kernel,
            in_specs=[vmem] * (2 * count),
            out_specs=vmem,
            out_shape=jax.ShapeDtypeStruct((width, total), BF),
            compiler_params=params,
            cost_estimate=cost,
            name="sums_other",
        )(*lefts, *rights)
    part = width // (blocks * outs)
    return pl.pallas_call(
        partial(sums_own_kernel, count=count, outs=outs),
        in_specs=[pl.BlockSpec(memory_space=pltpu.SMEM)] + [vmem] * (2 * count + 1),
        out_specs=[vmem] * outs,
        out_shape=[jax.ShapeDtypeStruct((blocks, part, total), BF)] * outs,
        scratch_shapes=[pltpu.VMEM((width, total), BF)],
        compiler_params=params,
        cost_estimate=cost,
        name="sums_own",
    )(place, other, *lefts, *rights)


def assemble_kernel(spots_ref, pack_ref, *refs, ring):
    far_refs, near_ref, out_ref = refs[:ring], refs[ring], refs[-1]
    me, place = spots_ref[0], spots_ref[1]
    part = out_ref.shape[1]
    cut = far_refs[0].shape[2]
    for number in range(ring):
        piece = slice(number * part, (number + 1) * part)
        out_ref[me * ring + number, :, :cut] = pack_ref[piece, :cut]
        for z in range(near_ref.shape[0]):
            out_ref[z * ring + number, :, cut:] = near_ref[z, piece]
    for bit, far_ref in enumerate(far_refs):
        for other in range(far_ref.shape[0]):
            out_ref[(me ^ (other + 1)) * ring + (place ^ bit), :, :cut] = far_ref[other]


def run_assemble(spots, pack, far_parts, near_parts):
    vmem = pl.BlockSpec(memory_space=pltpu.VMEM)
    ring = len(far_parts)
    part = pack.shape[0] // ring
    return pl.pallas_call(
        partial(assemble_kernel, ring=ring),
        in_specs=[pl.BlockSpec(memory_space=pltpu.SMEM)] + [vmem] * (2 + ring),
        out_specs=vmem,
        out_shape=jax.ShapeDtypeStruct((near_parts.shape[0] * ring, part, pack.shape[1]), BF),
        compiler_params=pltpu.CompilerParams(vmem_limit_bytes=40 << 20),
        name="assemble_rows",
    )(spots, pack, *far_parts, near_parts)


SMALL = 64


def small_spots(chains, depth, inner_share):
    side = 2 * chains * inner_share
    return side, {
        "lr": 0, "n1": chains, "n2": chains + 1, "b1": chains + 2,
        "b2": 2 * chains + 2, "pg": 3 * chains + 2, "pb": 4 * chains + 2,
    }


def pack_weights_kernel(
    pick_ref, qkv_ref, gate_ref, lr_ref, n1_ref, n2_ref, w1_ref, b1_ref, w2_ref, b2_ref, pg_ref, pb_ref,
    out_ref, small_ref, *, chains,
):
    depth = gate_ref.shape[0]
    heads, head_dim, inner_share = w1_ref.shape
    cols = chains * head_dim
    all_cols = heads * head_dim
    side, spots = small_spots(chains, depth, inner_share)
    small_ref[...] = jnp.zeros_like(small_ref)

    def put(name, i, value):
        row = spots[name] + i
        small_ref[row : row + 1, side : side + value.shape[1]] = value.astype(F32)

    for option in range(heads // chains):

        @pl.when(pick_ref[0] == option)
        def _():
            at = option * cols
            for which in range(3):
                start = which * all_cols + at
                out_ref[:depth, which * cols : (which + 1) * cols] = qkv_ref[:, start : start + cols]
            out_ref[:depth, 3 * cols :] = gate_ref[:, at : at + cols]
            for i in range(chains):
                head = option * chains + i
                lanes = slice(i * inner_share, (i + 1) * inner_share)
                small_ref[:, lanes] = w1_ref[head].astype(F32)
                lanes = slice((chains + i) * inner_share, (chains + i + 1) * inner_share)
                small_ref[:, lanes] = w2_ref[head].astype(F32)
                for name, ref in (("lr", lr_ref), ("b1", b1_ref), ("b2", b2_ref), ("pg", pg_ref), ("pb", pb_ref)):
                    put(name, i, ref[head : head + 1, :])

    put("n1", 0, n1_ref[...])
    put("n2", 0, n2_ref[...])
    out_ref[depth:, :] = small_ref[...].astype(BF)


def halves_by_core(core, mine_ref, other_ref, work):
    @pl.when(core == 0)
    def _():
        work(mine_ref, other_ref)

    @pl.when(core != 0)
    def _():
        work(other_ref, mine_ref)


def unpack_weights_kernel(
    core_ref, mine_ref, other_ref,
    wc_ref, lrt_ref, n1_ref, n2_ref, w1_ref, b1_ref, w2_ref, b2_ref, pg_ref, pb_ref, lines_ref,
):
    shards, half, _ = mine_ref.shape
    chains, _, inner = w1_ref.shape
    inner_share = inner // shards
    depth = 2 * half - SMALL
    head_share = b2_ref.shape[2] // shards
    side, spots = small_spots(chains, depth, inner_share)
    lines_ref[...] = jnp.zeros_like(lines_ref)

    def work(low_ref, high_ref):
        for z in range(shards):
            wc_ref[z * depth : z * depth + half] = low_ref[z]
            wc_ref[z * depth + half : (z + 1) * depth] = high_ref[z, : depth - half]
            small = high_ref[z, depth - half :].astype(F32)

            def get(name, i, size):
                row = spots[name] + i
                return small[row : row + 1, side : side + size]

            here = slice(z * depth, (z + 1) * depth)
            n1_ref[:, here] = get("n1", 0, depth)
            n2_ref[:, here] = get("n2", 0, depth)
            for i in range(chains):
                lines_ref[i : i + 1, here] = get("lr", i, depth)
                lanes = slice(z * inner_share, (z + 1) * inner_share)
                w1_ref[i, :, lanes] = small[:, i * inner_share : (i + 1) * inner_share]
                w2_ref[i, :, lanes] = small[:, (chains + i) * inner_share : (chains + i + 1) * inner_share]
                b1_ref[i, :, lanes] = get("b1", i, inner_share)
                lanes = slice(z * head_share, (z + 1) * head_share)
                for name, ref in (("b2", b2_ref), ("pg", pg_ref), ("pb", pb_ref)):
                    ref[i, :, lanes] = get(name, i, head_share)

    halves_by_core(core_ref[0], mine_ref, other_ref, work)
    lrt_ref[...] = lines_ref[...].astype(BF)


def pack_grads_kernel(
    core_ref, gw_ref, glr_ref, n1_ref, n2_ref, w1_ref, b1_ref, w2_ref, b2_ref, pg_ref, pb_ref,
    keep_ref, send_ref, small_ref,
):
    shards, half, _ = keep_ref.shape
    chains, _, inner = w1_ref.shape
    inner_share = inner // shards
    depth = 2 * half - SMALL
    head_share = b2_ref.shape[2] // shards
    side, spots = small_spots(chains, depth, inner_share)

    def work(low_ref, high_ref):
        for z in range(shards):
            small_ref[...] = jnp.zeros_like(small_ref)

            def put(name, i, value):
                row = spots[name] + i
                small_ref[row : row + 1, side : side + value.shape[1]] = value

            here = slice(z * depth, (z + 1) * depth)
            low_ref[z] = gw_ref[z * depth : z * depth + half].astype(BF)
            high_ref[z, : depth - half] = gw_ref[z * depth + half : (z + 1) * depth].astype(BF)
            put("n1", 0, n1_ref[:, here])
            put("n2", 0, n2_ref[:, here])
            for i in range(chains):
                put("lr", i, glr_ref[i : i + 1, here])
                lanes = slice(z * inner_share, (z + 1) * inner_share)
                small_ref[:, i * inner_share : (i + 1) * inner_share] = w1_ref[i, :, lanes]
                small_ref[:, (chains + i) * inner_share : (chains + i + 1) * inner_share] = w2_ref[i, :, lanes]
                put("b1", i, b1_ref[i, :, lanes])
                lanes = slice(z * head_share, (z + 1) * head_share)
                for name, ref in (("b2", b2_ref), ("pg", pg_ref), ("pb", pb_ref)):
                    put(name, i, ref[i, :, lanes])
            high_ref[z, depth - half :] = small_ref[...].astype(BF)

    halves_by_core(core_ref[0], keep_ref, send_ref, work)


def unpack_grads_kernel(
    core_ref, mine_ref, other_ref,
    qkv_ref, gate_ref, lrt_ref, n1_ref, n2_ref, w1_ref, b1_ref, w2_ref, b2_ref, pg_ref, pb_ref, *, chains,
):
    ring, half, wide = mine_ref.shape
    cols = wide // 4
    heads, _, inner_share = w1_ref.shape
    depth = gate_ref.shape[0]
    head_share = b2_ref.shape[1]
    places = heads // chains
    side, spots = small_spots(chains, depth, inner_share)
    core = core_ref[0]

    def work(low_ref, high_ref):
        for p in range(places):
            place = core * places + p
            big = jnp.concatenate([low_ref[place], high_ref[place, : depth - half]], axis=0).astype(F32)
            small = high_ref[place, depth - half :].astype(F32)
            at = p * cols
            for which in range(3):
                qkv_ref[:, which, at : at + cols] = big[:, which * cols : (which + 1) * cols]
            gate_ref[:, at : at + cols] = big[:, 3 * cols :]
            for i in range(chains):
                head = p * chains + i
                w1_ref[head] = small[:, i * inner_share : (i + 1) * inner_share]
                w2_ref[head] = small[:, (chains + i) * inner_share : (chains + i + 1) * inner_share]
                for name, ref, size in (
                    ("lr", lrt_ref, depth), ("b1", b1_ref, inner_share), ("b2", b2_ref, head_share),
                    ("pg", pg_ref, head_share), ("pb", pb_ref, head_share),
                ):
                    row = spots[name] + i
                    ref[head : head + 1, :] = small[row : row + 1, side : side + size]
        for name, ref in (("n1", n1_ref), ("n2", n2_ref)):
            row = spots[name]
            total = jnp.zeros((1, depth), F32)
            for place in range(ring):
                lines = high_ref[place, depth - half :].astype(F32)
                total = total + lines[row : row + 1, side : side + depth]
            ref[...] = total

    halves_by_core(core, mine_ref, other_ref, work)


def fold_and_deal_kernel(place_ref, *refs, count):
    source_refs, out_refs = refs[:-count], refs[-count:]
    for bit, out_ref in enumerate(out_refs):
        which = place_ref[0] ^ bit
        if len(source_refs) > 1:
            values = [ref[which].astype(F32) for ref in source_refs]
        else:
            values = [source_refs[0][number, which].astype(F32) for number in range(source_refs[0].shape[0])]
        out_ref[...] = sum(values[1:], values[0]).astype(BF)


def fold_and_deal(sources, place, count):
    extent = sources[0].shape[-2:]
    return in_vmem(
        partial(fold_and_deal_kernel, count=count), "fold_and_deal", [(extent, BF)] * count, [], [place], *sources
    )


def add_and_deal_kernel(place_ref, keep_ref, other_ref, *out_refs):
    for bit, out_ref in enumerate(out_refs):
        which = place_ref[0] ^ bit
        out_ref[...] = (keep_ref[which].astype(F32) + other_ref[which].astype(F32)).astype(BF)


def in_vmem(kernel, name, shapes, scratch, scalars, *operands):
    vmem = pl.BlockSpec(memory_space=pltpu.VMEM)
    return pl.pallas_call(
        kernel,
        in_specs=[pl.BlockSpec(memory_space=pltpu.SMEM)] + [vmem] * len(operands),
        out_specs=[vmem] * len(shapes),
        out_shape=[jax.ShapeDtypeStruct(extent, dtype) for extent, dtype in shapes],
        scratch_shapes=[pltpu.VMEM(extent, F32) for extent in scratch],
        compiler_params=pltpu.CompilerParams(vmem_limit_bytes=40 << 20),
        name=name,
    )(jnp.stack(scalars).astype(jnp.int32), *operands)


def place_kernel(spots_ref, *refs):
    *sources, target = refs
    for number, source in enumerate(sources):
        target[spots_ref[number]] = source[...]


def placed(pieces, spots):
    return pl.pallas_call(
        place_kernel,
        in_specs=[pl.BlockSpec(memory_space=pltpu.SMEM)]
        + [pl.BlockSpec(memory_space=pltpu.VMEM)] * len(pieces),
        out_specs=pl.BlockSpec(memory_space=pltpu.VMEM),
        out_shape=jax.ShapeDtypeStruct((len(pieces),) + pieces[0].shape, pieces[0].dtype),
        compiler_params=pltpu.CompilerParams(vmem_limit_bytes=40 << 20),
        name="place_pieces",
    )(jnp.stack(spots).astype(jnp.int32), *pieces)


def exchanged(value, axis):
    size = lax.axis_size(axis)
    return [value] + [
        lax.ppermute(value, axis, [(source, source ^ bit) for source in range(size)])
        for bit in range(1, size)
    ]


def sent(taken, axis):
    return taken[:1] + [
        lax.ppermute(taken[bit], axis, [(source, source ^ bit) for source in range(len(taken))])
        for bit in range(1, len(taken))
    ]


def scattered(value, axis):
    size = lax.axis_size(axis)
    me = lax.axis_index(axis)
    return sent([lax.dynamic_index_in_dim(value, me ^ bit, 0, keepdims=False) for bit in range(size)], axis)


def placed_along(pieces, axis):
    me = lax.axis_index(axis)
    return placed(pieces, [me ^ bit for bit in range(len(pieces))])


def spread(value, axis):
    return placed_along(exchanged(value, axis), axis)


def tied(*values):
    return lax.optimization_barrier(values)


def in_turn(first, second):
    return jnp.where(lax.axis_index("tp") == 0, jnp.stack([first, second]), jnp.stack([second, first]))


def on_device(
    tokens,
    lengths,
    norm1_gain,
    qkv_weight,
    lr_weight,
    inner_w1,
    inner_b1,
    inner_w2,
    inner_b2,
    post_gain,
    post_bias,
    gate_weight,
    out_weight,
    norm2_gain,
    ffn_gate,
    ffn_up,
    ffn_down,
    cotangent,
):
    micro, span, width = tokens.shape
    ring = lax.axis_size("ctx")
    shards = lax.axis_size("shard")
    pair = lax.axis_size("tp")
    place = lax.axis_index("ctx")
    core = lax.axis_index("tp")
    local_heads, head_dim, inner_share = inner_w1.shape
    head_share = inner_b2.shape[1]
    depth = norm1_gain.shape[0]
    inner = inner_share * shards
    total_heads = local_heads * pair
    chains = -(-total_heads // ring)
    span_all = ring * span
    count = span_all // MINI
    cols = chains * head_dim
    wide = 4 * cols

    row_tokens = lax.dynamic_index_in_dim(tokens, core, 0, keepdims=False)
    token_parts = exchanged(row_tokens, "ctx")

    first_head = jnp.minimum(place * chains, total_heads - chains)
    owner = first_head // local_heads
    local_first = first_head - owner * local_heads

    packed = in_vmem(
        partial(pack_weights_kernel, chains=chains), "pack_weights",
        [((depth + SMALL, wide), BF)], [(SMALL, wide)], [local_first // chains],
        qkv_weight.reshape(depth, -1), gate_weight, lr_weight.T, norm1_gain[None], norm2_gain[None],
        inner_w1, inner_b1, inner_w2, inner_b2, post_gain, post_bias,
    )[0]
    half_rows = (depth + SMALL) // 2
    packed = jnp.where(core == owner, packed, swap(packed))
    gathered = exchanged(lax.dynamic_slice_in_dim(packed, core * half_rows, half_rows, 0), "shard")
    gathered, token_parts = tied(gathered, token_parts)

    units = ffn_gate.shape[1]
    half_out = out_weight.shape[0]
    row_pack = jnp.concatenate([ffn_gate, ffn_up, ffn_down.T, out_weight.T], axis=1)
    part = depth // ring
    cut = 3 * row_pack.shape[1] // 4 // 128 * 128
    row_near = row_pack[:, cut:]
    row_part = lax.dynamic_slice(row_pack, (place * part, 0), (part, cut))
    row_part, row_near, gathered = tied(row_part, row_near, gathered)
    row_parts = exchanged(row_part, "shard")
    slot_tokens = placed_along(token_parts, "ctx").reshape(span_all, width)
    gathered = placed_along(gathered, "shard")

    padded = -(-chains // 16) * 16
    w_chain, rate_rows, gain_row, gain_two, *rest = in_vmem(
        unpack_weights_kernel, "unpack_weights",
        [
            ((width, wide), BF), ((padded, width), BF), ((1, width), F32), ((1, width), F32),
            ((chains, head_dim, inner), F32), ((chains, 1, inner), F32),
            ((chains, head_dim, inner), F32), ((chains, 1, head_dim), F32),
            ((chains, 1, head_dim), F32), ((chains, 1, head_dim), F32),
        ],
        [(padded, width)], [core], gathered, swap(gathered),
    )
    state, (norm_gain, norm_bias) = tuple(rest[:4]), rest[4:]

    slot_length = lax.dynamic_index_in_dim(lengths, core, 0, keepdims=True)
    steps = span_all // (GROUP * MINI)
    middle = 3 * steps // 8

    def forward(first, last, begin):
        done = run_fwd(
            first, last, slot_length, slot_tokens, gain_row, w_chain, rate_rows, norm_gain, norm_bias, begin
        )
        return done[0], done[1:-4], done[-4:]

    post_low, saved_low, state_low = forward(0, middle, state)
    state_low, row_parts = tied(state_low, row_parts)
    far = jnp.stack(row_parts[1:])
    state_low, far = tied(state_low, far)
    row_near, far = tied(row_near, far)
    far_parts, near_parts = exchanged(far, "ctx"), lax.all_gather(row_near, "shard", axis=0)
    post_high, saved_high, _ = forward(middle, steps, tuple(state_low))
    post_high, far_parts, near_parts = tied(post_high, far_parts, near_parts)
    post_chain = jnp.concatenate([post_low, post_high])

    def to_rows(value):
        return lax.all_to_all(value.reshape(ring, span, -1), "ctx", 0, 0)

    post = to_rows(post_chain)

    number = jnp.stack([lax.axis_index("shard"), place]).astype(jnp.int32)
    w_own = run_assemble(number, row_pack, far_parts, near_parts).reshape(width, -1)
    w_other = swap(w_own)
    spots = jnp.stack([core, place * span, slot_length[0], place]).astype(jnp.int32)
    cot = lax.dynamic_index_in_dim(cotangent, core, 0, keepdims=False)
    output, grad_hidden, normed_two, grad_hidden_low, back_low, grad_gain_two, *kept = run_rows(
        spots, post, w_own, w_other, row_tokens, cot, gain_two, half_out
    )
    row_in = row_tokens.astype(F32)
    joined, acts = kept[:2], (kept[2:5], kept[5:8])

    def folded(values):
        return sum(value.astype(F32) for value in values).astype(BF)

    me = lax.axis_index("shard")

    def operands(half, second):
        if second:
            return (back_low, grad_hidden_low), (acts[half][2], joined[half])
        return (normed_two, normed_two), (acts[half][0], acts[half][1])

    def other_sums(second):
        return swap(run_sums(*operands(1, second)))

    def taken(second, other):
        if part % 16 == 0:
            if second:
                here = jnp.zeros((1,), jnp.int32)
                return run_sums(*operands(0, second), other, here, shards * ring)[0]
            here = jnp.stack([place]).astype(jnp.int32)
            return list(run_sums(*operands(0, second), other, here, shards, ring))
        own = run_sums(*operands(0, second)).astype(F32)
        both = (own + other.astype(F32)).astype(BF).reshape(shards, ring, part, -1)
        if second:
            return both
        return [lax.dynamic_index_in_dim(both, place ^ bit, 1, keepdims=False) for bit in range(ring)]

    grad_post = sent(list(kept[8:]), "ctx")

    def backward(first, last, base, begin, saved):
        done = run_bwd(
            first, last, base, slot_tokens, gain_row, w_chain, rate_rows, norm_gain, grad_post, sums, begin, saved
        )
        return done[0], tuple(done[1:])

    sums = ((width, wide), (padded, width), (1, width), (chains, 1, head_dim), (chains, 1, head_dim))
    sums += tuple(value.shape for value in state)
    other_a, other_b = other_sums(False), other_sums(True)
    (grad_post, sum_rights) = tied(grad_post, (other_a, other_b))
    taken_a, taken_b = taken(False, sum_rights[0]), taken(True, sum_rights[1])
    grad_post, taken_a, taken_b = tied(grad_post, taken_a, taken_b)
    grad_post = placed_along(grad_post, "ctx").reshape(span_all, cols)
    taken_b = taken_b.reshape(shards, ring, part, -1)
    sum_a, sum_b = sent(taken_a, "ctx"), lax.all_to_all(taken_b, "shard", 0, 0)
    back_high, ending = backward(middle, steps, middle, (), saved_high)
    ending, sum_a = tied(ending, sum_a)
    sum_a = fold_and_deal(sum_a, me, shards)
    ending, sum_a = tied(ending, sum_a)
    sum_a = sent(list(sum_a), "shard")
    back_low_half, ending = backward(0, middle, 0, ending, saved_low)
    ending, back_low_half, sum_a, sum_b = tied(ending, back_low_half, sum_a, sum_b)
    back_part = jnp.concatenate([back_low_half, back_high])
    grad_big, grad_lr, grad_gain_one, grad_norm_gain, grad_norm_bias, *grad_state = ending
    block = ((shards, half_rows, wide), BF)
    keep, send = in_vmem(
        pack_grads_kernel, "pack_grads", [block, block], [(SMALL, wide)], [core],
        grad_big, grad_lr, grad_gain_one, grad_gain_two, *grad_state, grad_norm_gain, grad_norm_bias,
    )
    dealt = in_vmem(
        add_and_deal_kernel, "add_and_deal", [((half_rows, wide), BF)] * shards, [],
        [lax.axis_index("shard")], keep, swap(send),
    )
    sum_b = sent(list(fold_and_deal([sum_b], place, ring)), "ctx")
    back_rows = to_rows(back_part)
    chain_sum = sent(list(dealt), "shard")
    chain_sum, back_rows, sum_a, sum_b = tied(chain_sum, back_rows, sum_a, sum_b)
    chain_parts = exchanged(folded(chain_sum), "ctx")
    row_sum = jnp.concatenate([folded(sum_a), folded(sum_b)], axis=-1)
    chain_parts, row_sum = tied(chain_parts, row_sum)
    chain_sum = placed_along(chain_parts, "ctx")
    g_qkv, g_gate, g_lr, g_n1, g_n2, *g_rest = in_vmem(
        partial(unpack_grads_kernel, chains=chains), "unpack_grads",
        [
            ((depth, 3, local_heads * head_dim), F32), ((depth, local_heads * head_dim), F32),
            ((local_heads, depth), F32), ((1, depth), F32), ((1, depth), F32),
            (inner_w1.shape, F32), (inner_b1.shape, F32), (inner_w2.shape, F32), (inner_b2.shape, F32),
            (post_gain.shape, F32), (post_bias.shape, F32),
        ],
        [], [core], chain_sum, swap(chain_sum),
    )

    row_sum = spread(row_sum, "ctx")
    row_sum = row_sum.reshape(depth, -1).astype(F32)
    g_ffn_gate = row_sum[:, :units]
    g_ffn_up = row_sum[:, units : 2 * units]
    g_ffn_down = row_sum[:, 2 * units : 3 * units].T
    g_out = row_sum[:, 3 * units :].T

    back_one = jnp.sum(back_rows.astype(F32), axis=0)
    scale_one = row_scale(row_in)
    lifted = back_one * gain_row
    input_grad = (
        grad_hidden
        + scale_one * lifted
        - row_in * scale_one**3 * jnp.mean(lifted * row_in, axis=-1, keepdims=True)
    ).astype(BF)


    return (
        in_turn(output, swap(output)),
        in_turn(input_grad, swap(input_grad)),
        g_n1[0],
        g_qkv,
        g_lr.T,
        *g_rest,
        g_gate,
        g_out,
        g_n2[0],
        g_ffn_gate,
        g_ffn_up,
        g_ffn_down,
    )


def solution(mesh):
    in_specs = (
        P("shard", "ctx", None),
        P("shard"),
        P("shard"),
        P("shard", None, "tp"),
        P("shard", "tp"),
        P("tp", None, "shard"),
        P("tp", "shard"),
        P("tp", None, "shard"),
        P("tp", "shard"),
        P("tp", "shard"),
        P("tp", "shard"),
        P("shard", "tp"),
        P("tp", "shard"),
        P("shard"),
        P("shard", "tp"),
        P("shard", "tp"),
        P("tp", "shard"),
        P("shard", "ctx", None),
    )
    out_specs = (
        P("shard", "ctx", None),
        P("shard", "ctx", None),
        P("shard"),
        P("shard", None, "tp"),
        P("shard", "tp"),
        P("tp", None, "shard"),
        P("tp", "shard"),
        P("tp", None, "shard"),
        P("tp", "shard"),
        P("tp", "shard"),
        P("tp", "shard"),
        P("shard", "tp"),
        P("tp", "shard"),
        P("shard"),
        P("shard", "tp"),
        P("shard", "tp"),
        P("tp", "shard"),
    )
    return jax.shard_map(
        on_device, mesh=mesh, in_specs=in_specs, out_specs=out_specs, check_vma=False
    )
```

```python
from functools import partial
import jax
import jax.numpy as jnp
from jax import lax
from jax.experimental import pallas as pl
from jax.experimental.pallas import tpu as pltpu
from jax.sharding import PartitionSpec as P

MINI = 16
EPSILON = 1e-06
ETA_BASE = 0.5
BF = jnp.bfloat16
F32 = jnp.float32


def mm(left, right):
    return lax.dot_general(left, right, (((1,), (0,)), ((), ())), preferred_element_type=F32)


def mm_nt(left, right):
    return lax.dot_general(left, right, (((1,), (1,)), ((), ())), preferred_element_type=F32)


def mm_tn(left, right):
    return lax.dot_general(left, right, (((0,), (0,)), ((), ())), preferred_element_type=F32)


def gelu_parts(value):
    cdf = 0.5 + 0.5 * lax.erf(value * 0.7071067811865476)
    pdf = jnp.exp(-0.5 * value * value) * 0.3989422804014327
    return cdf, pdf


def row_scale(value):
    return lax.rsqrt(jnp.mean(value * value, axis=-1, keepdims=True) + EPSILON)


def mini_masks(rows):
    row = lax.broadcasted_iota(jnp.int32, (rows, rows), 0)
    col = lax.broadcasted_iota(jnp.int32, (rows, rows), 1)
    within = (lax.div(row, MINI) == lax.div(col, MINI)) & (col <= row)
    scale = jnp.where(within, 1.0 / (lax.rem(row, MINI) + 1).astype(F32), 0.0)
    return scale, jnp.where(row == col, 1.0 / MINI, 0.0)


def minis(value):
    return [value[at : at + MINI] for at in range(0, value.shape[0], MINI)]


def flat_rows(value):
    return value.reshape(value.shape[0] * value.shape[1], value.shape[2])


class Rows:
    def __init__(self, ref, start, size):
        self.ref, self.start, self.size = ref, start, size

    def spot(self, key):
        key = key if isinstance(key, tuple) else (key, slice(None))
        first, last = 0, self.size
        if len(key) == 3:
            first, last, _ = key[2].indices(self.size)
        return key[0], key[1], slice(self.start + first, self.start + last)

    def __getitem__(self, key):
        return self.ref[self.spot(key)]

    def __setitem__(self, key, value):
        self.ref[self.spot(key)] = value


class Plane:
    def __init__(self, ref, number, lane=None):
        self.ref, self.number = ref, number
        self.lanes = slice(None) if lane is None else slice(lane, lane + 1)

    def __getitem__(self, key):
        if isinstance(key, tuple):
            return self.ref[key[0], self.number, key[1] * MINI : (key[1] + 1) * MINI, self.lanes]
        return self.ref[key, self.number, :, self.lanes]

    def __setitem__(self, key, value):
        self.ref[key, self.number, :, self.lanes] = value


def named_parts(narrow_ref, plane_ref, state_ref, low_ref, high_ref):
    head_dim = narrow_ref.shape[3]
    return (
        Rows(narrow_ref, 0, 2 * MINI), Rows(narrow_ref, 2 * MINI, MINI),
        *(Plane(plane_ref, number) for number in range(3)), Plane(plane_ref, 3, 0), Plane(plane_ref, 3, 1),
        Rows(state_ref, 0, head_dim), Rows(state_ref, head_dim, head_dim),
        *(Rows(low_ref, at, MINI) for at in (0, MINI, 2 * MINI)),
        *(Rows(high_ref, at, MINI) for at in (0, MINI, 2 * MINI)),
    )


def fwd_kernel(
    length_ref, x_ref, gain_ref, wc_ref, lrt_ref, w1i_ref, c1i_ref, w2i_ref, c2i_ref, pg_ref, pb_ref,
    post_ref, fac_ref, narrow_ref, plane_ref, state_ref, low_ref, high_ref,
    w1_ref, c1_ref, w2_ref, c2_ref, kmv_ref, next_ref, kk_ref, pq_ref, c2s_ref, *, first,
):
    kq_ref, g2_ref, gl_ref, gs_ref, unit_ref, rate_ref, hscale_ref, w1s_ref, w2s_ref, h_ref, r_ref, g1_ref, *rest = (
        named_parts(narrow_ref, plane_ref, state_ref, low_ref, high_ref)
    )
    ga_ref, ug_ref, gp_ref = rest
    chains, group, _, head_dim = narrow_ref.shape
    rows = group * MINI
    cols = chains * head_dim
    every = range(chains)

    @pl.when(pl.program_id(0) == 0)
    def _():
        w1_ref[...] = w1i_ref[...]
        c1_ref[...] = c1i_ref[...]
        w2_ref[...] = w2i_ref[...]
        c2_ref[...] = c2i_ref[...]

    start = (first + pl.program_id(0)) * rows
    padded = lrt_ref.shape[0]
    x = x_ref[...].astype(F32)
    normed = (x * row_scale(x) * gain_ref[...]).astype(BF)
    proj = mm(normed, wc_ref[...])
    length = length_ref[0]
    live_col = start + lax.broadcasted_iota(jnp.int32, (rows, padded), 0) < length
    live_row = start + lax.broadcasted_iota(jnp.int32, (padded, rows), 1) < length
    eta_col = jnp.where(live_col, jax.nn.sigmoid(mm_nt(normed, lrt_ref[...])), 0.0) * (ETA_BASE / head_dim)
    rate = jax.nn.sigmoid(mm_nt(lrt_ref[...], normed))
    eta_row = jnp.where(live_row, rate, 0.0) * (ETA_BASE / head_dim)
    fac_ref[0, :padded] = eta_row * (1.0 - rate)
    fac_ref[0, padded:] = eta_row
    for i in every:
        at = i * head_dim
        k = proj[:, cols + at : cols + at + head_dim]
        v = proj[:, 2 * cols + at : 2 * cols + at + head_dim]
        kb, qb = k.astype(BF), proj[:, at : at + head_dim].astype(BF)
        k_minis = kb.reshape(group, MINI, head_dim)
        q_minis = qb.reshape(group, MINI, head_dim)
        kq_ref[i, :, :MINI] = k_minis
        kq_ref[i, :, MINI:] = q_minis
        next_ref[i, : group - 1, :MINI] = k_minis[1:]
        next_ref[i, group - 1 :, :MINI] = k_minis[:1]
        next_ref[i, :, MINI:] = q_minis
        kmv_ref[i] = (k - v).reshape(group, MINI, head_dim)
        rate_ref[i] = eta_col[:, i : i + 1] * (1.0 / MINI)
        cross = (mm_nt(kb, kb) + 1.0) * (eta_row[i : i + 1] * (1.0 / MINI))
        for j in range(group - 1):
            at = j * MINI
            kk_ref[i, j] = cross[at + MINI : at + 2 * MINI, at : at + MINI].astype(BF)

    key_pre = [mm(kq_ref[i, 0, :MINI], w1_ref[i].astype(BF)) + c1_ref[i] for i in every]
    for j in range(group):
        rate = [rate_ref[i, j] for i in every]
        kmv = [kmv_ref[i, j] for i in every]
        stacked = [next_ref[i, j] for i in every]
        k = [kq_ref[i, j, :MINI] for i in every]
        kk = [kk_ref[i, j] for i in every] if j < group - 1 else None
        w1 = [w1_ref[i] for i in every]
        w2 = [w2_ref[i] for i in every]
        c1 = [c1_ref[i] for i in every]
        c2 = [c2_ref[i] for i in every]
        w1b = [w1[i].astype(BF) for i in every]
        w2b = [w2[i].astype(BF) for i in every]
        parts = [gelu_parts(key_pre[i]) for i in every]
        hb = [(key_pre[i] * parts[i][0]).astype(BF) for i in every]
        g2 = [mm_nt(hb[i], w2b[i]) + c2[i] + kmv[i] for i in every]
        slope = [parts[i][0] + key_pre[i] * parts[i][1] for i in every]
        curve = [parts[i][1] * (2.0 - key_pre[i] * key_pre[i]) for i in every]
        both = [mm(stacked[i], w1b[i]) + c1[i] for i in every]
        g2b = [g2[i].astype(BF) for i in every]
        u = [mm(g2b[i], w2b[i]) for i in every]
        fg2 = [rate[i] * g2[i] for i in every]
        w2n = [w2[i] - mm_tn(fg2[i].astype(BF), hb[i]) for i in every]
        c2n = [c2[i] - jnp.sum(fg2[i], axis=0, keepdims=True) for i in every]
        g1 = [u[i] * slope[i] for i in every]
        g1b = [g1[i].astype(BF) for i in every]
        if j < group - 1:
            key_pre = [both[i][:MINI] - mm(kk[i], g1b[i]) for i in every]
        fg1 = [rate[i] * g1[i] for i in every]
        w1n = [w1[i] - mm_tn(k[i], fg1[i].astype(BF)) for i in every]
        c1n = [c1[i] - jnp.sum(fg1[i], axis=0, keepdims=True) for i in every]
        for i in every:
            w1s_ref[i, j] = w1b[i]
            w2s_ref[i, j] = w2b[i]
            c2s_ref[i, j] = c2[i]
            h_ref[i, j] = hb[i]
            g1_ref[i, j] = g1b[i]
            g2_ref[i, j] = g2b[i]
            ga_ref[i, j] = slope[i]
            ug_ref[i, j] = u[i] * curve[i]
            pq_ref[i, j] = both[i][MINI:]
            w1_ref[i] = w1n[i]
            w2_ref[i] = w2n[i]
            c1_ref[i] = c1n[i]
            c2_ref[i] = c2n[i]

    scale = mini_masks(rows)[0]
    for i in every:
        at = i * head_dim
        q = proj[:, at : at + head_dim]
        gate = proj[:, 3 * cols + at : 3 * cols + at + head_dim]
        kb, qb = flat_rows(kq_ref[i, :, :MINI]), flat_rows(kq_ref[i, :, MINI:])
        hb, g1b, g2b = flat_rows(h_ref[i]), flat_rows(g1_ref[i]), flat_rows(g2_ref[i])
        mix = scale * eta_row[i : i + 1]
        query_pre = flat_rows(pq_ref[i]) - mm((mix * (mm_nt(qb, kb) + 1.0)).astype(BF), g1b)
        cdf, pdf = gelu_parts(query_pre)
        gp_ref[i] = (cdf + query_pre * pdf).reshape(group, MINI, -1)
        rb = (query_pre * cdf).astype(BF)
        r_ref[i] = rb.reshape(group, MINI, -1)
        s2 = (mix * (mm_nt(rb, hb) + 1.0)).astype(BF)
        through = [mm_nt(piece, w2s_ref[i, j]) + c2s_ref[i, j] for j, piece in enumerate(minis(rb))]
        mixed = q + jnp.concatenate(through, axis=0) - mm(s2, g2b)
        centered = mixed - jnp.mean(mixed, axis=-1, keepdims=True)
        hscale = row_scale(centered)
        unit = centered * hscale
        out = unit * pg_ref[i] + pb_ref[i]
        cdf, pdf = gelu_parts(gate)
        post_ref[:, at : at + head_dim] = (gate * cdf * out).astype(BF)
        gl_ref[i] = gate * cdf
        gs_ref[i] = (cdf + gate * pdf) * out
        unit_ref[i] = unit
        hscale_ref[i] = hscale


def bwd_kernel(
    x_ref, gain_ref, wc_ref, lrt_ref, pg_ref, gpost_ref,
    fac_ref, narrow_ref, plane_ref, state_ref, low_ref, high_ref, *refs, begun,
):
    before, refs = (refs[:9], refs[10:]) if begun else ((), refs)
    (back_ref, gw_ref, glr_ref, gain_grad_ref, gpg_ref, gpb_ref, dw1_ref, dc1_ref, dw2_ref, dc2_ref, d_ref, g1a_ref, g2a_ref, ha_ref, ka_ref, dp_ref, kc_ref, dk_ref, da_ref, df_ref, de_ref, all_ref) = refs
    kq_ref, g2_ref, gl_ref, gs_ref, unit_ref, rate_ref, hscale_ref, w1s_ref, w2s_ref, h_ref, r_ref, g1_ref, *rest = (
        named_parts(narrow_ref, plane_ref, state_ref, low_ref, high_ref)
    )
    ga_ref, ug_ref, gp_ref = rest
    chains, group, _, head_dim = narrow_ref.shape
    rows = group * MINI
    cols = chains * head_dim
    every = range(chains)

    @pl.when(pl.program_id(0) == 0)
    def _():
        totals = (gw_ref, glr_ref, gain_grad_ref, gpg_ref, gpb_ref, dw1_ref, dc1_ref, dw2_ref, dc2_ref)
        for number, total in enumerate(totals):
            total[...] = before[number][...] if begun else jnp.zeros_like(total)

    scale, eye = mini_masks(rows)
    padded = lrt_ref.shape[0]
    gpost = gpost_ref[...].astype(F32)
    for i in every:
        at = i * head_dim
        piece = gpost[:, at : at + head_dim]
        all_ref[:, 3 * cols + at : 3 * cols + at + head_dim] = (piece * gs_ref[i]).astype(BF)
        head = piece * gl_ref[i]
        unit = unit_ref[i]
        gpg_ref[i] += jnp.sum(head * unit, axis=0, keepdims=True)
        gpb_ref[i] += jnp.sum(head, axis=0, keepdims=True)
        lifted = head * pg_ref[i]
        d = hscale_ref[i] * (
            lifted
            - jnp.mean(lifted, axis=-1, keepdims=True)
            - unit * jnp.mean(lifted * unit, axis=-1, keepdims=True)
        )
        d_ref[i] = d.reshape(group, MINI, head_dim)
        db = d.astype(BF)
        kb, qb = flat_rows(kq_ref[i, :, :MINI]), flat_rows(kq_ref[i, :, MINI:])
        hb, rb, g1b, g2b = (flat_rows(ref[i]) for ref in (h_ref, r_ref, g1_ref, g2_ref))
        mix = scale * fac_ref[0, padded + i : padded + i + 1]
        ds2 = -mm_nt(db, g2b)
        x2 = mm_nt(rb, hb) + 1.0
        x1 = mm_nt(qb, kb) + 1.0
        dx2 = (ds2 * mix).astype(BF)
        dr = jnp.concatenate([mm(part, w2s_ref[i, j]) for j, part in enumerate(minis(db))], axis=0)
        dp = (dr + mm(dx2, hb)) * flat_rows(gp_ref[i])
        dpb = dp.astype(BF)
        ds1 = -mm_nt(dpb, g1b)
        dx1 = (ds1 * mix).astype(BF)
        dq = jnp.concatenate([mm_nt(part, w1s_ref[i, j]) for j, part in enumerate(minis(dpb))], axis=0)
        all_ref[:, at : at + head_dim] = (d + dq + mm(dx1, kb)).astype(BF)
        g1a_ref[i] = -mm_tn((mix * x1).astype(BF), dpb).reshape(group, MINI, -1)
        g2a_ref[i] = -mm_tn((mix * x2).astype(BF), db).reshape(group, MINI, -1)
        ha_ref[i] = mm_tn(dx2, rb).reshape(group, MINI, -1)
        ka_ref[i] = mm_tn(dx1, qb).reshape(group, MINI, -1)
        dp_ref[i] = dpb.reshape(group, MINI, -1)
        de_ref[i] = jnp.sum((ds2 * x2 + ds1 * x1) * scale, axis=0, keepdims=True)
        kk = mm_nt(kb, kb) + 1.0
        kx = mm_nt(kb, qb) + 1.0
        for j in range(group - 1):
            own, after = slice(j * MINI, (j + 1) * MINI), slice((j + 1) * MINI, (j + 2) * MINI)
            kc_ref[i, j] = jnp.concatenate([kk[own, after], kx[own, after]], axis=1).astype(BF)

    t1 = [mm(kq_ref[i, group - 1, :MINI], dw1_ref[i].astype(BF)) + dc1_ref[i] for i in every]
    for j in reversed(range(group)):

        def all_of(ref):
            return [ref[i, j] for i in every]

        d, kq, rate, w2b, hb, rb, g1b, g2b = (
            all_of(ref) for ref in (d_ref, kq_ref, rate_ref, w2s_ref, h_ref, r_ref, g1_ref, g2_ref)
        )
        ga, ug, dpb, g1a, g2a, ha = (
            all_of(ref) for ref in (ga_ref, ug_ref, dp_ref, g1a_ref, g2a_ref, ha_ref)
        )
        dw1 = [dw1_ref[i] for i in every]
        dw2 = [dw2_ref[i] for i in every]
        dc1 = [dc1_ref[i] for i in every]
        dc2 = [dc2_ref[i] for i in every]
        g1 = [g1b[i].astype(F32) for i in every]
        g2 = [g2b[i].astype(F32) for i in every]
        dw1b = [dw1[i].astype(BF) for i in every]
        dw2b = [dw2[i].astype(BF) for i in every]
        dg1 = [g1a[i] - rate[i] * t1[i] for i in every]
        dub = [(dg1[i] * ga[i]).astype(BF) for i in every]
        through = [mm_nt(dub[i], w2b[i]) for i in every]
        t2 = [mm_nt(hb[i], dw2b[i]) + dc2[i] for i in every]
        dha = [ha[i] - mm((rate[i] * g2[i]).astype(BF), dw2b[i]) for i in every]
        dg2 = [through[i] + (g2a[i] - rate[i] * t2[i]) for i in every]
        dg2b = [dg2[i].astype(BF) for i in every]
        dh = [mm(dg2b[i], w2b[i]) + dha[i] for i in every]
        if j > 0:
            base = [mm(kq_ref[i, j - 1, :MINI], dw1b[i]) + dc1[i] for i in every]
        dk = [dg2[i] - mm_nt((rate[i] * g1[i]).astype(BF), dw1b[i]) for i in every]
        df = [
            -(
                jnp.sum(g1[i] * t1[i], axis=1, keepdims=True)
                + jnp.sum(g2[i] * t2[i], axis=1, keepdims=True)
            )
            for i in every
        ]
        da = [dg1[i] * ug[i] + dh[i] * ga[i] for i in every]
        dab = [da[i].astype(BF) for i in every]
        both = [jnp.concatenate([dab[i], dpb[i]], axis=0) for i in every]
        if j > 0:
            t1 = [base[i] + mm(kc_ref[i, j - 1], both[i]) for i in every]
        dw1n = [dw1[i] + mm_tn(kq[i], both[i]) for i in every]
        dc1n = [dc1[i] + jnp.sum(da[i] + dpb[i].astype(F32), axis=0, keepdims=True) for i in every]
        dw2n = [
            dw2[i]
            + mm_tn(
                jnp.concatenate([d[i].astype(BF), dg2b[i], g2b[i]], axis=0),
                jnp.concatenate([rb[i], hb[i], dub[i]], axis=0),
            )
            for i in every
        ]
        dc2n = [dc2[i] + jnp.sum(d[i] + dg2[i], axis=0, keepdims=True) for i in every]
        for i in every:
            piece, at = slice(j * MINI, (j + 1) * MINI), 2 * cols + i * head_dim
            all_ref[piece, at : at + head_dim] = (-dg2[i]).astype(BF)
            dk_ref[i, j] = dk[i]
            da_ref[i, j] = dab[i]
            df_ref[i, j] = df[i]
            dw1_ref[i] = dw1n[i]
            dc1_ref[i] = dc1n[i]
            dw2_ref[i] = dw2n[i]
            dc2_ref[i] = dc2n[i]

    x = x_ref[...].astype(F32)
    unit_in = x * row_scale(x)
    normed = (unit_in * gain_ref[...]).astype(BF)
    lrt = lrt_ref[...]
    which = lax.broadcasted_iota(jnp.int32, (padded, rows), 0)
    rates = jnp.zeros((padded, rows), F32)
    for i in every:
        at = cols + i * head_dim
        dk = jnp.concatenate([mm_nt(da_ref[i, j], w1s_ref[i, j]) for j in range(group)], axis=0)
        all_ref[:, at : at + head_dim] = (flat_rows(dk_ref[i]) + flat_rows(ka_ref[i]) + dk).astype(BF)
        line = de_ref[i] + jnp.sum(eye * flat_rows(df_ref[i]), axis=0, keepdims=True)
        rates = jnp.where(which == i, line, rates)
    rates = (rates * fac_ref[0, :padded]).astype(BF)
    grads = all_ref[...]
    back = mm_nt(grads, wc_ref[...]) + mm_tn(rates, lrt)
    gain_grad_ref[...] += jnp.sum(back * unit_in, axis=0, keepdims=True)
    back_ref[...] = back.astype(BF)
    gw_ref[...] += mm_tn(normed, grads)
    glr_ref[...] += mm(rates, normed)


GROUP = 8


def block_specs(chains, head_dim, inner, padded, place):
    rows = GROUP * MINI

    def mini(first, second):
        return pl.BlockSpec((chains, GROUP, first, second), lambda g: (0, place(g), 0, 0))

    return [
        pl.BlockSpec((1, 2 * padded, rows), lambda g: (place(g), 0, 0)),
        mini(3 * MINI, head_dim),
        pl.BlockSpec((chains, 4, rows, head_dim), lambda g: (0, 0, place(g), 0)),
        mini(2 * head_dim, inner), mini(3 * MINI, inner), mini(3 * MINI, inner),
    ]


def whole_spec(value):
    return pl.BlockSpec(value.shape, lambda g: (0,) * value.ndim)


def run_fwd(first, last, length, tokens, gain, wc, lrt, pg, pb, state):
    width = tokens.shape[1]
    chains, head_dim, inner = state[0].shape
    rows = GROUP * MINI
    steps = last - first
    count = steps * GROUP
    padded = lrt.shape[0]

    def mini(first_size, second_size, dtype):
        return jax.ShapeDtypeStruct((chains, count, first_size, second_size), dtype)

    row_spec = pl.BlockSpec((rows, width), lambda g: (first + g, 0))
    small = (gain, wc, lrt, *state, pg, pb)
    return pl.pallas_call(
        partial(fwd_kernel, first=first),
        grid=(steps,),
        in_specs=[pl.BlockSpec(memory_space=pltpu.SMEM), row_spec] + [whole_spec(v) for v in small],
        out_specs=[pl.BlockSpec((rows, chains * head_dim), lambda g: (g, 0))]
        + block_specs(chains, head_dim, inner, padded, lambda g: g)
        + [whole_spec(v) for v in state],
        out_shape=[
            jax.ShapeDtypeStruct((steps * rows, chains * head_dim), BF),
            jax.ShapeDtypeStruct((steps, 2 * padded, rows), F32),
            mini(3 * MINI, head_dim, BF),
            jax.ShapeDtypeStruct((chains, 4, steps * rows, head_dim), F32),
            mini(2 * head_dim, inner, BF), mini(3 * MINI, inner, BF), mini(3 * MINI, inner, F32),
        ]
        + [jax.ShapeDtypeStruct(v.shape, F32) for v in state],
        scratch_shapes=[
            pltpu.VMEM((chains, GROUP, MINI, head_dim), F32),
            pltpu.VMEM((chains, GROUP, 2 * MINI, head_dim), BF),
            pltpu.VMEM((chains, GROUP, MINI, MINI), BF),
            pltpu.VMEM((chains, GROUP, MINI, inner), F32),
            pltpu.VMEM((chains, GROUP, 1, head_dim), F32),
        ],
        compiler_params=pltpu.CompilerParams(vmem_limit_bytes=50 << 20),
        cost_estimate=pl.CostEstimate(
            flops=9_000_000_000 * steps, bytes_accessed=5_000_000 * steps, transcendentals=0
        ),
        name="chain_forward",
    )(length, tokens, *small)


def run_bwd(first, last, base, tokens, gain, wc, lrt, pg, gpost, shapes, state, saved, written=None):
    begun = written is not None
    width = tokens.shape[1]
    chains, head_dim, inner = shapes[5]
    rows = GROUP * MINI
    padded = lrt.shape[0]
    wide = wc.shape[1]
    steps = last - first

    def place(g):
        return steps - 1 - g

    def shape(*extent):
        return jax.ShapeDtypeStruct(extent, F32)

    small = (gain, wc, lrt, pg)
    outs = [shape(*extent) for extent in shapes]

    def scratch(first_size, second_size, dtype):
        return pltpu.VMEM((chains, GROUP, first_size, second_size), dtype)

    return pl.pallas_call(
        partial(bwd_kernel, begun=begun),
        grid=(steps,),
        in_specs=[pl.BlockSpec((rows, width), lambda g: (first + place(g), 0))]
        + [whole_spec(v) for v in small]
        + [pl.BlockSpec((rows, chains * head_dim), lambda g: (first + place(g), 0))]
        + block_specs(chains, head_dim, inner, padded, lambda g: first - base + place(g))
        + [whole_spec(v) for v in state]
        + [pl.BlockSpec(memory_space=pl.ANY)] * begun,
        out_specs=[pl.BlockSpec((rows, width), lambda g: (first + place(g), 0))] + [whole_spec(v) for v in outs],
        out_shape=[jax.ShapeDtypeStruct(tokens.shape, BF)] + outs,
        input_output_aliases={21: 0} if begun else {},
        scratch_shapes=[
            scratch(MINI, head_dim, F32), scratch(MINI, inner, F32), scratch(MINI, head_dim, F32),
            scratch(MINI, inner, F32), scratch(MINI, head_dim, F32), scratch(MINI, inner, BF),
            scratch(MINI, 2 * MINI, BF), scratch(MINI, head_dim, F32), scratch(MINI, inner, BF),
            scratch(MINI, 1, F32), pltpu.VMEM((chains, 1, rows), F32), pltpu.VMEM((rows, wide), BF),
        ],
        compiler_params=pltpu.CompilerParams(vmem_limit_bytes=50 << 20),
        cost_estimate=pl.CostEstimate(
            flops=11_000_000_000 * steps, bytes_accessed=5_000_000 * steps, transcendentals=0
        ),
        name="chain_backward",
    )(tokens, *small, gpost, *saved, *state, *((written,) if begun else ()))


def swap(value):
    return lax.ppermute(value, "tp", [(0, 1), (1, 0)])


def rows_kernel(
    spot_ref, post_ref, own_ref, other_ref, x_ref, cot_ref, gain_ref,
    out_ref, grad_ref, normed_ref, low_ref, back_ref, gain_grad_ref, cat0_ref, cat1_ref, *act_refs,
):
    *act_refs, gpost_ref = act_refs
    core, start, length = spot_ref[0], spot_ref[1], spot_ref[2]
    span, width = x_ref.shape
    cols = post_ref.shape[2]
    units = act_refs[0].shape[1]
    places = cat0_ref.shape[1] // cols
    x = x_ref[...].astype(F32)
    live = start + lax.broadcasted_iota(jnp.int32, (span, width), 0) < length
    back = jnp.where(live, cot_ref[...].astype(F32), 0.0)
    back_low = back.astype(BF)
    back_ref[...] = back_low
    halves = ((own_ref, core), (other_ref, 1 - core))
    hidden = x
    for half, (w_ref, side) in enumerate(halves):
        joined = jnp.concatenate([post_ref[side * places + p] for p in range(places)], axis=1)
        (cat0_ref, cat1_ref)[half][...] = joined
        hidden = hidden + mm_nt(joined, w_ref[:, 3 * units :])
    scale = row_scale(hidden)
    gain = gain_ref[...]
    normed = (hidden * scale * gain).astype(BF)
    normed_ref[...] = normed
    feed = jnp.zeros((span, width), F32)
    grad = jnp.zeros((span, width), F32)
    step = min(units, 512)
    for half, (w_ref, _) in enumerate(halves):
        for at in range(0, units, step):
            w_gate = w_ref[:, at : at + step]
            w_up = w_ref[:, units + at : units + at + step]
            w_down = w_ref[:, 2 * units + at : 2 * units + at + step]
            up_gate = mm(normed, w_gate)
            up_lin = mm(normed, w_up)
            grad_act = mm(back_low, w_down)
            gate = jax.nn.sigmoid(up_gate)
            silu = up_gate * gate
            act = (silu * up_lin).astype(BF)
            grad_gate = (grad_act * up_lin * (gate * (1.0 + up_gate * (1.0 - gate)))).astype(BF)
            grad_lin = (grad_act * silu).astype(BF)
            act_refs[3 * half + 0][:, at : at + step] = grad_gate
            act_refs[3 * half + 1][:, at : at + step] = grad_lin
            act_refs[3 * half + 2][:, at : at + step] = act
            feed += mm_nt(act, w_down)
            grad += mm_nt(grad_gate, w_gate) + mm_nt(grad_lin, w_up)
    out_ref[...] = (hidden + feed).astype(BF)
    lifted = grad * gain
    hat = hidden * scale
    gain_grad_ref[...] = jnp.sum(grad * hat, axis=0, keepdims=True)
    total = back + scale * (lifted - hat * jnp.mean(lifted * hat, axis=-1, keepdims=True))
    grad_ref[...] = total
    low = total.astype(BF)
    low_ref[...] = low
    for p in range(2 * places, gpost_ref.shape[0]):
        gpost_ref[p] = jnp.zeros(gpost_ref.shape[1:], BF)
    deal_refs = act_refs[6:]
    for w_ref, side in halves:
        gpost = mm(low, w_ref[:, 3 * units :]).astype(BF)
        for p in range(places):
            gpost_ref[side * places + p] = gpost[:, p * cols : (p + 1) * cols]
    for bit, deal_ref in enumerate(deal_refs):
        deal_ref[...] = gpost_ref[spot_ref[3] ^ bit]


def run_rows(spots, post, own, other, x, cot, gain, half_out):
    ring, span, cols = post.shape
    width = x.shape[1]
    units = (own.shape[1] - half_out) // 3
    vmem = pl.BlockSpec(memory_space=pltpu.VMEM)

    def shape(extent, dtype):
        return jax.ShapeDtypeStruct(extent, dtype)

    return pl.pallas_call(
        rows_kernel,
        in_specs=[pl.BlockSpec(memory_space=pltpu.SMEM)] + [vmem] * 6,
        out_specs=[vmem] * (14 + ring),
        out_shape=[
            shape((span, width), BF), shape((span, width), F32),
            shape((span, width), BF), shape((span, width), BF), shape((span, width), BF), shape((1, width), F32),
        ]
        + [shape((span, half_out), BF)] * 2
        + [shape((span, units), BF)] * 6
        + [shape((span, cols), BF)] * ring,
        scratch_shapes=[pltpu.VMEM((ring, span, cols), BF)],
        compiler_params=pltpu.CompilerParams(vmem_limit_bytes=52 << 20),
        cost_estimate=pl.CostEstimate(flops=20_000_000_000, bytes_accessed=20_000_000, transcendentals=0),
        name="rows_main",
    )(spots, post, own, other, x, cot, gain)


def products(pairs, parts, store):
    start = 0
    for left, right in zip(pairs, parts):
        size = right.shape[-1]
        step = 512 if size % 512 == 0 else size
        for at in range(0, size, step):
            store(start + at, mm_tn(left[...], right[:, at : at + step]))
        start += size


def sums_other_kernel(*refs):
    *sources, out_ref = refs
    count = len(sources) // 2

    def store(at, value):
        out_ref[:, at : at + value.shape[1]] = value.astype(BF)

    products(sources[:count], sources[count:], store)


def sums_own_kernel(place_ref, other_ref, *refs, count, outs):
    sources, out_refs, held_ref = refs[: 2 * count], refs[2 * count : 2 * count + outs], refs[-1]

    def store(at, value):
        piece = slice(at, at + value.shape[1])
        held_ref[:, piece] = (value + other_ref[:, piece].astype(F32)).astype(BF)

    products(sources[:count], sources[count:], store)
    for bit, out_ref in enumerate(out_refs):
        blocks, part = out_ref.shape[:2]
        for number in range(blocks):
            at = pl.multiple_of((number * outs + (place_ref[0] ^ bit)) * part, part)
            out_ref[number] = held_ref[pl.ds(at, part), :]


def run_sums(lefts, rights, other=None, place=None, blocks=1, outs=1):
    width = lefts[0].shape[1]
    total = sum(right.shape[1] for right in rights)
    vmem = pl.BlockSpec(memory_space=pltpu.VMEM)
    count = len(lefts)
    params = pltpu.CompilerParams(vmem_limit_bytes=40 << 20)
    cost = pl.CostEstimate(flops=5_000_000_000, bytes_accessed=6_000_000, transcendentals=0)
    if other is None:
        return pl.pallas_call(
            sums_other_kernel,
            in_specs=[vmem] * (2 * count),
            out_specs=vmem,
            out_shape=jax.ShapeDtypeStruct((width, total), BF),
            compiler_params=params,
            cost_estimate=cost,
            name="sums_other",
        )(*lefts, *rights)
    part = width // (blocks * outs)
    return pl.pallas_call(
        partial(sums_own_kernel, count=count, outs=outs),
        in_specs=[pl.BlockSpec(memory_space=pltpu.SMEM)] + [vmem] * (2 * count + 1),
        out_specs=[vmem] * outs,
        out_shape=[jax.ShapeDtypeStruct((blocks, part, total), BF)] * outs,
        scratch_shapes=[pltpu.VMEM((width, total), BF)],
        compiler_params=params,
        cost_estimate=cost,
        name="sums_own",
    )(place, other, *lefts, *rights)


def assemble_kernel(spots_ref, pack_ref, *refs, ring):
    far_refs, near_ref, out_ref = refs[:ring], refs[ring], refs[-1]
    me, place = spots_ref[0], spots_ref[1]
    part = out_ref.shape[1]
    cut = far_refs[0].shape[2]
    for number in range(ring):
        piece = slice(number * part, (number + 1) * part)
        out_ref[me * ring + number, :, :cut] = pack_ref[piece, :cut]
        for z in range(near_ref.shape[0]):
            out_ref[z * ring + number, :, cut:] = near_ref[z, piece]
    for bit, far_ref in enumerate(far_refs):
        for other in range(far_ref.shape[0]):
            out_ref[(me ^ (other + 1)) * ring + (place ^ bit), :, :cut] = far_ref[other]


def run_assemble(spots, pack, far_parts, near_parts):
    vmem = pl.BlockSpec(memory_space=pltpu.VMEM)
    ring = len(far_parts)
    part = pack.shape[0] // ring
    return pl.pallas_call(
        partial(assemble_kernel, ring=ring),
        in_specs=[pl.BlockSpec(memory_space=pltpu.SMEM)] + [vmem] * (2 + ring),
        out_specs=vmem,
        out_shape=jax.ShapeDtypeStruct((near_parts.shape[0] * ring, part, pack.shape[1]), BF),
        compiler_params=pltpu.CompilerParams(vmem_limit_bytes=40 << 20),
        name="assemble_rows",
    )(spots, pack, *far_parts, near_parts)


SMALL = 64


def small_spots(chains, depth, inner_share):
    side = 2 * chains * inner_share
    return side, {
        "lr": 0, "n1": chains, "n2": chains + 1, "b1": chains + 2,
        "b2": 2 * chains + 2, "pg": 3 * chains + 2, "pb": 4 * chains + 2,
    }


def pack_weights_kernel(
    pick_ref, qkv_ref, gate_ref, lr_ref, n1_ref, n2_ref, w1_ref, b1_ref, w2_ref, b2_ref, pg_ref, pb_ref,
    out_ref, small_ref, *, chains,
):
    depth = gate_ref.shape[0]
    heads, head_dim, inner_share = w1_ref.shape
    cols = chains * head_dim
    all_cols = heads * head_dim
    side, spots = small_spots(chains, depth, inner_share)
    small_ref[...] = jnp.zeros_like(small_ref)

    def put(name, i, value):
        row = spots[name] + i
        small_ref[row : row + 1, side : side + value.shape[1]] = value.astype(F32)

    for option in range(heads // chains):

        @pl.when(pick_ref[0] == option)
        def _():
            at = option * cols
            for which in range(3):
                start = which * all_cols + at
                out_ref[:depth, which * cols : (which + 1) * cols] = qkv_ref[:, start : start + cols]
            out_ref[:depth, 3 * cols :] = gate_ref[:, at : at + cols]
            for i in range(chains):
                head = option * chains + i
                lanes = slice(i * inner_share, (i + 1) * inner_share)
                small_ref[:, lanes] = w1_ref[head].astype(F32)
                lanes = slice((chains + i) * inner_share, (chains + i + 1) * inner_share)
                small_ref[:, lanes] = w2_ref[head].astype(F32)
                for name, ref in (("lr", lr_ref), ("b1", b1_ref), ("b2", b2_ref), ("pg", pg_ref), ("pb", pb_ref)):
                    put(name, i, ref[head : head + 1, :])

    put("n1", 0, n1_ref[...])
    put("n2", 0, n2_ref[...])
    out_ref[depth:, :] = small_ref[...].astype(BF)


def halves_by_core(core, mine_ref, other_ref, work):
    @pl.when(core == 0)
    def _():
        work(mine_ref, other_ref)

    @pl.when(core != 0)
    def _():
        work(other_ref, mine_ref)


def unpack_weights_kernel(
    core_ref, mine_ref, other_ref,
    wc_ref, lrt_ref, n1_ref, n2_ref, w1_ref, b1_ref, w2_ref, b2_ref, pg_ref, pb_ref, lines_ref,
):
    shards, half, _ = mine_ref.shape
    chains, _, inner = w1_ref.shape
    inner_share = inner // shards
    depth = 2 * half - SMALL
    head_share = b2_ref.shape[2] // shards
    side, spots = small_spots(chains, depth, inner_share)
    lines_ref[...] = jnp.zeros_like(lines_ref)

    def work(low_ref, high_ref):
        for z in range(shards):
            wc_ref[z * depth : z * depth + half] = low_ref[z]
            wc_ref[z * depth + half : (z + 1) * depth] = high_ref[z, : depth - half]
            small = high_ref[z, depth - half :].astype(F32)

            def get(name, i, size):
                row = spots[name] + i
                return small[row : row + 1, side : side + size]

            here = slice(z * depth, (z + 1) * depth)
            n1_ref[:, here] = get("n1", 0, depth)
            n2_ref[:, here] = get("n2", 0, depth)
            for i in range(chains):
                lines_ref[i : i + 1, here] = get("lr", i, depth)
                lanes = slice(z * inner_share, (z + 1) * inner_share)
                w1_ref[i, :, lanes] = small[:, i * inner_share : (i + 1) * inner_share]
                w2_ref[i, :, lanes] = small[:, (chains + i) * inner_share : (chains + i + 1) * inner_share]
                b1_ref[i, :, lanes] = get("b1", i, inner_share)
                lanes = slice(z * head_share, (z + 1) * head_share)
                for name, ref in (("b2", b2_ref), ("pg", pg_ref), ("pb", pb_ref)):
                    ref[i, :, lanes] = get(name, i, head_share)

    halves_by_core(core_ref[0], mine_ref, other_ref, work)
    lrt_ref[...] = lines_ref[...].astype(BF)


def pack_grads_kernel(
    core_ref, gw_ref, glr_ref, n1_ref, n2_ref, w1_ref, b1_ref, w2_ref, b2_ref, pg_ref, pb_ref,
    keep_ref, send_ref, small_ref,
):
    shards, half, _ = keep_ref.shape
    chains, _, inner = w1_ref.shape
    inner_share = inner // shards
    depth = 2 * half - SMALL
    head_share = b2_ref.shape[2] // shards
    side, spots = small_spots(chains, depth, inner_share)

    def work(low_ref, high_ref):
        for z in range(shards):
            small_ref[...] = jnp.zeros_like(small_ref)

            def put(name, i, value):
                row = spots[name] + i
                small_ref[row : row + 1, side : side + value.shape[1]] = value

            here = slice(z * depth, (z + 1) * depth)
            low_ref[z] = gw_ref[z * depth : z * depth + half].astype(BF)
            high_ref[z, : depth - half] = gw_ref[z * depth + half : (z + 1) * depth].astype(BF)
            put("n1", 0, n1_ref[:, here])
            put("n2", 0, n2_ref[:, here])
            for i in range(chains):
                put("lr", i, glr_ref[i : i + 1, here])
                lanes = slice(z * inner_share, (z + 1) * inner_share)
                small_ref[:, i * inner_share : (i + 1) * inner_share] = w1_ref[i, :, lanes]
                small_ref[:, (chains + i) * inner_share : (chains + i + 1) * inner_share] = w2_ref[i, :, lanes]
                put("b1", i, b1_ref[i, :, lanes])
                lanes = slice(z * head_share, (z + 1) * head_share)
                for name, ref in (("b2", b2_ref), ("pg", pg_ref), ("pb", pb_ref)):
                    put(name, i, ref[i, :, lanes])
            high_ref[z, depth - half :] = small_ref[...].astype(BF)

    halves_by_core(core_ref[0], keep_ref, send_ref, work)


def unpack_grads_kernel(
    core_ref, mine_ref, other_ref,
    qkv_ref, gate_ref, lrt_ref, n1_ref, n2_ref, w1_ref, b1_ref, w2_ref, b2_ref, pg_ref, pb_ref, *, chains,
):
    ring, half, wide = mine_ref.shape
    cols = wide // 4
    heads, _, inner_share = w1_ref.shape
    depth = gate_ref.shape[0]
    head_share = b2_ref.shape[1]
    places = heads // chains
    side, spots = small_spots(chains, depth, inner_share)
    core = core_ref[0]

    def work(low_ref, high_ref):
        for p in range(places):
            place = core * places + p
            big = jnp.concatenate([low_ref[place], high_ref[place, : depth - half]], axis=0).astype(F32)
            small = high_ref[place, depth - half :].astype(F32)
            at = p * cols
            for which in range(3):
                qkv_ref[:, which, at : at + cols] = big[:, which * cols : (which + 1) * cols]
            gate_ref[:, at : at + cols] = big[:, 3 * cols :]
            for i in range(chains):
                head = p * chains + i
                w1_ref[head] = small[:, i * inner_share : (i + 1) * inner_share]
                w2_ref[head] = small[:, (chains + i) * inner_share : (chains + i + 1) * inner_share]
                for name, ref, size in (
                    ("lr", lrt_ref, depth), ("b1", b1_ref, inner_share), ("b2", b2_ref, head_share),
                    ("pg", pg_ref, head_share), ("pb", pb_ref, head_share),
                ):
                    row = spots[name] + i
                    ref[head : head + 1, :] = small[row : row + 1, side : side + size]
        for name, ref in (("n1", n1_ref), ("n2", n2_ref)):
            row = spots[name]
            total = jnp.zeros((1, depth), F32)
            for place in range(ring):
                lines = high_ref[place, depth - half :].astype(F32)
                total = total + lines[row : row + 1, side : side + depth]
            ref[...] = total

    halves_by_core(core, mine_ref, other_ref, work)


def fold_and_deal_kernel(place_ref, *refs, count):
    source_refs, out_refs = refs[:-count], refs[-count:]
    for bit, out_ref in enumerate(out_refs):
        which = place_ref[0] ^ bit
        if len(source_refs) > 1:
            values = [ref[which].astype(F32) for ref in source_refs]
        else:
            values = [source_refs[0][number, which].astype(F32) for number in range(source_refs[0].shape[0])]
        out_ref[...] = sum(values[1:], values[0]).astype(BF)


def fold_and_deal(sources, place, count):
    extent = sources[0].shape[-2:]
    return in_vmem(
        partial(fold_and_deal_kernel, count=count), "fold_and_deal", [(extent, BF)] * count, [], [place], *sources
    )


def add_and_deal_kernel(place_ref, keep_ref, other_ref, *out_refs):
    for bit, out_ref in enumerate(out_refs):
        which = place_ref[0] ^ bit
        out_ref[...] = (keep_ref[which].astype(F32) + other_ref[which].astype(F32)).astype(BF)


def in_vmem(kernel, name, shapes, scratch, scalars, *operands):
    vmem = pl.BlockSpec(memory_space=pltpu.VMEM)
    return pl.pallas_call(
        kernel,
        in_specs=[pl.BlockSpec(memory_space=pltpu.SMEM)] + [vmem] * len(operands),
        out_specs=[vmem] * len(shapes),
        out_shape=[jax.ShapeDtypeStruct(extent, dtype) for extent, dtype in shapes],
        scratch_shapes=[pltpu.VMEM(extent, F32) for extent in scratch],
        compiler_params=pltpu.CompilerParams(vmem_limit_bytes=40 << 20),
        name=name,
    )(jnp.stack(scalars).astype(jnp.int32), *operands)


def place_kernel(spots_ref, *refs):
    *sources, target = refs
    for number, source in enumerate(sources):
        target[spots_ref[number]] = source[...]


def placed(pieces, spots):
    return pl.pallas_call(
        place_kernel,
        in_specs=[pl.BlockSpec(memory_space=pltpu.SMEM)]
        + [pl.BlockSpec(memory_space=pltpu.VMEM)] * len(pieces),
        out_specs=pl.BlockSpec(memory_space=pltpu.VMEM),
        out_shape=jax.ShapeDtypeStruct((len(pieces),) + pieces[0].shape, pieces[0].dtype),
        compiler_params=pltpu.CompilerParams(vmem_limit_bytes=40 << 20),
        name="place_pieces",
    )(jnp.stack(spots).astype(jnp.int32), *pieces)


def exchanged(value, axis):
    size = lax.axis_size(axis)
    return [value] + [
        lax.ppermute(value, axis, [(source, source ^ bit) for source in range(size)])
        for bit in range(1, size)
    ]


def sent(taken, axis):
    return taken[:1] + [
        lax.ppermute(taken[bit], axis, [(source, source ^ bit) for source in range(len(taken))])
        for bit in range(1, len(taken))
    ]


def scattered(value, axis):
    size = lax.axis_size(axis)
    me = lax.axis_index(axis)
    return sent([lax.dynamic_index_in_dim(value, me ^ bit, 0, keepdims=False) for bit in range(size)], axis)


def placed_along(pieces, axis):
    me = lax.axis_index(axis)
    return placed(pieces, [me ^ bit for bit in range(len(pieces))])


def spread(value, axis):
    return placed_along(exchanged(value, axis), axis)


def tied(*values):
    return lax.optimization_barrier(values)


def in_turn(first, second):
    return jnp.where(lax.axis_index("tp") == 0, jnp.stack([first, second]), jnp.stack([second, first]))


def on_device(
    tokens,
    lengths,
    norm1_gain,
    qkv_weight,
    lr_weight,
    inner_w1,
    inner_b1,
    inner_w2,
    inner_b2,
    post_gain,
    post_bias,
    gate_weight,
    out_weight,
    norm2_gain,
    ffn_gate,
    ffn_up,
    ffn_down,
    cotangent,
):
    micro, span, width = tokens.shape
    ring = lax.axis_size("ctx")
    shards = lax.axis_size("shard")
    pair = lax.axis_size("tp")
    place = lax.axis_index("ctx")
    core = lax.axis_index("tp")
    local_heads, head_dim, inner_share = inner_w1.shape
    head_share = inner_b2.shape[1]
    depth = norm1_gain.shape[0]
    inner = inner_share * shards
    total_heads = local_heads * pair
    chains = -(-total_heads // ring)
    span_all = ring * span
    count = span_all // MINI
    cols = chains * head_dim
    wide = 4 * cols

    row_tokens = lax.dynamic_index_in_dim(tokens, core, 0, keepdims=False)
    token_parts = exchanged(row_tokens, "ctx")

    first_head = jnp.minimum(place * chains, total_heads - chains)
    owner = first_head // local_heads
    local_first = first_head - owner * local_heads

    packed = in_vmem(
        partial(pack_weights_kernel, chains=chains), "pack_weights",
        [((depth + SMALL, wide), BF)], [(SMALL, wide)], [local_first // chains],
        qkv_weight.reshape(depth, -1), gate_weight, lr_weight.T, norm1_gain[None], norm2_gain[None],
        inner_w1, inner_b1, inner_w2, inner_b2, post_gain, post_bias,
    )[0]
    half_rows = (depth + SMALL) // 2
    packed = jnp.where(core == owner, packed, swap(packed))
    gathered = exchanged(lax.dynamic_slice_in_dim(packed, core * half_rows, half_rows, 0), "shard")
    gathered, token_parts = tied(gathered, token_parts)

    units = ffn_gate.shape[1]
    half_out = out_weight.shape[0]
    row_pack = jnp.concatenate([ffn_gate, ffn_up, ffn_down.T, out_weight.T], axis=1)
    part = depth // ring
    cut = 3 * row_pack.shape[1] // 4 // 128 * 128
    row_near = row_pack[:, cut:]
    row_part = lax.dynamic_slice(row_pack, (place * part, 0), (part, cut))
    row_part, row_near, gathered = tied(row_part, row_near, gathered)
    row_parts = exchanged(row_part, "shard")
    slot_tokens = placed_along(token_parts, "ctx").reshape(span_all, width)
    gathered = placed_along(gathered, "shard")

    padded = -(-chains // 16) * 16
    w_chain, rate_rows, gain_row, gain_two, *rest = in_vmem(
        unpack_weights_kernel, "unpack_weights",
        [
            ((width, wide), BF), ((padded, width), BF), ((1, width), F32), ((1, width), F32),
            ((chains, head_dim, inner), F32), ((chains, 1, inner), F32),
            ((chains, head_dim, inner), F32), ((chains, 1, head_dim), F32),
            ((chains, 1, head_dim), F32), ((chains, 1, head_dim), F32),
        ],
        [(padded, width)], [core], gathered, swap(gathered),
    )
    state, (norm_gain, norm_bias) = tuple(rest[:4]), rest[4:]

    slot_length = lax.dynamic_index_in_dim(lengths, core, 0, keepdims=True)
    steps = span_all // (GROUP * MINI)
    middle = 3 * steps // 8

    def forward(first, last, begin):
        done = run_fwd(
            first, last, slot_length, slot_tokens, gain_row, w_chain, rate_rows, norm_gain, norm_bias, begin
        )
        return done[0], done[1:-4], done[-4:]

    post_low, saved_low, state_low = forward(0, middle, state)
    state_low, row_parts = tied(state_low, row_parts)
    far = jnp.stack(row_parts[1:])
    state_low, far = tied(state_low, far)
    row_near, far = tied(row_near, far)
    far_parts, near_parts = exchanged(far, "ctx"), lax.all_gather(row_near, "shard", axis=0)
    post_high, saved_high, _ = forward(middle, steps, tuple(state_low))
    post_high, far_parts, near_parts = tied(post_high, far_parts, near_parts)
    post_chain = jnp.concatenate([post_low, post_high])

    def to_rows(value):
        return lax.all_to_all(value.reshape(ring, span, -1), "ctx", 0, 0)

    post = to_rows(post_chain)

    number = jnp.stack([lax.axis_index("shard"), place]).astype(jnp.int32)
    w_own = run_assemble(number, row_pack, far_parts, near_parts).reshape(width, -1)
    w_other = swap(w_own)
    spots = jnp.stack([core, place * span, slot_length[0], place]).astype(jnp.int32)
    cot = lax.dynamic_index_in_dim(cotangent, core, 0, keepdims=False)
    output, grad_hidden, normed_two, grad_hidden_low, back_low, grad_gain_two, *kept = run_rows(
        spots, post, w_own, w_other, row_tokens, cot, gain_two, half_out
    )
    row_in = row_tokens.astype(F32)
    joined, acts = kept[:2], (kept[2:5], kept[5:8])

    def folded(values):
        return sum(value.astype(F32) for value in values).astype(BF)

    me = lax.axis_index("shard")

    def operands(half, second):
        if second:
            return (back_low, grad_hidden_low), (acts[half][2], joined[half])
        return (normed_two, normed_two), (acts[half][0], acts[half][1])

    def other_sums(second):
        return swap(run_sums(*operands(1, second)))

    def taken(second, other):
        if part % 16 == 0:
            if second:
                here = jnp.zeros((1,), jnp.int32)
                return run_sums(*operands(0, second), other, here, shards * ring)[0]
            here = jnp.stack([place]).astype(jnp.int32)
            return list(run_sums(*operands(0, second), other, here, shards, ring))
        own = run_sums(*operands(0, second)).astype(F32)
        both = (own + other.astype(F32)).astype(BF).reshape(shards, ring, part, -1)
        if second:
            return both
        return [lax.dynamic_index_in_dim(both, place ^ bit, 1, keepdims=False) for bit in range(ring)]

    grad_post = sent(list(kept[8:]), "ctx")

    def backward(first, last, base, begin, saved, written=None):
        done = run_bwd(
            first, last, base, slot_tokens, gain_row, w_chain, rate_rows, norm_gain, grad_post, sums, begin, saved, written
        )
        return done[0], tuple(done[1:])

    sums = ((width, wide), (padded, width), (1, width), (chains, 1, head_dim), (chains, 1, head_dim))
    sums += tuple(value.shape for value in state)
    other_a, other_b = other_sums(False), other_sums(True)
    (grad_post, sum_rights) = tied(grad_post, (other_a, other_b))
    taken_a, taken_b = taken(False, sum_rights[0]), taken(True, sum_rights[1])
    grad_post, taken_a, taken_b = tied(grad_post, taken_a, taken_b)
    grad_post = placed_along(grad_post, "ctx").reshape(span_all, cols)
    taken_b = taken_b.reshape(shards, ring, part, -1)
    sum_a, sum_b = sent(taken_a, "ctx"), lax.all_to_all(taken_b, "shard", 0, 0)
    back_high, ending = backward(middle, steps, middle, (), saved_high)
    ending, sum_a = tied(ending, sum_a)
    sum_a = fold_and_deal(sum_a, me, shards)
    ending, sum_a = tied(ending, sum_a)
    sum_a = sent(list(sum_a), "shard")
    back_low_half, ending = backward(0, middle, 0, ending, saved_low, back_high)
    ending, back_low_half, sum_a, sum_b = tied(ending, back_low_half, sum_a, sum_b)
    back_part = back_low_half
    grad_big, grad_lr, grad_gain_one, grad_norm_gain, grad_norm_bias, *grad_state = ending
    block = ((shards, half_rows, wide), BF)
    keep, send = in_vmem(
        pack_grads_kernel, "pack_grads", [block, block], [(SMALL, wide)], [core],
        grad_big, grad_lr, grad_gain_one, grad_gain_two, *grad_state, grad_norm_gain, grad_norm_bias,
    )
    dealt = in_vmem(
        add_and_deal_kernel, "add_and_deal", [((half_rows, wide), BF)] * shards, [],
        [lax.axis_index("shard")], keep, swap(send),
    )
    dealt, sum_b, back_part = tied(dealt, sum_b, back_part)
    chain_sum = sent(list(dealt), "shard")
    sum_b = sent(list(fold_and_deal([sum_b], place, ring)), "ctx")
    back_rows = to_rows(back_part)
    chain_sum, back_rows, sum_a, sum_b = tied(chain_sum, back_rows, sum_a, sum_b)
    chain_parts = exchanged(folded(chain_sum), "ctx")
    row_sum = jnp.concatenate([folded(sum_a), folded(sum_b)], axis=-1)
    chain_parts, row_sum = tied(chain_parts, row_sum)
    chain_sum = placed_along(chain_parts, "ctx")
    g_qkv, g_gate, g_lr, g_n1, g_n2, *g_rest = in_vmem(
        partial(unpack_grads_kernel, chains=chains), "unpack_grads",
        [
            ((depth, 3, local_heads * head_dim), F32), ((depth, local_heads * head_dim), F32),
            ((local_heads, depth), F32), ((1, depth), F32), ((1, depth), F32),
            (inner_w1.shape, F32), (inner_b1.shape, F32), (inner_w2.shape, F32), (inner_b2.shape, F32),
            (post_gain.shape, F32), (post_bias.shape, F32),
        ],
        [], [core], chain_sum, swap(chain_sum),
    )

    row_sum = spread(row_sum, "ctx")
    row_sum = row_sum.reshape(depth, -1).astype(F32)
    g_ffn_gate = row_sum[:, :units]
    g_ffn_up = row_sum[:, units : 2 * units]
    g_ffn_down = row_sum[:, 2 * units : 3 * units].T
    g_out = row_sum[:, 3 * units :].T

    back_one = jnp.sum(back_rows.astype(F32), axis=0)
    scale_one = row_scale(row_in)
    lifted = back_one * gain_row
    input_grad = (
        grad_hidden
        + scale_one * lifted
        - row_in * scale_one**3 * jnp.mean(lifted * row_in, axis=-1, keepdims=True)
    ).astype(BF)


    return (
        in_turn(output, swap(output)),
        in_turn(input_grad, swap(input_grad)),
        g_n1[0],
        g_qkv,
        g_lr.T,
        *g_rest,
        g_gate,
        g_out,
        g_n2[0],
        g_ffn_gate,
        g_ffn_up,
        g_ffn_down,
    )


def solution(mesh):
    in_specs = (
        P("shard", "ctx", None),
        P("shard"),
        P("shard"),
        P("shard", None, "tp"),
        P("shard", "tp"),
        P("tp", None, "shard"),
        P("tp", "shard"),
        P("tp", None, "shard"),
        P("tp", "shard"),
        P("tp", "shard"),
        P("tp", "shard"),
        P("shard", "tp"),
        P("tp", "shard"),
        P("shard"),
        P("shard", "tp"),
        P("shard", "tp"),
        P("tp", "shard"),
        P("shard", "ctx", None),
    )
    out_specs = (
        P("shard", "ctx", None),
        P("shard", "ctx", None),
        P("shard"),
        P("shard", None, "tp"),
        P("shard", "tp"),
        P("tp", None, "shard"),
        P("tp", "shard"),
        P("tp", None, "shard"),
        P("tp", "shard"),
        P("tp", "shard"),
        P("tp", "shard"),
        P("shard", "tp"),
        P("tp", "shard"),
        P("shard"),
        P("shard", "tp"),
        P("shard", "tp"),
        P("tp", "shard"),
    )
    return jax.shard_map(
        on_device, mesh=mesh, in_specs=in_specs, out_specs=out_specs, check_vma=False
    )
```

```python
from functools import partial
import jax
import jax.numpy as jnp
from jax import lax
from jax.experimental import pallas as pl
from jax.experimental.pallas import tpu as pltpu
from jax.sharding import PartitionSpec as P

MINI = 16
EPSILON = 1e-06
ETA_BASE = 0.5
BF = jnp.bfloat16
F32 = jnp.float32


def mm(left, right):
    return lax.dot_general(left, right, (((1,), (0,)), ((), ())), preferred_element_type=F32)


def mm_nt(left, right):
    return lax.dot_general(left, right, (((1,), (1,)), ((), ())), preferred_element_type=F32)


def mm_tn(left, right):
    return lax.dot_general(left, right, (((0,), (0,)), ((), ())), preferred_element_type=F32)


def gelu_parts(value):
    cdf = 0.5 + 0.5 * lax.erf(value * 0.7071067811865476)
    pdf = jnp.exp(-0.5 * value * value) * 0.3989422804014327
    return cdf, pdf


def row_scale(value):
    return lax.rsqrt(jnp.mean(value * value, axis=-1, keepdims=True) + EPSILON)


def mini_masks(rows):
    row = lax.broadcasted_iota(jnp.int32, (rows, rows), 0)
    col = lax.broadcasted_iota(jnp.int32, (rows, rows), 1)
    within = (lax.div(row, MINI) == lax.div(col, MINI)) & (col <= row)
    scale = jnp.where(within, 1.0 / (lax.rem(row, MINI) + 1).astype(F32), 0.0)
    return scale, jnp.where(row == col, 1.0 / MINI, 0.0)


def minis(value):
    return [value[at : at + MINI] for at in range(0, value.shape[0], MINI)]


def flat_rows(value):
    return value.reshape(value.shape[0] * value.shape[1], value.shape[2])


class Rows:
    def __init__(self, ref, start, size):
        self.ref, self.start, self.size = ref, start, size

    def spot(self, key):
        key = key if isinstance(key, tuple) else (key, slice(None))
        first, last = 0, self.size
        if len(key) == 3:
            first, last, _ = key[2].indices(self.size)
        return key[0], key[1], slice(self.start + first, self.start + last)

    def __getitem__(self, key):
        return self.ref[self.spot(key)]

    def __setitem__(self, key, value):
        self.ref[self.spot(key)] = value


class Plane:
    def __init__(self, ref, number, lane=None):
        self.ref, self.number = ref, number
        self.lanes = slice(None) if lane is None else slice(lane, lane + 1)

    def __getitem__(self, key):
        if isinstance(key, tuple):
            return self.ref[key[0], self.number, key[1] * MINI : (key[1] + 1) * MINI, self.lanes]
        return self.ref[key, self.number, :, self.lanes]

    def __setitem__(self, key, value):
        self.ref[key, self.number, :, self.lanes] = value


def named_parts(narrow_ref, plane_ref, state_ref, low_ref, high_ref):
    head_dim = narrow_ref.shape[3]
    return (
        Rows(narrow_ref, 0, 2 * MINI), Rows(narrow_ref, 2 * MINI, MINI),
        *(Plane(plane_ref, number) for number in range(3)), Plane(plane_ref, 3, 0), Plane(plane_ref, 3, 1),
        Rows(state_ref, 0, head_dim), Rows(state_ref, head_dim, head_dim),
        *(Rows(low_ref, at, MINI) for at in (0, MINI, 2 * MINI)),
        *(Rows(high_ref, at, MINI) for at in (0, MINI, 2 * MINI)),
    )


def fwd_kernel(
    length_ref, x_ref, gain_ref, wc_ref, lrt_ref, w1i_ref, c1i_ref, w2i_ref, c2i_ref, pg_ref, pb_ref,
    post_ref, fac_ref, narrow_ref, plane_ref, state_ref, low_ref, high_ref,
    w1_ref, c1_ref, w2_ref, c2_ref, kmv_ref, next_ref, kk_ref, pq_ref, c2s_ref, *, first,
):
    kq_ref, g2_ref, gl_ref, gs_ref, unit_ref, rate_ref, hscale_ref, w1s_ref, w2s_ref, h_ref, r_ref, g1_ref, *rest = (
        named_parts(narrow_ref, plane_ref, state_ref, low_ref, high_ref)
    )
    ga_ref, ug_ref, gp_ref = rest
    chains, group, _, head_dim = narrow_ref.shape
    rows = group * MINI
    cols = chains * head_dim
    every = range(chains)

    @pl.when(pl.program_id(0) == 0)
    def _():
        w1_ref[...] = w1i_ref[...]
        c1_ref[...] = c1i_ref[...]
        w2_ref[...] = w2i_ref[...]
        c2_ref[...] = c2i_ref[...]

    start = (first + pl.program_id(0)) * rows
    padded = lrt_ref.shape[0]
    x = x_ref[...].astype(F32)
    normed = (x * row_scale(x) * gain_ref[...]).astype(BF)
    proj = mm(normed, wc_ref[...])
    length = length_ref[0]
    live_col = start + lax.broadcasted_iota(jnp.int32, (rows, padded), 0) < length
    live_row = start + lax.broadcasted_iota(jnp.int32, (padded, rows), 1) < length
    eta_col = jnp.where(live_col, jax.nn.sigmoid(mm_nt(normed, lrt_ref[...])), 0.0) * (ETA_BASE / head_dim)
    rate = jax.nn.sigmoid(mm_nt(lrt_ref[...], normed))
    eta_row = jnp.where(live_row, rate, 0.0) * (ETA_BASE / head_dim)
    fac_ref[0, :padded] = eta_row * (1.0 - rate)
    fac_ref[0, padded:] = eta_row
    for i in every:
        at = i * head_dim
        k = proj[:, cols + at : cols + at + head_dim]
        v = proj[:, 2 * cols + at : 2 * cols + at + head_dim]
        kb, qb = k.astype(BF), proj[:, at : at + head_dim].astype(BF)
        k_minis = kb.reshape(group, MINI, head_dim)
        q_minis = qb.reshape(group, MINI, head_dim)
        kq_ref[i, :, :MINI] = k_minis
        kq_ref[i, :, MINI:] = q_minis
        next_ref[i, : group - 1, :MINI] = k_minis[1:]
        next_ref[i, group - 1 :, :MINI] = k_minis[:1]
        next_ref[i, :, MINI:] = q_minis
        kmv_ref[i] = (k - v).reshape(group, MINI, head_dim)
        rate_ref[i] = eta_col[:, i : i + 1] * (1.0 / MINI)
        cross = (mm_nt(kb, kb) + 1.0) * (eta_row[i : i + 1] * (1.0 / MINI))
        for j in range(group - 1):
            at = j * MINI
            kk_ref[i, j] = cross[at + MINI : at + 2 * MINI, at : at + MINI].astype(BF)

    key_pre = [mm(kq_ref[i, 0, :MINI], w1_ref[i].astype(BF)) + c1_ref[i] for i in every]
    for j in range(group):
        rate = [rate_ref[i, j] for i in every]
        kmv = [kmv_ref[i, j] for i in every]
        stacked = [next_ref[i, j] for i in every]
        k = [kq_ref[i, j, :MINI] for i in every]
        kk = [kk_ref[i, j] for i in every] if j < group - 1 else None
        w1 = [w1_ref[i] for i in every]
        w2 = [w2_ref[i] for i in every]
        c1 = [c1_ref[i] for i in every]
        c2 = [c2_ref[i] for i in every]
        w1b = [w1[i].astype(BF) for i in every]
        w2b = [w2[i].astype(BF) for i in every]
        parts = [gelu_parts(key_pre[i]) for i in every]
        hb = [(key_pre[i] * parts[i][0]).astype(BF) for i in every]
        g2 = [mm_nt(hb[i], w2b[i]) + c2[i] + kmv[i] for i in every]
        slope = [parts[i][0] + key_pre[i] * parts[i][1] for i in every]
        curve = [parts[i][1] * (2.0 - key_pre[i] * key_pre[i]) for i in every]
        both = [mm(stacked[i], w1b[i]) + c1[i] for i in every]
        g2b = [g2[i].astype(BF) for i in every]
        u = [mm(g2b[i], w2b[i]) for i in every]
        fg2 = [rate[i] * g2[i] for i in every]
        w2n = [w2[i] - mm_tn(fg2[i].astype(BF), hb[i]) for i in every]
        c2n = [c2[i] - jnp.sum(fg2[i], axis=0, keepdims=True) for i in every]
        g1 = [u[i] * slope[i] for i in every]
        g1b = [g1[i].astype(BF) for i in every]
        if j < group - 1:
            key_pre = [both[i][:MINI] - mm(kk[i], g1b[i]) for i in every]
        fg1 = [rate[i] * g1[i] for i in every]
        w1n = [w1[i] - mm_tn(k[i], fg1[i].astype(BF)) for i in every]
        c1n = [c1[i] - jnp.sum(fg1[i], axis=0, keepdims=True) for i in every]
        for i in every:
            w1s_ref[i, j] = w1b[i]
            w2s_ref[i, j] = w2b[i]
            c2s_ref[i, j] = c2[i]
            h_ref[i, j] = hb[i]
            g1_ref[i, j] = g1b[i]
            g2_ref[i, j] = g2b[i]
            ga_ref[i, j] = slope[i]
            ug_ref[i, j] = u[i] * curve[i]
            pq_ref[i, j] = both[i][MINI:]
            w1_ref[i] = w1n[i]
            w2_ref[i] = w2n[i]
            c1_ref[i] = c1n[i]
            c2_ref[i] = c2n[i]

    scale = mini_masks(rows)[0]
    for i in every:
        at = i * head_dim
        q = proj[:, at : at + head_dim]
        gate = proj[:, 3 * cols + at : 3 * cols + at + head_dim]
        kb, qb = flat_rows(kq_ref[i, :, :MINI]), flat_rows(kq_ref[i, :, MINI:])
        hb, g1b, g2b = flat_rows(h_ref[i]), flat_rows(g1_ref[i]), flat_rows(g2_ref[i])
        mix = scale * eta_row[i : i + 1]
        query_pre = flat_rows(pq_ref[i]) - mm((mix * (mm_nt(qb, kb) + 1.0)).astype(BF), g1b)
        cdf, pdf = gelu_parts(query_pre)
        gp_ref[i] = (cdf + query_pre * pdf).reshape(group, MINI, -1)
        rb = (query_pre * cdf).astype(BF)
        r_ref[i] = rb.reshape(group, MINI, -1)
        s2 = (mix * (mm_nt(rb, hb) + 1.0)).astype(BF)
        through = [mm_nt(piece, w2s_ref[i, j]) + c2s_ref[i, j] for j, piece in enumerate(minis(rb))]
        mixed = q + jnp.concatenate(through, axis=0) - mm(s2, g2b)
        centered = mixed - jnp.mean(mixed, axis=-1, keepdims=True)
        hscale = row_scale(centered)
        unit = centered * hscale
        out = unit * pg_ref[i] + pb_ref[i]
        cdf, pdf = gelu_parts(gate)
        post_ref[:, at : at + head_dim] = (gate * cdf * out).astype(BF)
        gl_ref[i] = gate * cdf
        gs_ref[i] = (cdf + gate * pdf) * out
        unit_ref[i] = unit
        hscale_ref[i] = hscale


def bwd_kernel(
    x_ref, gain_ref, wc_ref, lrt_ref, pg_ref, gpost_ref,
    fac_ref, narrow_ref, plane_ref, state_ref, low_ref, high_ref, *refs, begun,
):
    before, refs = (refs[:9], refs[10:]) if begun else ((), refs)
    (back_ref, gw_ref, glr_ref, gain_grad_ref, gpg_ref, gpb_ref, dw1_ref, dc1_ref, dw2_ref, dc2_ref, d_ref, g1a_ref, g2a_ref, ha_ref, ka_ref, dp_ref, kc_ref, dk_ref, da_ref, df_ref, de_ref, all_ref) = refs
    kq_ref, g2_ref, gl_ref, gs_ref, unit_ref, rate_ref, hscale_ref, w1s_ref, w2s_ref, h_ref, r_ref, g1_ref, *rest = (
        named_parts(narrow_ref, plane_ref, state_ref, low_ref, high_ref)
    )
    ga_ref, ug_ref, gp_ref = rest
    chains, group, _, head_dim = narrow_ref.shape
    rows = group * MINI
    cols = chains * head_dim
    every = range(chains)

    @pl.when(pl.program_id(0) == 0)
    def _():
        totals = (gw_ref, glr_ref, gain_grad_ref, gpg_ref, gpb_ref, dw1_ref, dc1_ref, dw2_ref, dc2_ref)
        for number, total in enumerate(totals):
            total[...] = before[number][...] if begun else jnp.zeros_like(total)

    scale, eye = mini_masks(rows)
    padded = lrt_ref.shape[0]
    gpost = gpost_ref[...].astype(F32)
    for i in every:
        at = i * head_dim
        piece = gpost[:, at : at + head_dim]
        all_ref[:, 3 * cols + at : 3 * cols + at + head_dim] = (piece * gs_ref[i]).astype(BF)
        head = piece * gl_ref[i]
        unit = unit_ref[i]
        gpg_ref[i] += jnp.sum(head * unit, axis=0, keepdims=True)
        gpb_ref[i] += jnp.sum(head, axis=0, keepdims=True)
        lifted = head * pg_ref[i]
        d = hscale_ref[i] * (
            lifted
            - jnp.mean(lifted, axis=-1, keepdims=True)
            - unit * jnp.mean(lifted * unit, axis=-1, keepdims=True)
        )
        d_ref[i] = d.reshape(group, MINI, head_dim)
        db = d.astype(BF)
        kb, qb = flat_rows(kq_ref[i, :, :MINI]), flat_rows(kq_ref[i, :, MINI:])
        hb, rb, g1b, g2b = (flat_rows(ref[i]) for ref in (h_ref, r_ref, g1_ref, g2_ref))
        mix = scale * fac_ref[0, padded + i : padded + i + 1]
        ds2 = -mm_nt(db, g2b)
        x2 = mm_nt(rb, hb) + 1.0
        x1 = mm_nt(qb, kb) + 1.0
        dx2 = (ds2 * mix).astype(BF)
        dr = jnp.concatenate([mm(part, w2s_ref[i, j]) for j, part in enumerate(minis(db))], axis=0)
        dp = (dr + mm(dx2, hb)) * flat_rows(gp_ref[i])
        dpb = dp.astype(BF)
        ds1 = -mm_nt(dpb, g1b)
        dx1 = (ds1 * mix).astype(BF)
        dq = jnp.concatenate([mm_nt(part, w1s_ref[i, j]) for j, part in enumerate(minis(dpb))], axis=0)
        all_ref[:, at : at + head_dim] = (d + dq + mm(dx1, kb)).astype(BF)
        g1a_ref[i] = -mm_tn((mix * x1).astype(BF), dpb).reshape(group, MINI, -1)
        g2a_ref[i] = -mm_tn((mix * x2).astype(BF), db).reshape(group, MINI, -1)
        ha_ref[i] = mm_tn(dx2, rb).reshape(group, MINI, -1)
        ka_ref[i] = mm_tn(dx1, qb).reshape(group, MINI, -1)
        dp_ref[i] = dpb.reshape(group, MINI, -1)
        de_ref[i] = jnp.sum((ds2 * x2 + ds1 * x1) * scale, axis=0, keepdims=True)
        kk = mm_nt(kb, kb) + 1.0
        kx = mm_nt(kb, qb) + 1.0
        for j in range(group - 1):
            own, after = slice(j * MINI, (j + 1) * MINI), slice((j + 1) * MINI, (j + 2) * MINI)
            kc_ref[i, j] = jnp.concatenate([kk[own, after], kx[own, after]], axis=1).astype(BF)

    t1 = [mm(kq_ref[i, group - 1, :MINI], dw1_ref[i].astype(BF)) + dc1_ref[i] for i in every]
    for j in reversed(range(group)):

        def all_of(ref):
            return [ref[i, j] for i in every]

        d, kq, rate, w2b, hb, rb, g1b, g2b = (
            all_of(ref) for ref in (d_ref, kq_ref, rate_ref, w2s_ref, h_ref, r_ref, g1_ref, g2_ref)
        )
        ga, ug, dpb, g1a, g2a, ha = (
            all_of(ref) for ref in (ga_ref, ug_ref, dp_ref, g1a_ref, g2a_ref, ha_ref)
        )
        dw1 = [dw1_ref[i] for i in every]
        dw2 = [dw2_ref[i] for i in every]
        dc1 = [dc1_ref[i] for i in every]
        dc2 = [dc2_ref[i] for i in every]
        g1 = [g1b[i].astype(F32) for i in every]
        g2 = [g2b[i].astype(F32) for i in every]
        dw1b = [dw1[i].astype(BF) for i in every]
        dw2b = [dw2[i].astype(BF) for i in every]
        dg1 = [g1a[i] - rate[i] * t1[i] for i in every]
        dub = [(dg1[i] * ga[i]).astype(BF) for i in every]
        through = [mm_nt(dub[i], w2b[i]) for i in every]
        t2 = [mm_nt(hb[i], dw2b[i]) + dc2[i] for i in every]
        dha = [ha[i] - mm((rate[i] * g2[i]).astype(BF), dw2b[i]) for i in every]
        dg2 = [through[i] + (g2a[i] - rate[i] * t2[i]) for i in every]
        dg2b = [dg2[i].astype(BF) for i in every]
        dh = [mm(dg2b[i], w2b[i]) + dha[i] for i in every]
        if j > 0:
            base = [mm(kq_ref[i, j - 1, :MINI], dw1b[i]) + dc1[i] for i in every]
        dk = [dg2[i] - mm_nt((rate[i] * g1[i]).astype(BF), dw1b[i]) for i in every]
        df = [
            -(
                jnp.sum(g1[i] * t1[i], axis=1, keepdims=True)
                + jnp.sum(g2[i] * t2[i], axis=1, keepdims=True)
            )
            for i in every
        ]
        da = [dg1[i] * ug[i] + dh[i] * ga[i] for i in every]
        dab = [da[i].astype(BF) for i in every]
        both = [jnp.concatenate([dab[i], dpb[i]], axis=0) for i in every]
        if j > 0:
            t1 = [base[i] + mm(kc_ref[i, j - 1], both[i]) for i in every]
        dw1n = [dw1[i] + mm_tn(kq[i], both[i]) for i in every]
        dc1n = [dc1[i] + jnp.sum(da[i] + dpb[i].astype(F32), axis=0, keepdims=True) for i in every]
        dw2n = [
            dw2[i]
            + mm_tn(
                jnp.concatenate([d[i].astype(BF), dg2b[i], g2b[i]], axis=0),
                jnp.concatenate([rb[i], hb[i], dub[i]], axis=0),
            )
            for i in every
        ]
        dc2n = [dc2[i] + jnp.sum(d[i] + dg2[i], axis=0, keepdims=True) for i in every]
        for i in every:
            piece, at = slice(j * MINI, (j + 1) * MINI), 2 * cols + i * head_dim
            all_ref[piece, at : at + head_dim] = (-dg2[i]).astype(BF)
            dk_ref[i, j] = dk[i]
            da_ref[i, j] = dab[i]
            df_ref[i, j] = df[i]
            dw1_ref[i] = dw1n[i]
            dc1_ref[i] = dc1n[i]
            dw2_ref[i] = dw2n[i]
            dc2_ref[i] = dc2n[i]

    x = x_ref[...].astype(F32)
    unit_in = x * row_scale(x)
    normed = (unit_in * gain_ref[...]).astype(BF)
    lrt = lrt_ref[...]
    which = lax.broadcasted_iota(jnp.int32, (padded, rows), 0)
    rates = jnp.zeros((padded, rows), F32)
    for i in every:
        at = cols + i * head_dim
        dk = jnp.concatenate([mm_nt(da_ref[i, j], w1s_ref[i, j]) for j in range(group)], axis=0)
        all_ref[:, at : at + head_dim] = (flat_rows(dk_ref[i]) + flat_rows(ka_ref[i]) + dk).astype(BF)
        line = de_ref[i] + jnp.sum(eye * flat_rows(df_ref[i]), axis=0, keepdims=True)
        rates = jnp.where(which == i, line, rates)
    rates = (rates * fac_ref[0, :padded]).astype(BF)
    grads = all_ref[...]
    back = mm_nt(grads, wc_ref[...]) + mm_tn(rates, lrt)
    gain_grad_ref[...] += jnp.sum(back * unit_in, axis=0, keepdims=True)
    back_ref[...] = back.astype(BF)
    gw_ref[...] += mm_tn(normed, grads)
    glr_ref[...] += mm(rates, normed)


GROUP = 8


def block_specs(chains, head_dim, inner, padded, place):
    rows = GROUP * MINI

    def mini(first, second):
        return pl.BlockSpec((chains, GROUP, first, second), lambda g: (0, place(g), 0, 0))

    return [
        pl.BlockSpec((1, 2 * padded, rows), lambda g: (place(g), 0, 0)),
        mini(3 * MINI, head_dim),
        pl.BlockSpec((chains, 4, rows, head_dim), lambda g: (0, 0, place(g), 0)),
        mini(2 * head_dim, inner), mini(3 * MINI, inner), mini(3 * MINI, inner),
    ]


def whole_spec(value):
    return pl.BlockSpec(value.shape, lambda g: (0,) * value.ndim)


def run_fwd(first, last, length, tokens, gain, wc, lrt, pg, pb, state):
    width = tokens.shape[1]
    chains, head_dim, inner = state[0].shape
    rows = GROUP * MINI
    steps = last - first
    count = steps * GROUP
    padded = lrt.shape[0]

    def mini(first_size, second_size, dtype):
        return jax.ShapeDtypeStruct((chains, count, first_size, second_size), dtype)

    row_spec = pl.BlockSpec((rows, width), lambda g: (first + g, 0))
    small = (gain, wc, lrt, *state, pg, pb)
    return pl.pallas_call(
        partial(fwd_kernel, first=first),
        grid=(steps,),
        in_specs=[pl.BlockSpec(memory_space=pltpu.SMEM), row_spec] + [whole_spec(v) for v in small],
        out_specs=[pl.BlockSpec((rows, chains * head_dim), lambda g: (g, 0))]
        + block_specs(chains, head_dim, inner, padded, lambda g: g)
        + [whole_spec(v) for v in state],
        out_shape=[
            jax.ShapeDtypeStruct((steps * rows, chains * head_dim), BF),
            jax.ShapeDtypeStruct((steps, 2 * padded, rows), F32),
            mini(3 * MINI, head_dim, BF),
            jax.ShapeDtypeStruct((chains, 4, steps * rows, head_dim), F32),
            mini(2 * head_dim, inner, BF), mini(3 * MINI, inner, BF), mini(3 * MINI, inner, F32),
        ]
        + [jax.ShapeDtypeStruct(v.shape, F32) for v in state],
        scratch_shapes=[
            pltpu.VMEM((chains, GROUP, MINI, head_dim), F32),
            pltpu.VMEM((chains, GROUP, 2 * MINI, head_dim), BF),
            pltpu.VMEM((chains, GROUP, MINI, MINI), BF),
            pltpu.VMEM((chains, GROUP, MINI, inner), F32),
            pltpu.VMEM((chains, GROUP, 1, head_dim), F32),
        ],
        compiler_params=pltpu.CompilerParams(vmem_limit_bytes=50 << 20),
        cost_estimate=pl.CostEstimate(
            flops=9_000_000_000 * steps, bytes_accessed=5_000_000 * steps, transcendentals=0
        ),
        name="chain_forward",
    )(length, tokens, *small)


def run_bwd(first, last, base, tokens, gain, wc, lrt, pg, gpost, shapes, state, saved, written=None):
    begun = written is not None
    width = tokens.shape[1]
    chains, head_dim, inner = shapes[5]
    rows = GROUP * MINI
    padded = lrt.shape[0]
    wide = wc.shape[1]
    steps = last - first

    def place(g):
        return steps - 1 - g

    def shape(*extent):
        return jax.ShapeDtypeStruct(extent, F32)

    small = (gain, wc, lrt, pg)
    outs = [shape(*extent) for extent in shapes]

    def scratch(first_size, second_size, dtype):
        return pltpu.VMEM((chains, GROUP, first_size, second_size), dtype)

    return pl.pallas_call(
        partial(bwd_kernel, begun=begun),
        grid=(steps,),
        in_specs=[pl.BlockSpec((rows, width), lambda g: (first + place(g), 0))]
        + [whole_spec(v) for v in small]
        + [pl.BlockSpec((rows, chains * head_dim), lambda g: (first + place(g), 0))]
        + block_specs(chains, head_dim, inner, padded, lambda g: first - base + place(g))
        + [whole_spec(v) for v in state]
        + [pl.BlockSpec(memory_space=pl.ANY)] * begun,
        out_specs=[pl.BlockSpec((rows, width), lambda g: (first + place(g), 0))] + [whole_spec(v) for v in outs],
        out_shape=[jax.ShapeDtypeStruct(tokens.shape, BF)] + outs,
        input_output_aliases={21: 0} if begun else {},
        scratch_shapes=[
            scratch(MINI, head_dim, F32), scratch(MINI, inner, F32), scratch(MINI, head_dim, F32),
            scratch(MINI, inner, F32), scratch(MINI, head_dim, F32), scratch(MINI, inner, BF),
            scratch(MINI, 2 * MINI, BF), scratch(MINI, head_dim, F32), scratch(MINI, inner, BF),
            scratch(MINI, 1, F32), pltpu.VMEM((chains, 1, rows), F32), pltpu.VMEM((rows, wide), BF),
        ],
        compiler_params=pltpu.CompilerParams(vmem_limit_bytes=50 << 20),
        cost_estimate=pl.CostEstimate(
            flops=11_000_000_000 * steps, bytes_accessed=5_000_000 * steps, transcendentals=0
        ),
        name="chain_backward",
    )(tokens, *small, gpost, *saved, *state, *((written,) if begun else ()))


def swap(value):
    return lax.ppermute(value, "tp", [(0, 1), (1, 0)])


def rows_kernel(
    spot_ref, post_ref, own_ref, other_ref, x_ref, cot_ref, gain_ref,
    out_ref, grad_ref, normed_ref, low_ref, back_ref, gain_grad_ref, cat0_ref, cat1_ref, *act_refs,
):
    *act_refs, gpost_ref = act_refs
    core, start, length = spot_ref[0], spot_ref[1], spot_ref[2]
    span, width = x_ref.shape
    cols = post_ref.shape[2]
    units = act_refs[0].shape[1]
    places = cat0_ref.shape[1] // cols
    x = x_ref[...].astype(F32)
    live = start + lax.broadcasted_iota(jnp.int32, (span, width), 0) < length
    back = jnp.where(live, cot_ref[...].astype(F32), 0.0)
    back_low = back.astype(BF)
    back_ref[...] = back_low
    halves = ((own_ref, core), (other_ref, 1 - core))
    hidden = x
    for half, (w_ref, side) in enumerate(halves):
        joined = jnp.concatenate([post_ref[side * places + p] for p in range(places)], axis=1)
        (cat0_ref, cat1_ref)[half][...] = joined
        hidden = hidden + mm_nt(joined, w_ref[:, 3 * units :])
    scale = row_scale(hidden)
    gain = gain_ref[...]
    normed = (hidden * scale * gain).astype(BF)
    normed_ref[...] = normed
    feed = jnp.zeros((span, width), F32)
    grad = jnp.zeros((span, width), F32)
    step = min(units, 512)
    for half, (w_ref, _) in enumerate(halves):
        for at in range(0, units, step):
            w_gate = w_ref[:, at : at + step]
            w_up = w_ref[:, units + at : units + at + step]
            w_down = w_ref[:, 2 * units + at : 2 * units + at + step]
            up_gate = mm(normed, w_gate)
            up_lin = mm(normed, w_up)
            grad_act = mm(back_low, w_down)
            gate = jax.nn.sigmoid(up_gate)
            silu = up_gate * gate
            act = (silu * up_lin).astype(BF)
            grad_gate = (grad_act * up_lin * (gate * (1.0 + up_gate * (1.0 - gate)))).astype(BF)
            grad_lin = (grad_act * silu).astype(BF)
            act_refs[3 * half + 0][:, at : at + step] = grad_gate
            act_refs[3 * half + 1][:, at : at + step] = grad_lin
            act_refs[3 * half + 2][:, at : at + step] = act
            feed += mm_nt(act, w_down)
            grad += mm_nt(grad_gate, w_gate) + mm_nt(grad_lin, w_up)
    out_ref[...] = (hidden + feed).astype(BF)
    lifted = grad * gain
    hat = hidden * scale
    gain_grad_ref[...] = jnp.sum(grad * hat, axis=0, keepdims=True)
    total = back + scale * (lifted - hat * jnp.mean(lifted * hat, axis=-1, keepdims=True))
    grad_ref[...] = total
    low = total.astype(BF)
    low_ref[...] = low
    for p in range(2 * places, gpost_ref.shape[0]):
        gpost_ref[p] = jnp.zeros(gpost_ref.shape[1:], BF)
    deal_refs = act_refs[6:]
    for w_ref, side in halves:
        gpost = mm(low, w_ref[:, 3 * units :]).astype(BF)
        for p in range(places):
            gpost_ref[side * places + p] = gpost[:, p * cols : (p + 1) * cols]
    for bit, deal_ref in enumerate(deal_refs):
        deal_ref[...] = gpost_ref[spot_ref[3] ^ bit]


def run_rows(spots, post, own, other, x, cot, gain, half_out):
    ring, span, cols = post.shape
    width = x.shape[1]
    units = (own.shape[1] - half_out) // 3
    vmem = pl.BlockSpec(memory_space=pltpu.VMEM)

    def shape(extent, dtype):
        return jax.ShapeDtypeStruct(extent, dtype)

    return pl.pallas_call(
        rows_kernel,
        in_specs=[pl.BlockSpec(memory_space=pltpu.SMEM)] + [vmem] * 6,
        out_specs=[vmem] * (14 + ring),
        out_shape=[
            shape((span, width), BF), shape((span, width), F32),
            shape((span, width), BF), shape((span, width), BF), shape((span, width), BF), shape((1, width), F32),
        ]
        + [shape((span, half_out), BF)] * 2
        + [shape((span, units), BF)] * 6
        + [shape((span, cols), BF)] * ring,
        scratch_shapes=[pltpu.VMEM((ring, span, cols), BF)],
        compiler_params=pltpu.CompilerParams(vmem_limit_bytes=52 << 20),
        cost_estimate=pl.CostEstimate(flops=20_000_000_000, bytes_accessed=20_000_000, transcendentals=0),
        name="rows_main",
    )(spots, post, own, other, x, cot, gain)


def products(pairs, parts, store):
    start = 0
    for left, right in zip(pairs, parts):
        size = right.shape[-1]
        step = 512 if size % 512 == 0 else size
        for at in range(0, size, step):
            store(start + at, mm_tn(left[...], right[:, at : at + step]))
        start += size


def sums_other_kernel(*refs):
    *sources, out_ref = refs
    count = len(sources) // 2

    def store(at, value):
        out_ref[:, at : at + value.shape[1]] = value.astype(BF)

    products(sources[:count], sources[count:], store)


def sums_own_kernel(place_ref, other_ref, *refs, count, outs):
    sources, out_refs, held_ref = refs[: 2 * count], refs[2 * count : 2 * count + outs], refs[-1]

    def store(at, value):
        piece = slice(at, at + value.shape[1])
        held_ref[:, piece] = (value + other_ref[:, piece].astype(F32)).astype(BF)

    products(sources[:count], sources[count:], store)
    for bit, out_ref in enumerate(out_refs):
        blocks, part = out_ref.shape[:2]
        for number in range(blocks):
            at = pl.multiple_of((number * outs + (place_ref[0] ^ bit)) * part, part)
            out_ref[number] = held_ref[pl.ds(at, part), :]


def run_sums(lefts, rights, other=None, place=None, blocks=1, outs=1):
    width = lefts[0].shape[1]
    total = sum(right.shape[1] for right in rights)
    vmem = pl.BlockSpec(memory_space=pltpu.VMEM)
    count = len(lefts)
    params = pltpu.CompilerParams(vmem_limit_bytes=40 << 20)
    cost = pl.CostEstimate(flops=5_000_000_000, bytes_accessed=6_000_000, transcendentals=0)
    if other is None:
        return pl.pallas_call(
            sums_other_kernel,
            in_specs=[vmem] * (2 * count),
            out_specs=vmem,
            out_shape=jax.ShapeDtypeStruct((width, total), BF),
            compiler_params=params,
            cost_estimate=cost,
            name="sums_other",
        )(*lefts, *rights)
    part = width // (blocks * outs)
    return pl.pallas_call(
        partial(sums_own_kernel, count=count, outs=outs),
        in_specs=[pl.BlockSpec(memory_space=pltpu.SMEM)] + [vmem] * (2 * count + 1),
        out_specs=[vmem] * outs,
        out_shape=[jax.ShapeDtypeStruct((blocks, part, total), BF)] * outs,
        scratch_shapes=[pltpu.VMEM((width, total), BF)],
        compiler_params=params,
        cost_estimate=cost,
        name="sums_own",
    )(place, other, *lefts, *rights)


def assemble_kernel(spots_ref, pack_ref, *refs, ring):
    far_refs, near_ref, out_ref = refs[:ring], refs[ring], refs[-1]
    me, place = spots_ref[0], spots_ref[1]
    part = out_ref.shape[1]
    cut = far_refs[0].shape[2]
    for number in range(ring):
        piece = slice(number * part, (number + 1) * part)
        out_ref[me * ring + number, :, :cut] = pack_ref[piece, :cut]
        for z in range(near_ref.shape[0]):
            out_ref[z * ring + number, :, cut:] = near_ref[z, piece]
    for bit, far_ref in enumerate(far_refs):
        for other in range(far_ref.shape[0]):
            out_ref[(me ^ (other + 1)) * ring + (place ^ bit), :, :cut] = far_ref[other]


def run_assemble(spots, pack, far_parts, near_parts):
    vmem = pl.BlockSpec(memory_space=pltpu.VMEM)
    ring = len(far_parts)
    part = pack.shape[0] // ring
    return pl.pallas_call(
        partial(assemble_kernel, ring=ring),
        in_specs=[pl.BlockSpec(memory_space=pltpu.SMEM)] + [vmem] * (2 + ring),
        out_specs=vmem,
        out_shape=jax.ShapeDtypeStruct((near_parts.shape[0] * ring, part, pack.shape[1]), BF),
        compiler_params=pltpu.CompilerParams(vmem_limit_bytes=40 << 20),
        name="assemble_rows",
    )(spots, pack, *far_parts, near_parts)


SMALL = 64


def small_spots(chains, depth, inner_share):
    side = 2 * chains * inner_share
    return side, {
        "lr": 0, "n1": chains, "n2": chains + 1, "b1": chains + 2,
        "b2": 2 * chains + 2, "pg": 3 * chains + 2, "pb": 4 * chains + 2,
    }


def pack_weights_kernel(
    pick_ref, qkv_ref, gate_ref, lr_ref, n1_ref, n2_ref, w1_ref, b1_ref, w2_ref, b2_ref, pg_ref, pb_ref,
    out_ref, small_ref, *, chains,
):
    depth = gate_ref.shape[0]
    heads, head_dim, inner_share = w1_ref.shape
    cols = chains * head_dim
    all_cols = heads * head_dim
    side, spots = small_spots(chains, depth, inner_share)
    small_ref[...] = jnp.zeros_like(small_ref)

    def put(name, i, value):
        row = spots[name] + i
        small_ref[row : row + 1, side : side + value.shape[1]] = value.astype(F32)

    for option in range(heads // chains):

        @pl.when(pick_ref[0] == option)
        def _():
            at = option * cols
            for which in range(3):
                start = which * all_cols + at
                out_ref[:depth, which * cols : (which + 1) * cols] = qkv_ref[:, start : start + cols]
            out_ref[:depth, 3 * cols :] = gate_ref[:, at : at + cols]
            for i in range(chains):
                head = option * chains + i
                lanes = slice(i * inner_share, (i + 1) * inner_share)
                small_ref[:, lanes] = w1_ref[head].astype(F32)
                lanes = slice((chains + i) * inner_share, (chains + i + 1) * inner_share)
                small_ref[:, lanes] = w2_ref[head].astype(F32)
                for name, ref in (("lr", lr_ref), ("b1", b1_ref), ("b2", b2_ref), ("pg", pg_ref), ("pb", pb_ref)):
                    put(name, i, ref[head : head + 1, :])

    put("n1", 0, n1_ref[...])
    put("n2", 0, n2_ref[...])
    out_ref[depth:, :] = small_ref[...].astype(BF)


def halves_by_core(core, mine_ref, other_ref, work):
    @pl.when(core == 0)
    def _():
        work(mine_ref, other_ref)

    @pl.when(core != 0)
    def _():
        work(other_ref, mine_ref)


def unpack_weights_kernel(
    core_ref, mine_ref, other_ref,
    wc_ref, lrt_ref, n1_ref, n2_ref, w1_ref, b1_ref, w2_ref, b2_ref, pg_ref, pb_ref, lines_ref,
):
    shards, half, _ = mine_ref.shape
    chains, _, inner = w1_ref.shape
    inner_share = inner // shards
    depth = 2 * half - SMALL
    head_share = b2_ref.shape[2] // shards
    side, spots = small_spots(chains, depth, inner_share)
    lines_ref[...] = jnp.zeros_like(lines_ref)

    def work(low_ref, high_ref):
        for z in range(shards):
            wc_ref[z * depth : z * depth + half] = low_ref[z]
            wc_ref[z * depth + half : (z + 1) * depth] = high_ref[z, : depth - half]
            small = high_ref[z, depth - half :].astype(F32)

            def get(name, i, size):
                row = spots[name] + i
                return small[row : row + 1, side : side + size]

            here = slice(z * depth, (z + 1) * depth)
            n1_ref[:, here] = get("n1", 0, depth)
            n2_ref[:, here] = get("n2", 0, depth)
            for i in range(chains):
                lines_ref[i : i + 1, here] = get("lr", i, depth)
                lanes = slice(z * inner_share, (z + 1) * inner_share)
                w1_ref[i, :, lanes] = small[:, i * inner_share : (i + 1) * inner_share]
                w2_ref[i, :, lanes] = small[:, (chains + i) * inner_share : (chains + i + 1) * inner_share]
                b1_ref[i, :, lanes] = get("b1", i, inner_share)
                lanes = slice(z * head_share, (z + 1) * head_share)
                for name, ref in (("b2", b2_ref), ("pg", pg_ref), ("pb", pb_ref)):
                    ref[i, :, lanes] = get(name, i, head_share)

    halves_by_core(core_ref[0], mine_ref, other_ref, work)
    lrt_ref[...] = lines_ref[...].astype(BF)


def pack_grads_kernel(
    core_ref, gw_ref, glr_ref, n1_ref, n2_ref, w1_ref, b1_ref, w2_ref, b2_ref, pg_ref, pb_ref,
    keep_ref, send_ref, small_ref,
):
    shards, half, _ = keep_ref.shape
    chains, _, inner = w1_ref.shape
    inner_share = inner // shards
    depth = 2 * half - SMALL
    head_share = b2_ref.shape[2] // shards
    side, spots = small_spots(chains, depth, inner_share)

    def work(low_ref, high_ref):
        for z in range(shards):
            small_ref[...] = jnp.zeros_like(small_ref)

            def put(name, i, value):
                row = spots[name] + i
                small_ref[row : row + 1, side : side + value.shape[1]] = value

            here = slice(z * depth, (z + 1) * depth)
            low_ref[z] = gw_ref[z * depth : z * depth + half].astype(BF)
            high_ref[z, : depth - half] = gw_ref[z * depth + half : (z + 1) * depth].astype(BF)
            put("n1", 0, n1_ref[:, here])
            put("n2", 0, n2_ref[:, here])
            for i in range(chains):
                put("lr", i, glr_ref[i : i + 1, here])
                lanes = slice(z * inner_share, (z + 1) * inner_share)
                small_ref[:, i * inner_share : (i + 1) * inner_share] = w1_ref[i, :, lanes]
                small_ref[:, (chains + i) * inner_share : (chains + i + 1) * inner_share] = w2_ref[i, :, lanes]
                put("b1", i, b1_ref[i, :, lanes])
                lanes = slice(z * head_share, (z + 1) * head_share)
                for name, ref in (("b2", b2_ref), ("pg", pg_ref), ("pb", pb_ref)):
                    put(name, i, ref[i, :, lanes])
            high_ref[z, depth - half :] = small_ref[...].astype(BF)

    halves_by_core(core_ref[0], keep_ref, send_ref, work)


def unpack_grads_kernel(
    core_ref, mine_ref, other_ref,
    qkv_ref, gate_ref, lrt_ref, n1_ref, n2_ref, w1_ref, b1_ref, w2_ref, b2_ref, pg_ref, pb_ref, *, chains,
):
    ring, half, wide = mine_ref.shape
    cols = wide // 4
    heads, _, inner_share = w1_ref.shape
    depth = gate_ref.shape[0]
    head_share = b2_ref.shape[1]
    places = heads // chains
    side, spots = small_spots(chains, depth, inner_share)
    core = core_ref[0]

    def work(low_ref, high_ref):
        for p in range(places):
            place = core * places + p
            big = jnp.concatenate([low_ref[place], high_ref[place, : depth - half]], axis=0).astype(F32)
            small = high_ref[place, depth - half :].astype(F32)
            at = p * cols
            for which in range(3):
                qkv_ref[:, which, at : at + cols] = big[:, which * cols : (which + 1) * cols]
            gate_ref[:, at : at + cols] = big[:, 3 * cols :]
            for i in range(chains):
                head = p * chains + i
                w1_ref[head] = small[:, i * inner_share : (i + 1) * inner_share]
                w2_ref[head] = small[:, (chains + i) * inner_share : (chains + i + 1) * inner_share]
                for name, ref, size in (
                    ("lr", lrt_ref, depth), ("b1", b1_ref, inner_share), ("b2", b2_ref, head_share),
                    ("pg", pg_ref, head_share), ("pb", pb_ref, head_share),
                ):
                    row = spots[name] + i
                    ref[head : head + 1, :] = small[row : row + 1, side : side + size]
        for name, ref in (("n1", n1_ref), ("n2", n2_ref)):
            row = spots[name]
            total = jnp.zeros((1, depth), F32)
            for place in range(ring):
                lines = high_ref[place, depth - half :].astype(F32)
                total = total + lines[row : row + 1, side : side + depth]
            ref[...] = total

    halves_by_core(core, mine_ref, other_ref, work)


def fold_and_deal_kernel(place_ref, *refs, count):
    source_refs, out_refs = refs[:-count], refs[-count:]
    for bit, out_ref in enumerate(out_refs):
        which = place_ref[0] ^ bit
        if len(source_refs) > 1:
            values = [ref[which].astype(F32) for ref in source_refs]
        else:
            values = [source_refs[0][number, which].astype(F32) for number in range(source_refs[0].shape[0])]
        out_ref[...] = sum(values[1:], values[0]).astype(BF)


def fold_and_deal(sources, place, count):
    extent = sources[0].shape[-2:]
    return in_vmem(
        partial(fold_and_deal_kernel, count=count), "fold_and_deal", [(extent, BF)] * count, [], [place], *sources
    )


def add_and_deal_kernel(place_ref, keep_ref, other_ref, *out_refs):
    for bit, out_ref in enumerate(out_refs):
        which = place_ref[0] ^ bit
        out_ref[...] = (keep_ref[which].astype(F32) + other_ref[which].astype(F32)).astype(BF)


def in_vmem(kernel, name, shapes, scratch, scalars, *operands):
    vmem = pl.BlockSpec(memory_space=pltpu.VMEM)
    return pl.pallas_call(
        kernel,
        in_specs=[pl.BlockSpec(memory_space=pltpu.SMEM)] + [vmem] * len(operands),
        out_specs=[vmem] * len(shapes),
        out_shape=[jax.ShapeDtypeStruct(extent, dtype) for extent, dtype in shapes],
        scratch_shapes=[pltpu.VMEM(extent, F32) for extent in scratch],
        compiler_params=pltpu.CompilerParams(vmem_limit_bytes=40 << 20),
        name=name,
    )(jnp.stack(scalars).astype(jnp.int32), *operands)


def place_kernel(spots_ref, *refs):
    *sources, target = refs
    for number, source in enumerate(sources):
        target[spots_ref[number]] = source[...]


def placed(pieces, spots):
    return pl.pallas_call(
        place_kernel,
        in_specs=[pl.BlockSpec(memory_space=pltpu.SMEM)]
        + [pl.BlockSpec(memory_space=pltpu.VMEM)] * len(pieces),
        out_specs=pl.BlockSpec(memory_space=pltpu.VMEM),
        out_shape=jax.ShapeDtypeStruct((len(pieces),) + pieces[0].shape, pieces[0].dtype),
        compiler_params=pltpu.CompilerParams(vmem_limit_bytes=40 << 20),
        name="place_pieces",
    )(jnp.stack(spots).astype(jnp.int32), *pieces)


def exchanged(value, axis):
    size = lax.axis_size(axis)
    return [value] + [
        lax.ppermute(value, axis, [(source, source ^ bit) for source in range(size)])
        for bit in range(1, size)
    ]


def sent(taken, axis):
    return taken[:1] + [
        lax.ppermute(taken[bit], axis, [(source, source ^ bit) for source in range(len(taken))])
        for bit in range(1, len(taken))
    ]


def scattered(value, axis):
    size = lax.axis_size(axis)
    me = lax.axis_index(axis)
    return sent([lax.dynamic_index_in_dim(value, me ^ bit, 0, keepdims=False) for bit in range(size)], axis)


def placed_along(pieces, axis):
    me = lax.axis_index(axis)
    return placed(pieces, [me ^ bit for bit in range(len(pieces))])


def spread(value, axis):
    return placed_along(exchanged(value, axis), axis)


def tied(*values):
    return lax.optimization_barrier(values)


def in_turn(first, second):
    return jnp.where(lax.axis_index("tp") == 0, jnp.stack([first, second]), jnp.stack([second, first]))


def on_device(
    tokens,
    lengths,
    norm1_gain,
    qkv_weight,
    lr_weight,
    inner_w1,
    inner_b1,
    inner_w2,
    inner_b2,
    post_gain,
    post_bias,
    gate_weight,
    out_weight,
    norm2_gain,
    ffn_gate,
    ffn_up,
    ffn_down,
    cotangent,
):
    micro, span, width = tokens.shape
    ring = lax.axis_size("ctx")
    shards = lax.axis_size("shard")
    pair = lax.axis_size("tp")
    place = lax.axis_index("ctx")
    core = lax.axis_index("tp")
    local_heads, head_dim, inner_share = inner_w1.shape
    head_share = inner_b2.shape[1]
    depth = norm1_gain.shape[0]
    inner = inner_share * shards
    total_heads = local_heads * pair
    chains = -(-total_heads // ring)
    span_all = ring * span
    count = span_all // MINI
    cols = chains * head_dim
    wide = 4 * cols

    row_tokens = lax.dynamic_index_in_dim(tokens, core, 0, keepdims=False)
    token_parts = exchanged(row_tokens, "ctx")

    first_head = jnp.minimum(place * chains, total_heads - chains)
    owner = first_head // local_heads
    local_first = first_head - owner * local_heads

    packed = in_vmem(
        partial(pack_weights_kernel, chains=chains), "pack_weights",
        [((depth + SMALL, wide), BF)], [(SMALL, wide)], [local_first // chains],
        qkv_weight.reshape(depth, -1), gate_weight, lr_weight.T, norm1_gain[None], norm2_gain[None],
        inner_w1, inner_b1, inner_w2, inner_b2, post_gain, post_bias,
    )[0]
    half_rows = (depth + SMALL) // 2
    packed = jnp.where(core == owner, packed, swap(packed))
    gathered = exchanged(lax.dynamic_slice_in_dim(packed, core * half_rows, half_rows, 0), "shard")
    gathered, token_parts = tied(gathered, token_parts)

    units = ffn_gate.shape[1]
    half_out = out_weight.shape[0]
    row_pack = jnp.concatenate([ffn_gate, ffn_up, ffn_down.T, out_weight.T], axis=1)
    part = depth // ring
    cut = 3 * row_pack.shape[1] // 4 // 128 * 128
    row_near = row_pack[:, cut:]
    row_part = lax.dynamic_slice(row_pack, (place * part, 0), (part, cut))
    row_part, row_near, gathered = tied(row_part, row_near, gathered)
    row_parts = exchanged(row_part, "shard")
    slot_tokens = placed_along(token_parts, "ctx").reshape(span_all, width)
    gathered = placed_along(gathered, "shard")

    padded = -(-chains // 16) * 16
    w_chain, rate_rows, gain_row, gain_two, *rest = in_vmem(
        unpack_weights_kernel, "unpack_weights",
        [
            ((width, wide), BF), ((padded, width), BF), ((1, width), F32), ((1, width), F32),
            ((chains, head_dim, inner), F32), ((chains, 1, inner), F32),
            ((chains, head_dim, inner), F32), ((chains, 1, head_dim), F32),
            ((chains, 1, head_dim), F32), ((chains, 1, head_dim), F32),
        ],
        [(padded, width)], [core], gathered, swap(gathered),
    )
    state, (norm_gain, norm_bias) = tuple(rest[:4]), rest[4:]

    slot_length = lax.dynamic_index_in_dim(lengths, core, 0, keepdims=True)
    steps = span_all // (GROUP * MINI)
    middle = 3 * steps // 8

    def forward(first, last, begin):
        done = run_fwd(
            first, last, slot_length, slot_tokens, gain_row, w_chain, rate_rows, norm_gain, norm_bias, begin
        )
        return done[0], done[1:-4], done[-4:]

    post_low, saved_low, state_low = forward(0, middle, state)
    state_low, row_parts = tied(state_low, row_parts)
    far = jnp.stack(row_parts[1:])
    state_low, far = tied(state_low, far)
    row_near, far = tied(row_near, far)
    far_parts, near_parts = exchanged(far, "ctx"), lax.all_gather(row_near, "shard", axis=0)
    post_high, saved_high, _ = forward(middle, steps, tuple(state_low))
    post_high, far_parts, near_parts = tied(post_high, far_parts, near_parts)
    post_chain = jnp.concatenate([post_low, post_high])

    def to_rows(value):
        return lax.all_to_all(value.reshape(ring, span, -1), "ctx", 0, 0)

    post = to_rows(post_chain)

    number = jnp.stack([lax.axis_index("shard"), place]).astype(jnp.int32)
    w_own = run_assemble(number, row_pack, far_parts, near_parts).reshape(width, -1)
    w_other = swap(w_own)
    spots = jnp.stack([core, place * span, slot_length[0], place]).astype(jnp.int32)
    cot = lax.dynamic_index_in_dim(cotangent, core, 0, keepdims=False)
    output, grad_hidden, normed_two, grad_hidden_low, back_low, grad_gain_two, *kept = run_rows(
        spots, post, w_own, w_other, row_tokens, cot, gain_two, half_out
    )
    row_in = row_tokens.astype(F32)
    joined, acts = kept[:2], (kept[2:5], kept[5:8])

    def folded(values):
        return sum(value.astype(F32) for value in values).astype(BF)

    me = lax.axis_index("shard")

    def operands(half, second):
        if second:
            return (back_low, grad_hidden_low), (acts[half][2], joined[half])
        return (normed_two, normed_two), (acts[half][0], acts[half][1])

    def other_sums(second):
        return swap(run_sums(*operands(1, second)))

    def taken(second, other):
        if part % 16 == 0:
            if second:
                here = jnp.zeros((1,), jnp.int32)
                return run_sums(*operands(0, second), other, here, shards * ring)[0]
            here = jnp.stack([place]).astype(jnp.int32)
            return list(run_sums(*operands(0, second), other, here, shards, ring))
        own = run_sums(*operands(0, second)).astype(F32)
        both = (own + other.astype(F32)).astype(BF).reshape(shards, ring, part, -1)
        if second:
            return both
        return [lax.dynamic_index_in_dim(both, place ^ bit, 1, keepdims=False) for bit in range(ring)]

    grad_post = sent(list(kept[8:]), "ctx")

    def backward(first, last, base, begin, saved, written=None):
        done = run_bwd(
            first, last, base, slot_tokens, gain_row, w_chain, rate_rows, norm_gain, grad_post, sums, begin, saved, written
        )
        return done[0], tuple(done[1:])

    sums = ((width, wide), (padded, width), (1, width), (chains, 1, head_dim), (chains, 1, head_dim))
    sums += tuple(value.shape for value in state)
    other_a, other_b = other_sums(False), other_sums(True)
    (grad_post, sum_rights) = tied(grad_post, (other_a, other_b))
    taken_a, taken_b = taken(False, sum_rights[0]), taken(True, sum_rights[1])
    grad_post, taken_a, taken_b, other_out = tied(grad_post, taken_a, taken_b, swap(output))
    grad_post = placed_along(grad_post, "ctx").reshape(span_all, cols)
    taken_b = taken_b.reshape(shards, ring, part, -1)
    sum_a, sum_b = sent(taken_a, "ctx"), lax.all_to_all(taken_b, "shard", 0, 0)
    back_high, ending = backward(middle, steps, middle, (), saved_high)
    ending, sum_a = tied(ending, sum_a)
    sum_a = fold_and_deal(sum_a, me, shards)
    _, sum_b = tied(sum_a[0], sum_b)
    sum_a = sent(list(sum_a), "shard")
    sum_b = folded([sum_b[number] for number in range(shards)])
    ending, sum_b = tied(ending, sum_b)
    sum_b = lax.psum_scatter(sum_b, "ctx", scatter_dimension=0, tiled=False)
    back_low_half, ending = backward(0, middle, 0, ending, saved_low, back_high)
    ending, back_low_half, sum_a, sum_b = tied(ending, back_low_half, sum_a, sum_b)
    back_part = back_low_half
    grad_big, grad_lr, grad_gain_one, grad_norm_gain, grad_norm_bias, *grad_state = ending
    block = ((shards, half_rows, wide), BF)
    keep, send = in_vmem(
        pack_grads_kernel, "pack_grads", [block, block], [(SMALL, wide)], [core],
        grad_big, grad_lr, grad_gain_one, grad_gain_two, *grad_state, grad_norm_gain, grad_norm_bias,
    )
    dealt = in_vmem(
        add_and_deal_kernel, "add_and_deal", [((half_rows, wide), BF)] * shards, [],
        [lax.axis_index("shard")], keep, swap(send),
    )
    back_rows = to_rows(back_part)
    chain_sum = sent(list(dealt), "shard")
    chain_sum, back_rows, sum_a, sum_b = tied(chain_sum, back_rows, sum_a, sum_b)
    chain_parts = exchanged(folded(chain_sum), "ctx")
    row_sum = jnp.concatenate([folded(sum_a), sum_b], axis=-1)
    chain_parts, row_sum = tied(chain_parts, row_sum)
    chain_sum = placed_along(chain_parts, "ctx")
    g_qkv, g_gate, g_lr, g_n1, g_n2, *g_rest = in_vmem(
        partial(unpack_grads_kernel, chains=chains), "unpack_grads",
        [
            ((depth, 3, local_heads * head_dim), F32), ((depth, local_heads * head_dim), F32),
            ((local_heads, depth), F32), ((1, depth), F32), ((1, depth), F32),
            (inner_w1.shape, F32), (inner_b1.shape, F32), (inner_w2.shape, F32), (inner_b2.shape, F32),
            (post_gain.shape, F32), (post_bias.shape, F32),
        ],
        [], [core], chain_sum, swap(chain_sum),
    )

    row_sum = spread(row_sum, "ctx")
    row_sum = row_sum.reshape(depth, -1).astype(F32)
    g_ffn_gate = row_sum[:, :units]
    g_ffn_up = row_sum[:, units : 2 * units]
    g_ffn_down = row_sum[:, 2 * units : 3 * units].T
    g_out = row_sum[:, 3 * units :].T

    back_one = jnp.sum(back_rows.astype(F32), axis=0)
    scale_one = row_scale(row_in)
    lifted = back_one * gain_row
    input_grad = (
        grad_hidden
        + scale_one * lifted
        - row_in * scale_one**3 * jnp.mean(lifted * row_in, axis=-1, keepdims=True)
    ).astype(BF)


    return (
        in_turn(output, other_out),
        in_turn(input_grad, swap(input_grad)),
        g_n1[0],
        g_qkv,
        g_lr.T,
        *g_rest,
        g_gate,
        g_out,
        g_n2[0],
        g_ffn_gate,
        g_ffn_up,
        g_ffn_down,
    )


def solution(mesh):
    in_specs = (
        P("shard", "ctx", None),
        P("shard"),
        P("shard"),
        P("shard", None, "tp"),
        P("shard", "tp"),
        P("tp", None, "shard"),
        P("tp", "shard"),
        P("tp", None, "shard"),
        P("tp", "shard"),
        P("tp", "shard"),
        P("tp", "shard"),
        P("shard", "tp"),
        P("tp", "shard"),
        P("shard"),
        P("shard", "tp"),
        P("shard", "tp"),
        P("tp", "shard"),
        P("shard", "ctx", None),
    )
    out_specs = (
        P("shard", "ctx", None),
        P("shard", "ctx", None),
        P("shard"),
        P("shard", None, "tp"),
        P("shard", "tp"),
        P("tp", None, "shard"),
        P("tp", "shard"),
        P("tp", None, "shard"),
        P("tp", "shard"),
        P("tp", "shard"),
        P("tp", "shard"),
        P("shard", "tp"),
        P("tp", "shard"),
        P("shard"),
        P("shard", "tp"),
        P("shard", "tp"),
        P("tp", "shard"),
    )
    return jax.shard_map(
        on_device, mesh=mesh, in_specs=in_specs, out_specs=out_specs, check_vma=False
    )
```

```python
from functools import partial
import jax
import jax.numpy as jnp
from jax import lax
from jax.experimental import pallas as pl
from jax.experimental.pallas import tpu as pltpu
from jax.sharding import PartitionSpec as P

MINI = 16
EPSILON = 1e-06
ETA_BASE = 0.5
BF = jnp.bfloat16
F32 = jnp.float32


def mm(left, right):
    return lax.dot_general(left, right, (((1,), (0,)), ((), ())), preferred_element_type=F32)


def mm_nt(left, right):
    return lax.dot_general(left, right, (((1,), (1,)), ((), ())), preferred_element_type=F32)


def mm_tn(left, right):
    return lax.dot_general(left, right, (((0,), (0,)), ((), ())), preferred_element_type=F32)


def gelu_parts(value):
    cdf = 0.5 + 0.5 * lax.erf(value * 0.7071067811865476)
    pdf = jnp.exp(-0.5 * value * value) * 0.3989422804014327
    return cdf, pdf


def row_scale(value):
    return lax.rsqrt(jnp.mean(value * value, axis=-1, keepdims=True) + EPSILON)


def mini_masks(rows):
    row = lax.broadcasted_iota(jnp.int32, (rows, rows), 0)
    col = lax.broadcasted_iota(jnp.int32, (rows, rows), 1)
    within = (lax.div(row, MINI) == lax.div(col, MINI)) & (col <= row)
    scale = jnp.where(within, 1.0 / (lax.rem(row, MINI) + 1).astype(F32), 0.0)
    return scale, jnp.where(row == col, 1.0 / MINI, 0.0)


def minis(value):
    return [value[at : at + MINI] for at in range(0, value.shape[0], MINI)]


def flat_rows(value):
    return value.reshape(value.shape[0] * value.shape[1], value.shape[2])


class Rows:
    def __init__(self, ref, start, size):
        self.ref, self.start, self.size = ref, start, size

    def spot(self, key):
        key = key if isinstance(key, tuple) else (key, slice(None))
        first, last = 0, self.size
        if len(key) == 3:
            first, last, _ = key[2].indices(self.size)
        return key[0], key[1], slice(self.start + first, self.start + last)

    def __getitem__(self, key):
        return self.ref[self.spot(key)]

    def __setitem__(self, key, value):
        self.ref[self.spot(key)] = value


class Plane:
    def __init__(self, ref, number, lane=None):
        self.ref, self.number = ref, number
        self.lanes = slice(None) if lane is None else slice(lane, lane + 1)

    def __getitem__(self, key):
        if isinstance(key, tuple):
            return self.ref[key[0], self.number, key[1] * MINI : (key[1] + 1) * MINI, self.lanes]
        return self.ref[key, self.number, :, self.lanes]

    def __setitem__(self, key, value):
        self.ref[key, self.number, :, self.lanes] = value


def named_parts(narrow_ref, plane_ref, state_ref, low_ref, high_ref):
    head_dim = narrow_ref.shape[3]
    return (
        Rows(narrow_ref, 0, 2 * MINI), Rows(narrow_ref, 2 * MINI, MINI),
        *(Plane(plane_ref, number) for number in range(3)), Plane(plane_ref, 3, 0), Plane(plane_ref, 3, 1),
        Rows(state_ref, 0, head_dim), Rows(state_ref, head_dim, head_dim),
        *(Rows(low_ref, at, MINI) for at in (0, MINI, 2 * MINI)),
        *(Rows(high_ref, at, MINI) for at in (0, MINI, 2 * MINI)),
    )


def fwd_kernel(
    length_ref, x_ref, gain_ref, wc_ref, lrt_ref, w1i_ref, c1i_ref, w2i_ref, c2i_ref, pg_ref, pb_ref,
    post_ref, fac_ref, narrow_ref, plane_ref, state_ref, low_ref, high_ref,
    w1_ref, c1_ref, w2_ref, c2_ref, kmv_ref, next_ref, kk_ref, pq_ref, c2s_ref, *, first,
):
    kq_ref, g2_ref, gl_ref, gs_ref, unit_ref, rate_ref, hscale_ref, w1s_ref, w2s_ref, h_ref, r_ref, g1_ref, *rest = (
        named_parts(narrow_ref, plane_ref, state_ref, low_ref, high_ref)
    )
    ga_ref, ug_ref, gp_ref = rest
    chains, group, _, head_dim = narrow_ref.shape
    rows = group * MINI
    cols = chains * head_dim
    every = range(chains)

    @pl.when(pl.program_id(0) == 0)
    def _():
        w1_ref[...] = w1i_ref[...]
        c1_ref[...] = c1i_ref[...]
        w2_ref[...] = w2i_ref[...]
        c2_ref[...] = c2i_ref[...]

    start = (first + pl.program_id(0)) * rows
    padded = lrt_ref.shape[0]
    x = x_ref[...].astype(F32)
    normed = (x * row_scale(x) * gain_ref[...]).astype(BF)
    proj = mm(normed, wc_ref[...])
    length = length_ref[0]
    live_col = start + lax.broadcasted_iota(jnp.int32, (rows, padded), 0) < length
    live_row = start + lax.broadcasted_iota(jnp.int32, (padded, rows), 1) < length
    eta_col = jnp.where(live_col, jax.nn.sigmoid(mm_nt(normed, lrt_ref[...])), 0.0) * (ETA_BASE / head_dim)
    rate = jax.nn.sigmoid(mm_nt(lrt_ref[...], normed))
    eta_row = jnp.where(live_row, rate, 0.0) * (ETA_BASE / head_dim)
    fac_ref[0, :padded] = eta_row * (1.0 - rate)
    fac_ref[0, padded:] = eta_row
    for i in every:
        at = i * head_dim
        k = proj[:, cols + at : cols + at + head_dim]
        v = proj[:, 2 * cols + at : 2 * cols + at + head_dim]
        kb, qb = k.astype(BF), proj[:, at : at + head_dim].astype(BF)
        k_minis = kb.reshape(group, MINI, head_dim)
        q_minis = qb.reshape(group, MINI, head_dim)
        kq_ref[i, :, :MINI] = k_minis
        kq_ref[i, :, MINI:] = q_minis
        next_ref[i, : group - 1, :MINI] = k_minis[1:]
        next_ref[i, group - 1 :, :MINI] = k_minis[:1]
        next_ref[i, :, MINI:] = q_minis
        kmv_ref[i] = (k - v).reshape(group, MINI, head_dim)
        rate_ref[i] = eta_col[:, i : i + 1] * (1.0 / MINI)
        cross = (mm_nt(kb, kb) + 1.0) * (eta_row[i : i + 1] * (1.0 / MINI))
        for j in range(group - 1):
            at = j * MINI
            kk_ref[i, j] = cross[at + MINI : at + 2 * MINI, at : at + MINI].astype(BF)

    key_pre = [mm(kq_ref[i, 0, :MINI], w1_ref[i].astype(BF)) + c1_ref[i] for i in every]
    for j in range(group):
        rate = [rate_ref[i, j] for i in every]
        kmv = [kmv_ref[i, j] for i in every]
        stacked = [next_ref[i, j] for i in every]
        k = [kq_ref[i, j, :MINI] for i in every]
        kk = [kk_ref[i, j] for i in every] if j < group - 1 else None
        w1 = [w1_ref[i] for i in every]
        w2 = [w2_ref[i] for i in every]
        c1 = [c1_ref[i] for i in every]
        c2 = [c2_ref[i] for i in every]
        w1b = [w1[i].astype(BF) for i in every]
        w2b = [w2[i].astype(BF) for i in every]
        parts = [gelu_parts(key_pre[i]) for i in every]
        hb = [(key_pre[i] * parts[i][0]).astype(BF) for i in every]
        g2 = [mm_nt(hb[i], w2b[i]) + c2[i] + kmv[i] for i in every]
        slope = [parts[i][0] + key_pre[i] * parts[i][1] for i in every]
        curve = [parts[i][1] * (2.0 - key_pre[i] * key_pre[i]) for i in every]
        both = [mm(stacked[i], w1b[i]) + c1[i] for i in every]
        g2b = [g2[i].astype(BF) for i in every]
        u = [mm(g2b[i], w2b[i]) for i in every]
        fg2 = [rate[i] * g2[i] for i in every]
        w2n = [w2[i] - mm_tn(fg2[i].astype(BF), hb[i]) for i in every]
        c2n = [c2[i] - jnp.sum(fg2[i], axis=0, keepdims=True) for i in every]
        g1 = [u[i] * slope[i] for i in every]
        g1b = [g1[i].astype(BF) for i in every]
        if j < group - 1:
            key_pre = [both[i][:MINI] - mm(kk[i], g1b[i]) for i in every]
        fg1 = [rate[i] * g1[i] for i in every]
        w1n = [w1[i] - mm_tn(k[i], fg1[i].astype(BF)) for i in every]
        c1n = [c1[i] - jnp.sum(fg1[i], axis=0, keepdims=True) for i in every]
        for i in every:
            w1s_ref[i, j] = w1b[i]
            w2s_ref[i, j] = w2b[i]
            c2s_ref[i, j] = c2[i]
            h_ref[i, j] = hb[i]
            g1_ref[i, j] = g1b[i]
            g2_ref[i, j] = g2b[i]
            ga_ref[i, j] = slope[i]
            ug_ref[i, j] = u[i] * curve[i]
            pq_ref[i, j] = both[i][MINI:]
            w1_ref[i] = w1n[i]
            w2_ref[i] = w2n[i]
            c1_ref[i] = c1n[i]
            c2_ref[i] = c2n[i]

    scale = mini_masks(rows)[0]
    for i in every:
        at = i * head_dim
        q = proj[:, at : at + head_dim]
        gate = proj[:, 3 * cols + at : 3 * cols + at + head_dim]
        kb, qb = flat_rows(kq_ref[i, :, :MINI]), flat_rows(kq_ref[i, :, MINI:])
        hb, g1b, g2b = flat_rows(h_ref[i]), flat_rows(g1_ref[i]), flat_rows(g2_ref[i])
        mix = scale * eta_row[i : i + 1]
        query_pre = flat_rows(pq_ref[i]) - mm((mix * (mm_nt(qb, kb) + 1.0)).astype(BF), g1b)
        cdf, pdf = gelu_parts(query_pre)
        gp_ref[i] = (cdf + query_pre * pdf).reshape(group, MINI, -1)
        rb = (query_pre * cdf).astype(BF)
        r_ref[i] = rb.reshape(group, MINI, -1)
        s2 = (mix * (mm_nt(rb, hb) + 1.0)).astype(BF)
        through = [mm_nt(piece, w2s_ref[i, j]) + c2s_ref[i, j] for j, piece in enumerate(minis(rb))]
        mixed = q + jnp.concatenate(through, axis=0) - mm(s2, g2b)
        centered = mixed - jnp.mean(mixed, axis=-1, keepdims=True)
        hscale = row_scale(centered)
        unit = centered * hscale
        out = unit * pg_ref[i] + pb_ref[i]
        cdf, pdf = gelu_parts(gate)
        post_ref[:, at : at + head_dim] = (gate * cdf * out).astype(BF)
        gl_ref[i] = gate * cdf
        gs_ref[i] = (cdf + gate * pdf) * out
        unit_ref[i] = unit
        hscale_ref[i] = hscale


def bwd_kernel(
    x_ref, gain_ref, wc_ref, lrt_ref, pg_ref, gpost_ref,
    fac_ref, narrow_ref, plane_ref, state_ref, low_ref, high_ref, *refs, begun,
):
    before, refs = (refs[:9], refs[10:]) if begun else ((), refs)
    (back_ref, gw_ref, glr_ref, gain_grad_ref, gpg_ref, gpb_ref, dw1_ref, dc1_ref, dw2_ref, dc2_ref, d_ref, g1a_ref, g2a_ref, ha_ref, ka_ref, dp_ref, kc_ref, dk_ref, da_ref, df_ref, de_ref, all_ref) = refs
    kq_ref, g2_ref, gl_ref, gs_ref, unit_ref, rate_ref, hscale_ref, w1s_ref, w2s_ref, h_ref, r_ref, g1_ref, *rest = (
        named_parts(narrow_ref, plane_ref, state_ref, low_ref, high_ref)
    )
    ga_ref, ug_ref, gp_ref = rest
    chains, group, _, head_dim = narrow_ref.shape
    rows = group * MINI
    cols = chains * head_dim
    every = range(chains)

    @pl.when(pl.program_id(0) == 0)
    def _():
        totals = (gw_ref, glr_ref, gain_grad_ref, gpg_ref, gpb_ref, dw1_ref, dc1_ref, dw2_ref, dc2_ref)
        for number, total in enumerate(totals):
            total[...] = before[number][...] if begun else jnp.zeros_like(total)

    scale, eye = mini_masks(rows)
    padded = lrt_ref.shape[0]
    gpost = gpost_ref[...].astype(F32)
    for i in every:
        at = i * head_dim
        piece = gpost[:, at : at + head_dim]
        all_ref[:, 3 * cols + at : 3 * cols + at + head_dim] = (piece * gs_ref[i]).astype(BF)
        head = piece * gl_ref[i]
        unit = unit_ref[i]
        gpg_ref[i] += jnp.sum(head * unit, axis=0, keepdims=True)
        gpb_ref[i] += jnp.sum(head, axis=0, keepdims=True)
        lifted = head * pg_ref[i]
        d = hscale_ref[i] * (
            lifted
            - jnp.mean(lifted, axis=-1, keepdims=True)
            - unit * jnp.mean(lifted * unit, axis=-1, keepdims=True)
        )
        d_ref[i] = d.reshape(group, MINI, head_dim)
        db = d.astype(BF)
        kb, qb = flat_rows(kq_ref[i, :, :MINI]), flat_rows(kq_ref[i, :, MINI:])
        hb, rb, g1b, g2b = (flat_rows(ref[i]) for ref in (h_ref, r_ref, g1_ref, g2_ref))
        mix = scale * fac_ref[0, padded + i : padded + i + 1]
        ds2 = -mm_nt(db, g2b)
        x2 = mm_nt(rb, hb) + 1.0
        x1 = mm_nt(qb, kb) + 1.0
        dx2 = (ds2 * mix).astype(BF)
        dr = jnp.concatenate([mm(part, w2s_ref[i, j]) for j, part in enumerate(minis(db))], axis=0)
        dp = (dr + mm(dx2, hb)) * flat_rows(gp_ref[i])
        dpb = dp.astype(BF)
        ds1 = -mm_nt(dpb, g1b)
        dx1 = (ds1 * mix).astype(BF)
        dq = jnp.concatenate([mm_nt(part, w1s_ref[i, j]) for j, part in enumerate(minis(dpb))], axis=0)
        all_ref[:, at : at + head_dim] = (d + dq + mm(dx1, kb)).astype(BF)
        g1a_ref[i] = -mm_tn((mix * x1).astype(BF), dpb).reshape(group, MINI, -1)
        g2a_ref[i] = -mm_tn((mix * x2).astype(BF), db).reshape(group, MINI, -1)
        ha_ref[i] = mm_tn(dx2, rb).reshape(group, MINI, -1)
        ka_ref[i] = mm_tn(dx1, qb).reshape(group, MINI, -1)
        dp_ref[i] = dpb.reshape(group, MINI, -1)
        de_ref[i] = jnp.sum((ds2 * x2 + ds1 * x1) * scale, axis=0, keepdims=True)
        kk = mm_nt(kb, kb) + 1.0
        kx = mm_nt(kb, qb) + 1.0
        for j in range(group - 1):
            own, after = slice(j * MINI, (j + 1) * MINI), slice((j + 1) * MINI, (j + 2) * MINI)
            kc_ref[i, j] = jnp.concatenate([kk[own, after], kx[own, after]], axis=1).astype(BF)

    t1 = [mm(kq_ref[i, group - 1, :MINI], dw1_ref[i].astype(BF)) + dc1_ref[i] for i in every]
    for j in reversed(range(group)):

        def all_of(ref):
            return [ref[i, j] for i in every]

        d, kq, rate, w2b, hb, rb, g1b, g2b = (
            all_of(ref) for ref in (d_ref, kq_ref, rate_ref, w2s_ref, h_ref, r_ref, g1_ref, g2_ref)
        )
        ga, ug, dpb, g1a, g2a, ha = (
            all_of(ref) for ref in (ga_ref, ug_ref, dp_ref, g1a_ref, g2a_ref, ha_ref)
        )
        dw1 = [dw1_ref[i] for i in every]
        dw2 = [dw2_ref[i] for i in every]
        dc1 = [dc1_ref[i] for i in every]
        dc2 = [dc2_ref[i] for i in every]
        g1 = [g1b[i].astype(F32) for i in every]
        g2 = [g2b[i].astype(F32) for i in every]
        dw1b = [dw1[i].astype(BF) for i in every]
        dw2b = [dw2[i].astype(BF) for i in every]
        dg1 = [g1a[i] - rate[i] * t1[i] for i in every]
        dub = [(dg1[i] * ga[i]).astype(BF) for i in every]
        through = [mm_nt(dub[i], w2b[i]) for i in every]
        t2 = [mm_nt(hb[i], dw2b[i]) + dc2[i] for i in every]
        dha = [ha[i] - mm((rate[i] * g2[i]).astype(BF), dw2b[i]) for i in every]
        dg2 = [through[i] + (g2a[i] - rate[i] * t2[i]) for i in every]
        dg2b = [dg2[i].astype(BF) for i in every]
        dh = [mm(dg2b[i], w2b[i]) + dha[i] for i in every]
        if j > 0:
            base = [mm(kq_ref[i, j - 1, :MINI], dw1b[i]) + dc1[i] for i in every]
        dk = [dg2[i] - mm_nt((rate[i] * g1[i]).astype(BF), dw1b[i]) for i in every]
        df = [
            -(
                jnp.sum(g1[i] * t1[i], axis=1, keepdims=True)
                + jnp.sum(g2[i] * t2[i], axis=1, keepdims=True)
            )
            for i in every
        ]
        da = [dg1[i] * ug[i] + dh[i] * ga[i] for i in every]
        dab = [da[i].astype(BF) for i in every]
        both = [jnp.concatenate([dab[i], dpb[i]], axis=0) for i in every]
        if j > 0:
            t1 = [base[i] + mm(kc_ref[i, j - 1], both[i]) for i in every]
        dw1n = [dw1[i] + mm_tn(kq[i], both[i]) for i in every]
        dc1n = [dc1[i] + jnp.sum(da[i] + dpb[i].astype(F32), axis=0, keepdims=True) for i in every]
        dw2n = [
            dw2[i]
            + mm_tn(
                jnp.concatenate([d[i].astype(BF), dg2b[i], g2b[i]], axis=0),
                jnp.concatenate([rb[i], hb[i], dub[i]], axis=0),
            )
            for i in every
        ]
        dc2n = [dc2[i] + jnp.sum(d[i] + dg2[i], axis=0, keepdims=True) for i in every]
        for i in every:
            piece, at = slice(j * MINI, (j + 1) * MINI), 2 * cols + i * head_dim
            all_ref[piece, at : at + head_dim] = (-dg2[i]).astype(BF)
            dk_ref[i, j] = dk[i]
            da_ref[i, j] = dab[i]
            df_ref[i, j] = df[i]
            dw1_ref[i] = dw1n[i]
            dc1_ref[i] = dc1n[i]
            dw2_ref[i] = dw2n[i]
            dc2_ref[i] = dc2n[i]

    x = x_ref[...].astype(F32)
    unit_in = x * row_scale(x)
    normed = (unit_in * gain_ref[...]).astype(BF)
    lrt = lrt_ref[...]
    which = lax.broadcasted_iota(jnp.int32, (padded, rows), 0)
    rates = jnp.zeros((padded, rows), F32)
    for i in every:
        at = cols + i * head_dim
        dk = jnp.concatenate([mm_nt(da_ref[i, j], w1s_ref[i, j]) for j in range(group)], axis=0)
        all_ref[:, at : at + head_dim] = (flat_rows(dk_ref[i]) + flat_rows(ka_ref[i]) + dk).astype(BF)
        line = de_ref[i] + jnp.sum(eye * flat_rows(df_ref[i]), axis=0, keepdims=True)
        rates = jnp.where(which == i, line, rates)
    rates = (rates * fac_ref[0, :padded]).astype(BF)
    grads = all_ref[...]
    back = mm_nt(grads, wc_ref[...]) + mm_tn(rates, lrt)
    gain_grad_ref[...] += jnp.sum(back * unit_in, axis=0, keepdims=True)
    back_ref[...] = back.astype(BF)
    gw_ref[...] += mm_tn(normed, grads)
    glr_ref[...] += mm(rates, normed)


GROUP = 8


def block_specs(chains, head_dim, inner, padded, place):
    rows = GROUP * MINI

    def mini(first, second):
        return pl.BlockSpec((chains, GROUP, first, second), lambda g: (0, place(g), 0, 0))

    return [
        pl.BlockSpec((1, 2 * padded, rows), lambda g: (place(g), 0, 0)),
        mini(3 * MINI, head_dim),
        pl.BlockSpec((chains, 4, rows, head_dim), lambda g: (0, 0, place(g), 0)),
        mini(2 * head_dim, inner), mini(3 * MINI, inner), mini(3 * MINI, inner),
    ]


def whole_spec(value):
    return pl.BlockSpec(value.shape, lambda g: (0,) * value.ndim)


def run_fwd(first, last, length, tokens, gain, wc, lrt, pg, pb, state):
    width = tokens.shape[1]
    chains, head_dim, inner = state[0].shape
    rows = GROUP * MINI
    steps = last - first
    count = steps * GROUP
    padded = lrt.shape[0]

    def mini(first_size, second_size, dtype):
        return jax.ShapeDtypeStruct((chains, count, first_size, second_size), dtype)

    row_spec = pl.BlockSpec((rows, width), lambda g: (first + g, 0))
    small = (gain, wc, lrt, *state, pg, pb)
    return pl.pallas_call(
        partial(fwd_kernel, first=first),
        grid=(steps,),
        in_specs=[pl.BlockSpec(memory_space=pltpu.SMEM), row_spec] + [whole_spec(v) for v in small],
        out_specs=[pl.BlockSpec((rows, chains * head_dim), lambda g: (g, 0))]
        + block_specs(chains, head_dim, inner, padded, lambda g: g)
        + [whole_spec(v) for v in state],
        out_shape=[
            jax.ShapeDtypeStruct((steps * rows, chains * head_dim), BF),
            jax.ShapeDtypeStruct((steps, 2 * padded, rows), F32),
            mini(3 * MINI, head_dim, BF),
            jax.ShapeDtypeStruct((chains, 4, steps * rows, head_dim), F32),
            mini(2 * head_dim, inner, BF), mini(3 * MINI, inner, BF), mini(3 * MINI, inner, F32),
        ]
        + [jax.ShapeDtypeStruct(v.shape, F32) for v in state],
        scratch_shapes=[
            pltpu.VMEM((chains, GROUP, MINI, head_dim), F32),
            pltpu.VMEM((chains, GROUP, 2 * MINI, head_dim), BF),
            pltpu.VMEM((chains, GROUP, MINI, MINI), BF),
            pltpu.VMEM((chains, GROUP, MINI, inner), F32),
            pltpu.VMEM((chains, GROUP, 1, head_dim), F32),
        ],
        compiler_params=pltpu.CompilerParams(vmem_limit_bytes=50 << 20),
        cost_estimate=pl.CostEstimate(
            flops=9_000_000_000 * steps, bytes_accessed=5_000_000 * steps, transcendentals=0
        ),
        name="chain_forward",
    )(length, tokens, *small)


def run_bwd(first, last, base, tokens, gain, wc, lrt, pg, gpost, shapes, state, saved, written=None):
    begun = written is not None
    width = tokens.shape[1]
    chains, head_dim, inner = shapes[5]
    rows = GROUP * MINI
    padded = lrt.shape[0]
    wide = wc.shape[1]
    steps = last - first

    def place(g):
        return steps - 1 - g

    def shape(*extent):
        return jax.ShapeDtypeStruct(extent, F32)

    small = (gain, wc, lrt, pg)
    outs = [shape(*extent) for extent in shapes]

    def scratch(first_size, second_size, dtype):
        return pltpu.VMEM((chains, GROUP, first_size, second_size), dtype)

    return pl.pallas_call(
        partial(bwd_kernel, begun=begun),
        grid=(steps,),
        in_specs=[pl.BlockSpec((rows, width), lambda g: (first + place(g), 0))]
        + [whole_spec(v) for v in small]
        + [pl.BlockSpec((rows, chains * head_dim), lambda g: (first + place(g), 0))]
        + block_specs(chains, head_dim, inner, padded, lambda g: first - base + place(g))
        + [whole_spec(v) for v in state]
        + [pl.BlockSpec(memory_space=pl.ANY)] * begun,
        out_specs=[pl.BlockSpec((rows, width), lambda g: (first + place(g), 0))] + [whole_spec(v) for v in outs],
        out_shape=[jax.ShapeDtypeStruct(tokens.shape, BF)] + outs,
        input_output_aliases={21: 0} if begun else {},
        scratch_shapes=[
            scratch(MINI, head_dim, F32), scratch(MINI, inner, F32), scratch(MINI, head_dim, F32),
            scratch(MINI, inner, F32), scratch(MINI, head_dim, F32), scratch(MINI, inner, BF),
            scratch(MINI, 2 * MINI, BF), scratch(MINI, head_dim, F32), scratch(MINI, inner, BF),
            scratch(MINI, 1, F32), pltpu.VMEM((chains, 1, rows), F32), pltpu.VMEM((rows, wide), BF),
        ],
        compiler_params=pltpu.CompilerParams(vmem_limit_bytes=56 << 20),
        cost_estimate=pl.CostEstimate(
            flops=11_000_000_000 * steps, bytes_accessed=5_000_000 * steps, transcendentals=0
        ),
        name="chain_backward",
    )(tokens, *small, gpost, *saved, *state, *((written,) if begun else ()))


def swap(value):
    return lax.ppermute(value, "tp", [(0, 1), (1, 0)])


def rows_kernel(
    spot_ref, post_ref, own_ref, other_ref, x_ref, cot_ref, gain_ref,
    out_ref, grad_ref, normed_ref, low_ref, back_ref, gain_grad_ref, cat0_ref, cat1_ref, *act_refs,
):
    *act_refs, gpost_ref = act_refs
    core, start, length = spot_ref[0], spot_ref[1], spot_ref[2]
    span, width = x_ref.shape
    cols = post_ref.shape[2]
    units = act_refs[0].shape[1]
    places = cat0_ref.shape[1] // cols
    x = x_ref[...].astype(F32)
    live = start + lax.broadcasted_iota(jnp.int32, (span, width), 0) < length
    back = jnp.where(live, cot_ref[...].astype(F32), 0.0)
    back_low = back.astype(BF)
    back_ref[...] = back_low
    halves = ((own_ref, core), (other_ref, 1 - core))
    hidden = x
    for half, (w_ref, side) in enumerate(halves):
        joined = jnp.concatenate([post_ref[side * places + p] for p in range(places)], axis=1)
        (cat0_ref, cat1_ref)[half][...] = joined
        hidden = hidden + mm_nt(joined, w_ref[:, 3 * units :])
    scale = row_scale(hidden)
    gain = gain_ref[...]
    normed = (hidden * scale * gain).astype(BF)
    normed_ref[...] = normed
    feed = jnp.zeros((span, width), F32)
    grad = jnp.zeros((span, width), F32)
    step = min(units, 512)
    for half, (w_ref, _) in enumerate(halves):
        for at in range(0, units, step):
            w_gate = w_ref[:, at : at + step]
            w_up = w_ref[:, units + at : units + at + step]
            w_down = w_ref[:, 2 * units + at : 2 * units + at + step]
            up_gate = mm(normed, w_gate)
            up_lin = mm(normed, w_up)
            grad_act = mm(back_low, w_down)
            gate = jax.nn.sigmoid(up_gate)
            silu = up_gate * gate
            act = (silu * up_lin).astype(BF)
            grad_gate = (grad_act * up_lin * (gate * (1.0 + up_gate * (1.0 - gate)))).astype(BF)
            grad_lin = (grad_act * silu).astype(BF)
            act_refs[3 * half + 0][:, at : at + step] = grad_gate
            act_refs[3 * half + 1][:, at : at + step] = grad_lin
            act_refs[3 * half + 2][:, at : at + step] = act
            feed += mm_nt(act, w_down)
            grad += mm_nt(grad_gate, w_gate) + mm_nt(grad_lin, w_up)
    out_ref[...] = (hidden + feed).astype(BF)
    lifted = grad * gain
    hat = hidden * scale
    gain_grad_ref[...] = jnp.sum(grad * hat, axis=0, keepdims=True)
    total = back + scale * (lifted - hat * jnp.mean(lifted * hat, axis=-1, keepdims=True))
    grad_ref[...] = total
    low = total.astype(BF)
    low_ref[...] = low
    for p in range(2 * places, gpost_ref.shape[0]):
        gpost_ref[p] = jnp.zeros(gpost_ref.shape[1:], BF)
    deal_refs = act_refs[6:]
    for w_ref, side in halves:
        gpost = mm(low, w_ref[:, 3 * units :]).astype(BF)
        for p in range(places):
            gpost_ref[side * places + p] = gpost[:, p * cols : (p + 1) * cols]
    for bit, deal_ref in enumerate(deal_refs):
        deal_ref[...] = gpost_ref[spot_ref[3] ^ bit]


def run_rows(spots, post, own, other, x, cot, gain, half_out):
    ring, span, cols = post.shape
    width = x.shape[1]
    units = (own.shape[1] - half_out) // 3
    vmem = pl.BlockSpec(memory_space=pltpu.VMEM)

    def shape(extent, dtype):
        return jax.ShapeDtypeStruct(extent, dtype)

    return pl.pallas_call(
        rows_kernel,
        in_specs=[pl.BlockSpec(memory_space=pltpu.SMEM)] + [vmem] * 6,
        out_specs=[vmem] * (14 + ring),
        out_shape=[
            shape((span, width), BF), shape((span, width), F32),
            shape((span, width), BF), shape((span, width), BF), shape((span, width), BF), shape((1, width), F32),
        ]
        + [shape((span, half_out), BF)] * 2
        + [shape((span, units), BF)] * 6
        + [shape((span, cols), BF)] * ring,
        scratch_shapes=[pltpu.VMEM((ring, span, cols), BF)],
        compiler_params=pltpu.CompilerParams(vmem_limit_bytes=52 << 20),
        cost_estimate=pl.CostEstimate(flops=20_000_000_000, bytes_accessed=20_000_000, transcendentals=0),
        name="rows_main",
    )(spots, post, own, other, x, cot, gain)


def products(pairs, parts, store):
    start = 0
    for left, right in zip(pairs, parts):
        size = right.shape[-1]
        step = 512 if size % 512 == 0 else size
        for at in range(0, size, step):
            store(start + at, mm_tn(left[...], right[:, at : at + step]))
        start += size


def sums_other_kernel(*refs):
    *sources, out_ref = refs
    count = len(sources) // 2

    def store(at, value):
        out_ref[:, at : at + value.shape[1]] = value.astype(BF)

    products(sources[:count], sources[count:], store)


def sums_own_kernel(place_ref, other_ref, *refs, count, outs):
    sources, out_refs, held_ref = refs[: 2 * count], refs[2 * count : 2 * count + outs], refs[-1]

    def store(at, value):
        piece = slice(at, at + value.shape[1])
        held_ref[:, piece] = (value + other_ref[:, piece].astype(F32)).astype(BF)

    products(sources[:count], sources[count:], store)
    for bit, out_ref in enumerate(out_refs):
        blocks, part = out_ref.shape[:2]
        for number in range(blocks):
            at = pl.multiple_of((number * outs + (place_ref[0] ^ bit)) * part, part)
            out_ref[number] = held_ref[pl.ds(at, part), :]


def run_sums(lefts, rights, other=None, place=None, blocks=1, outs=1):
    width = lefts[0].shape[1]
    total = sum(right.shape[1] for right in rights)
    vmem = pl.BlockSpec(memory_space=pltpu.VMEM)
    count = len(lefts)
    params = pltpu.CompilerParams(vmem_limit_bytes=40 << 20)
    cost = pl.CostEstimate(flops=5_000_000_000, bytes_accessed=6_000_000, transcendentals=0)
    if other is None:
        return pl.pallas_call(
            sums_other_kernel,
            in_specs=[vmem] * (2 * count),
            out_specs=vmem,
            out_shape=jax.ShapeDtypeStruct((width, total), BF),
            compiler_params=params,
            cost_estimate=cost,
            name="sums_other",
        )(*lefts, *rights)
    part = width // (blocks * outs)
    return pl.pallas_call(
        partial(sums_own_kernel, count=count, outs=outs),
        in_specs=[pl.BlockSpec(memory_space=pltpu.SMEM)] + [vmem] * (2 * count + 1),
        out_specs=[vmem] * outs,
        out_shape=[jax.ShapeDtypeStruct((blocks, part, total), BF)] * outs,
        scratch_shapes=[pltpu.VMEM((width, total), BF)],
        compiler_params=params,
        cost_estimate=cost,
        name="sums_own",
    )(place, other, *lefts, *rights)


def assemble_kernel(spots_ref, pack_ref, *refs, ring):
    far_refs, near_ref, out_ref = refs[:ring], refs[ring], refs[-1]
    me, place = spots_ref[0], spots_ref[1]
    part = out_ref.shape[1]
    cut = far_refs[0].shape[2]
    for number in range(ring):
        piece = slice(number * part, (number + 1) * part)
        out_ref[me * ring + number, :, :cut] = pack_ref[piece, :cut]
        for z in range(near_ref.shape[0]):
            out_ref[z * ring + number, :, cut:] = near_ref[z, piece]
    for bit, far_ref in enumerate(far_refs):
        for other in range(far_ref.shape[0]):
            out_ref[(me ^ (other + 1)) * ring + (place ^ bit), :, :cut] = far_ref[other]


def run_assemble(spots, pack, far_parts, near_parts):
    vmem = pl.BlockSpec(memory_space=pltpu.VMEM)
    ring = len(far_parts)
    part = pack.shape[0] // ring
    return pl.pallas_call(
        partial(assemble_kernel, ring=ring),
        in_specs=[pl.BlockSpec(memory_space=pltpu.SMEM)] + [vmem] * (2 + ring),
        out_specs=vmem,
        out_shape=jax.ShapeDtypeStruct((near_parts.shape[0] * ring, part, pack.shape[1]), BF),
        compiler_params=pltpu.CompilerParams(vmem_limit_bytes=40 << 20),
        name="assemble_rows",
    )(spots, pack, *far_parts, near_parts)


SMALL = 64


def small_spots(chains, depth, inner_share):
    side = 2 * chains * inner_share
    return side, {
        "lr": 0, "n1": chains, "n2": chains + 1, "b1": chains + 2,
        "b2": 2 * chains + 2, "pg": 3 * chains + 2, "pb": 4 * chains + 2,
    }


def pack_weights_kernel(
    pick_ref, qkv_ref, gate_ref, lr_ref, n1_ref, n2_ref, w1_ref, b1_ref, w2_ref, b2_ref, pg_ref, pb_ref,
    out_ref, small_ref, *, chains,
):
    depth = gate_ref.shape[0]
    heads, head_dim, inner_share = w1_ref.shape
    cols = chains * head_dim
    all_cols = heads * head_dim
    side, spots = small_spots(chains, depth, inner_share)
    small_ref[...] = jnp.zeros_like(small_ref)

    def put(name, i, value):
        row = spots[name] + i
        small_ref[row : row + 1, side : side + value.shape[1]] = value.astype(F32)

    for option in range(heads // chains):

        @pl.when(pick_ref[0] == option)
        def _():
            at = option * cols
            for which in range(3):
                start = which * all_cols + at
                out_ref[:depth, which * cols : (which + 1) * cols] = qkv_ref[:, start : start + cols]
            out_ref[:depth, 3 * cols :] = gate_ref[:, at : at + cols]
            for i in range(chains):
                head = option * chains + i
                lanes = slice(i * inner_share, (i + 1) * inner_share)
                small_ref[:, lanes] = w1_ref[head].astype(F32)
                lanes = slice((chains + i) * inner_share, (chains + i + 1) * inner_share)
                small_ref[:, lanes] = w2_ref[head].astype(F32)
                for name, ref in (("lr", lr_ref), ("b1", b1_ref), ("b2", b2_ref), ("pg", pg_ref), ("pb", pb_ref)):
                    put(name, i, ref[head : head + 1, :])

    put("n1", 0, n1_ref[...])
    put("n2", 0, n2_ref[...])
    out_ref[depth:, :] = small_ref[...].astype(BF)


def halves_by_core(core, mine_ref, other_ref, work):
    @pl.when(core == 0)
    def _():
        work(mine_ref, other_ref)

    @pl.when(core != 0)
    def _():
        work(other_ref, mine_ref)


def unpack_weights_kernel(
    core_ref, mine_ref, other_ref,
    wc_ref, lrt_ref, n1_ref, n2_ref, w1_ref, b1_ref, w2_ref, b2_ref, pg_ref, pb_ref, lines_ref,
):
    shards, half, _ = mine_ref.shape
    chains, _, inner = w1_ref.shape
    inner_share = inner // shards
    depth = 2 * half - SMALL
    head_share = b2_ref.shape[2] // shards
    side, spots = small_spots(chains, depth, inner_share)
    lines_ref[...] = jnp.zeros_like(lines_ref)

    def work(low_ref, high_ref):
        for z in range(shards):
            wc_ref[z * depth : z * depth + half] = low_ref[z]
            wc_ref[z * depth + half : (z + 1) * depth] = high_ref[z, : depth - half]
            small = high_ref[z, depth - half :].astype(F32)

            def get(name, i, size):
                row = spots[name] + i
                return small[row : row + 1, side : side + size]

            here = slice(z * depth, (z + 1) * depth)
            n1_ref[:, here] = get("n1", 0, depth)
            n2_ref[:, here] = get("n2", 0, depth)
            for i in range(chains):
                lines_ref[i : i + 1, here] = get("lr", i, depth)
                lanes = slice(z * inner_share, (z + 1) * inner_share)
                w1_ref[i, :, lanes] = small[:, i * inner_share : (i + 1) * inner_share]
                w2_ref[i, :, lanes] = small[:, (chains + i) * inner_share : (chains + i + 1) * inner_share]
                b1_ref[i, :, lanes] = get("b1", i, inner_share)
                lanes = slice(z * head_share, (z + 1) * head_share)
                for name, ref in (("b2", b2_ref), ("pg", pg_ref), ("pb", pb_ref)):
                    ref[i, :, lanes] = get(name, i, head_share)

    halves_by_core(core_ref[0], mine_ref, other_ref, work)
    lrt_ref[...] = lines_ref[...].astype(BF)


def pack_grads_kernel(
    core_ref, gw_ref, glr_ref, n1_ref, n2_ref, w1_ref, b1_ref, w2_ref, b2_ref, pg_ref, pb_ref,
    keep_ref, send_ref, small_ref,
):
    shards, half, _ = keep_ref.shape
    chains, _, inner = w1_ref.shape
    inner_share = inner // shards
    depth = 2 * half - SMALL
    head_share = b2_ref.shape[2] // shards
    side, spots = small_spots(chains, depth, inner_share)

    def work(low_ref, high_ref):
        for z in range(shards):
            small_ref[...] = jnp.zeros_like(small_ref)

            def put(name, i, value):
                row = spots[name] + i
                small_ref[row : row + 1, side : side + value.shape[1]] = value

            here = slice(z * depth, (z + 1) * depth)
            low_ref[z] = gw_ref[z * depth : z * depth + half].astype(BF)
            high_ref[z, : depth - half] = gw_ref[z * depth + half : (z + 1) * depth].astype(BF)
            put("n1", 0, n1_ref[:, here])
            put("n2", 0, n2_ref[:, here])
            for i in range(chains):
                put("lr", i, glr_ref[i : i + 1, here])
                lanes = slice(z * inner_share, (z + 1) * inner_share)
                small_ref[:, i * inner_share : (i + 1) * inner_share] = w1_ref[i, :, lanes]
                small_ref[:, (chains + i) * inner_share : (chains + i + 1) * inner_share] = w2_ref[i, :, lanes]
                put("b1", i, b1_ref[i, :, lanes])
                lanes = slice(z * head_share, (z + 1) * head_share)
                for name, ref in (("b2", b2_ref), ("pg", pg_ref), ("pb", pb_ref)):
                    put(name, i, ref[i, :, lanes])
            high_ref[z, depth - half :] = small_ref[...].astype(BF)

    halves_by_core(core_ref[0], keep_ref, send_ref, work)


def unpack_grads_kernel(
    core_ref, mine_ref, other_ref,
    qkv_ref, gate_ref, lrt_ref, n1_ref, n2_ref, w1_ref, b1_ref, w2_ref, b2_ref, pg_ref, pb_ref, *, chains,
):
    ring, half, wide = mine_ref.shape
    cols = wide // 4
    heads, _, inner_share = w1_ref.shape
    depth = gate_ref.shape[0]
    head_share = b2_ref.shape[1]
    places = heads // chains
    side, spots = small_spots(chains, depth, inner_share)
    core = core_ref[0]

    def work(low_ref, high_ref):
        for p in range(places):
            place = core * places + p
            big = jnp.concatenate([low_ref[place], high_ref[place, : depth - half]], axis=0).astype(F32)
            small = high_ref[place, depth - half :].astype(F32)
            at = p * cols
            for which in range(3):
                qkv_ref[:, which, at : at + cols] = big[:, which * cols : (which + 1) * cols]
            gate_ref[:, at : at + cols] = big[:, 3 * cols :]
            for i in range(chains):
                head = p * chains + i
                w1_ref[head] = small[:, i * inner_share : (i + 1) * inner_share]
                w2_ref[head] = small[:, (chains + i) * inner_share : (chains + i + 1) * inner_share]
                for name, ref, size in (
                    ("lr", lrt_ref, depth), ("b1", b1_ref, inner_share), ("b2", b2_ref, head_share),
                    ("pg", pg_ref, head_share), ("pb", pb_ref, head_share),
                ):
                    row = spots[name] + i
                    ref[head : head + 1, :] = small[row : row + 1, side : side + size]
        for name, ref in (("n1", n1_ref), ("n2", n2_ref)):
            row = spots[name]
            total = jnp.zeros((1, depth), F32)
            for place in range(ring):
                lines = high_ref[place, depth - half :].astype(F32)
                total = total + lines[row : row + 1, side : side + depth]
            ref[...] = total

    halves_by_core(core, mine_ref, other_ref, work)


def fold_and_deal_kernel(place_ref, *refs, count):
    source_refs, out_refs = refs[:-count], refs[-count:]
    for bit, out_ref in enumerate(out_refs):
        which = place_ref[0] ^ bit
        if len(source_refs) > 1:
            values = [ref[which].astype(F32) for ref in source_refs]
        else:
            values = [source_refs[0][number, which].astype(F32) for number in range(source_refs[0].shape[0])]
        out_ref[...] = sum(values[1:], values[0]).astype(BF)


def fold_and_deal(sources, place, count):
    extent = sources[0].shape[-2:]
    return in_vmem(
        partial(fold_and_deal_kernel, count=count), "fold_and_deal", [(extent, BF)] * count, [], [place], *sources
    )


def add_and_deal_kernel(place_ref, keep_ref, other_ref, *out_refs):
    for bit, out_ref in enumerate(out_refs):
        which = place_ref[0] ^ bit
        out_ref[...] = (keep_ref[which].astype(F32) + other_ref[which].astype(F32)).astype(BF)


def in_vmem(kernel, name, shapes, scratch, scalars, *operands):
    vmem = pl.BlockSpec(memory_space=pltpu.VMEM)
    return pl.pallas_call(
        kernel,
        in_specs=[pl.BlockSpec(memory_space=pltpu.SMEM)] + [vmem] * len(operands),
        out_specs=[vmem] * len(shapes),
        out_shape=[jax.ShapeDtypeStruct(extent, dtype) for extent, dtype in shapes],
        scratch_shapes=[pltpu.VMEM(extent, F32) for extent in scratch],
        compiler_params=pltpu.CompilerParams(vmem_limit_bytes=40 << 20),
        name=name,
    )(jnp.stack(scalars).astype(jnp.int32), *operands)


def place_kernel(spots_ref, *refs):
    *sources, target = refs
    for number, source in enumerate(sources):
        target[spots_ref[number]] = source[...]


def placed(pieces, spots):
    return pl.pallas_call(
        place_kernel,
        in_specs=[pl.BlockSpec(memory_space=pltpu.SMEM)]
        + [pl.BlockSpec(memory_space=pltpu.VMEM)] * len(pieces),
        out_specs=pl.BlockSpec(memory_space=pltpu.VMEM),
        out_shape=jax.ShapeDtypeStruct((len(pieces),) + pieces[0].shape, pieces[0].dtype),
        compiler_params=pltpu.CompilerParams(vmem_limit_bytes=40 << 20),
        name="place_pieces",
    )(jnp.stack(spots).astype(jnp.int32), *pieces)


def exchanged(value, axis):
    size = lax.axis_size(axis)
    return [value] + [
        lax.ppermute(value, axis, [(source, source ^ bit) for source in range(size)])
        for bit in range(1, size)
    ]


def sent(taken, axis):
    return taken[:1] + [
        lax.ppermute(taken[bit], axis, [(source, source ^ bit) for source in range(len(taken))])
        for bit in range(1, len(taken))
    ]


def scattered(value, axis):
    size = lax.axis_size(axis)
    me = lax.axis_index(axis)
    return sent([lax.dynamic_index_in_dim(value, me ^ bit, 0, keepdims=False) for bit in range(size)], axis)


def placed_along(pieces, axis):
    me = lax.axis_index(axis)
    return placed(pieces, [me ^ bit for bit in range(len(pieces))])


def spread(value, axis):
    return placed_along(exchanged(value, axis), axis)


def tied(*values):
    return lax.optimization_barrier(values)


def in_turn(first, second):
    return jnp.where(lax.axis_index("tp") == 0, jnp.stack([first, second]), jnp.stack([second, first]))


def on_device(
    tokens,
    lengths,
    norm1_gain,
    qkv_weight,
    lr_weight,
    inner_w1,
    inner_b1,
    inner_w2,
    inner_b2,
    post_gain,
    post_bias,
    gate_weight,
    out_weight,
    norm2_gain,
    ffn_gate,
    ffn_up,
    ffn_down,
    cotangent,
):
    micro, span, width = tokens.shape
    ring = lax.axis_size("ctx")
    shards = lax.axis_size("shard")
    pair = lax.axis_size("tp")
    place = lax.axis_index("ctx")
    core = lax.axis_index("tp")
    local_heads, head_dim, inner_share = inner_w1.shape
    head_share = inner_b2.shape[1]
    depth = norm1_gain.shape[0]
    inner = inner_share * shards
    total_heads = local_heads * pair
    chains = -(-total_heads // ring)
    span_all = ring * span
    count = span_all // MINI
    cols = chains * head_dim
    wide = 4 * cols

    row_tokens = lax.dynamic_index_in_dim(tokens, core, 0, keepdims=False)
    token_parts = exchanged(row_tokens, "ctx")

    first_head = jnp.minimum(place * chains, total_heads - chains)
    owner = first_head // local_heads
    local_first = first_head - owner * local_heads

    packed = in_vmem(
        partial(pack_weights_kernel, chains=chains), "pack_weights",
        [((depth + SMALL, wide), BF)], [(SMALL, wide)], [local_first // chains],
        qkv_weight.reshape(depth, -1), gate_weight, lr_weight.T, norm1_gain[None], norm2_gain[None],
        inner_w1, inner_b1, inner_w2, inner_b2, post_gain, post_bias,
    )[0]
    half_rows = (depth + SMALL) // 2
    packed = jnp.where(core == owner, packed, swap(packed))
    gathered = exchanged(lax.dynamic_slice_in_dim(packed, core * half_rows, half_rows, 0), "shard")
    gathered, token_parts = tied(gathered, token_parts)

    units = ffn_gate.shape[1]
    half_out = out_weight.shape[0]
    row_pack = jnp.concatenate([ffn_gate, ffn_up, ffn_down.T, out_weight.T], axis=1)
    part = depth // ring
    cut = 3 * row_pack.shape[1] // 4 // 128 * 128
    row_near = row_pack[:, cut:]
    row_part = lax.dynamic_slice(row_pack, (place * part, 0), (part, cut))
    row_part, row_near, gathered = tied(row_part, row_near, gathered)
    row_parts = exchanged(row_part, "shard")
    slot_tokens = placed_along(token_parts, "ctx").reshape(span_all, width)
    gathered = placed_along(gathered, "shard")

    padded = -(-chains // 16) * 16
    w_chain, rate_rows, gain_row, gain_two, *rest = in_vmem(
        unpack_weights_kernel, "unpack_weights",
        [
            ((width, wide), BF), ((padded, width), BF), ((1, width), F32), ((1, width), F32),
            ((chains, head_dim, inner), F32), ((chains, 1, inner), F32),
            ((chains, head_dim, inner), F32), ((chains, 1, head_dim), F32),
            ((chains, 1, head_dim), F32), ((chains, 1, head_dim), F32),
        ],
        [(padded, width)], [core], gathered, swap(gathered),
    )
    state, (norm_gain, norm_bias) = tuple(rest[:4]), rest[4:]

    slot_length = lax.dynamic_index_in_dim(lengths, core, 0, keepdims=True)
    steps = span_all // (GROUP * MINI)
    middle = 3 * steps // 8

    def forward(first, last, begin):
        done = run_fwd(
            first, last, slot_length, slot_tokens, gain_row, w_chain, rate_rows, norm_gain, norm_bias, begin
        )
        return done[0], done[1:-4], done[-4:]

    post_low, saved_low, state_low = forward(0, middle, state)
    state_low, row_parts = tied(state_low, row_parts)
    far = jnp.stack(row_parts[1:])
    state_low, far = tied(state_low, far)
    row_near, far = tied(row_near, far)
    far_parts, near_parts = exchanged(far, "ctx"), lax.all_gather(row_near, "shard", axis=0)
    post_high, saved_high, _ = forward(middle, steps, tuple(state_low))
    post_high, far_parts, near_parts = tied(post_high, far_parts, near_parts)
    post_chain = jnp.concatenate([post_low, post_high])

    def to_rows(value):
        return lax.all_to_all(value.reshape(ring, span, -1), "ctx", 0, 0)

    post = to_rows(post_chain)

    number = jnp.stack([lax.axis_index("shard"), place]).astype(jnp.int32)
    w_own = run_assemble(number, row_pack, far_parts, near_parts).reshape(width, -1)
    w_other = swap(w_own)
    spots = jnp.stack([core, place * span, slot_length[0], place]).astype(jnp.int32)
    cot = lax.dynamic_index_in_dim(cotangent, core, 0, keepdims=False)
    output, grad_hidden, normed_two, grad_hidden_low, back_low, grad_gain_two, *kept = run_rows(
        spots, post, w_own, w_other, row_tokens, cot, gain_two, half_out
    )
    row_in = row_tokens.astype(F32)
    joined, acts = kept[:2], (kept[2:5], kept[5:8])

    def folded(values):
        return sum(value.astype(F32) for value in values).astype(BF)

    me = lax.axis_index("shard")

    def operands(half, second):
        if second:
            return (back_low, grad_hidden_low), (acts[half][2], joined[half])
        return (normed_two, normed_two), (acts[half][0], acts[half][1])

    def other_sums(second):
        return swap(run_sums(*operands(1, second)))

    def taken(second, other):
        if part % 16 == 0:
            if second:
                here = jnp.zeros((1,), jnp.int32)
                return run_sums(*operands(0, second), other, here, shards * ring)[0]
            here = jnp.stack([place]).astype(jnp.int32)
            return list(run_sums(*operands(0, second), other, here, shards, ring))
        own = run_sums(*operands(0, second)).astype(F32)
        both = (own + other.astype(F32)).astype(BF).reshape(shards, ring, part, -1)
        if second:
            return both
        return [lax.dynamic_index_in_dim(both, place ^ bit, 1, keepdims=False) for bit in range(ring)]

    grad_post = sent(list(kept[8:]), "ctx")

    def backward(first, last, base, begin, saved, written=None):
        done = run_bwd(
            first, last, base, slot_tokens, gain_row, w_chain, rate_rows, norm_gain, grad_post, sums, begin, saved, written
        )
        return done[0], tuple(done[1:])

    sums = ((width, wide), (padded, width), (1, width), (chains, 1, head_dim), (chains, 1, head_dim))
    sums += tuple(value.shape for value in state)
    other_a, other_b = other_sums(False), other_sums(True)
    (grad_post, sum_rights) = tied(grad_post, (other_a, other_b))
    taken_a, taken_b = taken(False, sum_rights[0]), taken(True, sum_rights[1])
    grad_post, taken_a, taken_b, other_out = tied(grad_post, taken_a, taken_b, swap(output))
    grad_post = placed_along(grad_post, "ctx").reshape(span_all, cols)
    taken_b = taken_b.reshape(shards, ring, part, -1)
    sum_a, sum_b = sent(taken_a, "ctx"), lax.all_to_all(taken_b, "shard", 0, 0)
    back_high, ending = backward(middle, steps, middle, (), saved_high)
    ending, sum_a = tied(ending, sum_a)
    sum_a = fold_and_deal(sum_a, me, shards)
    _, sum_b = tied(sum_a[0], sum_b)
    sum_a = sent(list(sum_a), "shard")
    sum_b = folded([sum_b[number] for number in range(shards)])
    ending, sum_b = tied(ending, sum_b)
    sum_b = lax.psum_scatter(sum_b, "ctx", scatter_dimension=0, tiled=False)
    back_low_half, ending = backward(0, middle, 0, ending, saved_low, back_high)
    ending, back_low_half, sum_a, sum_b = tied(ending, back_low_half, sum_a, sum_b)
    back_part = back_low_half
    grad_big, grad_lr, grad_gain_one, grad_norm_gain, grad_norm_bias, *grad_state = ending
    block = ((shards, half_rows, wide), BF)
    keep, send = in_vmem(
        pack_grads_kernel, "pack_grads", [block, block], [(SMALL, wide)], [core],
        grad_big, grad_lr, grad_gain_one, grad_gain_two, *grad_state, grad_norm_gain, grad_norm_bias,
    )
    dealt = in_vmem(
        add_and_deal_kernel, "add_and_deal", [((half_rows, wide), BF)] * shards, [],
        [lax.axis_index("shard")], keep, swap(send),
    )
    back_rows = to_rows(back_part)
    chain_sum = sent(list(dealt), "shard")
    chain_sum, back_rows, sum_a, sum_b = tied(chain_sum, back_rows, sum_a, sum_b)
    chain_parts = exchanged(folded(chain_sum), "ctx")
    row_sum = jnp.concatenate([folded(sum_a), sum_b], axis=-1)
    chain_parts, row_sum = tied(chain_parts, row_sum)
    chain_sum = placed_along(chain_parts, "ctx")
    g_qkv, g_gate, g_lr, g_n1, g_n2, *g_rest = in_vmem(
        partial(unpack_grads_kernel, chains=chains), "unpack_grads",
        [
            ((depth, 3, local_heads * head_dim), F32), ((depth, local_heads * head_dim), F32),
            ((local_heads, depth), F32), ((1, depth), F32), ((1, depth), F32),
            (inner_w1.shape, F32), (inner_b1.shape, F32), (inner_w2.shape, F32), (inner_b2.shape, F32),
            (post_gain.shape, F32), (post_bias.shape, F32),
        ],
        [], [core], chain_sum, swap(chain_sum),
    )

    row_sum = spread(row_sum, "ctx")
    row_sum = row_sum.reshape(depth, -1).astype(F32)
    g_ffn_gate = row_sum[:, :units]
    g_ffn_up = row_sum[:, units : 2 * units]
    g_ffn_down = row_sum[:, 2 * units : 3 * units].T
    g_out = row_sum[:, 3 * units :].T

    back_one = jnp.sum(back_rows.astype(F32), axis=0)
    scale_one = row_scale(row_in)
    lifted = back_one * gain_row
    input_grad = (
        grad_hidden
        + scale_one * lifted
        - row_in * scale_one**3 * jnp.mean(lifted * row_in, axis=-1, keepdims=True)
    ).astype(BF)


    return (
        in_turn(output, other_out),
        in_turn(input_grad, swap(input_grad)),
        g_n1[0],
        g_qkv,
        g_lr.T,
        *g_rest,
        g_gate,
        g_out,
        g_n2[0],
        g_ffn_gate,
        g_ffn_up,
        g_ffn_down,
    )


def solution(mesh):
    in_specs = (
        P("shard", "ctx", None),
        P("shard"),
        P("shard"),
        P("shard", None, "tp"),
        P("shard", "tp"),
        P("tp", None, "shard"),
        P("tp", "shard"),
        P("tp", None, "shard"),
        P("tp", "shard"),
        P("tp", "shard"),
        P("tp", "shard"),
        P("shard", "tp"),
        P("tp", "shard"),
        P("shard"),
        P("shard", "tp"),
        P("shard", "tp"),
        P("tp", "shard"),
        P("shard", "ctx", None),
    )
    out_specs = (
        P("shard", "ctx", None),
        P("shard", "ctx", None),
        P("shard"),
        P("shard", None, "tp"),
        P("shard", "tp"),
        P("tp", None, "shard"),
        P("tp", "shard"),
        P("tp", None, "shard"),
        P("tp", "shard"),
        P("tp", "shard"),
        P("tp", "shard"),
        P("shard", "tp"),
        P("tp", "shard"),
        P("shard"),
        P("shard", "tp"),
        P("shard", "tp"),
        P("tp", "shard"),
    )
    return jax.shard_map(
        on_device, mesh=mesh, in_specs=in_specs, out_specs=out_specs, check_vma=False
    )
```
